32 devices in a mesh: group: 2 (over y), row: 4 (over z), col: 4 (over x, core).
Axes of the slice: x: 2, y: 2, z: 4, core: 2. Of those that a mesh axis runs over, the one named last changes fastest.
Arguments:
- pair_acts: bfloat16 [128, 64, 128], P(('group', 'row'), 'col'), parts along dimension 0, may hold values from -6 to 6
- pair_mask: int32 [128, 64], P(('group', 'row'), 'col'), parts along dimension 0, may hold values 0 or 1
- crop_length: int32 [2], P('group'), parts along dimension 0, may hold values from 32 to 64
- cotangent: bfloat16 [128, 64, 128], P(('group', 'row'), 'col'), parts along dimension 0, may hold values from -6 to 6
- in_weights: bfloat16 [128, 640], replicated, may hold values from -0.5 to 0.5
- out_weight: bfloat16 [128, 128], replicated, may hold values from -0.5 to 0.5
Outputs:
- update: bfloat16 [128, 64, 128], P(('group', 'row'), 'col'), parts along dimension 0
- pair_grad: bfloat16 [128, 64, 128], P(('group', 'row'), 'col'), parts along dimension 0
The draws below stay inside these ranges and needn't reach their ends.
There are 2 independent parts, one for each index of `group`. The reference program is written for one: setup_inputs(seed, part) draws one part's arguments, and reference() takes and returns one part's arrays. A program takes and returns all parts, laid end to end along the dimension named above; an argument that names none is the same for every part. Nothing has to cross between parts.
Inputs may be any that keep to these rules, and one draw needn't show every extreme that they name: `pair_mask`: 1 marks a token pair that takes part, 0 one that does not. Tokens at positions crop_length and beyond are padding.
All inputs are finite; a program needn't handle non-finite values. No bound on the sum of `pair_mask` on one device may be relied on, other than what follows from the above.
Results may differ from the reference program's by a relative error of at most 0.014.
Values may be sent and summed in bfloat16 or wider, within the bound.
No kernel may reach another device: no remote copies, remote signals or barrier semaphores. Data moves between devices by JAX's collectives and lax.ppermute only.
A program may use at most 128 MiB of HBM per device.

```python
import jax
import jax.numpy as jnp
from jax import lax

C = 128
N = 64


def touch_ends(result, stream_key, smallest, high):
    spot = [jax.random.randint(jax.random.fold_in(stream_key, axis), (), 0, length) for axis, length in enumerate(result.shape)]
    longest = result.shape.index(max(result.shape))
    next_to = spot[:longest] + [(spot[longest] + 1) % result.shape[longest]] + spot[longest + 1:]
    return result.at[tuple(spot)].set(smallest).at[tuple(next_to)].set(high)


def steps_of(own_key, extent, split, low, high):
    factor_of, own = 1.0, jax.random.fold_in(own_key, 6)
    for position, parts in split:
        steps = jnp.exp(jax.random.uniform(jax.random.fold_in(own, position), (parts,), jnp.float32, low / len(split), high / len(split)))
        factor_of = factor_of * jnp.repeat(steps, extent[position] // parts).reshape([-1 if axis == position else 1 for axis in range(len(extent))])
    return factor_of


def scatter_about(rng, shape, deviation, limit, cuts=(), dtype=jnp.bfloat16):
    result = deviation * jax.random.normal(rng, shape, jnp.float32)
    if cuts:
        result = result * steps_of(rng, shape, cuts, -0.22, 0.18)
    return jnp.clip(result, -limit, limit).astype(dtype)


def setup_inputs(seed: int = 0, part: int = 0) -> dict:
    arg_keys = jax.random.split(jax.random.key(seed), 7)
    part_keys = jax.random.split(jax.random.fold_in(arg_keys[6], part), 7)
    return {
        "pair_acts": scatter_about(part_keys[0], (N, N, C), 1.0, 6.0, ((0, 4), (1, 4))),
        "pair_mask": touch_ends((jax.random.randint(part_keys[1], (N, N), 0, 8) < 7).astype(jnp.int32), jax.random.fold_in(part_keys[1], 1), 0, 1),
        "crop_length": jax.random.randint(part_keys[2], (1,), N // 2, N + 1).astype(jnp.int32),
        "cotangent": scatter_about(part_keys[3], (N, N, C), 1.0, 6.0, ((0, 4), (1, 4))),
        "in_weights": scatter_about(arg_keys[4], (C, 5 * C), C ** -0.5, 0.5),
        "out_weight": scatter_about(arg_keys[5], (C, C), C ** -0.5, 0.5),
    }


epsilon = 1e-05

def normalize(values):
    center = values - lax.optimization_barrier(jnp.mean(values, axis=-1, keepdims=True))
    variance = lax.optimization_barrier(jnp.mean(center * center, axis=-1, keepdims=True))
    scale = lax.rsqrt(variance + epsilon)
    return (center * scale, scale)

def normalize_back(normed, scale, upstream):
    average = lax.optimization_barrier(jnp.mean(upstream, axis=-1, keepdims=True))
    project = lax.optimization_barrier(jnp.mean(upstream * normed, axis=-1, keepdims=True))
    return scale * (upstream - average - normed * project)

def reference(pair_acts, pair_mask, crop_length, cotangent, in_weights, out_weight):
    tokens = pair_acts.shape[0]
    channels = pair_acts.shape[2]
    live = (jnp.arange(tokens).astype(jnp.int32) < crop_length[0]).astype(jnp.float32)
    pair_keep = (pair_mask.astype(jnp.float32) * live[:, None] * live[None, :])[:, :, None]
    normed, scale_in = normalize(pair_acts.astype(jnp.float32))
    projected = jnp.dot(normed.astype(jnp.bfloat16).reshape(-1, channels), in_weights, preferred_element_type=jnp.float32).reshape(tokens, tokens, 5, channels)
    left_value = projected[:, :, 0]
    left_gate = projected[:, :, 1]
    right_value = projected[:, :, 2]
    right_gate = projected[:, :, 3]
    out_gate = projected[:, :, 4]
    left_open = jax.nn.sigmoid(left_gate)
    right_open = jax.nn.sigmoid(right_gate)
    out_open = jax.nn.sigmoid(out_gate)
    left_tile = (left_open * left_value * pair_keep).astype(jnp.bfloat16)
    right_tile = (right_open * right_value * pair_keep).astype(jnp.bfloat16)
    left_wide = left_tile.astype(jnp.float32)
    right_wide = right_tile.astype(jnp.float32)
    triangle = jnp.einsum('kic,kjc->ijc', left_wide, right_wide)
    tri_normed, tri_scale = normalize(triangle)
    linear = jnp.dot(tri_normed.astype(jnp.bfloat16).reshape(-1, channels), out_weight, preferred_element_type=jnp.float32).reshape(tokens, tokens, channels)
    update = (out_open * linear).astype(jnp.bfloat16)
    upstream = cotangent.astype(jnp.float32)
    lin_grad = (upstream * out_open).astype(jnp.bfloat16)
    out_gate_grad = upstream * linear * out_open * (1.0 - out_open)
    tri_normed_grad = jnp.dot(lin_grad.reshape(-1, channels), out_weight.T, preferred_element_type=jnp.float32).reshape(tokens, tokens, channels)
    tri_grad = normalize_back(tri_normed, tri_scale, tri_normed_grad).astype(jnp.bfloat16)
    tri_wide = tri_grad.astype(jnp.float32)
    left_grad = jnp.einsum('ijc,kjc->kic', tri_wide, right_wide)
    right_grad = jnp.einsum('ijc,kic->kjc', tri_wide, left_wide)
    left_back = left_grad * pair_keep
    right_back = right_grad * pair_keep
    grads = jnp.stack([left_back * left_open, left_back * left_value * left_open * (1.0 - left_open), right_back * right_open, right_back * right_value * right_open * (1.0 - right_open), out_gate_grad], axis=2)
    normed_grad = jnp.dot(grads.astype(jnp.bfloat16).reshape(-1, 5 * channels), in_weights.T, preferred_element_type=jnp.float32).reshape(tokens, tokens, channels)
    pair_grad = normalize_back(normed, scale_in, normed_grad).astype(jnp.bfloat16)
    return (update, pair_grad)
```

```python
import functools

import jax
import jax.numpy as jnp
from jax import lax
from jax.experimental import pallas as pl
from jax.experimental.pallas import tpu as pltpu
from jax.sharding import PartitionSpec as P

epsilon = 1e-05
f32 = jnp.float32
bf16 = jnp.bfloat16


def mean_lanes(values):
    return jnp.sum(values, axis=-1, keepdims=True) * (1.0 / values.shape[-1])


def normalize(values):
    center = values - mean_lanes(values)
    variance = mean_lanes(center * center)
    scale = lax.rsqrt(variance + epsilon)
    return (center * scale, scale)


def normalize_back(normed, scale, upstream):
    average = mean_lanes(upstream)
    project = mean_lanes(upstream * normed)
    return scale * (upstream - average - normed * project)


def sigmoid(values):
    return 1.0 / (1.0 + jnp.exp(-values))


def dot(a, b):
    return jnp.dot(a, b, preferred_element_type=f32)


def dot_t(a, b):
    return lax.dot_general(a, b, (((1,), (1,)), ((), ())), preferred_element_type=f32)


def keep_rows(mask_ref, crop_ref):
    size = mask_ref.shape[0]
    rows = lax.axis_index("row") * size + lax.broadcasted_iota(jnp.int32, (size, size), 0)
    cols = lax.axis_index("col") * size + lax.broadcasted_iota(jnp.int32, (size, size), 1)
    live = jnp.where(jnp.maximum(rows, cols) < crop_ref[0], 1.0, 0.0)
    keep = (mask_ref[...].astype(f32) * live).astype(bf16)
    pair = lax.broadcasted_iota(jnp.int32, (size * size, size), 0)
    lane = lax.broadcasted_iota(jnp.int32, (size * size, size), 1)
    pick_row = jnp.where(pair // size == lane, 1.0, 0.0).astype(bf16)
    pick_col = jnp.where(pair % size == lane, 1.0, 0.0)
    spread = (dot(pick_row, keep) * pick_col).astype(bf16)
    return dot(spread, jnp.ones((size, 128), bf16))


def tiles_kernel(acts_ref, mask_ref, crop_ref, weights_ref, left_ref, right_ref):
    size, _, channels = acts_ref.shape
    normed, _ = normalize(acts_ref[...].astype(f32).reshape(size * size, channels))
    projected = dot(normed.astype(bf16), weights_ref[:, : 4 * channels])
    keep = keep_rows(mask_ref, crop_ref)
    for block, out_ref in ((0, left_ref), (2, right_ref)):
        value = projected[:, block * channels : (block + 1) * channels]
        gate = projected[:, (block + 1) * channels : (block + 2) * channels]
        tile = (sigmoid(gate) * value * keep).astype(bf16)
        out_ref[...] = tile.reshape(size, size, channels)


def factors_kernel(
    acts_ref, mask_ref, crop_ref, cotangent_ref, weights_ref, out_weight_ref,
    normed_ref, scale_ref, factor_ref, open_ref, gate_factor_ref, upstream_ref,
):
    size, _, channels = acts_ref.shape
    pairs = size * size
    normed, scale = normalize(acts_ref[...].astype(f32).reshape(pairs, channels))
    normed_ref[...] = normed
    scale_ref[...] = jnp.broadcast_to(scale, (pairs, channels))
    projected = dot(normed.astype(bf16), weights_ref[...])
    keep = keep_rows(mask_ref, crop_ref)
    for block in (0, 2):
        value = projected[:, block * channels : (block + 1) * channels]
        gate = projected[:, (block + 1) * channels : (block + 2) * channels]
        opened = sigmoid(gate)
        factor_ref[block] = keep * opened
        factor_ref[block + 1] = keep * value * opened * (1.0 - opened)
    out_open = sigmoid(projected[:, 4 * channels :])
    cotangent = cotangent_ref[...].astype(f32).reshape(pairs, channels)
    lin_grad = (cotangent * out_open).astype(bf16)
    open_ref[...] = out_open
    gate_factor_ref[...] = cotangent * out_open * (1.0 - out_open)
    upstream_ref[...] = dot_t(lin_grad, out_weight_ref[...])


def triangle_kernel(grid_size, *refs):
    left_in, right_in = refs[:grid_size], refs[grid_size : 2 * grid_size]
    upstream_ref = refs[2 * grid_size]
    outs = refs[2 * grid_size + 1 :]
    tri_normed_ref = outs[0]
    left_out, right_out = outs[1 : grid_size + 1], outs[grid_size + 1 : 2 * grid_size + 1]
    left, right, grad = outs[2 * grid_size + 1 :]
    size, _, channels = left_in[0].shape
    row, col = lax.axis_index("row"), lax.axis_index("col")
    for shift in range(grid_size):
        start = lax.rem(col + (grid_size - shift), grid_size) * size
        left[pl.ds(start, size)] = left_in[shift][...].astype(f32)
        start = lax.rem(row + (grid_size - shift), grid_size) * size
        right[pl.ds(start, size)] = right_in[shift][...].astype(f32)

    def step(k, sums):
        other = right[k]
        return tuple(sums[i] + left[k, pl.ds(i, 1), :] * other for i in range(size))

    zero = jnp.zeros((size, channels), f32)
    sums = lax.fori_loop(0, grid_size * size, step, (zero,) * size)
    for i in range(size):
        here = pl.ds(i * size, size)
        tri_normed, scale = normalize(sums[i])
        tri_normed_ref[here, :] = tri_normed
        back = normalize_back(tri_normed, scale, upstream_ref[here, :])
        grad[here, :] = back.astype(bf16).astype(f32)

    grads = [grad[pl.ds(i * size, size), :] for i in range(size)]
    for shift in range(grid_size):
        start = lax.rem(row + shift, grid_size) * size
        out = right_out[shift]

        def step(k, _):
            total = left[start + k, pl.ds(0, 1), :] * grads[0]
            for i in range(1, size):
                total = total + left[start + k, pl.ds(i, 1), :] * grads[i]
            out[k] = total.astype(bf16)
            return 0

        lax.fori_loop(0, size, step, 0)

    grads_t = [grad[pl.ds(j, size, stride=size), :] for j in range(size)]
    for shift in range(grid_size):
        start = lax.rem(col + shift, grid_size) * size
        out = left_out[shift]

        def step(k, _):
            total = right[start + k, pl.ds(0, 1), :] * grads_t[0]
            for j in range(1, size):
                total = total + right[start + k, pl.ds(j, 1), :] * grads_t[j]
            out[k] = total.astype(bf16)
            return 0

        lax.fori_loop(0, size, step, 0)


def update_kernel(
    tri_normed_ref, open_ref, gate_factor_ref, weights_ref, out_weight_ref, update_ref, normed_grad_ref
):
    size, _, channels = update_ref.shape
    linear = dot(tri_normed_ref[...].astype(bf16), out_weight_ref[...])
    update = (open_ref[...] * linear).astype(bf16)
    update_ref[...] = update.reshape(size, size, channels)
    out_gate_grad = (gate_factor_ref[...] * linear).astype(bf16)
    normed_grad_ref[...] = dot_t(out_gate_grad, weights_ref[:, 4 * channels :])


def sum_kernel(grid_size, *refs):
    total = refs[0][...].astype(f32)
    for ref in refs[1:grid_size]:
        total = total + ref[...].astype(f32)
    refs[grid_size][...] = total.astype(bf16)


def back_kernel(grid_size, left_ref, *refs):
    right_in = refs[:grid_size]
    normed_ref, scale_ref, factor_ref, partial_ref, weights_ref, out_ref = refs[grid_size:]
    size, _, channels = out_ref.shape
    pairs = size * size
    left = left_ref[...].astype(f32).reshape(pairs, channels)
    right = right_in[0][...].astype(f32)
    for ref in right_in[1:]:
        right = right + ref[...].astype(f32)
    right = right.astype(bf16).astype(f32).reshape(pairs, channels)
    grads = jnp.concatenate(
        [(total * factor_ref[block]).astype(bf16) for block, total in enumerate((left, left, right, right))],
        axis=1,
    )
    normed_grad = partial_ref[...] + dot_t(grads, weights_ref[:, : 4 * channels])
    back = normalize_back(normed_ref[...], scale_ref[...], normed_grad)
    out_ref[...] = back.astype(bf16).reshape(size, size, channels)


def call(kernel, outs, *args, scratch=(), flops=0, smem=()):
    spec = pl.BlockSpec(memory_space=pltpu.VMEM)
    total = sum(a.size * a.dtype.itemsize for a in (*args, *outs))
    return pl.pallas_call(
        kernel,
        out_shape=tuple(outs),
        in_specs=[pl.BlockSpec(memory_space=pltpu.SMEM) if n in smem else spec for n in range(len(args))],
        out_specs=(spec,) * len(outs),
        scratch_shapes=scratch,
        compiler_params=pltpu.CompilerParams(vmem_limit_bytes=24 * 2**20),
        cost_estimate=pl.CostEstimate(flops=flops, bytes_accessed=total, transcendentals=0),
    )(*args)


def local(pair_acts, pair_mask, crop_length, cotangent, in_weights, out_weight):
    size, _, channels = pair_acts.shape
    pairs = size * size
    n = lax.axis_size("row")
    tile = jax.ShapeDtypeStruct((size, size, channels), bf16)
    flat = jax.ShapeDtypeStruct((pairs, channels), f32)

    def shift_by(values, axis, shift):
        if shift == 0:
            return values
        return lax.ppermute(values, axis, [(a, (a + shift) % n) for a in range(n)])

    def mirror(values):
        return lax.ppermute(values, ("row", "col"), [(a * n + b, b * n + a) for a in range(n) for b in range(n)])

    left, right = call(
        tiles_kernel, (tile, tile), pair_acts, pair_mask, crop_length, in_weights,
        smem=(2,), flops=2 * pairs * channels * 4 * channels,
    )
    mirrored = mirror(left)
    rights = [shift_by(right, "row", shift) for shift in range(n)]
    normed, scale, factors, out_open, gate_factor, upstream = call(
        factors_kernel,
        (flat, flat, jax.ShapeDtypeStruct((4, pairs, channels), f32), flat, flat, flat),
        pair_acts, pair_mask, crop_length, cotangent, in_weights, out_weight,
        smem=(2,), flops=2 * pairs * channels * 6 * channels,
    )
    lefts = [shift_by(mirrored, "col", shift) for shift in range(n)]
    tri_normed, *terms = call(
        functools.partial(triangle_kernel, n),
        (flat,) + (tile,) * (2 * n),
        *lefts, *rights, upstream,
        scratch=[
            pltpu.VMEM((n * size, size, channels), f32),
            pltpu.VMEM((n * size, size, channels), f32),
            pltpu.VMEM((pairs, channels), f32),
        ],
        flops=6 * n * size * pairs * channels,
    )
    left_terms = [shift_by(values, "col", shift) for shift, values in enumerate(terms[:n])]
    right_terms = [shift_by(values, "row", shift) for shift, values in enumerate(terms[n:])]
    update, partial = call(
        update_kernel, (tile, flat), tri_normed, out_open, gate_factor, in_weights, out_weight,
        flops=4 * pairs * channels * channels,
    )
    (left_sum,) = call(functools.partial(sum_kernel, n), (tile,), *left_terms)
    left_grad = mirror(left_sum)
    (pair_grad,) = call(
        functools.partial(back_kernel, n), (tile,),
        left_grad, *right_terms, normed, scale, factors, partial, in_weights,
        flops=2 * pairs * channels * 4 * channels,
    )
    return (update, pair_grad)


def solution(mesh):
    return jax.shard_map(
        local,
        mesh=mesh,
        in_specs=(
            P(("group", "row"), "col", None),
            P(("group", "row"), "col"),
            P("group"),
            P(("group", "row"), "col", None),
            P(),
            P(),
        ),
        out_specs=(P(("group", "row"), "col", None), P(("group", "row"), "col", None)),
        check_vma=False,
    )
```

```python
import functools

import jax
import jax.numpy as jnp
from jax import lax
from jax.experimental import pallas as pl
from jax.experimental.pallas import tpu as pltpu
from jax.sharding import PartitionSpec as P

epsilon = 1e-05
f32 = jnp.float32
bf16 = jnp.bfloat16


def mean_lanes(values):
    return jnp.sum(values, axis=-1, keepdims=True) * (1.0 / values.shape[-1])


def normalize(values):
    center = values - mean_lanes(values)
    variance = mean_lanes(center * center)
    scale = lax.rsqrt(variance + epsilon)
    return (center * scale, scale)


def normalize_back(normed, scale, upstream):
    average = mean_lanes(upstream)
    project = mean_lanes(upstream * normed)
    return scale * (upstream - average - normed * project)


def sigmoid(values):
    return 1.0 / (1.0 + jnp.exp(-values))


def dot(a, b):
    return jnp.dot(a, b, preferred_element_type=f32)


def dot_t(a, b):
    return lax.dot_general(a, b, (((1,), (1,)), ((), ())), preferred_element_type=f32)


def keep_rows(mask_ref, crop_ref):
    size = mask_ref.shape[0]
    rows = lax.axis_index("row") * size + lax.broadcasted_iota(jnp.int32, (size, size), 0)
    cols = lax.axis_index("col") * size + lax.broadcasted_iota(jnp.int32, (size, size), 1)
    live = jnp.where(jnp.maximum(rows, cols) < crop_ref[0], 1.0, 0.0)
    keep = (mask_ref[...].astype(f32) * live).astype(bf16)
    pair = lax.broadcasted_iota(jnp.int32, (size * size, size), 0)
    lane = lax.broadcasted_iota(jnp.int32, (size * size, size), 1)
    pick_row = jnp.where(pair // size == lane, 1.0, 0.0).astype(bf16)
    pick_col = jnp.where(pair % size == lane, 1.0, 0.0)
    spread = (dot(pick_row, keep) * pick_col).astype(bf16)
    return dot(spread, jnp.ones((size, 128), bf16))


def start_copies(sems, *pairs):
    copies = [pltpu.make_async_copy(src, dst, sems.at[n]) for n, (src, dst) in enumerate(pairs)]
    for copy in copies:
        copy.start()
    return copies


def tiles_kernel(
    acts_in, mask_in, crop_ref, weights_in, left_ref, right_ref, acts_ref, mask_ref, weights_ref, sems
):
    copies = start_copies(sems, (acts_in, acts_ref), (weights_in, weights_ref), (mask_in, mask_ref))
    size, _, channels = acts_ref.shape
    copies[0].wait()
    normed, _ = normalize(acts_ref[...].astype(f32).reshape(size * size, channels))
    normed = normed.astype(bf16)
    copies[1].wait()
    copies[2].wait()
    projected = dot(normed, weights_ref[:, : 4 * channels])
    keep = keep_rows(mask_ref, crop_ref)
    for block, out_ref in ((0, left_ref), (2, right_ref)):
        value = projected[:, block * channels : (block + 1) * channels]
        gate = projected[:, (block + 1) * channels : (block + 2) * channels]
        tile = (sigmoid(gate) * value * keep).astype(bf16)
        out_ref[...] = tile.reshape(size, size, channels)


def factors_kernel(
    acts_in, mask_in, crop_ref, cotangent_in, weights_in, out_weight_in,
    normed_ref, scale_ref, factor_ref, open_ref, gate_factor_ref, upstream_ref,
    acts_ref, mask_ref, cotangent_ref, weights_ref, out_weight_ref, sems,
):
    copies = start_copies(
        sems, (acts_in, acts_ref), (weights_in, weights_ref), (mask_in, mask_ref),
        (cotangent_in, cotangent_ref), (out_weight_in, out_weight_ref),
    )
    size, _, channels = acts_ref.shape
    pairs = size * size
    copies[0].wait()
    normed, scale = normalize(acts_ref[...].astype(f32).reshape(pairs, channels))
    normed_ref[...] = normed
    scale_ref[...] = jnp.broadcast_to(scale, (pairs, channels))
    for copy in copies[1:]:
        copy.wait()
    projected = dot(normed.astype(bf16), weights_ref[...])
    keep = keep_rows(mask_ref, crop_ref)
    for block in (0, 2):
        value = projected[:, block * channels : (block + 1) * channels]
        gate = projected[:, (block + 1) * channels : (block + 2) * channels]
        opened = sigmoid(gate)
        factor_ref[block] = keep * opened
        factor_ref[block + 1] = keep * value * opened * (1.0 - opened)
    out_open = sigmoid(projected[:, 4 * channels :])
    cotangent = cotangent_ref[...].astype(f32).reshape(pairs, channels)
    lin_grad = (cotangent * out_open).astype(bf16)
    open_ref[...] = out_open
    gate_factor_ref[...] = cotangent * out_open * (1.0 - out_open)
    upstream_ref[...] = dot_t(lin_grad, out_weight_ref[...])


def weighted_sums(weights, start, terms, out):
    def step(k, _):
        total = weights[start + k, pl.ds(0, 1), :] * terms[0]
        for n in range(1, len(terms)):
            total = total + weights[start + k, pl.ds(n, 1), :] * terms[n]
        out[k] = total.astype(bf16)
        return 0

    lax.fori_loop(0, out.shape[0], step, 0)


def triangle_kernel(grid_size, *refs):
    left_in, right_in = refs[:grid_size], refs[grid_size : 2 * grid_size]
    upstream_ref = refs[2 * grid_size]
    tri_normed_ref, left, grad, *left_out = refs[2 * grid_size + 1 : -1]
    right = refs[-1]
    size, _, channels = left_in[0].shape
    row, col = lax.axis_index("row"), lax.axis_index("col")
    for step in range(grid_size):
        left[pl.ds((col ^ step) * size, size)] = left_in[step][...].astype(f32)
        right[pl.ds((row ^ step) * size, size)] = right_in[step][...].astype(f32)

    def step(k, sums):
        other = right[k]
        return tuple(sums[i] + left[k, pl.ds(i, 1), :] * other for i in range(size))

    zero = jnp.zeros((size, channels), f32)
    sums = lax.fori_loop(0, grid_size * size, step, (zero,) * size)
    for i in range(size):
        here = pl.ds(i * size, size)
        tri_normed, scale = normalize(sums[i])
        tri_normed_ref[here, :] = tri_normed
        back = normalize_back(tri_normed, scale, upstream_ref[here, :])
        grad[here, :] = back.astype(bf16).astype(f32)

    grads = [grad[pl.ds(j, size, stride=size), :] for j in range(size)]
    for step in range(grid_size):
        weighted_sums(right, (col ^ step) * size, grads, left_out[step])


def right_kernel(grid_size, left, grad, *right_out):
    size = right_out[0].shape[0]
    row = lax.axis_index("row")
    grads = [grad[pl.ds(i * size, size), :] for i in range(size)]
    for step in range(grid_size):
        weighted_sums(left, (row ^ step) * size, grads, right_out[step])


def update_kernel(
    tri_normed_ref, open_ref, gate_factor_ref, weights_ref, out_weight_ref, update_ref, normed_grad_ref
):
    size, _, channels = update_ref.shape
    linear = dot(tri_normed_ref[...].astype(bf16), out_weight_ref[...])
    update = (open_ref[...] * linear).astype(bf16)
    update_ref[...] = update.reshape(size, size, channels)
    out_gate_grad = (gate_factor_ref[...] * linear).astype(bf16)
    normed_grad_ref[...] = dot_t(out_gate_grad, weights_ref[:, 4 * channels :])


def sum_kernel(grid_size, *refs):
    total = refs[0][...].astype(f32)
    for ref in refs[1:grid_size]:
        total = total + ref[...].astype(f32)
    refs[grid_size][...] = total.astype(bf16)


def back_kernel(grid_size, left_ref, *refs):
    right_in = refs[:grid_size]
    normed_ref, scale_ref, factor_ref, partial_ref, weights_ref, out_ref = refs[grid_size:]
    size, _, channels = out_ref.shape
    pairs = size * size
    left = left_ref[...].astype(f32).reshape(pairs, channels)
    right = right_in[0][...].astype(f32)
    for ref in right_in[1:]:
        right = right + ref[...].astype(f32)
    right = right.astype(bf16).astype(f32).reshape(pairs, channels)
    grads = jnp.concatenate(
        [(total * factor_ref[block]).astype(bf16) for block, total in enumerate((left, left, right, right))],
        axis=1,
    )
    normed_grad = partial_ref[...] + dot_t(grads, weights_ref[:, : 4 * channels])
    back = normalize_back(normed_ref[...], scale_ref[...], normed_grad)
    out_ref[...] = back.astype(bf16).reshape(size, size, channels)


def call(kernel, outs, *args, scratch=(), flops=0, smem=(), hbm=()):
    spec = pl.BlockSpec(memory_space=pltpu.VMEM)
    total = sum(a.size * a.dtype.itemsize for a in (*args, *outs))
    specs = [spec] * len(args)
    for n in smem:
        specs[n] = pl.BlockSpec(memory_space=pltpu.SMEM)
    args = list(args)
    for n in hbm:
        specs[n] = pl.BlockSpec(memory_space=pltpu.HBM)
        args[n] = pltpu.with_memory_space_constraint(args[n], pltpu.HBM)
    return pl.pallas_call(
        kernel,
        out_shape=tuple(outs),
        in_specs=specs,
        out_specs=(spec,) * len(outs),
        scratch_shapes=scratch,
        compiler_params=pltpu.CompilerParams(vmem_limit_bytes=24 * 2**20),
        cost_estimate=pl.CostEstimate(flops=flops, bytes_accessed=total, transcendentals=0),
    )(*args)


def local(pair_acts, pair_mask, crop_length, cotangent, in_weights, out_weight):
    size, _, channels = pair_acts.shape
    pairs = size * size
    n = lax.axis_size("row")
    tile = jax.ShapeDtypeStruct((size, size, channels), bf16)
    flat = jax.ShapeDtypeStruct((pairs, channels), f32)

    def swap(values, axis, step):
        return lax.ppermute(values, axis, [(a, a ^ step) for a in range(n)])

    def mirror(values):
        return lax.ppermute(values, ("row", "col"), [(a * n + b, b * n + a) for a in range(n) for b in range(n)])

    left, right = call(
        tiles_kernel, (tile, tile), pair_acts, pair_mask, crop_length, in_weights,
        smem=(2,), hbm=(0, 1, 3), flops=2 * pairs * channels * 4 * channels,
        scratch=[
            pltpu.VMEM(pair_acts.shape, bf16),
            pltpu.VMEM(pair_mask.shape, jnp.int32),
            pltpu.VMEM(in_weights.shape, bf16),
            pltpu.SemaphoreType.DMA((3,)),
        ],
    )
    mirrored = mirror(left)
    rights = [right] + [swap(right, "row", step) for step in range(n - 1, 0, -1)][::-1]
    normed, scale, factors, out_open, gate_factor, upstream = call(
        factors_kernel,
        (flat, flat, jax.ShapeDtypeStruct((4, pairs, channels), f32), flat, flat, flat),
        pair_acts, pair_mask, crop_length, cotangent, in_weights, out_weight,
        smem=(2,), hbm=(0, 1, 3, 4, 5), flops=2 * pairs * channels * 6 * channels,
        scratch=[
            pltpu.VMEM(pair_acts.shape, bf16),
            pltpu.VMEM(pair_mask.shape, jnp.int32),
            pltpu.VMEM(cotangent.shape, bf16),
            pltpu.VMEM(in_weights.shape, bf16),
            pltpu.VMEM(out_weight.shape, bf16),
            pltpu.SemaphoreType.DMA((5,)),
        ],
    )
    lefts = [mirrored] + [swap(mirrored, "col", step) for step in range(1, n)]
    panel = jax.ShapeDtypeStruct((n * size, size, channels), f32)
    tri_normed, left_panel, tri_grad, *left_terms = call(
        functools.partial(triangle_kernel, n),
        (flat, panel, flat) + (tile,) * n,
        *lefts, *rights, upstream,
        scratch=[pltpu.VMEM(panel.shape, f32)],
        flops=4 * n * size * pairs * channels,
    )
    left_terms = [left_terms[0]] + [swap(left_terms[step], "col", step) for step in range(1, n)]
    right_terms = call(
        functools.partial(right_kernel, n), (tile,) * n, left_panel, tri_grad,
        flops=2 * n * size * pairs * channels,
    )
    right_terms = [right_terms[0]] + [swap(right_terms[step], "row", step) for step in range(1, n)]
    update, partial = call(
        update_kernel, (tile, flat), tri_normed, out_open, gate_factor, in_weights, out_weight,
        flops=4 * pairs * channels * channels,
    )
    (left_sum,) = call(functools.partial(sum_kernel, n), (tile,), *left_terms)
    left_grad = mirror(left_sum)
    (pair_grad,) = call(
        functools.partial(back_kernel, n), (tile,),
        left_grad, *right_terms, normed, scale, factors, partial, in_weights,
        flops=2 * pairs * channels * 4 * channels,
    )
    return (update, pair_grad)


def solution(mesh):
    return jax.shard_map(
        local,
        mesh=mesh,
        in_specs=(
            P(("group", "row"), "col", None),
            P(("group", "row"), "col"),
            P("group"),
            P(("group", "row"), "col", None),
            P(),
            P(),
        ),
        out_specs=(P(("group", "row"), "col", None), P(("group", "row"), "col", None)),
        check_vma=False,
    )
```

```python
import functools

import jax
import jax.numpy as jnp
from jax import lax
from jax.experimental import pallas as pl
from jax.experimental.pallas import tpu as pltpu
from jax.sharding import PartitionSpec as P

epsilon = 1e-05
f32 = jnp.float32
bf16 = jnp.bfloat16


def mean_lanes(values):
    return jnp.sum(values, axis=-1, keepdims=True) * (1.0 / values.shape[-1])


def normalize(values):
    center = values - mean_lanes(values)
    variance = mean_lanes(center * center)
    scale = lax.rsqrt(variance + epsilon)
    return (center * scale, scale)


def normalize_back(normed, scale, upstream):
    average = mean_lanes(upstream)
    project = mean_lanes(upstream * normed)
    return scale * (upstream - average - normed * project)


def sigmoid(values):
    return 1.0 / (1.0 + jnp.exp(-values))


def dot(a, b):
    return jnp.dot(a, b, preferred_element_type=f32)


def dot_t(a, b):
    return lax.dot_general(a, b, (((1,), (1,)), ((), ())), preferred_element_type=f32)


def keep_rows(mask_ref, crop_ref):
    size = mask_ref.shape[0]
    rows = lax.axis_index("row") * size + lax.broadcasted_iota(jnp.int32, (size, size), 0)
    cols = lax.axis_index("col") * size + lax.broadcasted_iota(jnp.int32, (size, size), 1)
    live = jnp.where(jnp.maximum(rows, cols) < crop_ref[0], 1.0, 0.0)
    keep = (mask_ref[...].astype(f32) * live).astype(bf16)
    pair = lax.broadcasted_iota(jnp.int32, (size * size, size), 0)
    lane = lax.broadcasted_iota(jnp.int32, (size * size, size), 1)
    pick_row = jnp.where(pair // size == lane, 1.0, 0.0).astype(bf16)
    pick_col = jnp.where(pair % size == lane, 1.0, 0.0)
    spread = (dot(pick_row, keep) * pick_col).astype(bf16)
    return dot(spread, jnp.ones((size, 128), bf16))


def start_copies(sems, *pairs):
    copies = [pltpu.make_async_copy(src, dst, sems.at[n]) for n, (src, dst) in enumerate(pairs)]
    for copy in copies:
        copy.start()
    return copies


def tiles_kernel(
    acts_in, mask_in, crop_ref, weights_in, left_ref, right_ref, acts_ref, mask_ref, weights_ref, sems
):
    copies = start_copies(sems, (acts_in, acts_ref), (weights_in, weights_ref), (mask_in, mask_ref))
    size, _, channels = acts_ref.shape
    copies[0].wait()
    normed, _ = normalize(acts_ref[...].astype(f32).reshape(size * size, channels))
    normed = normed.astype(bf16)
    copies[1].wait()
    copies[2].wait()
    projected = dot(normed, weights_ref[:, : 4 * channels])
    keep = keep_rows(mask_ref, crop_ref)
    for block, out_ref in ((0, left_ref), (2, right_ref)):
        value = projected[:, block * channels : (block + 1) * channels]
        gate = projected[:, (block + 1) * channels : (block + 2) * channels]
        tile = (sigmoid(gate) * value * keep).astype(bf16)
        out_ref[...] = tile.reshape(size, size, channels)


def factors_kernel(
    acts_in, mask_in, crop_ref, cotangent_in, weights_in, out_weight_in,
    normed_ref, scale_ref, factor_ref, open_ref, gate_factor_ref, upstream_ref,
    acts_ref, mask_ref, cotangent_ref, weights_ref, out_weight_ref, sems,
):
    copies = start_copies(
        sems, (acts_in, acts_ref), (weights_in, weights_ref), (mask_in, mask_ref),
        (cotangent_in, cotangent_ref), (out_weight_in, out_weight_ref),
    )
    size, _, channels = acts_ref.shape
    pairs = size * size
    copies[0].wait()
    normed, scale = normalize(acts_ref[...].astype(f32).reshape(pairs, channels))
    normed_ref[...] = normed
    scale_ref[...] = jnp.broadcast_to(scale, (pairs, channels))
    for copy in copies[1:]:
        copy.wait()
    projected = dot(normed.astype(bf16), weights_ref[...])
    keep = keep_rows(mask_ref, crop_ref)
    for block in (0, 2):
        value = projected[:, block * channels : (block + 1) * channels]
        gate = projected[:, (block + 1) * channels : (block + 2) * channels]
        opened = sigmoid(gate)
        factor_ref[block] = keep * opened
        factor_ref[block + 1] = keep * value * opened * (1.0 - opened)
    out_open = sigmoid(projected[:, 4 * channels :])
    cotangent = cotangent_ref[...].astype(f32).reshape(pairs, channels)
    lin_grad = (cotangent * out_open).astype(bf16)
    open_ref[...] = out_open
    gate_factor_ref[...] = cotangent * out_open * (1.0 - out_open)
    upstream_ref[...] = dot_t(lin_grad, out_weight_ref[...])


def weighted_sums(weights, start, terms, out, base=None):
    def step(k, _):
        total = weights[start + k, pl.ds(0, 1), :] * terms[0]
        for n in range(1, len(terms)):
            total = total + weights[start + k, pl.ds(n, 1), :] * terms[n]
        if base is not None:
            total = total + base[k]
        out[k] = total.astype(out.dtype)
        return 0

    lax.fori_loop(0, out.shape[0], step, 0)


def flip(grid_size):
    return lax.rem(lax.axis_index("row"), 2) * (grid_size // 2)


def triangle_kernel(grid_size, *refs):
    left_in, right_in = refs[:grid_size], refs[grid_size : 2 * grid_size]
    upstream_ref, tri_normed_ref, right, grad, left = refs[2 * grid_size :]
    size, _, channels = left_in[0].shape
    row, held = lax.axis_index("row"), lax.axis_index("col") ^ flip(grid_size)
    for step in range(grid_size):
        left[pl.ds((held ^ step) * size, size)] = left_in[step][...].astype(f32)
        right[pl.ds((row ^ step) * size, size)] = right_in[step][...].astype(f32)

    def step(k, sums):
        other = right[k]
        return tuple(sums[i] + left[k, pl.ds(i, 1), :] * other for i in range(size))

    zero = jnp.zeros((size, channels), f32)
    sums = lax.fori_loop(0, grid_size * size, step, (zero,) * size)
    for i in range(size):
        here = pl.ds(i * size, size)
        tri_normed, scale = normalize(sums[i])
        tri_normed_ref[here, :] = tri_normed
        back = normalize_back(tri_normed, scale, upstream_ref[here, :])
        grad[i] = back.astype(bf16)


def left_terms_kernel(grid_size, steps, right, grad_ref, *refs):
    out, grad = refs[:-1], refs[-1]
    size, _, channels = grad_ref.shape
    grad[...] = grad_ref[...].astype(f32).reshape(size * size, channels)
    held = lax.axis_index("col") ^ flip(grid_size)
    grads = [grad[pl.ds(j, size, stride=size), :] for j in range(size)]
    for step, ref in zip(steps, out):
        weighted_sums(right, (held ^ step) * size, grads, ref)


def panel_kernel(grid_size, *refs):
    panel = refs[grid_size]
    size = refs[0].shape[0]
    col = lax.axis_index("col")
    for step in range(grid_size):
        panel[pl.ds((col ^ step) * size, size)] = refs[step][...].astype(f32)


def right_grad_kernel(steps, panel, *refs):
    grads, refs = refs[: len(steps)], refs[len(steps) :]
    out, base = refs[-1], refs[0] if len(refs) > 1 else None
    size = out.shape[0]
    for step, grad in zip(steps, grads):
        start = (lax.axis_index("row") ^ step) * size
        weighted_sums(panel, start, [grad[i].astype(f32) for i in range(size)], out, base)
        base = out


def update_kernel(
    tri_normed_ref, open_ref, gate_factor_ref, weights_ref, out_weight_ref, update_ref, normed_grad_ref
):
    size, _, channels = update_ref.shape
    linear = dot(tri_normed_ref[...].astype(bf16), out_weight_ref[...])
    update = (open_ref[...] * linear).astype(bf16)
    update_ref[...] = update.reshape(size, size, channels)
    out_gate_grad = (gate_factor_ref[...] * linear).astype(bf16)
    normed_grad_ref[...] = dot_t(out_gate_grad, weights_ref[:, 4 * channels :])


def sum_kernel(*refs):
    total = refs[0][...].astype(f32)
    for ref in refs[1:-1]:
        total = total + ref[...].astype(f32)
    refs[-1][...] = total.astype(bf16)


def back_kernel(step, left_ref, grad_ref, base, panel, normed_ref, scale_ref, factor_ref, partial_ref, weights_ref,
                out_ref, right_ref):
    right_grad_kernel((step,), panel, grad_ref, base, right_ref)
    size, _, channels = out_ref.shape
    pairs = size * size
    left = left_ref[...].astype(f32).reshape(pairs, channels)
    right = right_ref[...].reshape(pairs, channels)
    grads = jnp.concatenate(
        [(total * factor_ref[block]).astype(bf16) for block, total in enumerate((left, left, right, right))],
        axis=1,
    )
    normed_grad = partial_ref[...] + dot_t(grads, weights_ref[:, : 4 * channels])
    back = normalize_back(normed_ref[...], scale_ref[...], normed_grad)
    out_ref[...] = back.astype(bf16).reshape(size, size, channels)


def call(kernel, outs, *args, scratch=(), flops=0, smem=(), hbm=()):
    spec = pl.BlockSpec(memory_space=pltpu.VMEM)
    total = sum(a.size * a.dtype.itemsize for a in (*args, *outs))
    specs = [spec] * len(args)
    for n in smem:
        specs[n] = pl.BlockSpec(memory_space=pltpu.SMEM)
    args = list(args)
    for n in hbm:
        specs[n] = pl.BlockSpec(memory_space=pltpu.HBM)
        args[n] = pltpu.with_memory_space_constraint(args[n], pltpu.HBM)
    return pl.pallas_call(
        kernel,
        out_shape=tuple(outs),
        in_specs=specs,
        out_specs=(spec,) * len(outs),
        scratch_shapes=scratch,
        compiler_params=pltpu.CompilerParams(vmem_limit_bytes=24 * 2**20),
        cost_estimate=pl.CostEstimate(flops=flops, bytes_accessed=total, transcendentals=0),
    )(*args)


def local(pair_acts, pair_mask, crop_length, cotangent, in_weights, out_weight):
    size, _, channels = pair_acts.shape
    pairs = size * size
    n = lax.axis_size("row")
    tile = jax.ShapeDtypeStruct((size, size, channels), bf16)
    flat = jax.ShapeDtypeStruct((pairs, channels), f32)

    wide = jax.ShapeDtypeStruct((size, size, channels), f32)
    panel = jax.ShapeDtypeStruct((n * size, size, channels), f32)

    def swap(values, axis, step):
        return lax.ppermute(values, axis, [(a, a ^ step) for a in range(n)])

    def gather(values, axis):
        held = {0: values}
        bit = n // 2
        while bit:
            held.update({step ^ bit: swap(held[step], axis, bit) for step in list(held)})
            bit //= 2
        return [held[step] for step in range(n)]

    def seat(a, b):
        return b * n + (a ^ (b % 2 * (n // 2)))

    def mirror(values, back=False):
        pairs = [(a * n + b, seat(a, b)) for a in range(n) for b in range(n)]
        return lax.ppermute(values, ("row", "col"), [(t, s) if back else (s, t) for s, t in pairs])

    left, right = call(
        tiles_kernel, (tile, tile), pair_acts, pair_mask, crop_length, in_weights,
        smem=(2,), hbm=(0, 1, 3), flops=2 * pairs * channels * 4 * channels,
        scratch=[
            pltpu.VMEM(pair_acts.shape, bf16),
            pltpu.VMEM(pair_mask.shape, jnp.int32),
            pltpu.VMEM(in_weights.shape, bf16),
            pltpu.SemaphoreType.DMA((3,)),
        ],
    )
    mirrored = mirror(left)
    rights = gather(right, "row")
    own_lefts = gather(left, "col")
    normed, scale, factors, out_open, gate_factor, upstream = call(
        factors_kernel,
        (flat, flat, jax.ShapeDtypeStruct((4, pairs, channels), f32), flat, flat, flat),
        pair_acts, pair_mask, crop_length, cotangent, in_weights, out_weight,
        smem=(2,), hbm=(0, 1, 3, 4, 5), flops=2 * pairs * channels * 6 * channels,
        scratch=[
            pltpu.VMEM(pair_acts.shape, bf16),
            pltpu.VMEM(pair_mask.shape, jnp.int32),
            pltpu.VMEM(cotangent.shape, bf16),
            pltpu.VMEM(in_weights.shape, bf16),
            pltpu.VMEM(out_weight.shape, bf16),
            pltpu.SemaphoreType.DMA((5,)),
        ],
    )
    lefts = gather(mirrored, "col")
    tri_normed, right_panel, tri_grad = call(
        functools.partial(triangle_kernel, n),
        (flat, panel, tile),
        *lefts, *rights, upstream,
        scratch=[pltpu.VMEM(panel.shape, f32)],
        flops=2 * n * size * pairs * channels,
    )
    terms = {}
    for steps in (tuple(range(n - 1, 1, -1)), (1, 0)):
        outs = call(
            functools.partial(left_terms_kernel, n, steps), (tile,) * len(steps), right_panel, tri_grad,
            scratch=[pltpu.VMEM((pairs, channels), f32)],
            flops=2 * len(steps) * size * pairs * channels,
        )
        terms.update({step: swap(out, "col", step) if step else out for step, out in zip(steps, outs)})
    grads = gather(tri_grad, "row")
    (own_panel,) = call(functools.partial(panel_kernel, n), (panel,), *own_lefts)
    update, partial = call(
        update_kernel, (tile, flat), tri_normed, out_open, gate_factor, in_weights, out_weight,
        flops=4 * pairs * channels * channels,
    )
    early = tuple(range(n - 1))
    (right_grad,) = call(
        functools.partial(right_grad_kernel, early), (wide,), own_panel, *grads[:-1],
        flops=2 * len(early) * size * pairs * channels,
    )
    (left_sum,) = call(sum_kernel, (tile,), *terms.values())
    left_grad = mirror(left_sum, back=True)
    (pair_grad,) = call(
        functools.partial(back_kernel, n - 1), (tile,),
        left_grad, grads[-1], right_grad, own_panel, normed, scale, factors, partial, in_weights,
        scratch=[pltpu.VMEM(wide.shape, f32)],
        flops=2 * pairs * channels * (4 * channels + size),
    )
    return (update, pair_grad)


def solution(mesh):
    return jax.shard_map(
        local,
        mesh=mesh,
        in_specs=(
            P(("group", "row"), "col", None),
            P(("group", "row"), "col"),
            P("group"),
            P(("group", "row"), "col", None),
            P(),
            P(),
        ),
        out_specs=(P(("group", "row"), "col", None), P(("group", "row"), "col", None)),
        check_vma=False,
    )
```

```python
import functools

import jax
import jax.numpy as jnp
from jax import lax
from jax.experimental import pallas as pl
from jax.experimental.pallas import tpu as pltpu
from jax.sharding import PartitionSpec as P

epsilon = 1e-05
f32 = jnp.float32
bf16 = jnp.bfloat16


def mean_lanes(values):
    return jnp.sum(values, axis=-1, keepdims=True) * (1.0 / values.shape[-1])


def normalize(values):
    center = values - mean_lanes(values)
    variance = mean_lanes(center * center)
    scale = lax.rsqrt(variance + epsilon)
    return (center * scale, scale)


def normalize_back(normed, scale, upstream):
    average = mean_lanes(upstream)
    project = mean_lanes(upstream * normed)
    return scale * (upstream - average - normed * project)


def sigmoid(values):
    return 1.0 / (1.0 + jnp.exp(-values))


def dot(a, b):
    return jnp.dot(a, b, preferred_element_type=f32)


def dot_t(a, b):
    return lax.dot_general(a, b, (((1,), (1,)), ((), ())), preferred_element_type=f32)


def keep_rows(mask_ref, crop_ref):
    size = mask_ref.shape[0]
    rows = lax.axis_index("row") * size + lax.broadcasted_iota(jnp.int32, (size, size), 0)
    cols = lax.axis_index("col") * size + lax.broadcasted_iota(jnp.int32, (size, size), 1)
    live = jnp.where(jnp.maximum(rows, cols) < crop_ref[0], 1.0, 0.0)
    keep = (mask_ref[...].astype(f32) * live).astype(bf16)
    pair = lax.broadcasted_iota(jnp.int32, (size * size, size), 0)
    lane = lax.broadcasted_iota(jnp.int32, (size * size, size), 1)
    pick_row = jnp.where(pair // size == lane, 1.0, 0.0).astype(bf16)
    pick_col = jnp.where(pair % size == lane, 1.0, 0.0)
    spread = (dot(pick_row, keep) * pick_col).astype(bf16)
    return dot(spread, jnp.ones((size, 128), bf16))


def start_copies(sems, *pairs):
    copies = [pltpu.make_async_copy(src, dst, sems.at[n]) for n, (src, dst) in enumerate(pairs)]
    for copy in copies:
        copy.start()
    return copies


def tiles_kernel(
    acts_in, mask_in, crop_ref, weights_in, left_ref, right_ref, acts_ref, mask_ref, weights_ref, sems
):
    copies = start_copies(sems, (acts_in, acts_ref), (weights_in, weights_ref), (mask_in, mask_ref))
    size, _, channels = acts_ref.shape
    copies[0].wait()
    normed, _ = normalize(acts_ref[...].astype(f32).reshape(size * size, channels))
    normed = normed.astype(bf16)
    copies[1].wait()
    copies[2].wait()
    projected = dot(normed, weights_ref[:, : 4 * channels])
    keep = keep_rows(mask_ref, crop_ref)
    for block, out_ref in ((0, left_ref), (2, right_ref)):
        value = projected[:, block * channels : (block + 1) * channels]
        gate = projected[:, (block + 1) * channels : (block + 2) * channels]
        tile = (sigmoid(gate) * value * keep).astype(bf16)
        out_ref[...] = tile.reshape(size, size, channels)


def factors_kernel(
    acts_in, mask_in, crop_ref, cotangent_in, weights_in, out_weight_in,
    normed_ref, scale_ref, factor_ref, open_ref, gate_factor_ref, upstream_ref,
    acts_ref, mask_ref, cotangent_ref, weights_ref, out_weight_ref, sems,
):
    copies = start_copies(
        sems, (acts_in, acts_ref), (weights_in, weights_ref), (mask_in, mask_ref),
        (cotangent_in, cotangent_ref), (out_weight_in, out_weight_ref),
    )
    size, _, channels = acts_ref.shape
    pairs = size * size
    copies[0].wait()
    normed, scale = normalize(acts_ref[...].astype(f32).reshape(pairs, channels))
    normed_ref[...] = normed
    scale_ref[...] = jnp.broadcast_to(scale, (pairs, channels))
    for copy in copies[1:]:
        copy.wait()
    projected = dot(normed.astype(bf16), weights_ref[...])
    keep = keep_rows(mask_ref, crop_ref)
    for block in (0, 2):
        value = projected[:, block * channels : (block + 1) * channels]
        gate = projected[:, (block + 1) * channels : (block + 2) * channels]
        opened = sigmoid(gate)
        factor_ref[block] = keep * opened
        factor_ref[block + 1] = keep * value * opened * (1.0 - opened)
    out_open = sigmoid(projected[:, 4 * channels :])
    cotangent = cotangent_ref[...].astype(f32).reshape(pairs, channels)
    lin_grad = (cotangent * out_open).astype(bf16)
    open_ref[...] = out_open
    gate_factor_ref[...] = cotangent * out_open * (1.0 - out_open)
    upstream_ref[...] = dot_t(lin_grad, out_weight_ref[...])


def weighted_sums(weights, start, terms, out, base=None):
    def step(k, _):
        total = weights[start + k, pl.ds(0, 1), :] * terms[0]
        for n in range(1, len(terms)):
            total = total + weights[start + k, pl.ds(n, 1), :] * terms[n]
        if base is not None:
            total = total + base[k]
        out[k] = total.astype(out.dtype)
        return 0

    lax.fori_loop(0, out.shape[0], step, 0)


def panel_kernel(grid_size, *refs):
    col, size, panel = lax.axis_index("col"), refs[0].shape[0], refs[grid_size]
    for step in range(grid_size):
        panel[pl.ds((col ^ step) * size, size)] = refs[step][...].astype(f32)


def partial_kernel(steps, panel, right_ref, *outs):
    size, _, channels = right_ref.shape
    for step, out in zip(steps, outs):
        start = (lax.axis_index("row") ^ step) * size

        def add(k, sums):
            other = right_ref[k].astype(f32)
            return tuple(sums[i] + panel[start + k, pl.ds(i, 1), :] * other for i in range(size))

        zero = jnp.zeros((size, channels), f32)
        sums = lax.fori_loop(0, size, add, (zero,) * size)
        for i in range(size):
            out[i] = sums[i].astype(out.dtype)


def triangle_kernel(*refs):
    upstream_ref, tri_normed_ref, grad_ref = refs[-3:]
    size = grad_ref.shape[0]
    for i in range(size):
        total = refs[0][i]
        for ref in refs[1:-3]:
            total = total + ref[i].astype(f32)
        here = pl.ds(i * size, size)
        tri_normed, scale = normalize(total)
        tri_normed_ref[here, :] = tri_normed
        grad_ref[i] = normalize_back(tri_normed, scale, upstream_ref[here, :]).astype(bf16)


def left_terms_kernel(grid_size, steps, right_ref, *refs):
    grads, outs = refs[:grid_size], refs[grid_size : -2]
    panel, right = refs[-2:]
    size, _, channels = right_ref.shape
    pairs = size * size
    row, col = lax.axis_index("row"), lax.axis_index("col")
    for step in range(grid_size):
        panel[pl.ds((row ^ step) * pairs, pairs), :] = grads[step][...].astype(f32).reshape(pairs, channels)
    right[...] = right_ref[...].astype(f32)
    for step, out in zip(steps, outs):
        start = (col ^ step) * pairs
        weighted_sums(right, 0, [panel[pl.ds(start + j, size, stride=size), :] for j in range(size)], out)


def right_grad_kernel(steps, panel, *refs):
    out, base = refs[-1], None
    size = out.shape[0]
    for step, grad in zip(steps, refs):
        start = (lax.axis_index("row") ^ step) * size
        weighted_sums(panel, start, [grad[i].astype(f32) for i in range(size)], out, base)
        base = out


def update_kernel(
    tri_normed_ref, open_ref, gate_factor_ref, weights_ref, out_weight_ref, update_ref, normed_grad_ref
):
    size, _, channels = update_ref.shape
    linear = dot(tri_normed_ref[...].astype(bf16), out_weight_ref[...])
    update = (open_ref[...] * linear).astype(bf16)
    update_ref[...] = update.reshape(size, size, channels)
    out_gate_grad = (gate_factor_ref[...] * linear).astype(bf16)
    normed_grad_ref[...] = dot_t(out_gate_grad, weights_ref[:, 4 * channels :])


def back_kernel(grid_size, *refs):
    left_in = refs[:grid_size]
    right_ref, normed_ref, scale_ref, factor_ref, partial_ref, weights_ref, out_ref = refs[grid_size:]
    size, _, channels = out_ref.shape
    pairs = size * size
    left = left_in[0][...]
    for ref in left_in[1:]:
        left = left + ref[...].astype(f32)
    left = left.reshape(pairs, channels)
    right = right_ref[...].reshape(pairs, channels)
    grads = jnp.concatenate(
        [(total * factor_ref[block]).astype(bf16) for block, total in enumerate((left, left, right, right))],
        axis=1,
    )
    normed_grad = partial_ref[...] + dot_t(grads, weights_ref[:, : 4 * channels])
    back = normalize_back(normed_ref[...], scale_ref[...], normed_grad)
    out_ref[...] = back.astype(bf16).reshape(size, size, channels)


def call(kernel, outs, *args, scratch=(), flops=0, smem=(), hbm=()):
    spec = pl.BlockSpec(memory_space=pltpu.VMEM)
    total = sum(a.size * a.dtype.itemsize for a in (*args, *outs))
    specs = [spec] * len(args)
    for n in smem:
        specs[n] = pl.BlockSpec(memory_space=pltpu.SMEM)
    args = list(args)
    for n in hbm:
        specs[n] = pl.BlockSpec(memory_space=pltpu.HBM)
        args[n] = pltpu.with_memory_space_constraint(args[n], pltpu.HBM)
    return pl.pallas_call(
        kernel,
        out_shape=tuple(outs),
        in_specs=specs,
        out_specs=(spec,) * len(outs),
        scratch_shapes=scratch,
        compiler_params=pltpu.CompilerParams(vmem_limit_bytes=24 * 2**20),
        cost_estimate=pl.CostEstimate(flops=flops, bytes_accessed=total, transcendentals=0),
    )(*args)


def local(pair_acts, pair_mask, crop_length, cotangent, in_weights, out_weight):
    size, _, channels = pair_acts.shape
    pairs = size * size
    n = lax.axis_size("row")
    tile = jax.ShapeDtypeStruct((size, size, channels), bf16)
    flat = jax.ShapeDtypeStruct((pairs, channels), f32)

    wide = jax.ShapeDtypeStruct((size, size, channels), f32)
    panel = jax.ShapeDtypeStruct((n * size, size, channels), f32)

    def swap(values, axis, step):
        return lax.ppermute(values, axis, [(a, a ^ step) for a in range(n)])

    def swaps(values, axis):
        return [swap(each, axis, step) if step else each for step, each in enumerate(values)]

    left, right = call(
        tiles_kernel, (tile, tile), pair_acts, pair_mask, crop_length, in_weights,
        smem=(2,), hbm=(0, 1, 3), flops=2 * pairs * channels * 4 * channels,
        scratch=[
            pltpu.VMEM(pair_acts.shape, bf16),
            pltpu.VMEM(pair_mask.shape, jnp.int32),
            pltpu.VMEM(in_weights.shape, bf16),
            pltpu.SemaphoreType.DMA((3,)),
        ],
    )
    lefts = swaps([left] * n, "col")
    (left_panel,) = call(functools.partial(panel_kernel, n), (panel,), *lefts)
    parts = [None] * n
    for steps in [(step,) for step in range(n - 1, 1, -1)] + [(1, 0)]:
        outs = call(
            functools.partial(partial_kernel, steps), tuple(tile if step else wide for step in steps),
            left_panel, right, flops=2 * len(steps) * size * pairs * channels,
        )
        for step, out in zip(steps, outs):
            parts[step] = out
    parts = swaps(parts, "row")
    normed, scale, factors, out_open, gate_factor, upstream = call(
        factors_kernel,
        (flat, flat, jax.ShapeDtypeStruct((4, pairs, channels), f32), flat, flat, flat),
        pair_acts, pair_mask, crop_length, cotangent, in_weights, out_weight,
        smem=(2,), hbm=(0, 1, 3, 4, 5), flops=2 * pairs * channels * 6 * channels,
        scratch=[
            pltpu.VMEM(pair_acts.shape, bf16),
            pltpu.VMEM(pair_mask.shape, jnp.int32),
            pltpu.VMEM(cotangent.shape, bf16),
            pltpu.VMEM(in_weights.shape, bf16),
            pltpu.VMEM(out_weight.shape, bf16),
            pltpu.SemaphoreType.DMA((5,)),
        ],
    )
    tri_normed, tri_grad = call(
        triangle_kernel, (flat, tile), *parts, upstream, flops=20 * pairs * channels,
    )
    grads = swaps([tri_grad] * n, "row")
    update, partial = call(
        update_kernel, (tile, flat), tri_normed, out_open, gate_factor, in_weights, out_weight,
        flops=4 * pairs * channels * channels,
    )
    terms = [None] * n
    for steps in (tuple(range(n - 1, 1, -1)), (1, 0)):
        outs = call(
            functools.partial(left_terms_kernel, n, steps), tuple(tile if step else wide for step in steps),
            right, *grads,
            scratch=[pltpu.VMEM((n * pairs, channels), f32), pltpu.VMEM(wide.shape, f32)],
            flops=2 * len(steps) * size * pairs * channels,
        )
        for step, out in zip(steps, outs):
            terms[step] = out
    terms = swaps(terms, "col")
    (right_grad,) = call(
        functools.partial(right_grad_kernel, tuple(range(n))), (wide,), left_panel, *grads,
        flops=2 * n * size * pairs * channels,
    )
    (pair_grad,) = call(
        functools.partial(back_kernel, n), (tile,),
        *terms, right_grad, normed, scale, factors, partial, in_weights,
        flops=2 * pairs * channels * 4 * channels,
    )
    return (update, pair_grad)


def solution(mesh):
    return jax.shard_map(
        local,
        mesh=mesh,
        in_specs=(
            P(("group", "row"), "col", None),
            P(("group", "row"), "col"),
            P("group"),
            P(("group", "row"), "col", None),
            P(),
            P(),
        ),
        out_specs=(P(("group", "row"), "col", None), P(("group", "row"), "col", None)),
        check_vma=False,
    )
```

```python
import functools

import jax
import jax.numpy as jnp
from jax import lax
from jax.experimental import pallas as pl
from jax.experimental.pallas import tpu as pltpu
from jax.sharding import PartitionSpec as P

epsilon = 1e-05
f32 = jnp.float32
bf16 = jnp.bfloat16


def mean_lanes(values):
    return jnp.sum(values, axis=-1, keepdims=True) * (1.0 / values.shape[-1])


def normalize(values):
    center = values - mean_lanes(values)
    variance = mean_lanes(center * center)
    scale = lax.rsqrt(variance + epsilon)
    return (center * scale, scale)


def normalize_back(normed, scale, upstream):
    average = mean_lanes(upstream)
    project = mean_lanes(upstream * normed)
    return scale * (upstream - average - normed * project)


def sigmoid(values):
    return 1.0 / (1.0 + jnp.exp(-values))


def dot(a, b):
    return jnp.dot(a, b, preferred_element_type=f32)


def dot_t(a, b):
    return lax.dot_general(a, b, (((1,), (1,)), ((), ())), preferred_element_type=f32)


def keep_rows(mask_ref, crop_ref, channels):
    size = mask_ref.shape[0]
    rows = lax.axis_index("row") * size + lax.broadcasted_iota(jnp.int32, (size, size), 0)
    cols = lax.axis_index("col") * size + lax.broadcasted_iota(jnp.int32, (size, size), 1)
    live = jnp.where(jnp.maximum(rows, cols) < crop_ref[0], 1.0, 0.0)
    keep = (mask_ref[...].astype(f32) * live).astype(bf16)
    pair = lax.broadcasted_iota(jnp.int32, (size * size, size), 0)
    lane = lax.broadcasted_iota(jnp.int32, (size * size, size), 1)
    pick_row = jnp.where(pair // size == lane, 1.0, 0.0).astype(bf16)
    pick_col = jnp.where(pair % size == lane, 1.0, 0.0)
    spread = (dot(pick_row, keep) * pick_col).astype(bf16)
    return dot(spread, jnp.ones((size, channels), bf16))


def start_copies(sems, *pairs):
    copies = [pltpu.make_async_copy(src, dst, sems.at[n]) for n, (src, dst) in enumerate(pairs)]
    for copy in copies:
        copy.start()
    return copies


def gated(projected, block, keep):
    channels = keep.shape[1]
    value = projected[:, block * channels : (block + 1) * channels]
    opened = sigmoid(projected[:, (block + 1) * channels : (block + 2) * channels])
    return (opened * value * keep).astype(bf16), opened, value


def left_kernel(acts_in, mask_in, crop_ref, weights_in, left_ref, acts_ref, mask_ref, weights_ref, sems):
    size, _, channels = acts_ref.shape
    copies = start_copies(
        sems, (acts_in, acts_ref), (weights_in.at[:, pl.ds(0, 2 * channels)], weights_ref), (mask_in, mask_ref),
    )
    copies[0].wait()
    normed, _ = normalize(acts_ref[...].astype(f32).reshape(size * size, channels))
    normed = normed.astype(bf16)
    for copy in copies[1:]:
        copy.wait()
    left, _, _ = gated(dot(normed, weights_ref[...]), 0, keep_rows(mask_ref, crop_ref, channels))
    left_ref[...] = left.reshape(size, size, channels)


def factors_kernel(
    acts_in, mask_in, crop_ref, cotangent_in, weights_in, out_weight_in,
    right_ref, normed_ref, scale_ref, factor_ref, open_ref, gate_factor_ref, upstream_ref,
    acts_ref, mask_ref, cotangent_ref, weights_ref, out_weight_ref, sems,
):
    copies = start_copies(
        sems, (acts_in, acts_ref), (weights_in, weights_ref), (mask_in, mask_ref),
        (cotangent_in, cotangent_ref), (out_weight_in, out_weight_ref),
    )
    size, _, channels = acts_ref.shape
    pairs = size * size
    copies[0].wait()
    normed, scale = normalize(acts_ref[...].astype(f32).reshape(pairs, channels))
    normed_ref[...] = normed
    scale_ref[...] = jnp.broadcast_to(scale, (pairs, channels))
    for copy in copies[1:]:
        copy.wait()
    projected = dot(normed.astype(bf16), weights_ref[...])
    keep = keep_rows(mask_ref, crop_ref, channels)
    for block in (0, 2):
        tile, opened, value = gated(projected, block, keep)
        factor_ref[block] = keep * opened
        factor_ref[block + 1] = keep * value * opened * (1.0 - opened)
    right_ref[...] = tile.reshape(size, size, channels)
    out_open = sigmoid(projected[:, 4 * channels :])
    cotangent = cotangent_ref[...].astype(f32).reshape(pairs, channels)
    lin_grad = (cotangent * out_open).astype(bf16)
    open_ref[...] = out_open
    gate_factor_ref[...] = cotangent * out_open * (1.0 - out_open)
    upstream_ref[...] = dot_t(lin_grad, out_weight_ref[...])


def weighted_sums(weights, start, terms, out, base=None):
    def step(k, _):
        total = weights[start + k, pl.ds(0, 1), :] * terms[0]
        for n in range(1, len(terms)):
            total = total + weights[start + k, pl.ds(n, 1), :] * terms[n]
        if base is not None:
            total = total + base[k]
        out[k] = total.astype(out.dtype)
        return 0

    lax.fori_loop(0, out.shape[0], step, 0)


def panel_kernel(axis, steps, *refs):
    here, rows, panel = lax.axis_index(axis), refs[0].shape[0], refs[-1]
    for step, ref in zip(steps, refs):
        panel[pl.ds((here ^ step) * rows, rows)] = ref[...].astype(f32)


def partial_kernel(steps, panel, right_ref, *outs):
    size, _, channels = right_ref.shape
    for step, out in zip(steps, outs):
        start = (lax.axis_index("row") ^ step) * size

        def add(k, sums):
            other = right_ref[k].astype(f32)
            return tuple(sums[i] + panel[start + k, pl.ds(i, 1), :] * other for i in range(size))

        zero = jnp.zeros((size, channels), f32)
        sums = lax.fori_loop(0, size, add, (zero,) * size)
        for i in range(size):
            out[i] = sums[i].astype(out.dtype)


def triangle_kernel(base, tile_ref, upstream_ref, tri_normed_ref, grad_ref):
    size = grad_ref.shape[0]
    for i in range(size):
        here = pl.ds(i * size, size)
        tri_normed, scale = normalize(base[i] + tile_ref[i].astype(f32))
        tri_normed_ref[here, :] = tri_normed
        grad_ref[i] = normalize_back(tri_normed, scale, upstream_ref[here, :]).astype(bf16)


def left_terms_kernel(step, panel, right_ref, out, grad, right):
    size, _, channels = right_ref.shape
    right[...] = right_ref[...].astype(f32)
    here = panel[pl.ds((lax.axis_index("col") ^ step) * size, size)]
    grad[...] = here.reshape(size * size, channels)
    weighted_sums(right, 0, [grad[pl.ds(j, size, stride=size), :] for j in range(size)], out)


def right_grad_kernel(steps, panel, *refs):
    out, base = refs[-1], None
    size = out.shape[0]
    for step, grad in zip(steps, refs):
        start = (lax.axis_index("row") ^ step) * size
        weighted_sums(panel, start, [grad[i].astype(f32) for i in range(size)], out, base)
        base = out


def add_kernel(base, tile_ref, out):
    out[...] = base[...] + tile_ref[...].astype(f32)


def update_kernel(
    tri_normed_ref, open_ref, gate_factor_ref, weights_ref, out_weight_ref, update_ref, normed_grad_ref
):
    size, _, channels = update_ref.shape
    linear = dot(tri_normed_ref[...].astype(bf16), out_weight_ref[...])
    update = (open_ref[...] * linear).astype(bf16)
    update_ref[...] = update.reshape(size, size, channels)
    out_gate_grad = (gate_factor_ref[...] * linear).astype(bf16)
    normed_grad_ref[...] = dot_t(out_gate_grad, weights_ref[:, 4 * channels :])


def back_kernel(
    base, tile_ref, right_ref, normed_ref, scale_ref, factor_ref, partial_ref, weights_ref, out_ref
):
    size, _, channels = out_ref.shape
    pairs = size * size
    left = (base[...] + tile_ref[...].astype(f32)).reshape(pairs, channels)
    right = right_ref[...].reshape(pairs, channels)
    grads = jnp.concatenate(
        [(total * factor_ref[block]).astype(bf16) for block, total in enumerate((left, left, right, right))],
        axis=1,
    )
    normed_grad = partial_ref[...] + dot_t(grads, weights_ref[:, : 4 * channels])
    back = normalize_back(normed_ref[...], scale_ref[...], normed_grad)
    out_ref[...] = back.astype(bf16).reshape(size, size, channels)


def call(kernel, outs, *args, scratch=(), flops=0, smem=(), hbm=()):
    spec = pl.BlockSpec(memory_space=pltpu.VMEM)
    total = sum(a.size * a.dtype.itemsize for a in (*args, *outs))
    specs = [spec] * len(args)
    for n in smem:
        specs[n] = pl.BlockSpec(memory_space=pltpu.SMEM)
    args = list(args)
    for n in hbm:
        specs[n] = pl.BlockSpec(memory_space=pltpu.HBM)
        args[n] = pltpu.with_memory_space_constraint(args[n], pltpu.HBM)
    return pl.pallas_call(
        kernel,
        out_shape=tuple(outs),
        in_specs=specs,
        out_specs=(spec,) * len(outs),
        scratch_shapes=scratch,
        compiler_params=pltpu.CompilerParams(vmem_limit_bytes=24 * 2**20),
        cost_estimate=pl.CostEstimate(flops=flops, bytes_accessed=total if flops else 0, transcendentals=0),
    )(*args)


def local(pair_acts, pair_mask, crop_length, cotangent, in_weights, out_weight):
    size, _, channels = pair_acts.shape
    pairs = size * size
    n = lax.axis_size("row")
    tile = jax.ShapeDtypeStruct((size, size, channels), bf16)
    flat = jax.ShapeDtypeStruct((pairs, channels), f32)

    wide = jax.ShapeDtypeStruct((size, size, channels), f32)
    panel = jax.ShapeDtypeStruct((n * size, size, channels), f32)
    work = 2 * size * pairs * channels
    wait = 2**31
    steps = [step for bit in range(n.bit_length() - 2, -1, -1) for step in range(2**bit, 2 ** (bit + 1))]


    def swap(values, axis, step):
        return lax.ppermute(values, axis, [(a, a ^ step) for a in range(n)])

    def gather(values, axis):
        return [values] + [swap(values, axis, step) for step in steps]

    (left,) = call(
        left_kernel, (tile,), pair_acts, pair_mask, crop_length, in_weights,
        smem=(2,), hbm=(0, 1, 3), flops=2 * pairs * channels * 2 * channels,
        scratch=[
            pltpu.VMEM(pair_acts.shape, bf16),
            pltpu.VMEM(pair_mask.shape, jnp.int32),
            pltpu.VMEM((channels, 2 * channels), bf16),
            pltpu.SemaphoreType.DMA((3,)),
        ],
    )
    lefts = gather(left, "col")
    right, normed, scale, factors, out_open, gate_factor, upstream = call(
        factors_kernel,
        (tile, flat, flat, jax.ShapeDtypeStruct((4, pairs, channels), f32), flat, flat, flat),
        pair_acts, pair_mask, crop_length, cotangent, in_weights, out_weight,
        smem=(2,), hbm=(0, 1, 3, 4, 5), flops=2 * pairs * channels * 6 * channels,
        scratch=[
            pltpu.VMEM(pair_acts.shape, bf16),
            pltpu.VMEM(pair_mask.shape, jnp.int32),
            pltpu.VMEM(cotangent.shape, bf16),
            pltpu.VMEM(in_weights.shape, bf16),
            pltpu.VMEM(out_weight.shape, bf16),
            pltpu.SemaphoreType.DMA((5,)),
        ],
    )
    (left_panel,) = call(functools.partial(panel_kernel, "col", [0] + steps), (panel,), *lefts)
    parts = {}
    for step in [0] + steps:
        (parts[step],) = call(
            functools.partial(partial_kernel, (step,)), (tile if step else wide,), left_panel, right, flops=work,
        )
    total = parts[0]
    for step in steps:
        part = swap(parts[step], "row", step)
        if step != steps[-1]:
            (total,) = call(add_kernel, (wide,), total, part, flops=wait)
    tri_normed, tri_grad = call(
        triangle_kernel, (flat, tile), total, part, upstream, flops=20 * pairs * channels,
    )
    grads = gather(tri_grad, "row")
    update, partial = call(
        update_kernel, (tile, flat), tri_normed, out_open, gate_factor, in_weights, out_weight,
        flops=4 * pairs * channels * channels,
    )
    right, partial = lax.optimization_barrier((right, partial))
    (grad_panel,) = call(functools.partial(panel_kernel, "row", [0] + steps), (panel,), *grads)
    terms = {}
    for step in [0] + steps:
        (terms[step],) = call(
            functools.partial(left_terms_kernel, step), (tile if step else wide,), grad_panel, right,
            scratch=[pltpu.VMEM((pairs, channels), f32), pltpu.VMEM(wide.shape, f32)], flops=work,
        )
    total = terms[0]
    for step in steps:
        term = swap(terms[step], "col", step)
        if step != steps[-1]:
            (total,) = call(add_kernel, (wide,), total, term, flops=wait)
    (right_grad,) = call(
        functools.partial(right_grad_kernel, [0] + steps), (wide,), left_panel, *grads,
        flops=2 * n * size * pairs * channels,
    )
    (pair_grad,) = call(
        back_kernel, (tile,),
        total, term, right_grad, normed, scale, factors, partial, in_weights,
        flops=2 * pairs * channels * 4 * channels,
    )
    return (update, pair_grad)


def solution(mesh):
    return jax.shard_map(
        local,
        mesh=mesh,
        in_specs=(
            P(("group", "row"), "col", None),
            P(("group", "row"), "col"),
            P("group"),
            P(("group", "row"), "col", None),
            P(),
            P(),
        ),
        out_specs=(P(("group", "row"), "col", None), P(("group", "row"), "col", None)),
        check_vma=False,
    )
```

```python
import functools

import jax
import jax.numpy as jnp
from jax import lax
from jax.experimental import pallas as pl
from jax.experimental.pallas import tpu as pltpu
from jax.sharding import PartitionSpec as P

epsilon = 1e-05
f32 = jnp.float32
bf16 = jnp.bfloat16


def mean_lanes(values):
    return jnp.sum(values, axis=-1, keepdims=True) * (1.0 / values.shape[-1])


def normalize(values):
    center = values - mean_lanes(values)
    variance = mean_lanes(center * center)
    scale = lax.rsqrt(variance + epsilon)
    return (center * scale, scale)


def normalize_back(normed, scale, upstream):
    average = mean_lanes(upstream)
    project = mean_lanes(upstream * normed)
    return scale * (upstream - average - normed * project)


def sigmoid(values):
    return 1.0 / (1.0 + jnp.exp(-values))


def dot(a, b):
    return jnp.dot(a, b, preferred_element_type=f32)


def dot_t(a, b):
    return lax.dot_general(a, b, (((1,), (1,)), ((), ())), preferred_element_type=f32)


def keep_rows(mask_ref, crop_ref, channels):
    size = mask_ref.shape[0]
    rows = lax.axis_index("row") * size + lax.broadcasted_iota(jnp.int32, (size, size), 0)
    cols = lax.axis_index("col") * size + lax.broadcasted_iota(jnp.int32, (size, size), 1)
    live = jnp.where(jnp.maximum(rows, cols) < crop_ref[0], 1.0, 0.0)
    keep = (mask_ref[...].astype(f32) * live).astype(bf16)
    pair = lax.broadcasted_iota(jnp.int32, (size * size, size), 0)
    lane = lax.broadcasted_iota(jnp.int32, (size * size, size), 1)
    pick_row = jnp.where(pair // size == lane, 1.0, 0.0).astype(bf16)
    pick_col = jnp.where(pair % size == lane, 1.0, 0.0)
    spread = (dot(pick_row, keep) * pick_col).astype(bf16)
    return dot(spread, jnp.ones((size, channels), bf16))


def start_copies(sems, *pairs):
    copies = [pltpu.make_async_copy(src, dst, sems.at[n]) for n, (src, dst) in enumerate(pairs)]
    for copy in copies:
        copy.start()
    return copies


def gated(projected, block, keep):
    channels = keep.shape[1]
    value = projected[:, block * channels : (block + 1) * channels]
    opened = sigmoid(projected[:, (block + 1) * channels : (block + 2) * channels])
    return (opened * value * keep).astype(bf16), opened, value


def left_kernel(acts_in, mask_in, crop_ref, weights_in, left_ref, acts_ref, mask_ref, weights_ref, sems):
    size, _, channels = acts_ref.shape
    copies = start_copies(
        sems, (acts_in, acts_ref), (weights_in.at[:, pl.ds(0, 2 * channels)], weights_ref), (mask_in, mask_ref),
    )
    copies[0].wait()
    normed, _ = normalize(acts_ref[...].astype(f32).reshape(size * size, channels))
    normed = normed.astype(bf16)
    copies[2].wait()
    keep = keep_rows(mask_ref, crop_ref, channels)
    copies[1].wait()
    left, _, _ = gated(dot(normed, weights_ref[...]), 0, keep)
    left_ref[...] = left.reshape(size, size, channels)


def factors_kernel(
    acts_in, mask_in, crop_ref, cotangent_in, weights_in, out_weight_in,
    right_ref, normed_ref, scale_ref, factor_ref, open_ref, gate_factor_ref, upstream_ref,
    acts_ref, mask_ref, cotangent_ref, weights_ref, out_weight_ref, sems,
):
    copies = start_copies(
        sems, (acts_in, acts_ref), (weights_in, weights_ref), (mask_in, mask_ref),
        (cotangent_in, cotangent_ref), (out_weight_in, out_weight_ref),
    )
    size, _, channels = acts_ref.shape
    pairs = size * size
    copies[0].wait()
    normed, scale = normalize(acts_ref[...].astype(f32).reshape(pairs, channels))
    normed_ref[...] = normed
    scale_ref[...] = jnp.broadcast_to(scale, (pairs, channels))
    for copy in copies[1:]:
        copy.wait()
    projected = dot(normed.astype(bf16), weights_ref[...])
    keep = keep_rows(mask_ref, crop_ref, channels)
    for block in (0, 2):
        tile, opened, value = gated(projected, block, keep)
        factor_ref[block] = keep * opened
        factor_ref[block + 1] = keep * value * opened * (1.0 - opened)
    right_ref[...] = tile.astype(f32).reshape(size, size, channels)
    out_open = sigmoid(projected[:, 4 * channels :])
    cotangent = cotangent_ref[...].astype(f32).reshape(pairs, channels)
    lin_grad = (cotangent * out_open).astype(bf16)
    open_ref[...] = out_open
    gate_factor_ref[...] = cotangent * out_open * (1.0 - out_open)
    upstream_ref[...] = dot_t(lin_grad, out_weight_ref[...])


def weighted_sums(weights, start, terms, out, base=None):
    def step(k, _):
        total = weights[start + k, pl.ds(0, 1), :] * terms[0]
        for n in range(1, len(terms)):
            total = total + weights[start + k, pl.ds(n, 1), :] * terms[n]
        if base is not None:
            total = total + base[k]
        out[k] = total.astype(out.dtype)
        return 0

    lax.fori_loop(0, out.shape[0], step, 0, unroll=4)


def panel_kernel(axis, steps, *refs):
    here, panel = lax.axis_index(axis), refs[-1]
    rows = panel.shape[0] // len(steps)
    for step, ref in zip(steps, refs):
        tile = ref[...].astype(f32)
        panel[pl.ds((here ^ step) * rows, rows)] = tile.reshape((rows,) + panel.shape[1:])


def partial_kernel(steps, panel, right_ref, *outs):
    size, _, channels = right_ref.shape
    for step, out in zip(steps, outs):
        start = (lax.axis_index("row") ^ step) * size

        def add(k, sums):
            other = right_ref[k]
            return tuple(sums[i] + panel[start + k, pl.ds(i, 1), :] * other for i in range(size))

        zero = jnp.zeros((size, channels), f32)
        sums = lax.fori_loop(0, size, add, (zero,) * size, unroll=4)
        for i in range(size):
            out[i] = sums[i].astype(out.dtype)


def triangle_kernel(base, tile_ref, upstream_ref, tri_normed_ref, grad_ref):
    size = grad_ref.shape[0]
    for i in range(size):
        here = pl.ds(i * size, size)
        tri_normed, scale = normalize(base[i] + tile_ref[i].astype(f32))
        tri_normed_ref[here, :] = tri_normed
        grad_ref[i] = normalize_back(tri_normed, scale, upstream_ref[here, :]).astype(bf16)


def left_terms_kernel(step, panel, right, out):
    size = out.shape[0]
    start = (lax.axis_index("col") ^ step) * (size * size)
    weighted_sums(right, 0, [panel[pl.ds(start + j, size, stride=size), :] for j in range(size)], out)


def right_grad_kernel(steps, panel, *refs):
    out, base = refs[-1], refs[len(steps)] if len(refs) > len(steps) + 1 else None
    size = out.shape[0]
    for step, grad in zip(steps, refs):
        start = (lax.axis_index("row") ^ step) * size
        weighted_sums(panel, start, [grad[i].astype(f32) for i in range(size)], out, base)
        base = out


def right_back_kernel(steps, panel, *refs):
    factor_ref, weights_ref, share_ref, out, right_ref = refs[-5:]
    right_grad_kernel(steps, panel, *refs[: len(steps) + 1], right_ref)
    pairs, channels = out.shape
    right = right_ref[...].reshape(pairs, channels)
    grads = jnp.concatenate([(right * factor_ref[block]).astype(bf16) for block in (2, 3)], axis=1)
    out[...] = share_ref[...] + dot_t(grads, weights_ref[:, 2 * channels : 4 * channels])


def add_kernel(base, tile_ref, out):
    out[...] = base[...] + tile_ref[...].astype(f32)


def update_kernel(
    tri_normed_ref, open_ref, gate_factor_ref, weights_ref, out_weight_ref, update_ref, normed_grad_ref
):
    size, _, channels = update_ref.shape
    linear = dot(tri_normed_ref[...].astype(bf16), out_weight_ref[...])
    update = (open_ref[...] * linear).astype(bf16)
    update_ref[...] = update.reshape(size, size, channels)
    out_gate_grad = (gate_factor_ref[...] * linear).astype(bf16)
    normed_grad_ref[...] = dot_t(out_gate_grad, weights_ref[:, 4 * channels :])


def back_kernel(base, tile_ref, normed_ref, scale_ref, factor_ref, share_ref, weights_ref, out, done, sems):
    size, _, channels = done.shape
    half = size // 2
    copies = []
    for part in range(2):
        tiles, rows = pl.ds(part * half, half), pl.ds(part * half * size, half * size)
        left = (base[tiles] + tile_ref[tiles].astype(f32)).reshape(half * size, channels)
        grads = jnp.concatenate([(left * factor_ref[block, rows]).astype(bf16) for block in (0, 1)], axis=1)
        normed_grad = share_ref[rows, :] + dot_t(grads, weights_ref[:, : 2 * channels])
        back = normalize_back(normed_ref[rows, :], scale_ref[rows, :], normed_grad)
        done[tiles] = back.astype(bf16).reshape(half, size, channels)
        copies.append(pltpu.make_async_copy(done.at[tiles], out.at[tiles], sems.at[part]))
        copies[-1].start()
    for copy in copies:
        copy.wait()


def call(kernel, outs, *args, scratch=(), flops=0, smem=(), hbm=(), out_space=pltpu.VMEM):
    spec = pl.BlockSpec(memory_space=pltpu.VMEM)
    total = sum(a.size * a.dtype.itemsize for a in (*args, *outs))
    specs = [spec] * len(args)
    for n in smem:
        specs[n] = pl.BlockSpec(memory_space=pltpu.SMEM)
    args = list(args)
    for n in hbm:
        specs[n] = pl.BlockSpec(memory_space=pltpu.HBM)
        args[n] = pltpu.with_memory_space_constraint(args[n], pltpu.HBM)
    return pl.pallas_call(
        kernel,
        out_shape=tuple(outs),
        in_specs=specs,
        out_specs=(pl.BlockSpec(memory_space=out_space),) * len(outs),
        scratch_shapes=scratch,
        compiler_params=pltpu.CompilerParams(vmem_limit_bytes=24 * 2**20),
        cost_estimate=pl.CostEstimate(flops=flops, bytes_accessed=total if flops else 0, transcendentals=0),
    )(*args)


def local(pair_acts, pair_mask, crop_length, cotangent, in_weights, out_weight):
    size, _, channels = pair_acts.shape
    pairs = size * size
    n = lax.axis_size("row")
    tile = jax.ShapeDtypeStruct((size, size, channels), bf16)
    flat = jax.ShapeDtypeStruct((pairs, channels), f32)

    wide = jax.ShapeDtypeStruct((size, size, channels), f32)
    panel = jax.ShapeDtypeStruct((n * size, size, channels), f32)
    work = 2 * size * pairs * channels
    wait = 2**31
    steps = [step for bit in range(n.bit_length() - 2, -1, -1) for step in range(2**bit, 2 ** (bit + 1))]


    def swap(values, axis, step):
        return lax.ppermute(values, axis, [(a, a ^ step) for a in range(n)])

    def gather(values, axis):
        return [values] + [swap(values, axis, step) for step in steps]

    (left,) = call(
        left_kernel, (tile,), pair_acts, pair_mask, crop_length, in_weights,
        smem=(2,), hbm=(0, 1, 3), flops=2 * pairs * channels * 2 * channels,
        scratch=[
            pltpu.VMEM(pair_acts.shape, bf16),
            pltpu.VMEM(pair_mask.shape, jnp.int32),
            pltpu.VMEM((channels, 2 * channels), bf16),
            pltpu.SemaphoreType.DMA((3,)),
        ],
    )
    lefts = gather(left, "col")
    right, normed, scale, factors, out_open, gate_factor, upstream = call(
        factors_kernel,
        (wide, flat, flat, jax.ShapeDtypeStruct((4, pairs, channels), f32), flat, flat, flat),
        pair_acts, pair_mask, crop_length, cotangent, in_weights, out_weight,
        smem=(2,), hbm=(0, 1, 3, 4, 5), flops=2 * pairs * channels * 6 * channels,
        scratch=[
            pltpu.VMEM(pair_acts.shape, bf16),
            pltpu.VMEM(pair_mask.shape, jnp.int32),
            pltpu.VMEM(cotangent.shape, bf16),
            pltpu.VMEM(in_weights.shape, bf16),
            pltpu.VMEM(out_weight.shape, bf16),
            pltpu.SemaphoreType.DMA((5,)),
        ],
    )
    (left_panel,) = call(functools.partial(panel_kernel, "col", [0] + steps), (panel,), *lefts)
    parts = {}
    for step in [0] + steps:
        (parts[step],) = call(
            functools.partial(partial_kernel, (step,)), (tile if step else wide,), left_panel, right, flops=work,
        )
    total = parts[0]
    for step in steps:
        part = swap(parts[step], "row", step)
        if step != steps[-1]:
            (total,) = call(add_kernel, (wide,), total, part, flops=wait)
    tri_normed, tri_grad = call(
        triangle_kernel, (flat, tile), total, part, upstream, flops=20 * pairs * channels,
    )
    grads = gather(tri_grad, "row")
    update, partial = call(
        update_kernel, (tile, flat), tri_normed, out_open, gate_factor, in_weights, out_weight,
        flops=4 * pairs * channels * channels,
    )
    (right_grad,) = call(functools.partial(right_grad_kernel, [0]), (wide,), left_panel, tri_grad)
    right, partial, right_grad = lax.optimization_barrier((right, partial, right_grad))
    (grad_panel,) = call(
        functools.partial(panel_kernel, "row", [0] + steps), (jax.ShapeDtypeStruct((n * pairs, channels), f32),), *grads
    )
    terms = {}
    for step in steps + [0]:
        if terms:
            right, terms[last] = lax.optimization_barrier((right, terms[last]))
        last = step
        (terms[step],) = call(
            functools.partial(left_terms_kernel, step), (tile if step else wide,), grad_panel, right,
            flops=work,
        )
    total = terms[0]
    for step in steps:
        term = swap(terms[step], "col", step)
        if step != steps[-1]:
            (total,) = call(add_kernel, (wide,), total, term, flops=wait)
    (share,) = call(
        functools.partial(right_back_kernel, steps), (flat,),
        left_panel, *grads[1:], right_grad, factors, in_weights, partial,
        scratch=[pltpu.VMEM(wide.shape, f32)],
    )
    (pair_grad,) = call(
        back_kernel, (tile,), total, term, normed, scale, factors, share, in_weights,
        scratch=[pltpu.VMEM(tile.shape, bf16), pltpu.SemaphoreType.DMA((2,))], out_space=pl.ANY,
        flops=2 * pairs * channels * 2 * channels,
    )
    return (update, pair_grad)


def solution(mesh):
    return jax.shard_map(
        local,
        mesh=mesh,
        in_specs=(
            P(("group", "row"), "col", None),
            P(("group", "row"), "col"),
            P("group"),
            P(("group", "row"), "col", None),
            P(),
            P(),
        ),
        out_specs=(P(("group", "row"), "col", None), P(("group", "row"), "col", None)),
        check_vma=False,
    )
```

```python
import functools

import jax
import jax.numpy as jnp
from jax import lax
from jax.experimental import pallas as pl
from jax.experimental.pallas import tpu as pltpu
from jax.sharding import PartitionSpec as P

epsilon = 1e-05
f32 = jnp.float32
bf16 = jnp.bfloat16


def mean_lanes(values):
    return jnp.sum(values, axis=-1, keepdims=True) * (1.0 / values.shape[-1])


def normalize(values):
    center = values - mean_lanes(values)
    variance = mean_lanes(center * center)
    scale = lax.rsqrt(variance + epsilon)
    return (center * scale, scale)


def normalize_back(normed, scale, upstream):
    average = mean_lanes(upstream)
    project = mean_lanes(upstream * normed)
    return scale * (upstream - average - normed * project)


def sigmoid(values):
    return 1.0 / (1.0 + jnp.exp(-values))


def dot(a, b):
    return jnp.dot(a, b, preferred_element_type=f32)


def dot_t(a, b):
    return lax.dot_general(a, b, (((1,), (1,)), ((), ())), preferred_element_type=f32)


def keep_rows(mask_ref, crop_ref, channels):
    size = mask_ref.shape[0]
    rows = lax.axis_index("row") * size + lax.broadcasted_iota(jnp.int32, (size, size), 0)
    cols = lax.axis_index("col") * size + lax.broadcasted_iota(jnp.int32, (size, size), 1)
    live = jnp.where(jnp.maximum(rows, cols) < crop_ref[0], 1.0, 0.0)
    keep = (mask_ref[...].astype(f32) * live).astype(bf16)
    pair = lax.broadcasted_iota(jnp.int32, (size * size, size), 0)
    lane = lax.broadcasted_iota(jnp.int32, (size * size, size), 1)
    pick_row = jnp.where(pair // size == lane, 1.0, 0.0).astype(bf16)
    pick_col = jnp.where(pair % size == lane, 1.0, 0.0)
    spread = (dot(pick_row, keep) * pick_col).astype(bf16)
    return dot(spread, jnp.ones((size, channels), bf16))


def start_copies(sems, *pairs):
    copies = [pltpu.make_async_copy(src, dst, sems.at[n]) for n, (src, dst) in enumerate(pairs)]
    for copy in copies:
        copy.start()
    return copies


def gated(projected, block, keep):
    channels = keep.shape[1]
    value = projected[:, block * channels : (block + 1) * channels]
    opened = sigmoid(projected[:, (block + 1) * channels : (block + 2) * channels])
    return (opened * value * keep).astype(bf16), opened, value


def left_kernel(acts_in, mask_in, crop_ref, weights_in, left_ref, acts_ref, mask_ref, weights_ref, sems):
    size, _, channels = acts_ref.shape
    copies = start_copies(
        sems, (acts_in, acts_ref), (weights_in.at[:, pl.ds(0, 2 * channels)], weights_ref), (mask_in, mask_ref),
    )
    copies[0].wait()
    normed, _ = normalize(acts_ref[...].astype(f32).reshape(size * size, channels))
    normed = normed.astype(bf16)
    for copy in copies[1:]:
        copy.wait()
    left, _, _ = gated(dot(normed, weights_ref[...]), 0, keep_rows(mask_ref, crop_ref, channels))
    left_ref[...] = left.reshape(size, size, channels)


def factors_kernel(
    acts_in, mask_in, crop_ref, cotangent_in, weights_in, out_weight_in,
    right_ref, normed_ref, scale_ref, factor_ref, open_ref, gate_factor_ref, upstream_ref,
    acts_ref, mask_ref, cotangent_ref, weights_ref, out_weight_ref, sems,
):
    copies = start_copies(
        sems, (acts_in, acts_ref), (weights_in, weights_ref), (mask_in, mask_ref),
        (cotangent_in, cotangent_ref), (out_weight_in, out_weight_ref),
    )
    size, _, channels = acts_ref.shape
    pairs = size * size
    copies[0].wait()
    normed, scale = normalize(acts_ref[...].astype(f32).reshape(pairs, channels))
    normed_ref[...] = normed
    scale_ref[...] = jnp.broadcast_to(scale, (pairs, channels))
    for copy in copies[1:]:
        copy.wait()
    projected = dot(normed.astype(bf16), weights_ref[...])
    keep = keep_rows(mask_ref, crop_ref, channels)
    for block in (0, 2):
        tile, opened, value = gated(projected, block, keep)
        factor_ref[block] = keep * opened
        factor_ref[block + 1] = keep * value * opened * (1.0 - opened)
    right_ref[...] = tile.astype(f32).reshape(size, size, channels)
    out_open = sigmoid(projected[:, 4 * channels :])
    cotangent = cotangent_ref[...].astype(f32).reshape(pairs, channels)
    lin_grad = (cotangent * out_open).astype(bf16)
    open_ref[...] = out_open
    gate_factor_ref[...] = cotangent * out_open * (1.0 - out_open)
    upstream_ref[...] = dot_t(lin_grad, out_weight_ref[...])


def weighted_sums(weights, start, terms, out, base=None):
    def step(k, _):
        total = weights[start + k, pl.ds(0, 1), :] * terms[0]
        for n in range(1, len(terms)):
            total = total + weights[start + k, pl.ds(n, 1), :] * terms[n]
        if base is not None:
            total = total + base[k]
        out[k] = total.astype(out.dtype)
        return 0

    lax.fori_loop(0, out.shape[0], step, 0, unroll=4)


def panel_kernel(axis, steps, *refs):
    here, panel = lax.axis_index(axis), refs[-1]
    rows = panel.shape[0] // len(steps)
    for step, ref in zip(steps, refs):
        tile = ref[...].astype(f32)
        panel[pl.ds((here ^ step) * rows, rows)] = tile.reshape((rows,) + panel.shape[1:])


def partial_kernel(steps, panel, right_ref, *outs):
    size, _, channels = right_ref.shape
    for step, out in zip(steps, outs):
        start = (lax.axis_index("row") ^ step) * size

        def add(k, sums):
            other = right_ref[k]
            return tuple(sums[i] + panel[start + k, pl.ds(i, 1), :] * other for i in range(size))

        zero = jnp.zeros((size, channels), f32)
        sums = lax.fori_loop(0, size, add, (zero,) * size, unroll=4)
        for i in range(size):
            out[i] = sums[i].astype(out.dtype)


def triangle_kernel(base, tile_ref, upstream_ref, tri_normed_ref, grad_ref):
    size = grad_ref.shape[0]
    for i in range(size):
        here = pl.ds(i * size, size)
        tri_normed, scale = normalize(base[i] + tile_ref[i].astype(f32))
        tri_normed_ref[here, :] = tri_normed
        grad_ref[i] = normalize_back(tri_normed, scale, upstream_ref[here, :]).astype(bf16)


def left_terms_kernel(steps, panel, right, *outs):
    size = right.shape[0]
    for step, out in zip(steps, outs):
        start = (lax.axis_index("col") ^ step) * (size * size)
        weighted_sums(right, 0, [panel[pl.ds(start + j, size, stride=size), :] for j in range(size)], out)


def right_grad_kernel(steps, panel, *refs):
    out, base = refs[-1], refs[len(steps)] if len(refs) > len(steps) + 1 else None
    size = out.shape[0]
    for step, grad in zip(steps, refs):
        start = (lax.axis_index("row") ^ step) * size
        weighted_sums(panel, start, [grad[i].astype(f32) for i in range(size)], out, base)
        base = out


def right_back_kernel(steps, panel, *refs):
    factor_ref, weights_ref, share_ref, out, right_ref = refs[-5:]
    right_grad_kernel(steps, panel, *refs[: len(steps) + 1], right_ref)
    pairs, channels = out.shape
    right = right_ref[...].reshape(pairs, channels)
    grads = jnp.concatenate([(right * factor_ref[block]).astype(bf16) for block in (2, 3)], axis=1)
    out[...] = share_ref[...] + dot_t(grads, weights_ref[:, 2 * channels : 4 * channels])


def add_kernel(base, tile_ref, out):
    out[...] = base[...] + tile_ref[...].astype(f32)


def update_kernel(
    tri_normed_ref, open_ref, gate_factor_ref, weights_ref, out_weight_ref, update_ref, normed_grad_ref
):
    size, _, channels = update_ref.shape
    linear = dot(tri_normed_ref[...].astype(bf16), out_weight_ref[...])
    update = (open_ref[...] * linear).astype(bf16)
    update_ref[...] = update.reshape(size, size, channels)
    out_gate_grad = (gate_factor_ref[...] * linear).astype(bf16)
    normed_grad_ref[...] = dot_t(out_gate_grad, weights_ref[:, 4 * channels :])


def back_kernel(base, *refs):
    *tiles, normed_ref, scale_ref, factor_ref, share_ref, weights_ref, out = refs
    size, _, channels = out.shape
    pairs = size * size
    left = base[...]
    for ref in tiles:
        left = left + ref[...].astype(f32)
    left = left.reshape(pairs, channels)
    grads = jnp.concatenate([(left * factor_ref[block]).astype(bf16) for block in (0, 1)], axis=1)
    normed_grad = share_ref[...] + dot_t(grads, weights_ref[:, : 2 * channels])
    back = normalize_back(normed_ref[...], scale_ref[...], normed_grad)
    out[...] = back.astype(bf16).reshape(size, size, channels)


def call(kernel, outs, *args, scratch=(), flops=0, smem=(), hbm=()):
    spec = pl.BlockSpec(memory_space=pltpu.VMEM)
    total = sum(a.size * a.dtype.itemsize for a in (*args, *outs))
    specs = [spec] * len(args)
    for n in smem:
        specs[n] = pl.BlockSpec(memory_space=pltpu.SMEM)
    args = list(args)
    for n in hbm:
        specs[n] = pl.BlockSpec(memory_space=pltpu.HBM)
        args[n] = pltpu.with_memory_space_constraint(args[n], pltpu.HBM)
    return pl.pallas_call(
        kernel,
        out_shape=tuple(outs),
        in_specs=specs,
        out_specs=(spec,) * len(outs),
        scratch_shapes=scratch,
        compiler_params=pltpu.CompilerParams(vmem_limit_bytes=24 * 2**20),
        cost_estimate=pl.CostEstimate(flops=flops, bytes_accessed=total if flops else 0, transcendentals=0),
    )(*args)


def local(pair_acts, pair_mask, crop_length, cotangent, in_weights, out_weight):
    size, _, channels = pair_acts.shape
    pairs = size * size
    n = lax.axis_size("row")
    tile = jax.ShapeDtypeStruct((size, size, channels), bf16)
    flat = jax.ShapeDtypeStruct((pairs, channels), f32)

    wide = jax.ShapeDtypeStruct((size, size, channels), f32)
    panel = jax.ShapeDtypeStruct((n * size, size, channels), f32)
    work = 2 * size * pairs * channels
    wait = 2**31
    steps = [step for bit in range(n.bit_length() - 2, -1, -1) for step in range(2**bit, 2 ** (bit + 1))]
    row_steps = [n // 2] + [step for step in range(1, n) if step != n // 2]


    def swap(values, axis, step):
        return lax.ppermute(values, axis, [(a, a ^ step) for a in range(n)])

    def gather(values, axis, steps):
        return [values] + [swap(values, axis, step) for step in steps]

    (left,) = call(
        left_kernel, (tile,), pair_acts, pair_mask, crop_length, in_weights,
        smem=(2,), hbm=(0, 1, 3), flops=2 * pairs * channels * 2 * channels,
        scratch=[
            pltpu.VMEM(pair_acts.shape, bf16),
            pltpu.VMEM(pair_mask.shape, jnp.int32),
            pltpu.VMEM((channels, 2 * channels), bf16),
            pltpu.SemaphoreType.DMA((3,)),
        ],
    )
    lefts = gather(left, "col", steps)
    right, normed, scale, factors, out_open, gate_factor, upstream = call(
        factors_kernel,
        (wide, flat, flat, jax.ShapeDtypeStruct((4, pairs, channels), f32), flat, flat, flat),
        pair_acts, pair_mask, crop_length, cotangent, in_weights, out_weight,
        smem=(2,), hbm=(0, 1, 3, 4, 5), flops=2 * pairs * channels * 6 * channels,
        scratch=[
            pltpu.VMEM(pair_acts.shape, bf16),
            pltpu.VMEM(pair_mask.shape, jnp.int32),
            pltpu.VMEM(cotangent.shape, bf16),
            pltpu.VMEM(in_weights.shape, bf16),
            pltpu.VMEM(out_weight.shape, bf16),
            pltpu.SemaphoreType.DMA((5,)),
        ],
    )
    (left_panel,) = call(functools.partial(panel_kernel, "col", [0] + steps), (panel,), *lefts)
    parts = {}
    for step in [0] + row_steps:
        (parts[step],) = call(
            functools.partial(partial_kernel, (step,)), (tile if step else wide,), left_panel, right, flops=work,
        )
    total = parts[0]
    for step in row_steps:
        part = swap(parts[step], "row", step)
        if step != row_steps[-1]:
            (total,) = call(add_kernel, (wide,), total, part, flops=wait)
    tri_normed, tri_grad = call(
        triangle_kernel, (flat, tile), total, part, upstream, flops=20 * pairs * channels,
    )
    grads = gather(tri_grad, "row", row_steps)
    update, partial = call(
        update_kernel, (tile, flat), tri_normed, out_open, gate_factor, in_weights, out_weight,
        flops=4 * pairs * channels * channels,
    )
    (right_grad,) = call(functools.partial(right_grad_kernel, [0]), (wide,), left_panel, tri_grad)
    right, partial, right_grad = lax.optimization_barrier((right, partial, right_grad))
    (grad_panel,) = call(
        functools.partial(panel_kernel, "row", [0] + row_steps), (jax.ShapeDtypeStruct((n * pairs, channels), f32),), *grads
    )
    terms = {}
    for group in (steps, [0]):
        if terms:
            right, terms[last] = lax.optimization_barrier((right, terms[last]))
        last = group[-1]
        outs = call(
            functools.partial(left_terms_kernel, group), (wide if group == [0] else tile,) * len(group),
            grad_panel, right, flops=work,
        )
        terms.update(zip(group, outs))
    total, last = terms[0], []
    for step in steps:
        term = swap(terms[step], "col", step)
        if step == steps[-1]:
            last.append(term)
        else:
            (total,) = call(add_kernel, (wide,), total, term, flops=wait)
    (share,) = call(
        functools.partial(right_back_kernel, row_steps), (flat,),
        left_panel, *grads[1:], right_grad, factors, in_weights, partial,
        scratch=[pltpu.VMEM(wide.shape, f32)],
    )
    (pair_grad,) = call(
        back_kernel, (tile,), total, *last[::-1], normed, scale, factors, share, in_weights,
        flops=2 * pairs * channels * 2 * channels,
    )
    return (update, pair_grad)


def solution(mesh):
    return jax.shard_map(
        local,
        mesh=mesh,
        in_specs=(
            P(("group", "row"), "col", None),
            P(("group", "row"), "col"),
            P("group"),
            P(("group", "row"), "col", None),
            P(),
            P(),
        ),
        out_specs=(P(("group", "row"), "col", None), P(("group", "row"), "col", None)),
        check_vma=False,
    )
```

```python
import functools

import jax
import jax.numpy as jnp
from jax import lax
from jax.experimental import pallas as pl
from jax.experimental.pallas import tpu as pltpu
from jax.sharding import PartitionSpec as P

epsilon = 1e-05
f32 = jnp.float32
bf16 = jnp.bfloat16


def mean_lanes(values):
    return jnp.sum(values, axis=-1, keepdims=True) * (1.0 / values.shape[-1])


def normalize(values):
    center = values - mean_lanes(values)
    variance = mean_lanes(center * center)
    scale = lax.rsqrt(variance + epsilon)
    return (center * scale, scale)


def normalize_back(normed, scale, upstream):
    average = mean_lanes(upstream)
    project = mean_lanes(upstream * normed)
    return scale * (upstream - average - normed * project)


def sigmoid(values):
    return 1.0 / (1.0 + jnp.exp(-values))


def dot(a, b):
    return jnp.dot(a, b, preferred_element_type=f32)


def dot_t(a, b):
    return lax.dot_general(a, b, (((1,), (1,)), ((), ())), preferred_element_type=f32)


def live_pairs(crop_ref, row, col, shape):
    rows = row * shape[0] + lax.broadcasted_iota(jnp.int32, shape, 0)
    cols = col * shape[1] + lax.broadcasted_iota(jnp.int32, shape, 1)
    return jnp.where(jnp.maximum(rows, cols) < crop_ref[0], 1.0, 0.0)


def spread(mask, channels):
    size = mask.shape[0]
    pair = lax.broadcasted_iota(jnp.int32, (size * size, size), 0)
    lane = lax.broadcasted_iota(jnp.int32, (size * size, size), 1)
    pick_row = jnp.where(pair // size == lane, 1.0, 0.0).astype(bf16)
    pick_col = jnp.where(pair % size == lane, 1.0, 0.0)
    picked = (dot(pick_row, mask.astype(bf16)) * pick_col).astype(bf16)
    return dot(picked, jnp.ones((size, channels), bf16))


def start_copies(sems, *pairs):
    copies = [pltpu.make_async_copy(src, dst, sems.at[n]) for n, (src, dst) in enumerate(pairs)]
    for copy in copies:
        copy.start()
    return copies


def gated(projected, block, keep):
    channels = keep.shape[1]
    value = projected[:, block * channels : (block + 1) * channels]
    opened = sigmoid(projected[:, (block + 1) * channels : (block + 2) * channels])
    return (opened * value * keep).astype(bf16), opened, value


def left_kernel(acts_in, mask_in, weights_in, left_ref, acts_ref, mask_ref, weights_ref, sems):
    size, _, channels = acts_ref.shape
    copies = start_copies(
        sems, (acts_in, acts_ref), (weights_in.at[:, pl.ds(0, 2 * channels)], weights_ref), (mask_in, mask_ref),
    )
    copies[0].wait()
    normed, _ = normalize(acts_ref[...].astype(f32).reshape(size * size, channels))
    normed = normed.astype(bf16)
    for copy in copies[1:]:
        copy.wait()
    left, _, _ = gated(dot(normed, weights_ref[...]), 0, spread(mask_ref[...].astype(f32), channels))
    left_ref[...] = left.reshape(size, size, channels)


def factors_kernel(
    acts_in, mask_in, crop_ref, cotangent_in, weights_in, out_weight_in,
    right_ref, normed_ref, scale_ref, factor_ref, open_ref, gate_factor_ref, upstream_ref,
    acts_ref, mask_ref, cotangent_ref, weights_ref, out_weight_ref, sems,
):
    copies = start_copies(
        sems, (acts_in, acts_ref), (weights_in, weights_ref), (mask_in, mask_ref),
        (cotangent_in, cotangent_ref), (out_weight_in, out_weight_ref),
    )
    size, _, channels = acts_ref.shape
    pairs = size * size
    copies[0].wait()
    normed, scale = normalize(acts_ref[...].astype(f32).reshape(pairs, channels))
    normed_ref[...] = normed
    scale_ref[...] = jnp.broadcast_to(scale, (pairs, channels))
    for copy in copies[1:]:
        copy.wait()
    projected = dot(normed.astype(bf16), weights_ref[...])
    live = live_pairs(crop_ref, lax.axis_index("row"), lax.axis_index("col"), (size, size))
    keep = spread(mask_ref[...].astype(f32) * live, channels)
    for block in (0, 2):
        tile, opened, value = gated(projected, block, keep)
        factor_ref[block] = keep * opened
        factor_ref[block + 1] = keep * value * opened * (1.0 - opened)
    right_ref[...] = tile.astype(f32).reshape(size, size, channels)
    out_open = sigmoid(projected[:, 4 * channels :])
    cotangent = cotangent_ref[...].astype(f32).reshape(pairs, channels)
    lin_grad = (cotangent * out_open).astype(bf16)
    open_ref[...] = out_open
    gate_factor_ref[...] = cotangent * out_open * (1.0 - out_open)
    upstream_ref[...] = dot_t(lin_grad, out_weight_ref[...])


def weighted_sums(weights, start, terms, out, base=None):
    def step(k, _):
        total = weights[start + k, pl.ds(0, 1), :] * terms[0]
        for n in range(1, len(terms)):
            total = total + weights[start + k, pl.ds(n, 1), :] * terms[n]
        if base is not None:
            total = total + base[k]
        out[k] = total.astype(out.dtype)
        return 0

    lax.fori_loop(0, out.shape[0], step, 0, unroll=4)


def panel_kernel(axis, steps, *refs):
    here, panel = lax.axis_index(axis), refs[-1]
    rows = panel.shape[0] // len(steps)
    for step, ref in zip(steps, refs):
        tile = ref[...].astype(f32)
        panel[pl.ds((here ^ step) * rows, rows)] = tile.reshape((rows,) + panel.shape[1:])


def left_panel_kernel(steps, crop_ref, *refs):
    row, col, panel = lax.axis_index("row"), lax.axis_index("col"), refs[-1]
    size = refs[0].shape[0]
    for step, ref in zip(steps, refs):
        place = col ^ step
        live = live_pairs(crop_ref, row, place, ref.shape)
        panel[pl.ds(place * size, size)] = ref[...].astype(f32) * live


def partial_kernel(steps, panel, right_ref, *outs):
    size, _, channels = right_ref.shape
    for step, out in zip(steps, outs):
        start = (lax.axis_index("row") ^ step) * size

        def add(k, sums):
            other = right_ref[k]
            return tuple(sums[i] + panel[start + k, pl.ds(i, 1), :] * other for i in range(size))

        zero = jnp.zeros((size, channels), f32)
        sums = lax.fori_loop(0, size, add, (zero,) * size, unroll=4)
        for i in range(size):
            out[i] = sums[i].astype(out.dtype)


def triangle_kernel(base, tile_ref, upstream_ref, tri_normed_ref, grad_ref):
    size = grad_ref.shape[0]
    for i in range(size):
        here = pl.ds(i * size, size)
        tri_normed, scale = normalize(base[i] + tile_ref[i].astype(f32))
        tri_normed_ref[here, :] = tri_normed
        grad_ref[i] = normalize_back(tri_normed, scale, upstream_ref[here, :]).astype(bf16)


def left_terms_kernel(steps, panel, right, *outs):
    size = right.shape[0]
    for step, out in zip(steps, outs):
        start = (lax.axis_index("col") ^ step) * (size * size)
        weighted_sums(right, 0, [panel[pl.ds(start + j, size, stride=size), :] for j in range(size)], out)


def right_grad_kernel(steps, panel, *refs):
    out, base = refs[-1], refs[len(steps)] if len(refs) > len(steps) + 1 else None
    size = out.shape[0]
    for step, grad in zip(steps, refs):
        start = (lax.axis_index("row") ^ step) * size
        weighted_sums(panel, start, [grad[i].astype(f32) for i in range(size)], out, base)
        base = out


def right_back_kernel(steps, panel, *refs):
    factor_ref, weights_ref, share_ref, out, right_ref = refs[-5:]
    right_grad_kernel(steps, panel, *refs[: len(steps) + 1], right_ref)
    pairs, channels = out.shape
    right = right_ref[...].reshape(pairs, channels)
    grads = jnp.concatenate([(right * factor_ref[block]).astype(bf16) for block in (2, 3)], axis=1)
    out[...] = share_ref[...] + dot_t(grads, weights_ref[:, 2 * channels : 4 * channels])


def add_kernel(base, tile_ref, out):
    out[...] = base[...] + tile_ref[...].astype(f32)


def update_kernel(
    tri_normed_ref, open_ref, gate_factor_ref, weights_ref, out_weight_ref, update_ref, normed_grad_ref
):
    size, _, channels = update_ref.shape
    linear = dot(tri_normed_ref[...].astype(bf16), out_weight_ref[...])
    update = (open_ref[...] * linear).astype(bf16)
    update_ref[...] = update.reshape(size, size, channels)
    out_gate_grad = (gate_factor_ref[...] * linear).astype(bf16)
    normed_grad_ref[...] = dot_t(out_gate_grad, weights_ref[:, 4 * channels :])


def back_kernel(base, *refs):
    *tiles, normed_ref, scale_ref, factor_ref, share_ref, weights_ref, out = refs
    size, _, channels = out.shape
    pairs = size * size
    left = base[...]
    for ref in tiles:
        left = left + ref[...].astype(f32)
    left = left.reshape(pairs, channels)
    grads = jnp.concatenate([(left * factor_ref[block]).astype(bf16) for block in (0, 1)], axis=1)
    normed_grad = share_ref[...] + dot_t(grads, weights_ref[:, : 2 * channels])
    back = normalize_back(normed_ref[...], scale_ref[...], normed_grad)
    out[...] = back.astype(bf16).reshape(size, size, channels)


def call(kernel, outs, *args, scratch=(), flops=0, smem=(), hbm=()):
    spec = pl.BlockSpec(memory_space=pltpu.VMEM)
    total = sum(a.size * a.dtype.itemsize for a in (*args, *outs))
    specs = [spec] * len(args)
    for n in smem:
        specs[n] = pl.BlockSpec(memory_space=pltpu.SMEM)
    args = list(args)
    for n in hbm:
        specs[n] = pl.BlockSpec(memory_space=pltpu.HBM)
        args[n] = pltpu.with_memory_space_constraint(args[n], pltpu.HBM)
    return pl.pallas_call(
        kernel,
        out_shape=tuple(outs),
        in_specs=specs,
        out_specs=(spec,) * len(outs),
        scratch_shapes=scratch,
        compiler_params=pltpu.CompilerParams(vmem_limit_bytes=24 * 2**20),
        cost_estimate=pl.CostEstimate(flops=flops, bytes_accessed=total if flops else 0, transcendentals=0),
    )(*args)


def local(pair_acts, pair_mask, crop_length, cotangent, in_weights, out_weight):
    size, _, channels = pair_acts.shape
    pairs = size * size
    n = lax.axis_size("row")
    tile = jax.ShapeDtypeStruct((size, size, channels), bf16)
    flat = jax.ShapeDtypeStruct((pairs, channels), f32)

    wide = jax.ShapeDtypeStruct((size, size, channels), f32)
    panel = jax.ShapeDtypeStruct((n * size, size, channels), f32)
    work = 2 * size * pairs * channels
    wait = 2**31
    steps = [step for bit in range(n.bit_length() - 2, -1, -1) for step in range(2**bit, 2 ** (bit + 1))]
    row_steps = [n // 2] + [step for step in range(1, n) if step != n // 2]


    def swap(values, axis, step):
        return lax.ppermute(values, axis, [(a, a ^ step) for a in range(n)])

    def gather(values, axis, steps):
        return [values] + [swap(values, axis, step) for step in steps]

    (left,) = call(
        left_kernel, (tile,), pair_acts, pair_mask, in_weights,
        hbm=(0, 1, 2), flops=2 * pairs * channels * 2 * channels,
        scratch=[
            pltpu.VMEM(pair_acts.shape, bf16),
            pltpu.VMEM(pair_mask.shape, jnp.int32),
            pltpu.VMEM((channels, 2 * channels), bf16),
            pltpu.SemaphoreType.DMA((3,)),
        ],
    )
    lefts = gather(left, "col", steps)
    right, normed, scale, factors, out_open, gate_factor, upstream = call(
        factors_kernel,
        (wide, flat, flat, jax.ShapeDtypeStruct((4, pairs, channels), f32), flat, flat, flat),
        pair_acts, pair_mask, crop_length, cotangent, in_weights, out_weight,
        smem=(2,), hbm=(0, 1, 3, 4, 5), flops=2 * pairs * channels * 6 * channels,
        scratch=[
            pltpu.VMEM(pair_acts.shape, bf16),
            pltpu.VMEM(pair_mask.shape, jnp.int32),
            pltpu.VMEM(cotangent.shape, bf16),
            pltpu.VMEM(in_weights.shape, bf16),
            pltpu.VMEM(out_weight.shape, bf16),
            pltpu.SemaphoreType.DMA((5,)),
        ],
    )
    (left_panel,) = call(
        functools.partial(left_panel_kernel, [0] + steps), (panel,), crop_length, *lefts, smem=(0,)
    )
    parts = {}
    for step in [0] + row_steps:
        (parts[step],) = call(
            functools.partial(partial_kernel, (step,)), (tile if step else wide,), left_panel, right, flops=work,
        )
    total = parts[0]
    for step in row_steps:
        part = swap(parts[step], "row", step)
        if step != row_steps[-1]:
            (total,) = call(add_kernel, (wide,), total, part, flops=wait)
    tri_normed, tri_grad = call(
        triangle_kernel, (flat, tile), total, part, upstream, flops=20 * pairs * channels,
    )
    grads = gather(tri_grad, "row", row_steps)
    update, partial = call(
        update_kernel, (tile, flat), tri_normed, out_open, gate_factor, in_weights, out_weight,
        flops=4 * pairs * channels * channels,
    )
    (right_grad,) = call(functools.partial(right_grad_kernel, [0]), (wide,), left_panel, tri_grad)
    right, partial, right_grad = lax.optimization_barrier((right, partial, right_grad))
    (grad_panel,) = call(
        functools.partial(panel_kernel, "row", [0] + row_steps), (jax.ShapeDtypeStruct((n * pairs, channels), f32),), *grads
    )
    terms = {}
    for group in (steps, [0]):
        if terms:
            right, terms[last] = lax.optimization_barrier((right, terms[last]))
        last = group[-1]
        outs = call(
            functools.partial(left_terms_kernel, group), (wide if group == [0] else tile,) * len(group),
            grad_panel, right, flops=work,
        )
        terms.update(zip(group, outs))
    total, last = terms[0], []
    for step in steps:
        term = swap(terms[step], "col", step)
        if step == steps[-1]:
            last.append(term)
        else:
            (total,) = call(add_kernel, (wide,), total, term, flops=wait)
    (share,) = call(
        functools.partial(right_back_kernel, row_steps), (flat,),
        left_panel, *grads[1:], right_grad, factors, in_weights, partial,
        scratch=[pltpu.VMEM(wide.shape, f32)],
    )
    (pair_grad,) = call(
        back_kernel, (tile,), total, *last[::-1], normed, scale, factors, share, in_weights,
        flops=2 * pairs * channels * 2 * channels,
    )
    return (update, pair_grad)


def solution(mesh):
    return jax.shard_map(
        local,
        mesh=mesh,
        in_specs=(
            P(("group", "row"), "col", None),
            P(("group", "row"), "col"),
            P("group"),
            P(("group", "row"), "col", None),
            P(),
            P(),
        ),
        out_specs=(P(("group", "row"), "col", None), P(("group", "row"), "col", None)),
        check_vma=False,
    )
```

```python
import functools

import jax
import jax.numpy as jnp
from jax import lax
from jax.experimental import pallas as pl
from jax.experimental.pallas import tpu as pltpu
from jax.sharding import PartitionSpec as P

epsilon = 1e-05
f32 = jnp.float32
bf16 = jnp.bfloat16


def mean_lanes(values):
    return jnp.sum(values, axis=-1, keepdims=True) * (1.0 / values.shape[-1])


def normalize(values):
    center = values - mean_lanes(values)
    variance = mean_lanes(center * center)
    scale = lax.rsqrt(variance + epsilon)
    return (center * scale, scale)


def normalize_back(normed, scale, upstream):
    average = mean_lanes(upstream)
    project = mean_lanes(upstream * normed)
    return scale * (upstream - average - normed * project)


def sigmoid(values):
    return 1.0 / (1.0 + jnp.exp(-values))


def dot(a, b):
    return jnp.dot(a, b, preferred_element_type=f32)


def dot_t(a, b):
    return lax.dot_general(a, b, (((1,), (1,)), ((), ())), preferred_element_type=f32)


def live_pairs(crop_ref, row, col, shape):
    rows = row * shape[0] + lax.broadcasted_iota(jnp.int32, shape, 0)
    cols = col * shape[1] + lax.broadcasted_iota(jnp.int32, shape, 1)
    return jnp.where(jnp.maximum(rows, cols) < crop_ref[0], 1.0, 0.0)


def spread(mask, channels):
    size = mask.shape[0]
    pair = lax.broadcasted_iota(jnp.int32, (size * size, size), 0)
    lane = lax.broadcasted_iota(jnp.int32, (size * size, size), 1)
    pick_row = jnp.where(pair // size == lane, 1.0, 0.0).astype(bf16)
    pick_col = jnp.where(pair % size == lane, 1.0, 0.0)
    picked = (dot(pick_row, mask.astype(bf16)) * pick_col).astype(bf16)
    return dot(picked, jnp.ones((size, channels), bf16))


def start_copies(sems, *pairs):
    copies = [pltpu.make_async_copy(src, dst, sems.at[n]) for n, (src, dst) in enumerate(pairs)]
    for copy in copies:
        copy.start()
    return copies


def gated(projected, block, keep):
    channels = keep.shape[1]
    value = projected[:, block * channels : (block + 1) * channels]
    opened = sigmoid(projected[:, (block + 1) * channels : (block + 2) * channels])
    return (opened * value * keep).astype(bf16), opened, value


def left_kernel(acts_in, mask_in, weights_in, left_ref, acts_ref, mask_ref, weights_ref, sems):
    size, _, channels = acts_ref.shape
    copies = start_copies(
        sems, (acts_in, acts_ref), (weights_in.at[:, pl.ds(0, 2 * channels)], weights_ref), (mask_in, mask_ref),
    )
    copies[0].wait()
    normed, _ = normalize(acts_ref[...].astype(f32).reshape(size * size, channels))
    normed = normed.astype(bf16)
    for copy in copies[1:]:
        copy.wait()
    left, _, _ = gated(dot(normed, weights_ref[...]), 0, spread(mask_ref[...].astype(f32), channels))
    left_ref[...] = left.reshape(size, size, channels)


def factors_kernel(
    acts_in, mask_in, crop_ref, cotangent_in, weights_in, out_weight_in,
    right_ref, normed_ref, scale_ref, factor_ref, open_ref, gate_factor_ref, upstream_ref,
    acts_ref, mask_ref, cotangent_ref, weights_ref, out_weight_ref, sems,
):
    copies = start_copies(
        sems, (acts_in, acts_ref), (weights_in, weights_ref), (mask_in, mask_ref),
        (cotangent_in, cotangent_ref), (out_weight_in, out_weight_ref),
    )
    size, _, channels = acts_ref.shape
    pairs = size * size
    copies[0].wait()
    normed, scale = normalize(acts_ref[...].astype(f32).reshape(pairs, channels))
    normed_ref[...] = normed
    scale_ref[...] = jnp.broadcast_to(scale, (pairs, channels))
    for copy in copies[1:]:
        copy.wait()
    projected = dot(normed.astype(bf16), weights_ref[...])
    live = live_pairs(crop_ref, lax.axis_index("row"), lax.axis_index("col"), (size, size))
    keep = spread(mask_ref[...].astype(f32) * live, channels)
    for block in (0, 2):
        tile, opened, value = gated(projected, block, keep)
        factor_ref[block] = keep * opened
        factor_ref[block + 1] = keep * value * opened * (1.0 - opened)
    right_ref[...] = tile.astype(f32).reshape(size, size, channels)
    out_open = sigmoid(projected[:, 4 * channels :])
    cotangent = cotangent_ref[...].astype(f32).reshape(pairs, channels)
    lin_grad = (cotangent * out_open).astype(bf16)
    open_ref[...] = out_open
    gate_factor_ref[...] = cotangent * out_open * (1.0 - out_open)
    upstream_ref[...] = dot_t(lin_grad, out_weight_ref[...])


def weighted_sums(weights, start, terms, out, base=None):
    def step(k, _):
        total = weights[start + k, pl.ds(0, 1), :] * terms[0]
        for n in range(1, len(terms)):
            total = total + weights[start + k, pl.ds(n, 1), :] * terms[n]
        if base is not None:
            total = total + base[k]
        out[k] = total.astype(out.dtype)
        return 0

    lax.fori_loop(0, out.shape[0], step, 0, unroll=4)


def panel_kernel(axis, steps, *refs):
    here, panel = lax.axis_index(axis), refs[-1]
    rows = panel.shape[0] // len(steps)
    for step, ref in zip(steps, refs):
        tile = ref[...].astype(f32)
        panel[pl.ds((here ^ step) * rows, rows)] = tile.reshape((rows,) + panel.shape[1:])


def left_panel_kernel(steps, crop_ref, *refs):
    row, col, panel = lax.axis_index("row"), lax.axis_index("col"), refs[-1]
    size, _, channels = refs[0].shape
    rows = row * size + lax.broadcasted_iota(jnp.int32, (size, 1, channels), 0)
    row_live = jnp.where(rows < crop_ref[0], 1.0, 0.0)
    for step, ref in zip(steps, refs):
        place = col ^ step
        cols = place * size + lax.broadcasted_iota(jnp.int32, (1, size, channels), 1)
        col_live = jnp.where(cols < crop_ref[0], 1.0, 0.0)
        panel[pl.ds(place * size, size)] = ref[...].astype(f32) * (row_live * col_live)


def partial_kernel(steps, panel, right_ref, *outs):
    size, _, channels = right_ref.shape
    for step, out in zip(steps, outs):
        start = (lax.axis_index("row") ^ step) * size

        def add(k, sums):
            other = right_ref[k]
            return tuple(sums[i] + panel[start + k, pl.ds(i, 1), :] * other for i in range(size))

        zero = jnp.zeros((size, channels), f32)
        sums = lax.fori_loop(0, size, add, (zero,) * size, unroll=4)
        for i in range(size):
            out[i] = sums[i].astype(out.dtype)


def triangle_kernel(base, tile_ref, upstream_ref, tri_normed_ref, grad_ref):
    size = grad_ref.shape[0]
    for i in range(size):
        here = pl.ds(i * size, size)
        tri_normed, scale = normalize(base[i] + tile_ref[i].astype(f32))
        tri_normed_ref[here, :] = tri_normed
        grad_ref[i] = normalize_back(tri_normed, scale, upstream_ref[here, :]).astype(bf16)


def left_terms_kernel(steps, panel, right, *outs):
    size = right.shape[0]
    for step, out in zip(steps, outs):
        start = (lax.axis_index("col") ^ step) * (size * size)
        weighted_sums(right, 0, [panel[pl.ds(start + j, size, stride=size), :] for j in range(size)], out)


def right_grad_kernel(steps, panel, *refs):
    out, base = refs[-1], refs[len(steps)] if len(refs) > len(steps) + 1 else None
    size = out.shape[0]
    for step, grad in zip(steps, refs):
        start = (lax.axis_index("row") ^ step) * size
        weighted_sums(panel, start, [grad[i].astype(f32) for i in range(size)], out, base)
        base = out


def right_back_kernel(steps, panel, *refs):
    factor_ref, weights_ref, share_ref, out, right_ref = refs[-5:]
    right_grad_kernel(steps, panel, *refs[: len(steps) + 1], right_ref)
    pairs, channels = out.shape
    right = right_ref[...].reshape(pairs, channels)
    grads = jnp.concatenate([(right * factor_ref[block]).astype(bf16) for block in (2, 3)], axis=1)
    out[...] = share_ref[...] + dot_t(grads, weights_ref[:, 2 * channels : 4 * channels])


def add_kernel(base, tile_ref, out):
    out[...] = base[...] + tile_ref[...].astype(f32)


def update_kernel(
    tri_normed_ref, open_ref, gate_factor_ref, weights_ref, out_weight_ref, update_ref, normed_grad_ref
):
    size, _, channels = update_ref.shape
    linear = dot(tri_normed_ref[...].astype(bf16), out_weight_ref[...])
    update = (open_ref[...] * linear).astype(bf16)
    update_ref[...] = update.reshape(size, size, channels)
    out_gate_grad = (gate_factor_ref[...] * linear).astype(bf16)
    normed_grad_ref[...] = dot_t(out_gate_grad, weights_ref[:, 4 * channels :])


def back_kernel(base, *refs):
    *tiles, normed_ref, scale_ref, factor_ref, share_ref, weights_ref, out = refs
    size, _, channels = out.shape
    pairs = size * size
    left = base[...]
    for ref in tiles:
        left = left + ref[...].astype(f32)
    left = left.reshape(pairs, channels)
    grads = jnp.concatenate([(left * factor_ref[block]).astype(bf16) for block in (0, 1)], axis=1)
    normed_grad = share_ref[...] + dot_t(grads, weights_ref[:, : 2 * channels])
    back = normalize_back(normed_ref[...], scale_ref[...], normed_grad)
    out[...] = back.astype(bf16).reshape(size, size, channels)


def call(kernel, outs, *args, scratch=(), flops=0, smem=(), hbm=()):
    spec = pl.BlockSpec(memory_space=pltpu.VMEM)
    total = sum(a.size * a.dtype.itemsize for a in (*args, *outs))
    specs = [spec] * len(args)
    for n in smem:
        specs[n] = pl.BlockSpec(memory_space=pltpu.SMEM)
    args = list(args)
    for n in hbm:
        specs[n] = pl.BlockSpec(memory_space=pltpu.HBM)
        args[n] = pltpu.with_memory_space_constraint(args[n], pltpu.HBM)
    return pl.pallas_call(
        kernel,
        out_shape=tuple(outs),
        in_specs=specs,
        out_specs=(spec,) * len(outs),
        scratch_shapes=scratch,
        compiler_params=pltpu.CompilerParams(vmem_limit_bytes=24 * 2**20),
        cost_estimate=pl.CostEstimate(flops=flops, bytes_accessed=total if flops else 0, transcendentals=0),
    )(*args)


def local(pair_acts, pair_mask, crop_length, cotangent, in_weights, out_weight):
    size, _, channels = pair_acts.shape
    pairs = size * size
    n = lax.axis_size("row")
    tile = jax.ShapeDtypeStruct((size, size, channels), bf16)
    flat = jax.ShapeDtypeStruct((pairs, channels), f32)

    wide = jax.ShapeDtypeStruct((size, size, channels), f32)
    panel = jax.ShapeDtypeStruct((n * size, size, channels), f32)
    work = 2 * size * pairs * channels
    wait = 2**31
    steps = [step for bit in range(n.bit_length() - 2, -1, -1) for step in range(2**bit, 2 ** (bit + 1))]
    row_steps = list(range(n - 1, 0, -1))


    def swap(values, axis, step):
        return lax.ppermute(values, axis, [(a, a ^ step) for a in range(n)])

    def gather(values, axis, steps):
        return [values] + [swap(values, axis, step) for step in steps]

    (left,) = call(
        left_kernel, (tile,), pair_acts, pair_mask, in_weights,
        hbm=(0, 1, 2), flops=2 * pairs * channels * 2 * channels,
        scratch=[
            pltpu.VMEM(pair_acts.shape, bf16),
            pltpu.VMEM(pair_mask.shape, jnp.int32),
            pltpu.VMEM((channels, 2 * channels), bf16),
            pltpu.SemaphoreType.DMA((3,)),
        ],
    )
    lefts = gather(left, "col", steps)
    right, normed, scale, factors, out_open, gate_factor, upstream = call(
        factors_kernel,
        (wide, flat, flat, jax.ShapeDtypeStruct((4, pairs, channels), f32), flat, flat, flat),
        pair_acts, pair_mask, crop_length, cotangent, in_weights, out_weight,
        smem=(2,), hbm=(0, 1, 3, 4, 5), flops=2 * pairs * channels * 6 * channels,
        scratch=[
            pltpu.VMEM(pair_acts.shape, bf16),
            pltpu.VMEM(pair_mask.shape, jnp.int32),
            pltpu.VMEM(cotangent.shape, bf16),
            pltpu.VMEM(in_weights.shape, bf16),
            pltpu.VMEM(out_weight.shape, bf16),
            pltpu.SemaphoreType.DMA((5,)),
        ],
    )
    (left_panel,) = call(
        functools.partial(left_panel_kernel, [0] + steps), (panel,), crop_length, *lefts, smem=(0,)
    )
    parts = {}
    for step in [0] + row_steps:
        (parts[step],) = call(
            functools.partial(partial_kernel, (step,)), (tile if step else wide,), left_panel, right, flops=work,
        )
    total = parts[0]
    for step in row_steps:
        part = swap(parts[step], "row", step)
        if step != row_steps[-1]:
            (total,) = call(add_kernel, (wide,), total, part, flops=wait)
    tri_normed, tri_grad = call(
        triangle_kernel, (flat, tile), total, part, upstream, flops=20 * pairs * channels,
    )
    grads = gather(tri_grad, "row", row_steps)
    update, partial = call(
        update_kernel, (tile, flat), tri_normed, out_open, gate_factor, in_weights, out_weight,
        flops=4 * pairs * channels * channels,
    )
    (right_grad,) = call(functools.partial(right_grad_kernel, [0]), (wide,), left_panel, tri_grad)
    right, partial, right_grad = lax.optimization_barrier((right, partial, right_grad))
    (grad_panel,) = call(
        functools.partial(panel_kernel, "row", [0] + row_steps), (jax.ShapeDtypeStruct((n * pairs, channels), f32),), *grads
    )
    terms = {}
    for group in (steps[: n // 2], steps[n // 2 :], [0]):
        if terms:
            right, terms[last] = lax.optimization_barrier((right, terms[last]))
        last = group[-1]
        outs = call(
            functools.partial(left_terms_kernel, group), (wide if group == [0] else tile,) * len(group),
            grad_panel, right, flops=work,
        )
        terms.update(zip(group, outs))
    total, last = terms[0], []
    for step in steps:
        term = swap(terms[step], "col", step)
        if step == steps[-1]:
            last.append(term)
        else:
            (total,) = call(add_kernel, (wide,), total, term, flops=wait)
    (share,) = call(
        functools.partial(right_back_kernel, row_steps), (flat,),
        left_panel, *grads[1:], right_grad, factors, in_weights, partial,
        scratch=[pltpu.VMEM(wide.shape, f32)],
    )
    (pair_grad,) = call(
        back_kernel, (tile,), total, *last[::-1], normed, scale, factors, share, in_weights,
        flops=2 * pairs * channels * 2 * channels,
    )
    return (update, pair_grad)


def solution(mesh):
    return jax.shard_map(
        local,
        mesh=mesh,
        in_specs=(
            P(("group", "row"), "col", None),
            P(("group", "row"), "col"),
            P("group"),
            P(("group", "row"), "col", None),
            P(),
            P(),
        ),
        out_specs=(P(("group", "row"), "col", None), P(("group", "row"), "col", None)),
        check_vma=False,
    )
```

```python
import functools

import jax
import jax.numpy as jnp
from jax import lax
from jax.experimental import pallas as pl
from jax.experimental.pallas import tpu as pltpu
from jax.sharding import PartitionSpec as P

epsilon = 1e-05
f32 = jnp.float32
bf16 = jnp.bfloat16


def mean_lanes(values):
    return jnp.sum(values, axis=-1, keepdims=True) * (1.0 / values.shape[-1])


def normalize(values):
    center = values - mean_lanes(values)
    variance = mean_lanes(center * center)
    scale = lax.rsqrt(variance + epsilon)
    return (center * scale, scale)


def normalize_back(normed, scale, upstream):
    average = mean_lanes(upstream)
    project = mean_lanes(upstream * normed)
    return scale * (upstream - average - normed * project)


def sigmoid(values):
    return 1.0 / (1.0 + jnp.exp(-values))


def dot(a, b):
    return jnp.dot(a, b, preferred_element_type=f32)


def dot_t(a, b):
    return lax.dot_general(a, b, (((1,), (1,)), ((), ())), preferred_element_type=f32)


def live_pairs(crop_ref, row, col, shape):
    rows = row * shape[0] + lax.broadcasted_iota(jnp.int32, shape, 0)
    cols = col * shape[1] + lax.broadcasted_iota(jnp.int32, shape, 1)
    return jnp.where(jnp.maximum(rows, cols) < crop_ref[0], 1.0, 0.0)


def spread(mask, channels):
    size = mask.shape[0]
    pair = lax.broadcasted_iota(jnp.int32, (size * size, size), 0)
    lane = lax.broadcasted_iota(jnp.int32, (size * size, size), 1)
    pick_row = jnp.where(pair // size == lane, 1.0, 0.0).astype(bf16)
    pick_col = jnp.where(pair % size == lane, 1.0, 0.0)
    picked = (dot(pick_row, mask.astype(bf16)) * pick_col).astype(bf16)
    return dot(picked, jnp.ones((size, channels), bf16))


def start_copies(sems, *pairs):
    copies = [pltpu.make_async_copy(src, dst, sems.at[n]) for n, (src, dst) in enumerate(pairs)]
    for copy in copies:
        copy.start()
    return copies


def gated(projected, block, keep):
    channels = keep.shape[1]
    value = projected[:, block * channels : (block + 1) * channels]
    opened = sigmoid(projected[:, (block + 1) * channels : (block + 2) * channels])
    return (opened * value * keep).astype(bf16), opened, value


def left_kernel(acts_in, mask_in, weights_in, left_ref, acts_ref, mask_ref, weights_ref, sems):
    size, _, channels = acts_ref.shape
    copies = start_copies(
        sems, (acts_in, acts_ref), (weights_in.at[:, pl.ds(0, 2 * channels)], weights_ref), (mask_in, mask_ref),
    )
    copies[0].wait()
    normed, _ = normalize(acts_ref[...].astype(f32).reshape(size * size, channels))
    normed = normed.astype(bf16)
    for copy in copies[1:]:
        copy.wait()
    left, _, _ = gated(dot(normed, weights_ref[...]), 0, spread(mask_ref[...].astype(f32), channels))
    left_ref[...] = left.reshape(size, size, channels)


def factors_kernel(
    acts_in, mask_in, crop_ref, cotangent_in, weights_in, out_weight_in,
    right_ref, normed_ref, scale_ref, factor_ref, open_ref, gate_factor_ref, upstream_ref,
    acts_ref, mask_ref, cotangent_ref, weights_ref, out_weight_ref, sems,
):
    copies = start_copies(
        sems, (acts_in, acts_ref), (weights_in, weights_ref), (mask_in, mask_ref),
        (cotangent_in, cotangent_ref), (out_weight_in, out_weight_ref),
    )
    size, _, channels = acts_ref.shape
    pairs = size * size
    copies[0].wait()
    normed, scale = normalize(acts_ref[...].astype(f32).reshape(pairs, channels))
    normed_ref[...] = normed
    scale_ref[...] = jnp.broadcast_to(scale, (pairs, channels))
    for copy in copies[1:]:
        copy.wait()
    projected = dot(normed.astype(bf16), weights_ref[...])
    live = live_pairs(crop_ref, lax.axis_index("row"), lax.axis_index("col"), (size, size))
    keep = spread(mask_ref[...].astype(f32) * live, channels)
    for block in (0, 2):
        tile, opened, value = gated(projected, block, keep)
        factor_ref[block] = keep * opened
        factor_ref[block + 1] = keep * value * opened * (1.0 - opened)
    right_ref[...] = tile.astype(f32).reshape(size, size, channels)
    out_open = sigmoid(projected[:, 4 * channels :])
    cotangent = cotangent_ref[...].astype(f32).reshape(pairs, channels)
    lin_grad = (cotangent * out_open).astype(bf16)
    open_ref[...] = out_open
    gate_factor_ref[...] = cotangent * out_open * (1.0 - out_open)
    upstream_ref[...] = dot_t(lin_grad, out_weight_ref[...])


def weighted_sums(weights, start, terms, out, base=None):
    def step(k, _):
        total = weights[start + k, pl.ds(0, 1), :] * terms[0]
        for n in range(1, len(terms)):
            total = total + weights[start + k, pl.ds(n, 1), :] * terms[n]
        if base is not None:
            total = total + base[k]
        out[k] = total.astype(out.dtype)
        return 0

    lax.fori_loop(0, out.shape[0], step, 0, unroll=4)


def left_panel_kernel(steps, crop_ref, *refs):
    row, col, panel = lax.axis_index("row"), lax.axis_index("col"), refs[-1]
    size, _, channels = refs[0].shape
    rows = row * size + lax.broadcasted_iota(jnp.int32, (size, 1, channels), 0)
    row_live = jnp.where(rows < crop_ref[0], 1.0, 0.0)
    for step, ref in zip(steps, refs):
        place = col ^ step
        cols = place * size + lax.broadcasted_iota(jnp.int32, (1, size, channels), 1)
        col_live = jnp.where(cols < crop_ref[0], 1.0, 0.0)
        panel[pl.ds(place * size, size)] = ref[...].astype(f32) * (row_live * col_live)


def partial_kernel(steps, crop_ref, *refs):
    count = len(steps)
    lefts, right_ref, outs, left = refs[:count], refs[count], refs[count + 1 : -1], refs[-1]
    size, _, channels = right_ref.shape
    rows = lax.axis_index("row") * size + lax.broadcasted_iota(jnp.int32, (size, 1, channels), 0)
    row_live = jnp.where(rows < crop_ref[0], 1.0, 0.0)
    for step, left_ref, out in zip(steps, lefts, outs):
        cols = (lax.axis_index("col") ^ step) * size + lax.broadcasted_iota(jnp.int32, (1, size, channels), 1)
        left[...] = left_ref[...].astype(f32) * (row_live * jnp.where(cols < crop_ref[0], 1.0, 0.0))

        def add(k, sums):
            other = right_ref[k]
            return tuple(sums[i] + left[k, pl.ds(i, 1), :] * other for i in range(size))

        zero = jnp.zeros((size, channels), f32)
        sums = lax.fori_loop(0, size, add, (zero,) * size, unroll=4)
        for i in range(size):
            out[i] = sums[i]


def pick_kernel(steps, *refs):
    here = lax.axis_index("row") ^ lax.axis_index("col")
    tiles, outs = refs[: len(steps)], refs[len(steps) :]
    for step, out in zip(steps, outs):
        for other, tile in enumerate(tiles):

            @pl.when((here ^ step) == other)
            def _():
                out[...] = tile[...].astype(out.dtype)


def triangle_kernel(base, tile_ref, upstream_ref, tri_normed_ref, grad_ref):
    size = grad_ref.shape[0]
    for i in range(size):
        here = pl.ds(i * size, size)
        tri_normed, scale = normalize(base[i] + tile_ref[i].astype(f32))
        tri_normed_ref[here, :] = tri_normed
        grad_ref[i] = normalize_back(tri_normed, scale, upstream_ref[here, :]).astype(bf16)


def left_terms_kernel(grad_ref, right, out, grad):
    size, _, channels = out.shape
    grad[...] = grad_ref[...].astype(f32).reshape(size * size, channels)
    weighted_sums(right, 0, [grad[pl.ds(j, size, stride=size), :] for j in range(size)], out)


def right_grad_kernel(steps, panel, *refs):
    out, base = refs[-1], refs[len(steps)] if len(refs) > len(steps) + 1 else None
    size = out.shape[0]
    for step, grad in zip(steps, refs):
        start = (lax.axis_index("row") ^ step) * size
        weighted_sums(panel, start, [grad[i].astype(f32) for i in range(size)], out, base)
        base = out


def right_back_kernel(steps, panel, *refs):
    factor_ref, weights_ref, share_ref, out, right_ref = refs[-5:]
    right_grad_kernel(steps, panel, *refs[: len(steps) + 1], right_ref)
    pairs, channels = out.shape
    right = right_ref[...].reshape(pairs, channels)
    grads = jnp.concatenate([(right * factor_ref[block]).astype(bf16) for block in (2, 3)], axis=1)
    out[...] = share_ref[...] + dot_t(grads, weights_ref[:, 2 * channels : 4 * channels])


def add_kernel(base, tile_ref, out):
    out[...] = base[...] + tile_ref[...].astype(f32)


def update_kernel(
    tri_normed_ref, open_ref, gate_factor_ref, weights_ref, out_weight_ref, update_ref, normed_grad_ref
):
    size, _, channels = update_ref.shape
    linear = dot(tri_normed_ref[...].astype(bf16), out_weight_ref[...])
    update = (open_ref[...] * linear).astype(bf16)
    update_ref[...] = update.reshape(size, size, channels)
    out_gate_grad = (gate_factor_ref[...] * linear).astype(bf16)
    normed_grad_ref[...] = dot_t(out_gate_grad, weights_ref[:, 4 * channels :])


def back_kernel(base, *refs):
    *tiles, normed_ref, scale_ref, factor_ref, share_ref, weights_ref, out = refs
    size, _, channels = out.shape
    pairs = size * size
    left = base[...]
    for ref in tiles:
        left = left + ref[...].astype(f32)
    left = left.reshape(pairs, channels)
    grads = jnp.concatenate([(left * factor_ref[block]).astype(bf16) for block in (0, 1)], axis=1)
    normed_grad = share_ref[...] + dot_t(grads, weights_ref[:, : 2 * channels])
    back = normalize_back(normed_ref[...], scale_ref[...], normed_grad)
    out[...] = back.astype(bf16).reshape(size, size, channels)


def call(kernel, outs, *args, scratch=(), flops=0, smem=(), hbm=()):
    spec = pl.BlockSpec(memory_space=pltpu.VMEM)
    total = sum(a.size * a.dtype.itemsize for a in (*args, *outs))
    specs = [spec] * len(args)
    for n in smem:
        specs[n] = pl.BlockSpec(memory_space=pltpu.SMEM)
    args = list(args)
    for n in hbm:
        specs[n] = pl.BlockSpec(memory_space=pltpu.HBM)
        args[n] = pltpu.with_memory_space_constraint(args[n], pltpu.HBM)
    return pl.pallas_call(
        kernel,
        out_shape=tuple(outs),
        in_specs=specs,
        out_specs=(spec,) * len(outs),
        scratch_shapes=scratch,
        compiler_params=pltpu.CompilerParams(vmem_limit_bytes=24 * 2**20),
        cost_estimate=pl.CostEstimate(flops=flops, bytes_accessed=total if flops else 0, transcendentals=0),
    )(*args)


def local(pair_acts, pair_mask, crop_length, cotangent, in_weights, out_weight):
    size, _, channels = pair_acts.shape
    pairs = size * size
    n = lax.axis_size("row")
    tile = jax.ShapeDtypeStruct((size, size, channels), bf16)
    flat = jax.ShapeDtypeStruct((pairs, channels), f32)

    wide = jax.ShapeDtypeStruct((size, size, channels), f32)
    panel = jax.ShapeDtypeStruct((n * size, size, channels), f32)
    work = 2 * size * pairs * channels
    wait = 2**31
    steps = [step for bit in range(n.bit_length() - 2, -1, -1) for step in range(2**bit, 2 ** (bit + 1))]
    row_steps = [n // 2] + [step for step in range(1, n) if step != n // 2]


    def swap(values, axis, step):
        return lax.ppermute(values, axis, [(a, a ^ step) for a in range(n)])

    def gather(values, axis, steps):
        return [values] + [swap(values, axis, step) for step in steps]

    (left,) = call(
        left_kernel, (tile,), pair_acts, pair_mask, in_weights,
        hbm=(0, 1, 2), flops=2 * pairs * channels * 2 * channels,
        scratch=[
            pltpu.VMEM(pair_acts.shape, bf16),
            pltpu.VMEM(pair_mask.shape, jnp.int32),
            pltpu.VMEM((channels, 2 * channels), bf16),
            pltpu.SemaphoreType.DMA((3,)),
        ],
    )
    lefts = gather(left, "col", steps)
    right, normed, scale, factors, out_open, gate_factor, upstream = call(
        factors_kernel,
        (wide, flat, flat, jax.ShapeDtypeStruct((4, pairs, channels), f32), flat, flat, flat),
        pair_acts, pair_mask, crop_length, cotangent, in_weights, out_weight,
        smem=(2,), hbm=(0, 1, 3, 4, 5), flops=2 * pairs * channels * 6 * channels,
        scratch=[
            pltpu.VMEM(pair_acts.shape, bf16),
            pltpu.VMEM(pair_mask.shape, jnp.int32),
            pltpu.VMEM(cotangent.shape, bf16),
            pltpu.VMEM(in_weights.shape, bf16),
            pltpu.VMEM(out_weight.shape, bf16),
            pltpu.SemaphoreType.DMA((5,)),
        ],
    )
    parts = []
    order = [0] + steps
    for group in [[at] for at in range(n - 2)] + [[n - 2, n - 1]]:
        parts += call(
            functools.partial(partial_kernel, [order[at] for at in group]), (wide,) * len(group),
            crop_length, *(lefts[at] for at in group), right, smem=(0,), flops=work,
            scratch=[pltpu.VMEM(wide.shape, f32)],
        )
    parts = [part for _, part in sorted(zip(order, parts), key=lambda each: each[0])]
    total, *parts = call(
        functools.partial(pick_kernel, [0] + row_steps), (wide,) + (tile,) * (n - 1), *parts,
        flops=pairs * channels,
    )
    (left_panel,) = call(
        functools.partial(left_panel_kernel, [0] + steps), (panel,), crop_length, *lefts, smem=(0,)
    )
    for step, part in zip(row_steps, parts):
        part = swap(part, "row", step)
        if step != row_steps[-1]:
            (total,) = call(add_kernel, (wide,), total, part, flops=wait)
    tri_normed, tri_grad = call(
        triangle_kernel, (flat, tile), total, part, upstream, flops=20 * pairs * channels,
    )
    grads = gather(tri_grad, "row", row_steps)
    update, partial = call(
        update_kernel, (tile, flat), tri_normed, out_open, gate_factor, in_weights, out_weight,
        flops=4 * pairs * channels * channels,
    )
    (right_grad,) = call(functools.partial(right_grad_kernel, [0]), (wide,), left_panel, tri_grad)
    right, partial, right_grad = lax.optimization_barrier((right, partial, right_grad))
    terms = [None] * n
    for step, grad in zip([0] + row_steps, grads):
        (terms[step],) = call(
            left_terms_kernel, (wide,), grad, right, scratch=[pltpu.VMEM((pairs, channels), f32)], flops=work,
        )
    total, *terms = call(
        functools.partial(pick_kernel, [0] + steps), (wide,) + (tile,) * (n - 1), *terms, flops=pairs * channels,
    )
    for step, term in zip(steps, terms):
        term = swap(term, "col", step)
        if step != steps[-1]:
            (total,) = call(add_kernel, (wide,), total, term, flops=wait)
    (share,) = call(
        functools.partial(right_back_kernel, row_steps), (flat,),
        left_panel, *grads[1:], right_grad, factors, in_weights, partial,
        scratch=[pltpu.VMEM(wide.shape, f32)],
    )
    (pair_grad,) = call(
        back_kernel, (tile,), total, term, normed, scale, factors, share, in_weights,
        flops=2 * pairs * channels * 2 * channels,
    )
    return (update, pair_grad)


def solution(mesh):
    return jax.shard_map(
        local,
        mesh=mesh,
        in_specs=(
            P(("group", "row"), "col", None),
            P(("group", "row"), "col"),
            P("group"),
            P(("group", "row"), "col", None),
            P(),
            P(),
        ),
        out_specs=(P(("group", "row"), "col", None), P(("group", "row"), "col", None)),
        check_vma=False,
    )
```

```python
import functools

import jax
import jax.numpy as jnp
from jax import lax
from jax.experimental import pallas as pl
from jax.experimental.pallas import tpu as pltpu
from jax.sharding import PartitionSpec as P

epsilon = 1e-05
f32 = jnp.float32
bf16 = jnp.bfloat16


def mean_lanes(values):
    return jnp.sum(values, axis=-1, keepdims=True) * (1.0 / values.shape[-1])


def normalize(values):
    center = values - mean_lanes(values)
    variance = mean_lanes(center * center)
    scale = lax.rsqrt(variance + epsilon)
    return (center * scale, scale)


def normalize_back(normed, scale, upstream):
    average = mean_lanes(upstream)
    project = mean_lanes(upstream * normed)
    return scale * (upstream - average - normed * project)


def sigmoid(values):
    return 1.0 / (1.0 + jnp.exp(-values))


def dot(a, b):
    return jnp.dot(a, b, preferred_element_type=f32)


def dot_t(a, b):
    return lax.dot_general(a, b, (((1,), (1,)), ((), ())), preferred_element_type=f32)


def live_factor(crop_ref, row, col, shape):
    rows = row * shape[0] + lax.broadcasted_iota(jnp.int32, (shape[0], 1, shape[2]), 0)
    cols = col * shape[1] + lax.broadcasted_iota(jnp.int32, (1, shape[1], shape[2]), 1)
    return jnp.where(rows < crop_ref[0], 1.0, 0.0) * jnp.where(cols < crop_ref[0], 1.0, 0.0)


def spread(mask, channels):
    size = mask.shape[0]
    pair = lax.broadcasted_iota(jnp.int32, (size * size, size), 0)
    lane = lax.broadcasted_iota(jnp.int32, (size * size, size), 1)
    pick_row = jnp.where(pair // size == lane, 1.0, 0.0).astype(bf16)
    pick_col = jnp.where(pair % size == lane, 1.0, 0.0)
    picked = (dot(pick_row, mask.astype(bf16)) * pick_col).astype(bf16)
    return dot(picked, jnp.ones((size, channels), bf16))


def start_copies(sems, *pairs):
    copies = [pltpu.make_async_copy(src, dst, sems.at[n]) for n, (src, dst) in enumerate(pairs)]
    for copy in copies:
        copy.start()
    return copies


def gated(projected, block, keep):
    channels = keep.shape[1]
    value = projected[:, block * channels : (block + 1) * channels]
    opened = sigmoid(projected[:, (block + 1) * channels : (block + 2) * channels])
    return (opened * value * keep).astype(bf16), opened, value


def tiles_kernel(acts_in, mask_in, weights_in, left_ref, right_ref, acts_ref, mask_ref, weights_ref, sems):
    size, _, channels = acts_ref.shape
    copies = start_copies(
        sems, (acts_in, acts_ref), (weights_in.at[:, pl.ds(0, 4 * channels)], weights_ref), (mask_in, mask_ref)
    )
    copies[0].wait()
    normed, _ = normalize(acts_ref[...].astype(f32).reshape(size * size, channels))
    normed = normed.astype(bf16)
    for copy in copies[1:]:
        copy.wait()
    projected = dot(normed, weights_ref[...])
    mask = spread(mask_ref[...].astype(f32), channels)
    for block, out in ((0, left_ref), (2, right_ref)):
        tile, _, _ = gated(projected, block, mask)
        out[...] = tile.reshape(size, size, channels)


def factors_kernel(
    acts_in, mask_in, crop_ref, cotangent_in, weights_in, out_weight_in, _,
    normed_ref, scale_ref, factor_ref, open_ref, gate_factor_ref, upstream_ref,
    acts_ref, mask_ref, cotangent_ref, weights_ref, out_weight_ref, sems,
):
    copies = start_copies(
        sems, (acts_in, acts_ref), (weights_in, weights_ref), (mask_in, mask_ref),
        (cotangent_in, cotangent_ref), (out_weight_in, out_weight_ref),
    )
    size, _, channels = acts_ref.shape
    pairs = size * size
    copies[0].wait()
    normed, scale = normalize(acts_ref[...].astype(f32).reshape(pairs, channels))
    normed_ref[...] = normed
    scale_ref[...] = jnp.broadcast_to(scale, (pairs, channels))
    for copy in copies[1:]:
        copy.wait()
    projected = dot(normed.astype(bf16), weights_ref[...])
    live = live_factor(crop_ref, lax.axis_index("row"), lax.axis_index("col"), acts_ref.shape)
    keep = spread(mask_ref[...].astype(f32), channels) * live.reshape(pairs, channels)
    for block in (0, 2):
        _, opened, value = gated(projected, block, keep)
        factor_ref[block] = keep * opened
        factor_ref[block + 1] = keep * value * opened * (1.0 - opened)
    out_open = sigmoid(projected[:, 4 * channels :])
    cotangent = cotangent_ref[...].astype(f32).reshape(pairs, channels)
    lin_grad = (cotangent * out_open).astype(bf16)
    open_ref[...] = out_open
    gate_factor_ref[...] = cotangent * out_open * (1.0 - out_open)
    upstream_ref[...] = dot_t(lin_grad, out_weight_ref[...])


def weighted_sums(weights, start, terms, out, base=None):
    def step(k, _):
        total = weights[start + k, pl.ds(0, 1), :] * terms[0]
        for n in range(1, len(terms)):
            total = total + weights[start + k, pl.ds(n, 1), :] * terms[n]
        if base is not None:
            total = total + base[k]
        out[k] = total.astype(out.dtype)
        return 0

    lax.fori_loop(0, out.shape[0], step, 0, unroll=4)


def place():
    row, col = lax.axis_index("row"), lax.axis_index("col")
    return row, col, row ^ col, (row ^ col) & 1


def panel_kernel(steps, crop_ref, *refs):
    row, col, _, _ = place()
    panel, size = refs[-1], refs[0].shape[0]
    for at, (step, ref) in enumerate(zip(steps, refs)):
        live = live_factor(crop_ref, row, col ^ step, ref.shape)
        panel[at * size : (at + 1) * size] = ref[...].astype(f32) * live


def left_panel_kernel(steps, crop_ref, *refs):
    row, col, _, _ = place()
    panel, size = refs[-1], refs[0].shape[0]
    for step, ref in zip(steps, refs):
        live = live_factor(crop_ref, row, col ^ step, ref.shape)
        panel[pl.ds(((col ^ step) // 2) * size, size)] = ref[...].astype(f32) * live


def partial_kernel(step, crop_ref, left_ref, rights, out, left):
    row, col, _, _ = place()
    size, _, channels = left_ref.shape
    left[...] = left_ref[...].astype(f32) * live_factor(crop_ref, row, col ^ step, left_ref.shape)
    for half in range(2):

        def add(k, sums):
            other = rights[half * size + k]
            return tuple(sums[i] + left[k, pl.ds(i, 1), :] * other for i in range(size))

        zero = jnp.zeros((size, channels), f32)
        sums = lax.fori_loop(0, size, add, (zero,) * size, unroll=4)
        for i in range(size):
            out[half, i] = sums[i]


def pick_parts_kernel(steps, *refs):
    _, _, away, differ = place()
    tiles, outs = refs[: -len(steps)], refs[-len(steps) :]
    for step, out in zip(steps, outs):
        for at, tile in enumerate(tiles):

            @pl.when((away ^ step) == 2 * at)
            def _():
                out[...] = tile[...].astype(out.dtype)

        if step == 0:

            @pl.when(differ == 1)
            def _():
                out[...] = jnp.zeros(out.shape, out.dtype)


def pick_terms_kernel(steps, *refs):
    _, _, away, differ = place()
    tiles, outs = refs[: -len(steps)], refs[-len(steps) :]
    for step, out in zip(steps, outs):
        for at, tile in enumerate(tiles):

            @pl.when((away ^ differ ^ step) == 2 * at)
            def _():
                out[...] = tile[...].astype(out.dtype)


def triangle_kernel(base, tile_ref, normed_ref, scale_ref, own_ref, other_ref):
    size, _, channels = own_ref.shape
    for half, out in enumerate((own_ref, other_ref)):
        for i in range(size):
            tri_normed, scale = normalize(base[half, i] + tile_ref[half, i].astype(f32))
            normed_ref[half, i] = tri_normed
            scale_ref[half, i] = jnp.broadcast_to(scale, (size, channels))
            out[i] = tri_normed.astype(bf16)


def triangle_back_kernel(normed_ref, scale_ref, upstream_ref, other_ref, grad_ref):
    size = grad_ref.shape[1]
    for half, upstream in enumerate((upstream_ref, other_ref)):
        for i in range(size):
            rows = pl.ds(i * size, size)
            grad_ref[half, i] = normalize_back(normed_ref[half, i], scale_ref[half, i], upstream[rows, :]).astype(bf16)


def select_grads(same_ref, differ_ref, out):
    _, _, _, differ = place()

    @pl.when(differ == 0)
    def _():
        out[...] = same_ref[...].astype(f32).reshape(out.shape)

    @pl.when(differ == 1)
    def _():
        out[...] = differ_ref[...].astype(f32).reshape(out.shape)


def left_terms_kernel(differ_ref, same_ref, rights, *refs):
    out, grad = refs[-2:]
    size, pairs = out.shape[0], out.shape[0] ** 2
    select_grads(same_ref, differ_ref, grad)
    for half in range(2):
        rows = [grad[pl.ds(half * pairs + j, size, stride=size), :] for j in range(size)]
        weighted_sums(rights, half * size, rows, out, out if half else None)


def right_grad_kernel(slot, panel, same_ref, differ_ref, *refs):
    outs, grad = refs[-3:-1], refs[-1]
    size = outs[0].shape[0]
    row, _, _, differ = place()
    select_grads(same_ref, differ_ref, grad)
    start = ((row ^ slot ^ differ) // 2) * size
    for half, out in enumerate(outs):
        rows = [grad[half, i] for i in range(size)]
        weighted_sums(panel, start, rows, out, refs[half] if len(refs) > 3 else None)


def add_kernel(base, tile_ref, out):
    out[...] = base[...] + tile_ref[...].astype(f32)


def update_kernel(
    normed_ref, other_ref, open_ref, gate_factor_ref, weights_ref, out_weight_ref, update_ref, share_ref, tri_normed
):
    size, _, channels = update_ref.shape
    _, _, _, differ = place()
    for parity, ref in enumerate((normed_ref, other_ref)):

        @pl.when(differ == parity)
        def _():
            tri_normed[...] = ref[...].reshape(tri_normed.shape)

    linear = dot(tri_normed[...], out_weight_ref[...])
    update = (open_ref[...] * linear).astype(bf16)
    update_ref[...] = update.reshape(size, size, channels)
    out_gate_grad = (gate_factor_ref[...] * linear).astype(bf16)
    share_ref[...] = dot_t(out_gate_grad, weights_ref[:, 4 * channels :])


def back_kernel(
    left_ref, right_ref, other_ref, normed_ref, scale_ref, factor_ref, share_ref, weights_ref, out
):
    size, _, channels = out.shape
    pairs = size * size
    left = left_ref[...].reshape(pairs, channels)
    right = (right_ref[...] + other_ref[...].astype(f32)).reshape(pairs, channels)
    grads = jnp.concatenate(
        [(total * factor_ref[block]).astype(bf16) for block, total in enumerate((left, left, right, right))],
        axis=1,
    )
    normed_grad = share_ref[...] + dot_t(grads, weights_ref[:, : 4 * channels])
    back = normalize_back(normed_ref[...], scale_ref[...], normed_grad)
    out[...] = back.astype(bf16).reshape(size, size, channels)


def call(kernel, outs, *args, scratch=(), flops=0, smem=(), hbm=()):
    spec = pl.BlockSpec(memory_space=pltpu.VMEM)
    total = sum(a.size * a.dtype.itemsize for a in (*args, *outs))
    specs = [spec] * len(args)
    for n in smem:
        specs[n] = pl.BlockSpec(memory_space=pltpu.SMEM)
    args = list(args)
    for n in hbm:
        specs[n] = pl.BlockSpec(memory_space=pltpu.HBM)
        args[n] = pltpu.with_memory_space_constraint(args[n], pltpu.HBM)
    return pl.pallas_call(
        kernel,
        out_shape=tuple(outs),
        in_specs=specs,
        out_specs=(spec,) * len(outs),
        scratch_shapes=scratch,
        compiler_params=pltpu.CompilerParams(vmem_limit_bytes=24 * 2**20),
        cost_estimate=pl.CostEstimate(flops=flops, bytes_accessed=total if flops else 0, transcendentals=0),
    )(*args)


def local(pair_acts, pair_mask, crop_length, cotangent, in_weights, out_weight):
    size, _, channels = pair_acts.shape
    pairs = size * size
    n = lax.axis_size("row")
    tile = jax.ShapeDtypeStruct((size, size, channels), bf16)
    flat = jax.ShapeDtypeStruct((pairs, channels), f32)

    wide = jax.ShapeDtypeStruct((size, size, channels), f32)
    work = 2 * size * pairs * channels
    wait = 2**31
    near = list(range(0, n, 2))
    row_steps = list(range(n - 1, 0, -2)) + list(range(n - 2, 0, -2))
    pair = jax.ShapeDtypeStruct((2, size, size, channels), bf16)
    wide_pair = jax.ShapeDtypeStruct(pair.shape, f32)
    pair_panel = jax.ShapeDtypeStruct((2 * size, size, channels), f32)
    left_panel = jax.ShapeDtypeStruct((n // 2 * size, size, channels), f32)

    def swap(values, step):
        return lax.ppermute(values, "col", [(a, a ^ step) for a in range(n)])

    def send(values, step, parity):
        pairs = [(a * n + b, (a ^ step) * n + b) for a in range(n) for b in range(n) if (a ^ b) % 2 == parity]
        return lax.ppermute(values, ("row", "col"), pairs)

    left, right = call(
        tiles_kernel, (tile, tile), pair_acts, pair_mask, in_weights,
        hbm=(0, 1, 2), flops=2 * pairs * channels * 4 * channels,
        scratch=[
            pltpu.VMEM(pair_acts.shape, bf16),
            pltpu.VMEM(pair_mask.shape, jnp.int32),
            pltpu.VMEM((channels, 4 * channels), bf16),
            pltpu.SemaphoreType.DMA((3,)),
        ],
    )
    lefts = [left] + [swap(left, step) for step in near[1:]]
    other_right = swap(right, 1)
    (rights,) = call(
        functools.partial(panel_kernel, (0, 1)), (pair_panel,), crop_length, right, other_right, smem=(0,)
    )
    parts = [
        call(
            functools.partial(partial_kernel, step), (wide_pair,), crop_length, tile_of, rights, smem=(0,),
            flops=work, scratch=[pltpu.VMEM(wide.shape, f32)],
        )[0]
        for step, tile_of in zip(near, lefts)
    ]
    total, *parts = call(
        functools.partial(pick_parts_kernel, [0] + row_steps), (wide_pair,) + (pair,) * (n - 1), *parts,
        flops=pairs * channels,
    )
    normed, scale, factors, out_open, gate_factor, upstream = call(
        factors_kernel,
        (flat, flat, jax.ShapeDtypeStruct((4, pairs, channels), f32), flat, flat, flat),
        pair_acts, pair_mask, crop_length, cotangent, in_weights, out_weight, total,
        smem=(2,), hbm=(0, 1, 3, 4, 5), flops=2 * pairs * channels * 6 * channels,
        scratch=[
            pltpu.VMEM(pair_acts.shape, bf16),
            pltpu.VMEM(pair_mask.shape, jnp.int32),
            pltpu.VMEM(cotangent.shape, bf16),
            pltpu.VMEM(in_weights.shape, bf16),
            pltpu.VMEM(out_weight.shape, bf16),
            pltpu.SemaphoreType.DMA((5,)),
        ],
    )
    other_upstream = swap(upstream, 1)
    (left_panel,) = call(
        functools.partial(left_panel_kernel, near), (left_panel,), crop_length, *lefts, smem=(0,)
    )
    for step, part in zip(row_steps, parts):
        part = send(part, step, step % 2)
        if step != row_steps[-1]:
            (total,) = call(add_kernel, (wide_pair,), total, part, flops=wait)
    wide_normed, wide_scale, tri_normed, other_normed = call(
        triangle_kernel, (wide_pair, wide_pair, tile, tile), total, part, flops=wait,
    )
    (tri_grad,) = call(
        triangle_back_kernel, (pair,), wide_normed, wide_scale, upstream, other_upstream,
        flops=20 * pairs * channels,
    )
    grads = {0: tri_grad}
    for step in row_steps:
        grads[step] = send(tri_grad, step, 0)
    other_normed = swap(other_normed, 1)
    update, share = call(
        update_kernel, (tile, flat), tri_normed, other_normed, out_open, gate_factor, in_weights, out_weight,
        flops=4 * pairs * channels * channels, scratch=[pltpu.VMEM((pairs, channels), bf16)],
    )
    terms = [
        call(
            left_terms_kernel, (wide,), grads[slot + 1], grads[slot], rights, share, left_panel,
            scratch=[pltpu.VMEM((2 * pairs, channels), f32)], flops=work,
        )[0]
        for slot in near[::-1]
    ][::-1]
    total, *terms = call(
        functools.partial(pick_terms_kernel, near), (wide,) + (tile,) * (n // 2 - 1), *terms, flops=pairs * channels
    )
    right_grads = ()
    for slot in near:
        right_grads = call(
            functools.partial(right_grad_kernel, slot), (wide, tile if slot == near[-1] else wide),
            left_panel, grads[slot], grads[slot + 1], *right_grads,
            scratch=[pltpu.VMEM(wide_pair.shape, f32)],
        )
    right_grad, other_grad = right_grads
    other_grad = swap(other_grad, 1)
    for step, term in zip(near[1:], terms):
        (total,) = call(add_kernel, (wide,), total, swap(term, step), flops=wait)
    (pair_grad,) = call(
        back_kernel, (tile,), total, right_grad, other_grad, normed, scale, factors, share, in_weights,
        flops=2 * pairs * channels * 4 * channels,
    )
    return (update, pair_grad)


def solution(mesh):
    return jax.shard_map(
        local,
        mesh=mesh,
        in_specs=(
            P(("group", "row"), "col", None),
            P(("group", "row"), "col"),
            P("group"),
            P(("group", "row"), "col", None),
            P(),
            P(),
        ),
        out_specs=(P(("group", "row"), "col", None), P(("group", "row"), "col", None)),
        check_vma=False,
    )
```

```python
import functools

import jax
import jax.numpy as jnp
from jax import lax
from jax.experimental import pallas as pl
from jax.experimental.pallas import tpu as pltpu
from jax.sharding import PartitionSpec as P

epsilon = 1e-05
f32 = jnp.float32
bf16 = jnp.bfloat16


def mean_lanes(values):
    return jnp.sum(values, axis=-1, keepdims=True) * (1.0 / values.shape[-1])


def normalize(values):
    center = values - mean_lanes(values)
    variance = mean_lanes(center * center)
    scale = lax.rsqrt(variance + epsilon)
    return (center * scale, scale)


def normalize_back(normed, scale, upstream):
    average = mean_lanes(upstream)
    project = mean_lanes(upstream * normed)
    return scale * (upstream - average - normed * project)


def sigmoid(values):
    return 1.0 / (1.0 + jnp.exp(-values))


def dot(a, b):
    return jnp.dot(a, b, preferred_element_type=f32)


def dot_t(a, b):
    return lax.dot_general(a, b, (((1,), (1,)), ((), ())), preferred_element_type=f32)


def live_pairs(crop_ref, row, col, shape):
    rows = row * shape[0] + lax.broadcasted_iota(jnp.int32, shape, 0)
    cols = col * shape[1] + lax.broadcasted_iota(jnp.int32, shape, 1)
    return jnp.where(jnp.maximum(rows, cols) < crop_ref[0], 1.0, 0.0)


def spread(mask, channels):
    size = mask.shape[0]
    pair = lax.broadcasted_iota(jnp.int32, (size * size, size), 0)
    lane = lax.broadcasted_iota(jnp.int32, (size * size, size), 1)
    pick_row = jnp.where(pair // size == lane, 1.0, 0.0).astype(bf16)
    pick_col = jnp.where(pair % size == lane, 1.0, 0.0)
    picked = (dot(pick_row, mask.astype(bf16)) * pick_col).astype(bf16)
    return dot(picked, jnp.ones((size, channels), bf16))


def start_copies(sems, *pairs):
    copies = [pltpu.make_async_copy(src, dst, sems.at[n]) for n, (src, dst) in enumerate(pairs)]
    for copy in copies:
        copy.start()
    return copies


def gated(projected, block, keep):
    channels = keep.shape[1]
    value = projected[:, block * channels : (block + 1) * channels]
    opened = sigmoid(projected[:, (block + 1) * channels : (block + 2) * channels])
    return (opened * value * keep).astype(bf16), opened, value


def left_kernel(acts_in, mask_in, weights_in, left_ref, acts_ref, mask_ref, weights_ref, sems):
    size, _, channels = acts_ref.shape
    copies = start_copies(
        sems, (acts_in, acts_ref), (weights_in.at[:, pl.ds(0, 2 * channels)], weights_ref), (mask_in, mask_ref),
    )
    copies[0].wait()
    normed, _ = normalize(acts_ref[...].astype(f32).reshape(size * size, channels))
    normed = normed.astype(bf16)
    for copy in copies[1:]:
        copy.wait()
    left, _, _ = gated(dot(normed, weights_ref[...]), 0, spread(mask_ref[...].astype(f32), channels))
    left_ref[...] = left.reshape(size, size, channels)


def factors_kernel(
    acts_in, mask_in, crop_ref, cotangent_in, weights_in, out_weight_in,
    right_ref, normed_ref, scale_ref, factor_ref, open_ref, gate_factor_ref, upstream_ref,
    acts_ref, mask_ref, cotangent_ref, weights_ref, out_weight_ref, sems,
):
    copies = start_copies(
        sems, (acts_in, acts_ref), (weights_in, weights_ref), (mask_in, mask_ref),
        (cotangent_in, cotangent_ref), (out_weight_in, out_weight_ref),
    )
    size, _, channels = acts_ref.shape
    pairs = size * size
    copies[0].wait()
    normed, scale = normalize(acts_ref[...].astype(f32).reshape(pairs, channels))
    normed_ref[...] = normed
    scale_ref[...] = jnp.broadcast_to(scale, (pairs, channels))
    for copy in copies[1:]:
        copy.wait()
    projected = dot(normed.astype(bf16), weights_ref[...])
    live = live_pairs(crop_ref, lax.axis_index("row"), lax.axis_index("col"), (size, size))
    keep = spread(mask_ref[...].astype(f32) * live, channels)
    for block in (0, 2):
        tile, opened, value = gated(projected, block, keep)
        factor_ref[block] = keep * opened
        factor_ref[block + 1] = keep * value * opened * (1.0 - opened)
    right_ref[...] = tile.astype(f32).reshape(size, size, channels)
    out_open = sigmoid(projected[:, 4 * channels :])
    cotangent = cotangent_ref[...].astype(f32).reshape(pairs, channels)
    lin_grad = (cotangent * out_open).astype(bf16)
    open_ref[...] = out_open
    gate_factor_ref[...] = cotangent * out_open * (1.0 - out_open)
    upstream_ref[...] = dot_t(lin_grad, out_weight_ref[...])


def weighted_sums(weights, start, terms, out, base=None):
    def step(k, _):
        total = weights[start + k, pl.ds(0, 1), :] * terms[0]
        for n in range(1, len(terms)):
            total = total + weights[start + k, pl.ds(n, 1), :] * terms[n]
        if base is not None:
            total = total + base[k]
        out[k] = total.astype(out.dtype)
        return 0

    lax.fori_loop(0, out.shape[0], step, 0, unroll=4)


def left_panel_kernel(steps, crop_ref, *refs):
    row, col, panel = lax.axis_index("row"), lax.axis_index("col"), refs[-1]
    size, _, channels = refs[0].shape
    rows = row * size + lax.broadcasted_iota(jnp.int32, (size, 1, channels), 0)
    row_live = jnp.where(rows < crop_ref[0], 1.0, 0.0)
    for step, ref in zip(steps, refs):
        place = col ^ step
        cols = place * size + lax.broadcasted_iota(jnp.int32, (1, size, channels), 1)
        col_live = jnp.where(cols < crop_ref[0], 1.0, 0.0)
        panel[pl.ds(place * size, size)] = ref[...].astype(f32) * (row_live * col_live)


def partial_kernel(steps, crop_ref, *refs):
    count = len(steps)
    lefts, right_ref, outs, left = refs[:count], refs[count], refs[count + 1 : -1], refs[-1]
    size, _, channels = right_ref.shape
    rows = lax.axis_index("row") * size + lax.broadcasted_iota(jnp.int32, (size, 1, channels), 0)
    row_live = jnp.where(rows < crop_ref[0], 1.0, 0.0)
    for step, left_ref, out in zip(steps, lefts, outs):
        cols = (lax.axis_index("col") ^ step) * size + lax.broadcasted_iota(jnp.int32, (1, size, channels), 1)
        left[...] = left_ref[...].astype(f32) * (row_live * jnp.where(cols < crop_ref[0], 1.0, 0.0))

        def add(k, sums):
            other = right_ref[k]
            return tuple(sums[i] + left[k, pl.ds(i, 1), :] * other for i in range(size))

        zero = jnp.zeros((size, channels), f32)
        sums = lax.fori_loop(0, size, add, (zero,) * size, unroll=4)
        for i in range(size):
            out[i] = sums[i]


def pick_kernel(steps, *refs):
    here = lax.axis_index("row") ^ lax.axis_index("col")
    tiles, outs = refs[: len(steps)], refs[len(steps) :]
    for step, out in zip(steps, outs):
        for other, tile in enumerate(tiles):

            @pl.when((here ^ step) == other)
            def _():
                out[...] = tile[...].astype(out.dtype)


def triangle_kernel(base, tile_ref, upstream_ref, tri_normed_ref, grad_ref):
    size = grad_ref.shape[0]
    for i in range(size):
        here = pl.ds(i * size, size)
        tri_normed, scale = normalize(base[i] + tile_ref[i].astype(f32))
        tri_normed_ref[here, :] = tri_normed
        grad_ref[i] = normalize_back(tri_normed, scale, upstream_ref[here, :]).astype(bf16)


def left_terms_kernel(grad_ref, right, out, grad):
    size, _, channels = out.shape
    grad[...] = grad_ref[...].astype(f32).reshape(size * size, channels)
    weighted_sums(right, 0, [grad[pl.ds(j, size, stride=size), :] for j in range(size)], out)


def right_grad_kernel(steps, panel, *refs):
    out, base = refs[-1], refs[len(steps)] if len(refs) > len(steps) + 1 else None
    size = out.shape[0]
    for step, grad in zip(steps, refs):
        start = (lax.axis_index("row") ^ step) * size
        weighted_sums(panel, start, [grad[i].astype(f32) for i in range(size)], out, base)
        base = out


def right_back_kernel(steps, panel, *refs):
    factor_ref, weights_ref, share_ref, out, right_ref = refs[-5:]
    right_grad_kernel(steps, panel, *refs[: len(steps) + 1], right_ref)
    pairs, channels = out.shape
    right = right_ref[...].reshape(pairs, channels)
    grads = jnp.concatenate([(right * factor_ref[block]).astype(bf16) for block in (2, 3)], axis=1)
    out[...] = share_ref[...] + dot_t(grads, weights_ref[:, 2 * channels : 4 * channels])


def add_kernel(base, tile_ref, out):
    out[...] = base[...] + tile_ref[...].astype(f32)


def update_kernel(
    tri_normed_ref, open_ref, gate_factor_ref, weights_ref, out_weight_ref, update_ref, normed_grad_ref
):
    size, _, channels = update_ref.shape
    linear = dot(tri_normed_ref[...].astype(bf16), out_weight_ref[...])
    update = (open_ref[...] * linear).astype(bf16)
    update_ref[...] = update.reshape(size, size, channels)
    out_gate_grad = (gate_factor_ref[...] * linear).astype(bf16)
    normed_grad_ref[...] = dot_t(out_gate_grad, weights_ref[:, 4 * channels :])


def back_kernel(base, *refs):
    *tiles, normed_ref, scale_ref, factor_ref, share_ref, weights_ref, out = refs
    size, _, channels = out.shape
    pairs = size * size
    left = base[...]
    for ref in tiles:
        left = left + ref[...].astype(f32)
    left = left.reshape(pairs, channels)
    grads = jnp.concatenate([(left * factor_ref[block]).astype(bf16) for block in (0, 1)], axis=1)
    normed_grad = share_ref[...] + dot_t(grads, weights_ref[:, : 2 * channels])
    back = normalize_back(normed_ref[...], scale_ref[...], normed_grad)
    out[...] = back.astype(bf16).reshape(size, size, channels)


def call(kernel, outs, *args, scratch=(), flops=0, smem=(), hbm=()):
    spec = pl.BlockSpec(memory_space=pltpu.VMEM)
    total = sum(a.size * a.dtype.itemsize for a in (*args, *outs))
    specs = [spec] * len(args)
    for n in smem:
        specs[n] = pl.BlockSpec(memory_space=pltpu.SMEM)
    args = list(args)
    for n in hbm:
        specs[n] = pl.BlockSpec(memory_space=pltpu.HBM)
        args[n] = pltpu.with_memory_space_constraint(args[n], pltpu.HBM)
    return pl.pallas_call(
        kernel,
        out_shape=tuple(outs),
        in_specs=specs,
        out_specs=(spec,) * len(outs),
        scratch_shapes=scratch,
        compiler_params=pltpu.CompilerParams(vmem_limit_bytes=24 * 2**20),
        cost_estimate=pl.CostEstimate(flops=flops, bytes_accessed=total if flops else 0, transcendentals=0),
    )(*args)


def local(pair_acts, pair_mask, crop_length, cotangent, in_weights, out_weight):
    size, _, channels = pair_acts.shape
    pairs = size * size
    n = lax.axis_size("row")
    tile = jax.ShapeDtypeStruct((size, size, channels), bf16)
    flat = jax.ShapeDtypeStruct((pairs, channels), f32)

    wide = jax.ShapeDtypeStruct((size, size, channels), f32)
    panel = jax.ShapeDtypeStruct((n * size, size, channels), f32)
    work = 2 * size * pairs * channels
    wait = 2**31
    steps = [step for bit in range(n.bit_length() - 2, -1, -1) for step in range(2**bit, 2 ** (bit + 1))]
    row_steps = list(range(n - 1, 0, -1))


    def swap(values, axis, step):
        return lax.ppermute(values, axis, [(a, a ^ step) for a in range(n)])

    def gather(values, axis, steps):
        return [values] + [swap(values, axis, step) for step in steps]

    (left,) = call(
        left_kernel, (tile,), pair_acts, pair_mask, in_weights,
        hbm=(0, 1, 2), flops=2 * pairs * channels * 2 * channels,
        scratch=[
            pltpu.VMEM(pair_acts.shape, bf16),
            pltpu.VMEM(pair_mask.shape, jnp.int32),
            pltpu.VMEM((channels, 2 * channels), bf16),
            pltpu.SemaphoreType.DMA((3,)),
        ],
    )
    lefts = gather(left, "col", steps)
    right, normed, scale, factors, out_open, gate_factor, upstream = call(
        factors_kernel,
        (wide, flat, flat, jax.ShapeDtypeStruct((4, pairs, channels), f32), flat, flat, flat),
        pair_acts, pair_mask, crop_length, cotangent, in_weights, out_weight,
        smem=(2,), hbm=(0, 1, 3, 4, 5), flops=2 * pairs * channels * 6 * channels,
        scratch=[
            pltpu.VMEM(pair_acts.shape, bf16),
            pltpu.VMEM(pair_mask.shape, jnp.int32),
            pltpu.VMEM(cotangent.shape, bf16),
            pltpu.VMEM(in_weights.shape, bf16),
            pltpu.VMEM(out_weight.shape, bf16),
            pltpu.SemaphoreType.DMA((5,)),
        ],
    )
    parts = []
    order = [0] + steps
    for group in [[at] for at in range(n - 2)] + [[n - 2, n - 1]]:
        parts += call(
            functools.partial(partial_kernel, [order[at] for at in group]), (wide,) * len(group),
            crop_length, *(lefts[at] for at in group), right, smem=(0,), flops=work,
            scratch=[pltpu.VMEM(wide.shape, f32)],
        )
    parts = [part for _, part in sorted(zip(order, parts), key=lambda each: each[0])]
    total, *parts = call(
        functools.partial(pick_kernel, [0] + row_steps), (wide,) + (tile,) * (n - 1), *parts,
        flops=pairs * channels,
    )
    (left_panel,) = call(
        functools.partial(left_panel_kernel, [0] + steps), (panel,), crop_length, *lefts, smem=(0,)
    )
    for step, part in zip(row_steps, parts):
        part = swap(part, "row", step)
        if step != row_steps[-1]:
            (total,) = call(add_kernel, (wide,), total, part, flops=wait)
    tri_normed, tri_grad = call(
        triangle_kernel, (flat, tile), total, part, upstream, flops=20 * pairs * channels,
    )
    grads = gather(tri_grad, "row", row_steps)
    update, partial = call(
        update_kernel, (tile, flat), tri_normed, out_open, gate_factor, in_weights, out_weight,
        flops=4 * pairs * channels * channels,
    )
    (right_grad,) = call(functools.partial(right_grad_kernel, [0]), (wide,), left_panel, tri_grad)
    right, partial, right_grad = lax.optimization_barrier((right, partial, right_grad))
    terms = [None] * n
    for step, grad in zip([0] + row_steps, grads):
        (terms[step],) = call(
            left_terms_kernel, (wide,), grad, right, scratch=[pltpu.VMEM((pairs, channels), f32)], flops=work,
        )
    total, *terms = call(
        functools.partial(pick_kernel, [0] + steps), (wide,) + (tile,) * (n - 1), *terms, flops=pairs * channels,
    )
    for step, term in zip(steps, terms):
        term = swap(term, "col", step)
        if step != steps[-1]:
            (total,) = call(add_kernel, (wide,), total, term, flops=wait)
    (share,) = call(
        functools.partial(right_back_kernel, row_steps), (flat,),
        left_panel, *grads[1:], right_grad, factors, in_weights, partial,
        scratch=[pltpu.VMEM(wide.shape, f32)],
    )
    (pair_grad,) = call(
        back_kernel, (tile,), total, term, normed, scale, factors, share, in_weights,
        flops=2 * pairs * channels * 2 * channels,
    )
    return (update, pair_grad)


def solution(mesh):
    return jax.shard_map(
        local,
        mesh=mesh,
        in_specs=(
            P(("group", "row"), "col", None),
            P(("group", "row"), "col"),
            P("group"),
            P(("group", "row"), "col", None),
            P(),
            P(),
        ),
        out_specs=(P(("group", "row"), "col", None), P(("group", "row"), "col", None)),
        check_vma=False,
    )
```

```python
import functools

import jax
import jax.numpy as jnp
from jax import lax
from jax.experimental import pallas as pl
from jax.experimental.pallas import tpu as pltpu
from jax.sharding import PartitionSpec as P

epsilon = 1e-05
f32 = jnp.float32
bf16 = jnp.bfloat16


def mean_lanes(values):
    return jnp.sum(values, axis=-1, keepdims=True) * (1.0 / values.shape[-1])


def normalize(values):
    center = values - mean_lanes(values)
    variance = mean_lanes(center * center)
    scale = lax.rsqrt(variance + epsilon)
    return (center * scale, scale)


def normalize_back(normed, scale, upstream):
    average = mean_lanes(upstream)
    project = mean_lanes(upstream * normed)
    return scale * (upstream - average - normed * project)


def sigmoid(values):
    return 1.0 / (1.0 + jnp.exp(-values))


def dot(a, b):
    return jnp.dot(a, b, preferred_element_type=f32)


def dot_t(a, b):
    return lax.dot_general(a, b, (((1,), (1,)), ((), ())), preferred_element_type=f32)


def live_pairs(crop_ref, row, col, shape):
    rows = row * shape[0] + lax.broadcasted_iota(jnp.int32, shape, 0)
    cols = col * shape[1] + lax.broadcasted_iota(jnp.int32, shape, 1)
    return jnp.where(jnp.maximum(rows, cols) < crop_ref[0], 1.0, 0.0)


def spread(mask, channels):
    size = mask.shape[0]
    pair = lax.broadcasted_iota(jnp.int32, (size * size, size), 0)
    lane = lax.broadcasted_iota(jnp.int32, (size * size, size), 1)
    pick_row = jnp.where(pair // size == lane, 1.0, 0.0).astype(bf16)
    pick_col = jnp.where(pair % size == lane, 1.0, 0.0)
    picked = (dot(pick_row, mask.astype(bf16)) * pick_col).astype(bf16)
    return dot(picked, jnp.ones((size, channels), bf16))


def start_copies(sems, *pairs):
    copies = [pltpu.make_async_copy(src, dst, sems.at[n]) for n, (src, dst) in enumerate(pairs)]
    for copy in copies:
        copy.start()
    return copies


def gated(projected, block, keep):
    channels = keep.shape[1]
    value = projected[:, block * channels : (block + 1) * channels]
    opened = sigmoid(projected[:, (block + 1) * channels : (block + 2) * channels])
    return (opened * value * keep).astype(bf16), opened, value


def left_kernel(acts_in, mask_in, weights_in, left_ref, acts_ref, mask_ref, weights_ref, sems):
    size, _, channels = acts_ref.shape
    copies = start_copies(
        sems, (acts_in, acts_ref), (weights_in.at[:, pl.ds(0, 2 * channels)], weights_ref), (mask_in, mask_ref),
    )
    copies[0].wait()
    normed, _ = normalize(acts_ref[...].astype(f32).reshape(size * size, channels))
    normed = normed.astype(bf16)
    for copy in copies[1:]:
        copy.wait()
    left, _, _ = gated(dot(normed, weights_ref[...]), 0, spread(mask_ref[...].astype(f32), channels))
    left_ref[...] = left.reshape(size, size, channels)


def factors_kernel(
    acts_in, mask_in, crop_ref, cotangent_in, weights_in, out_weight_in,
    right_ref, normed_ref, scale_ref, factor_ref, open_ref, gate_factor_ref, upstream_ref,
    acts_ref, mask_ref, cotangent_ref, weights_ref, out_weight_ref, sems,
):
    copies = start_copies(
        sems, (acts_in, acts_ref), (weights_in, weights_ref), (mask_in, mask_ref),
        (cotangent_in, cotangent_ref), (out_weight_in, out_weight_ref),
    )
    size, _, channels = acts_ref.shape
    pairs = size * size
    copies[0].wait()
    normed, scale = normalize(acts_ref[...].astype(f32).reshape(pairs, channels))
    normed_ref[...] = normed
    scale_ref[...] = jnp.broadcast_to(scale, (pairs, channels))
    for copy in copies[1:]:
        copy.wait()
    projected = dot(normed.astype(bf16), weights_ref[...])
    live = live_pairs(crop_ref, lax.axis_index("row"), lax.axis_index("col"), (size, size))
    keep = spread(mask_ref[...].astype(f32) * live, channels)
    for block in (0, 2):
        tile, opened, value = gated(projected, block, keep)
        factor_ref[block] = keep * opened
        factor_ref[block + 1] = keep * value * opened * (1.0 - opened)
    right_ref[...] = tile.astype(f32).reshape(size, size, channels)
    out_open = sigmoid(projected[:, 4 * channels :])
    cotangent = cotangent_ref[...].astype(f32).reshape(pairs, channels)
    lin_grad = (cotangent * out_open).astype(bf16)
    open_ref[...] = out_open
    gate_factor_ref[...] = cotangent * out_open * (1.0 - out_open)
    upstream_ref[...] = dot_t(lin_grad, out_weight_ref[...])


def weighted_sums(weights, start, terms, out, base=None):
    def step(k, _):
        total = weights[start + k, pl.ds(0, 1), :] * terms[0]
        for n in range(1, len(terms)):
            total = total + weights[start + k, pl.ds(n, 1), :] * terms[n]
        if base is not None:
            total = total + base[k]
        out[k] = total.astype(out.dtype)
        return 0

    lax.fori_loop(0, out.shape[0], step, 0, unroll=4)


def panel_kernel(axis, steps, *refs):
    here, panel = lax.axis_index(axis), refs[-1]
    rows = panel.shape[0] // len(steps)
    for step, ref in zip(steps, refs):
        tile = ref[...].astype(f32)
        panel[pl.ds((here ^ step) * rows, rows)] = tile.reshape((rows,) + panel.shape[1:])


def left_panel_kernel(steps, crop_ref, *refs):
    row, col, panel = lax.axis_index("row"), lax.axis_index("col"), refs[-1]
    size = refs[0].shape[0]
    for step, ref in zip(steps, refs):
        place = col ^ step
        live = live_pairs(crop_ref, row, place, ref.shape)
        panel[pl.ds(place * size, size)] = ref[...].astype(f32) * live


def partial_kernel(steps, panel, right_ref, *outs):
    size, _, channels = right_ref.shape
    for step, out in zip(steps, outs):
        start = (lax.axis_index("row") ^ step) * size

        def add(k, sums):
            other = right_ref[k]
            return tuple(sums[i] + panel[start + k, pl.ds(i, 1), :] * other for i in range(size))

        zero = jnp.zeros((size, channels), f32)
        sums = lax.fori_loop(0, size, add, (zero,) * size, unroll=4)
        for i in range(size):
            out[i] = sums[i].astype(out.dtype)


def triangle_kernel(base, tile_ref, upstream_ref, tri_normed_ref, grad_ref):
    size = grad_ref.shape[0]
    for i in range(size):
        here = pl.ds(i * size, size)
        tri_normed, scale = normalize(base[i] + tile_ref[i].astype(f32))
        tri_normed_ref[here, :] = tri_normed
        grad_ref[i] = normalize_back(tri_normed, scale, upstream_ref[here, :]).astype(bf16)


def left_terms_kernel(steps, panel, right, *outs):
    size = right.shape[0]
    for step, out in zip(steps, outs):
        start = (lax.axis_index("col") ^ step) * (size * size)
        weighted_sums(right, 0, [panel[pl.ds(start + j, size, stride=size), :] for j in range(size)], out)


def right_grad_kernel(steps, panel, *refs):
    out, base = refs[-1], refs[len(steps)] if len(refs) > len(steps) + 1 else None
    size = out.shape[0]
    for step, grad in zip(steps, refs):
        start = (lax.axis_index("row") ^ step) * size
        weighted_sums(panel, start, [grad[i].astype(f32) for i in range(size)], out, base)
        base = out


def right_back_kernel(steps, panel, *refs):
    factor_ref, weights_ref, share_ref, out, right_ref = refs[-5:]
    right_grad_kernel(steps, panel, *refs[: len(steps) + 1], right_ref)
    pairs, channels = out.shape
    right = right_ref[...].reshape(pairs, channels)
    grads = jnp.concatenate([(right * factor_ref[block]).astype(bf16) for block in (2, 3)], axis=1)
    out[...] = share_ref[...] + dot_t(grads, weights_ref[:, 2 * channels : 4 * channels])


def add_kernel(base, tile_ref, out):
    out[...] = base[...] + tile_ref[...].astype(f32)


def update_kernel(
    tri_normed_ref, open_ref, gate_factor_ref, weights_ref, out_weight_ref, update_ref, normed_grad_ref
):
    size, _, channels = update_ref.shape
    linear = dot(tri_normed_ref[...].astype(bf16), out_weight_ref[...])
    update = (open_ref[...] * linear).astype(bf16)
    update_ref[...] = update.reshape(size, size, channels)
    out_gate_grad = (gate_factor_ref[...] * linear).astype(bf16)
    normed_grad_ref[...] = dot_t(out_gate_grad, weights_ref[:, 4 * channels :])


def back_kernel(base, *refs):
    *tiles, normed_ref, scale_ref, factor_ref, share_ref, weights_ref, out = refs
    size, _, channels = out.shape
    pairs = size * size
    left = base[...]
    for ref in tiles:
        left = left + ref[...].astype(f32)
    left = left.reshape(pairs, channels)
    grads = jnp.concatenate([(left * factor_ref[block]).astype(bf16) for block in (0, 1)], axis=1)
    normed_grad = share_ref[...] + dot_t(grads, weights_ref[:, : 2 * channels])
    back = normalize_back(normed_ref[...], scale_ref[...], normed_grad)
    out[...] = back.astype(bf16).reshape(size, size, channels)


def call(kernel, outs, *args, scratch=(), flops=0, smem=(), hbm=()):
    spec = pl.BlockSpec(memory_space=pltpu.VMEM)
    total = sum(a.size * a.dtype.itemsize for a in (*args, *outs))
    specs = [spec] * len(args)
    for n in smem:
        specs[n] = pl.BlockSpec(memory_space=pltpu.SMEM)
    args = list(args)
    for n in hbm:
        specs[n] = pl.BlockSpec(memory_space=pltpu.HBM)
        args[n] = pltpu.with_memory_space_constraint(args[n], pltpu.HBM)
    return pl.pallas_call(
        kernel,
        out_shape=tuple(outs),
        in_specs=specs,
        out_specs=(spec,) * len(outs),
        scratch_shapes=scratch,
        compiler_params=pltpu.CompilerParams(vmem_limit_bytes=24 * 2**20),
        cost_estimate=pl.CostEstimate(flops=flops, bytes_accessed=total if flops else 0, transcendentals=0),
    )(*args)


def local(pair_acts, pair_mask, crop_length, cotangent, in_weights, out_weight):
    size, _, channels = pair_acts.shape
    pairs = size * size
    n = lax.axis_size("row")
    tile = jax.ShapeDtypeStruct((size, size, channels), bf16)
    flat = jax.ShapeDtypeStruct((pairs, channels), f32)

    wide = jax.ShapeDtypeStruct((size, size, channels), f32)
    panel = jax.ShapeDtypeStruct((n * size, size, channels), f32)
    work = 2 * size * pairs * channels
    wait = 2**31
    steps = [step for bit in range(n.bit_length() - 2, -1, -1) for step in range(2**bit, 2 ** (bit + 1))]
    row_steps = [n // 2] + [step for step in range(1, n) if step != n // 2]


    def swap(values, axis, step):
        return lax.ppermute(values, axis, [(a, a ^ step) for a in range(n)])

    def gather(values, axis, steps):
        return [values] + [swap(values, axis, step) for step in steps]

    (left,) = call(
        left_kernel, (tile,), pair_acts, pair_mask, in_weights,
        hbm=(0, 1, 2), flops=2 * pairs * channels * 2 * channels,
        scratch=[
            pltpu.VMEM(pair_acts.shape, bf16),
            pltpu.VMEM(pair_mask.shape, jnp.int32),
            pltpu.VMEM((channels, 2 * channels), bf16),
            pltpu.SemaphoreType.DMA((3,)),
        ],
    )
    lefts = gather(left, "col", steps)
    right, normed, scale, factors, out_open, gate_factor, upstream = call(
        factors_kernel,
        (wide, flat, flat, jax.ShapeDtypeStruct((4, pairs, channels), f32), flat, flat, flat),
        pair_acts, pair_mask, crop_length, cotangent, in_weights, out_weight,
        smem=(2,), hbm=(0, 1, 3, 4, 5), flops=2 * pairs * channels * 6 * channels,
        scratch=[
            pltpu.VMEM(pair_acts.shape, bf16),
            pltpu.VMEM(pair_mask.shape, jnp.int32),
            pltpu.VMEM(cotangent.shape, bf16),
            pltpu.VMEM(in_weights.shape, bf16),
            pltpu.VMEM(out_weight.shape, bf16),
            pltpu.SemaphoreType.DMA((5,)),
        ],
    )
    (left_panel,) = call(
        functools.partial(left_panel_kernel, [0] + steps), (panel,), crop_length, *lefts, smem=(0,)
    )
    parts = {}
    for step in [0] + row_steps:
        (parts[step],) = call(
            functools.partial(partial_kernel, (step,)), (tile if step else wide,), left_panel, right, flops=work,
        )
    total = parts[0]
    for step in row_steps:
        part = swap(parts[step], "row", step)
        if step != row_steps[-1]:
            (total,) = call(add_kernel, (wide,), total, part, flops=wait)
    tri_normed, tri_grad = call(
        triangle_kernel, (flat, tile), total, part, upstream, flops=20 * pairs * channels,
    )
    grads = gather(tri_grad, "row", row_steps)
    update, partial = call(
        update_kernel, (tile, flat), tri_normed, out_open, gate_factor, in_weights, out_weight,
        flops=4 * pairs * channels * channels,
    )
    (right_grad,) = call(functools.partial(right_grad_kernel, [0]), (wide,), left_panel, tri_grad)
    right, partial, right_grad = lax.optimization_barrier((right, partial, right_grad))
    (grad_panel,) = call(
        functools.partial(panel_kernel, "row", [0] + row_steps), (jax.ShapeDtypeStruct((n * pairs, channels), f32),), *grads
    )
    last_steps = list(range(n - 1, 0, -1))
    terms = {}
    for group in (last_steps, [0]):
        if terms:
            right, terms[last] = lax.optimization_barrier((right, terms[last]))
        last = group[-1]
        outs = call(
            functools.partial(left_terms_kernel, group), (wide if group == [0] else tile,) * len(group),
            grad_panel, right, flops=work,
        )
        terms.update(zip(group, outs))
    total, last = terms[0], []
    for step in last_steps:
        term = swap(terms[step], "col", step)
        if step == last_steps[-1]:
            last.append(term)
        else:
            (total,) = call(add_kernel, (wide,), total, term, flops=wait)
    (share,) = call(
        functools.partial(right_back_kernel, row_steps), (flat,),
        left_panel, *grads[1:], right_grad, factors, in_weights, partial,
        scratch=[pltpu.VMEM(wide.shape, f32)],
    )
    (pair_grad,) = call(
        back_kernel, (tile,), total, *last[::-1], normed, scale, factors, share, in_weights,
        flops=2 * pairs * channels * 2 * channels,
    )
    return (update, pair_grad)


def solution(mesh):
    return jax.shard_map(
        local,
        mesh=mesh,
        in_specs=(
            P(("group", "row"), "col", None),
            P(("group", "row"), "col"),
            P("group"),
            P(("group", "row"), "col", None),
            P(),
            P(),
        ),
        out_specs=(P(("group", "row"), "col", None), P(("group", "row"), "col", None)),
        check_vma=False,
    )
```

```python
import functools

import jax
import jax.numpy as jnp
from jax import lax
from jax.experimental import pallas as pl
from jax.experimental.pallas import tpu as pltpu
from jax.sharding import PartitionSpec as P

epsilon = 1e-05
f32 = jnp.float32
bf16 = jnp.bfloat16


def mean_lanes(values):
    return jnp.sum(values, axis=-1, keepdims=True) * (1.0 / values.shape[-1])


def normalize(values):
    center = values - mean_lanes(values)
    variance = mean_lanes(center * center)
    scale = lax.rsqrt(variance + epsilon)
    return (center * scale, scale)


def normalize_back(normed, scale, upstream):
    average = mean_lanes(upstream)
    project = mean_lanes(upstream * normed)
    return scale * (upstream - average - normed * project)


def sigmoid(values):
    return 1.0 / (1.0 + jnp.exp(-values))


def dot(a, b):
    return jnp.dot(a, b, preferred_element_type=f32)


def dot_t(a, b):
    return lax.dot_general(a, b, (((1,), (1,)), ((), ())), preferred_element_type=f32)


def live_pairs(crop_ref, row, col, shape):
    rows = row * shape[0] + lax.broadcasted_iota(jnp.int32, shape, 0)
    cols = col * shape[1] + lax.broadcasted_iota(jnp.int32, shape, 1)
    return jnp.where(jnp.maximum(rows, cols) < crop_ref[0], 1.0, 0.0)


def spread(mask, channels):
    size = mask.shape[0]
    pair = lax.broadcasted_iota(jnp.int32, (size * size, size), 0)
    lane = lax.broadcasted_iota(jnp.int32, (size * size, size), 1)
    pick_row = jnp.where(pair // size == lane, 1.0, 0.0).astype(bf16)
    pick_col = jnp.where(pair % size == lane, 1.0, 0.0)
    picked = (dot(pick_row, mask.astype(bf16)) * pick_col).astype(bf16)
    return dot(picked, jnp.ones((size, channels), bf16))


def start_copies(sems, *pairs):
    copies = [pltpu.make_async_copy(src, dst, sems.at[n]) for n, (src, dst) in enumerate(pairs)]
    for copy in copies:
        copy.start()
    return copies


def gated(projected, block, keep):
    channels = keep.shape[1]
    value = projected[:, block * channels : (block + 1) * channels]
    opened = sigmoid(projected[:, (block + 1) * channels : (block + 2) * channels])
    return (opened * value * keep).astype(bf16), opened, value


def left_kernel(acts_in, mask_in, weights_in, left_ref, acts_ref, mask_ref, weights_ref, sems):
    size, _, channels = acts_ref.shape
    copies = start_copies(
        sems, (acts_in, acts_ref), (weights_in.at[:, pl.ds(0, 2 * channels)], weights_ref), (mask_in, mask_ref),
    )
    copies[0].wait()
    normed, _ = normalize(acts_ref[...].astype(f32).reshape(size * size, channels))
    normed = normed.astype(bf16)
    for copy in copies[1:]:
        copy.wait()
    left, _, _ = gated(dot(normed, weights_ref[...]), 0, spread(mask_ref[...].astype(f32), channels))
    left_ref[...] = left.reshape(size, size, channels)


def factors_kernel(
    acts_in, mask_in, crop_ref, cotangent_in, weights_in, out_weight_in,
    right_ref, normed_ref, scale_ref, factor_ref, open_ref, gate_factor_ref, upstream_ref,
    acts_ref, mask_ref, cotangent_ref, weights_ref, out_weight_ref, sems,
):
    copies = start_copies(
        sems, (acts_in, acts_ref), (weights_in, weights_ref), (mask_in, mask_ref),
        (cotangent_in, cotangent_ref), (out_weight_in, out_weight_ref),
    )
    size, _, channels = acts_ref.shape
    pairs = size * size
    copies[0].wait()
    normed, scale = normalize(acts_ref[...].astype(f32).reshape(pairs, channels))
    normed_ref[...] = normed
    scale_ref[...] = jnp.broadcast_to(scale, (pairs, channels))
    for copy in copies[1:]:
        copy.wait()
    projected = dot(normed.astype(bf16), weights_ref[...])
    live = live_pairs(crop_ref, lax.axis_index("row"), lax.axis_index("col"), (size, size))
    keep = spread(mask_ref[...].astype(f32) * live, channels)
    for block in (0, 2):
        tile, opened, value = gated(projected, block, keep)
        factor_ref[block] = keep * opened
        factor_ref[block + 1] = keep * value * opened * (1.0 - opened)
    right_ref[...] = tile.astype(f32).reshape(size, size, channels)
    out_open = sigmoid(projected[:, 4 * channels :])
    cotangent = cotangent_ref[...].astype(f32).reshape(pairs, channels)
    lin_grad = (cotangent * out_open).astype(bf16)
    open_ref[...] = out_open
    gate_factor_ref[...] = cotangent * out_open * (1.0 - out_open)
    upstream_ref[...] = dot_t(lin_grad, out_weight_ref[...])


def weighted_sums(weights, start, terms, out, base=None):
    def step(k, _):
        total = weights[start + k, pl.ds(0, 1), :] * terms[0]
        for n in range(1, len(terms)):
            total = total + weights[start + k, pl.ds(n, 1), :] * terms[n]
        if base is not None:
            total = total + base[k]
        out[k] = total.astype(out.dtype)
        return 0

    lax.fori_loop(0, out.shape[0], step, 0, unroll=4)


def panel_kernel(axis, steps, *refs):
    here, panel = lax.axis_index(axis), refs[-1]
    rows = panel.shape[0] // len(steps)
    for step, ref in zip(steps, refs):
        tile = ref[...].astype(f32)
        panel[pl.ds((here ^ step) * rows, rows)] = tile.reshape((rows,) + panel.shape[1:])


def left_panel_kernel(steps, crop_ref, *refs):
    row, col, panel = lax.axis_index("row"), lax.axis_index("col"), refs[-1]
    size, _, channels = refs[0].shape
    rows = row * size + lax.broadcasted_iota(jnp.int32, (size, 1, channels), 0)
    row_live = jnp.where(rows < crop_ref[0], 1.0, 0.0)
    for step, ref in zip(steps, refs):
        place = col ^ step
        cols = place * size + lax.broadcasted_iota(jnp.int32, (1, size, channels), 1)
        col_live = jnp.where(cols < crop_ref[0], 1.0, 0.0)
        panel[pl.ds(place * size, size)] = ref[...].astype(f32) * (row_live * col_live)


def partial_kernel(steps, panel, right_ref, *outs):
    size, _, channels = right_ref.shape
    for step, out in zip(steps, outs):
        start = (lax.axis_index("row") ^ step) * size

        def add(k, sums):
            other = right_ref[k]
            return tuple(sums[i] + panel[start + k, pl.ds(i, 1), :] * other for i in range(size))

        zero = jnp.zeros((size, channels), f32)
        sums = lax.fori_loop(0, size, add, (zero,) * size, unroll=4)
        for i in range(size):
            out[i] = sums[i].astype(out.dtype)


def triangle_kernel(base, tile_ref, upstream_ref, tri_normed_ref, grad_ref):
    size = grad_ref.shape[0]
    for i in range(size):
        here = pl.ds(i * size, size)
        tri_normed, scale = normalize(base[i] + tile_ref[i].astype(f32))
        tri_normed_ref[here, :] = tri_normed
        grad_ref[i] = normalize_back(tri_normed, scale, upstream_ref[here, :]).astype(bf16)


def left_terms_kernel(steps, panel, right, *outs):
    size = right.shape[0]
    for step, out in zip(steps, outs):
        start = (lax.axis_index("col") ^ step) * (size * size)
        weighted_sums(right, 0, [panel[pl.ds(start + j, size, stride=size), :] for j in range(size)], out)


def right_grad_kernel(steps, panel, *refs):
    out, base = refs[-1], refs[len(steps)] if len(refs) > len(steps) + 1 else None
    size = out.shape[0]
    for step, grad in zip(steps, refs):
        start = (lax.axis_index("row") ^ step) * size
        weighted_sums(panel, start, [grad[i].astype(f32) for i in range(size)], out, base)
        base = out


def right_back_kernel(steps, panel, *refs):
    factor_ref, weights_ref, share_ref, out, right_ref = refs[-5:]
    right_grad_kernel(steps, panel, *refs[: len(steps) + 1], right_ref)
    pairs, channels = out.shape
    right = right_ref[...].reshape(pairs, channels)
    grads = jnp.concatenate([(right * factor_ref[block]).astype(bf16) for block in (2, 3)], axis=1)
    out[...] = share_ref[...] + dot_t(grads, weights_ref[:, 2 * channels : 4 * channels])


def add_kernel(base, tile_ref, out):
    out[...] = base[...] + tile_ref[...].astype(f32)


def update_kernel(
    tri_normed_ref, open_ref, gate_factor_ref, weights_ref, out_weight_ref, update_ref, normed_grad_ref
):
    size, _, channels = update_ref.shape
    linear = dot(tri_normed_ref[...].astype(bf16), out_weight_ref[...])
    update = (open_ref[...] * linear).astype(bf16)
    update_ref[...] = update.reshape(size, size, channels)
    out_gate_grad = (gate_factor_ref[...] * linear).astype(bf16)
    normed_grad_ref[...] = dot_t(out_gate_grad, weights_ref[:, 4 * channels :])


def back_kernel(base, *refs):
    *tiles, normed_ref, scale_ref, factor_ref, share_ref, weights_ref, out = refs
    size, _, channels = out.shape
    pairs = size * size
    left = base[...]
    for ref in tiles:
        left = left + ref[...].astype(f32)
    left = left.reshape(pairs, channels)
    grads = jnp.concatenate([(left * factor_ref[block]).astype(bf16) for block in (0, 1)], axis=1)
    normed_grad = share_ref[...] + dot_t(grads, weights_ref[:, : 2 * channels])
    back = normalize_back(normed_ref[...], scale_ref[...], normed_grad)
    out[...] = back.astype(bf16).reshape(size, size, channels)


def call(kernel, outs, *args, scratch=(), flops=0, smem=(), hbm=()):
    spec = pl.BlockSpec(memory_space=pltpu.VMEM)
    total = sum(a.size * a.dtype.itemsize for a in (*args, *outs))
    specs = [spec] * len(args)
    for n in smem:
        specs[n] = pl.BlockSpec(memory_space=pltpu.SMEM)
    args = list(args)
    for n in hbm:
        specs[n] = pl.BlockSpec(memory_space=pltpu.HBM)
        args[n] = pltpu.with_memory_space_constraint(args[n], pltpu.HBM)
    return pl.pallas_call(
        kernel,
        out_shape=tuple(outs),
        in_specs=specs,
        out_specs=(spec,) * len(outs),
        scratch_shapes=scratch,
        compiler_params=pltpu.CompilerParams(vmem_limit_bytes=24 * 2**20),
        cost_estimate=pl.CostEstimate(flops=flops, bytes_accessed=total if flops else 0, transcendentals=0),
    )(*args)


def local(pair_acts, pair_mask, crop_length, cotangent, in_weights, out_weight):
    size, _, channels = pair_acts.shape
    pairs = size * size
    n = lax.axis_size("row")
    tile = jax.ShapeDtypeStruct((size, size, channels), bf16)
    flat = jax.ShapeDtypeStruct((pairs, channels), f32)

    wide = jax.ShapeDtypeStruct((size, size, channels), f32)
    panel = jax.ShapeDtypeStruct((n * size, size, channels), f32)
    work = 2 * size * pairs * channels
    wait = 2**31
    steps = [step for bit in range(n.bit_length() - 2, -1, -1) for step in range(2**bit, 2 ** (bit + 1))]
    row_steps = list(range(n - 1, 0, -1))
    gather_steps = [n - 1] + list(range(1, n - 1))


    def swap(values, axis, step):
        return lax.ppermute(values, axis, [(a, a ^ step) for a in range(n)])

    def gather(values, axis, steps):
        return [values] + [swap(values, axis, step) for step in steps]

    (left,) = call(
        left_kernel, (tile,), pair_acts, pair_mask, in_weights,
        hbm=(0, 1, 2), flops=2 * pairs * channels * 2 * channels,
        scratch=[
            pltpu.VMEM(pair_acts.shape, bf16),
            pltpu.VMEM(pair_mask.shape, jnp.int32),
            pltpu.VMEM((channels, 2 * channels), bf16),
            pltpu.SemaphoreType.DMA((3,)),
        ],
    )
    lefts = gather(left, "col", steps)
    right, normed, scale, factors, out_open, gate_factor, upstream = call(
        factors_kernel,
        (wide, flat, flat, jax.ShapeDtypeStruct((4, pairs, channels), f32), flat, flat, flat),
        pair_acts, pair_mask, crop_length, cotangent, in_weights, out_weight,
        smem=(2,), hbm=(0, 1, 3, 4, 5), flops=2 * pairs * channels * 6 * channels,
        scratch=[
            pltpu.VMEM(pair_acts.shape, bf16),
            pltpu.VMEM(pair_mask.shape, jnp.int32),
            pltpu.VMEM(cotangent.shape, bf16),
            pltpu.VMEM(in_weights.shape, bf16),
            pltpu.VMEM(out_weight.shape, bf16),
            pltpu.SemaphoreType.DMA((5,)),
        ],
    )
    (left_panel,) = call(
        functools.partial(left_panel_kernel, [0] + steps), (panel,), crop_length, *lefts, smem=(0,)
    )
    parts = {}
    for step in [0] + row_steps:
        (parts[step],) = call(
            functools.partial(partial_kernel, (step,)), (tile if step else wide,), left_panel, right, flops=work,
        )
    total = parts[0]
    for step in row_steps:
        part = swap(parts[step], "row", step)
        if step != row_steps[-1]:
            (total,) = call(add_kernel, (wide,), total, part, flops=wait)
    tri_normed, tri_grad = call(
        triangle_kernel, (flat, tile), total, part, upstream, flops=20 * pairs * channels,
    )
    grads = gather(tri_grad, "row", gather_steps)
    update, partial = call(
        update_kernel, (tile, flat), tri_normed, out_open, gate_factor, in_weights, out_weight,
        flops=4 * pairs * channels * channels,
    )
    (right_grad,) = call(functools.partial(right_grad_kernel, [0]), (wide,), left_panel, tri_grad)
    right, partial, right_grad = lax.optimization_barrier((right, partial, right_grad))
    (grad_panel,) = call(
        functools.partial(panel_kernel, "row", [0] + gather_steps), (jax.ShapeDtypeStruct((n * pairs, channels), f32),), *grads
    )
    terms = {}
    for group in (steps, [0]):
        if terms:
            right, terms[last] = lax.optimization_barrier((right, terms[last]))
        last = group[-1]
        outs = call(
            functools.partial(left_terms_kernel, group), (wide if group == [0] else tile,) * len(group),
            grad_panel, right, flops=work,
        )
        terms.update(zip(group, outs))
    total, last = terms[0], []
    for step in steps:
        term = swap(terms[step], "col", step)
        if step == steps[-1]:
            last.append(term)
        else:
            (total,) = call(add_kernel, (wide,), total, term, flops=wait)
    (share,) = call(
        functools.partial(right_back_kernel, gather_steps), (flat,),
        left_panel, *grads[1:], right_grad, factors, in_weights, partial,
        scratch=[pltpu.VMEM(wide.shape, f32)],
    )
    (pair_grad,) = call(
        back_kernel, (tile,), total, *last[::-1], normed, scale, factors, share, in_weights,
        flops=2 * pairs * channels * 2 * channels,
    )
    return (update, pair_grad)


def solution(mesh):
    return jax.shard_map(
        local,
        mesh=mesh,
        in_specs=(
            P(("group", "row"), "col", None),
            P(("group", "row"), "col"),
            P("group"),
            P(("group", "row"), "col", None),
            P(),
            P(),
        ),
        out_specs=(P(("group", "row"), "col", None), P(("group", "row"), "col", None)),
        check_vma=False,
    )
```

```python
import functools

import jax
import jax.numpy as jnp
from jax import lax
from jax.experimental import pallas as pl
from jax.experimental.pallas import tpu as pltpu
from jax.sharding import PartitionSpec as P

epsilon = 1e-05
f32 = jnp.float32
bf16 = jnp.bfloat16


def mean_lanes(values):
    return jnp.sum(values, axis=-1, keepdims=True) * (1.0 / values.shape[-1])


def normalize(values):
    center = values - mean_lanes(values)
    variance = mean_lanes(center * center)
    scale = lax.rsqrt(variance + epsilon)
    return (center * scale, scale)


def normalize_back(normed, scale, upstream):
    average = mean_lanes(upstream)
    project = mean_lanes(upstream * normed)
    return scale * (upstream - average - normed * project)


def sigmoid(values):
    return 1.0 / (1.0 + jnp.exp(-values))


def dot(a, b):
    return jnp.dot(a, b, preferred_element_type=f32)


def dot_t(a, b):
    return lax.dot_general(a, b, (((1,), (1,)), ((), ())), preferred_element_type=f32)


def live_pairs(crop_ref, row, col, shape):
    rows = row * shape[0] + lax.broadcasted_iota(jnp.int32, shape, 0)
    cols = col * shape[1] + lax.broadcasted_iota(jnp.int32, shape, 1)
    return jnp.where(jnp.maximum(rows, cols) < crop_ref[0], 1.0, 0.0)


def spread(mask, channels):
    size = mask.shape[0]
    pair = lax.broadcasted_iota(jnp.int32, (size * size, size), 0)
    lane = lax.broadcasted_iota(jnp.int32, (size * size, size), 1)
    pick_row = jnp.where(pair // size == lane, 1.0, 0.0).astype(bf16)
    pick_col = jnp.where(pair % size == lane, 1.0, 0.0)
    picked = (dot(pick_row, mask.astype(bf16)) * pick_col).astype(bf16)
    return dot(picked, jnp.ones((size, channels), bf16))


def start_copies(sems, *pairs):
    copies = [pltpu.make_async_copy(src, dst, sems.at[n]) for n, (src, dst) in enumerate(pairs)]
    for copy in copies:
        copy.start()
    return copies


def gated(projected, block, keep):
    channels = keep.shape[1]
    value = projected[:, block * channels : (block + 1) * channels]
    opened = sigmoid(projected[:, (block + 1) * channels : (block + 2) * channels])
    return (opened * value * keep).astype(bf16), opened, value


def left_kernel(acts_in, mask_in, weights_in, left_ref, acts_ref, mask_ref, weights_ref, sems):
    size, _, channels = acts_ref.shape
    copies = start_copies(
        sems, (acts_in, acts_ref), (weights_in.at[:, pl.ds(0, 2 * channels)], weights_ref), (mask_in, mask_ref),
    )
    copies[0].wait()
    normed, _ = normalize(acts_ref[...].astype(f32).reshape(size * size, channels))
    normed = normed.astype(bf16)
    for copy in copies[1:]:
        copy.wait()
    left, _, _ = gated(dot(normed, weights_ref[...]), 0, spread(mask_ref[...].astype(f32), channels))
    left_ref[...] = left.reshape(size, size, channels)


def factors_kernel(
    acts_in, mask_in, crop_ref, cotangent_in, weights_in, out_weight_in,
    right_ref, normed_ref, scale_ref, factor_ref, open_ref, gate_factor_ref, upstream_ref,
    acts_ref, mask_ref, cotangent_ref, weights_ref, out_weight_ref, sems,
):
    copies = start_copies(
        sems, (acts_in, acts_ref), (weights_in, weights_ref), (mask_in, mask_ref),
        (cotangent_in, cotangent_ref), (out_weight_in, out_weight_ref),
    )
    size, _, channels = acts_ref.shape
    pairs = size * size
    copies[0].wait()
    normed, scale = normalize(acts_ref[...].astype(f32).reshape(pairs, channels))
    normed_ref[...] = normed
    scale_ref[...] = jnp.broadcast_to(scale, (pairs, channels))
    for copy in copies[1:]:
        copy.wait()
    projected = dot(normed.astype(bf16), weights_ref[...])
    live = live_pairs(crop_ref, lax.axis_index("row"), lax.axis_index("col"), (size, size))
    keep = spread(mask_ref[...].astype(f32) * live, channels)
    for block in (0, 2):
        tile, opened, value = gated(projected, block, keep)
        factor_ref[block] = keep * opened
        factor_ref[block + 1] = keep * value * opened * (1.0 - opened)
    right_ref[...] = tile.astype(f32).reshape(size, size, channels)
    out_open = sigmoid(projected[:, 4 * channels :])
    cotangent = cotangent_ref[...].astype(f32).reshape(pairs, channels)
    lin_grad = (cotangent * out_open).astype(bf16)
    open_ref[...] = out_open
    gate_factor_ref[...] = cotangent * out_open * (1.0 - out_open)
    upstream_ref[...] = dot_t(lin_grad, out_weight_ref[...])


def weighted_sums(weights, start, terms, out, base=None):
    def step(k, _):
        total = weights[start + k, pl.ds(0, 1), :] * terms[0]
        for n in range(1, len(terms)):
            total = total + weights[start + k, pl.ds(n, 1), :] * terms[n]
        if base is not None:
            total = total + base[k]
        out[k] = total.astype(out.dtype)
        return 0

    lax.fori_loop(0, out.shape[0], step, 0, unroll=4)


def panel_kernel(axis, steps, *refs):
    here, panel = lax.axis_index(axis), refs[-1]
    rows = panel.shape[0] // len(steps)
    for step, ref in zip(steps, refs):
        tile = ref[...].astype(f32)
        panel[pl.ds((here ^ step) * rows, rows)] = tile.reshape((rows,) + panel.shape[1:])


def left_panel_kernel(steps, crop_ref, *refs):
    row, col, panel = lax.axis_index("row"), lax.axis_index("col"), refs[-1]
    size, _, channels = refs[0].shape
    rows = row * size + lax.broadcasted_iota(jnp.int32, (size, 1, channels), 0)
    row_live = jnp.where(rows < crop_ref[0], 1.0, 0.0)
    for step, ref in zip(steps, refs):
        place = col ^ step
        cols = place * size + lax.broadcasted_iota(jnp.int32, (1, size, channels), 1)
        col_live = jnp.where(cols < crop_ref[0], 1.0, 0.0)
        panel[pl.ds(place * size, size)] = ref[...].astype(f32) * (row_live * col_live)


def partial_kernel(steps, crop_ref, *refs):
    count = len(steps)
    lefts, right_ref, outs, left = refs[:count], refs[count], refs[count + 1 : -1], refs[-1]
    size, _, channels = right_ref.shape
    rows = lax.axis_index("row") * size + lax.broadcasted_iota(jnp.int32, (size, 1, channels), 0)
    row_live = jnp.where(rows < crop_ref[0], 1.0, 0.0)
    for step, left_ref, out in zip(steps, lefts, outs):
        cols = (lax.axis_index("col") ^ step) * size + lax.broadcasted_iota(jnp.int32, (1, size, channels), 1)
        left[...] = left_ref[...].astype(f32) * (row_live * jnp.where(cols < crop_ref[0], 1.0, 0.0))

        def add(k, sums):
            other = right_ref[k]
            return tuple(sums[i] + left[k, pl.ds(i, 1), :] * other for i in range(size))

        zero = jnp.zeros((size, channels), f32)
        sums = lax.fori_loop(0, size, add, (zero,) * size, unroll=4)
        for i in range(size):
            out[i] = sums[i]


def pick_kernel(steps, *refs):
    here = lax.axis_index("row") ^ lax.axis_index("col")
    tiles, outs = refs[: len(steps)], refs[len(steps) :]
    for step, out in zip(steps, outs):
        for other, tile in enumerate(tiles):

            @pl.when((here ^ step) == other)
            def _():
                out[...] = tile[...].astype(out.dtype)


def triangle_kernel(base, tile_ref, upstream_ref, tri_normed_ref, grad_ref):
    size = grad_ref.shape[0]
    for i in range(size):
        here = pl.ds(i * size, size)
        tri_normed, scale = normalize(base[i] + tile_ref[i].astype(f32))
        tri_normed_ref[here, :] = tri_normed
        grad_ref[i] = normalize_back(tri_normed, scale, upstream_ref[here, :]).astype(bf16)


def left_terms_kernel(steps, panel, right, *outs):
    size = right.shape[0]
    for step, out in zip(steps, outs):
        start = (lax.axis_index("col") ^ step) * (size * size)
        weighted_sums(right, 0, [panel[pl.ds(start + j, size, stride=size), :] for j in range(size)], out)


def right_grad_kernel(steps, panel, *refs):
    out, base = refs[-1], refs[len(steps)] if len(refs) > len(steps) + 1 else None
    size = out.shape[0]
    for step, grad in zip(steps, refs):
        start = (lax.axis_index("row") ^ step) * size
        weighted_sums(panel, start, [grad[i].astype(f32) for i in range(size)], out, base)
        base = out


def right_back_kernel(steps, panel, *refs):
    factor_ref, weights_ref, share_ref, out, right_ref = refs[-5:]
    right_grad_kernel(steps, panel, *refs[: len(steps) + 1], right_ref)
    pairs, channels = out.shape
    right = right_ref[...].reshape(pairs, channels)
    grads = jnp.concatenate([(right * factor_ref[block]).astype(bf16) for block in (2, 3)], axis=1)
    out[...] = share_ref[...] + dot_t(grads, weights_ref[:, 2 * channels : 4 * channels])


def add_kernel(base, tile_ref, out):
    out[...] = base[...] + tile_ref[...].astype(f32)


def update_kernel(
    tri_normed_ref, open_ref, gate_factor_ref, weights_ref, out_weight_ref, update_ref, normed_grad_ref
):
    size, _, channels = update_ref.shape
    linear = dot(tri_normed_ref[...].astype(bf16), out_weight_ref[...])
    update = (open_ref[...] * linear).astype(bf16)
    update_ref[...] = update.reshape(size, size, channels)
    out_gate_grad = (gate_factor_ref[...] * linear).astype(bf16)
    normed_grad_ref[...] = dot_t(out_gate_grad, weights_ref[:, 4 * channels :])


def back_kernel(base, *refs):
    *tiles, normed_ref, scale_ref, factor_ref, share_ref, weights_ref, out = refs
    size, _, channels = out.shape
    pairs = size * size
    left = base[...]
    for ref in tiles:
        left = left + ref[...].astype(f32)
    left = left.reshape(pairs, channels)
    grads = jnp.concatenate([(left * factor_ref[block]).astype(bf16) for block in (0, 1)], axis=1)
    normed_grad = share_ref[...] + dot_t(grads, weights_ref[:, : 2 * channels])
    back = normalize_back(normed_ref[...], scale_ref[...], normed_grad)
    out[...] = back.astype(bf16).reshape(size, size, channels)


def call(kernel, outs, *args, scratch=(), flops=0, smem=(), hbm=()):
    spec = pl.BlockSpec(memory_space=pltpu.VMEM)
    total = sum(a.size * a.dtype.itemsize for a in (*args, *outs))
    specs = [spec] * len(args)
    for n in smem:
        specs[n] = pl.BlockSpec(memory_space=pltpu.SMEM)
    args = list(args)
    for n in hbm:
        specs[n] = pl.BlockSpec(memory_space=pltpu.HBM)
        args[n] = pltpu.with_memory_space_constraint(args[n], pltpu.HBM)
    return pl.pallas_call(
        kernel,
        out_shape=tuple(outs),
        in_specs=specs,
        out_specs=(spec,) * len(outs),
        scratch_shapes=scratch,
        compiler_params=pltpu.CompilerParams(vmem_limit_bytes=24 * 2**20),
        cost_estimate=pl.CostEstimate(flops=flops, bytes_accessed=total if flops else 0, transcendentals=0),
    )(*args)


def local(pair_acts, pair_mask, crop_length, cotangent, in_weights, out_weight):
    size, _, channels = pair_acts.shape
    pairs = size * size
    n = lax.axis_size("row")
    tile = jax.ShapeDtypeStruct((size, size, channels), bf16)
    flat = jax.ShapeDtypeStruct((pairs, channels), f32)

    wide = jax.ShapeDtypeStruct((size, size, channels), f32)
    panel = jax.ShapeDtypeStruct((n * size, size, channels), f32)
    work = 2 * size * pairs * channels
    wait = 2**31
    steps = [step for bit in range(n.bit_length() - 2, -1, -1) for step in range(2**bit, 2 ** (bit + 1))]
    row_steps = list(range(n - 1, 0, -1))
    gather_steps = [n - 1] + list(range(1, n - 1))


    def swap(values, axis, step):
        return lax.ppermute(values, axis, [(a, a ^ step) for a in range(n)])

    def gather(values, axis, steps):
        return [values] + [swap(values, axis, step) for step in steps]

    (left,) = call(
        left_kernel, (tile,), pair_acts, pair_mask, in_weights,
        hbm=(0, 1, 2), flops=2 * pairs * channels * 2 * channels,
        scratch=[
            pltpu.VMEM(pair_acts.shape, bf16),
            pltpu.VMEM(pair_mask.shape, jnp.int32),
            pltpu.VMEM((channels, 2 * channels), bf16),
            pltpu.SemaphoreType.DMA((3,)),
        ],
    )
    lefts = gather(left, "col", steps)
    right, normed, scale, factors, out_open, gate_factor, upstream = call(
        factors_kernel,
        (wide, flat, flat, jax.ShapeDtypeStruct((4, pairs, channels), f32), flat, flat, flat),
        pair_acts, pair_mask, crop_length, cotangent, in_weights, out_weight,
        smem=(2,), hbm=(0, 1, 3, 4, 5), flops=2 * pairs * channels * 6 * channels,
        scratch=[
            pltpu.VMEM(pair_acts.shape, bf16),
            pltpu.VMEM(pair_mask.shape, jnp.int32),
            pltpu.VMEM(cotangent.shape, bf16),
            pltpu.VMEM(in_weights.shape, bf16),
            pltpu.VMEM(out_weight.shape, bf16),
            pltpu.SemaphoreType.DMA((5,)),
        ],
    )
    parts = []
    order = [0] + steps
    for group in [[at] for at in range(n - 2)] + [[n - 2, n - 1]]:
        parts += call(
            functools.partial(partial_kernel, [order[at] for at in group]), (wide,) * len(group),
            crop_length, *(lefts[at] for at in group), right, smem=(0,), flops=work,
            scratch=[pltpu.VMEM(wide.shape, f32)],
        )
    parts = [part for _, part in sorted(zip(order, parts), key=lambda each: each[0])]
    total, *parts = call(
        functools.partial(pick_kernel, [0] + row_steps), (wide,) + (tile,) * (n - 1), *parts,
        flops=pairs * channels,
    )
    (left_panel,) = call(
        functools.partial(left_panel_kernel, [0] + steps), (panel,), crop_length, *lefts, smem=(0,)
    )
    for step, part in zip(row_steps, parts):
        part = swap(part, "row", step)
        if step != row_steps[-1]:
            (total,) = call(add_kernel, (wide,), total, part, flops=wait)
    tri_normed, tri_grad = call(
        triangle_kernel, (flat, tile), total, part, upstream, flops=20 * pairs * channels,
    )
    grads = gather(tri_grad, "row", gather_steps)
    update, partial = call(
        update_kernel, (tile, flat), tri_normed, out_open, gate_factor, in_weights, out_weight,
        flops=4 * pairs * channels * channels,
    )
    (right_grad,) = call(functools.partial(right_grad_kernel, [0]), (wide,), left_panel, tri_grad)
    right, partial, right_grad = lax.optimization_barrier((right, partial, right_grad))
    (grad_panel,) = call(
        functools.partial(panel_kernel, "row", [0] + gather_steps), (jax.ShapeDtypeStruct((n * pairs, channels), f32),), *grads
    )
    terms = {}
    for group in (steps[:1], steps[1:], [0]):
        if terms:
            right, terms[last] = lax.optimization_barrier((right, terms[last]))
        last = group[-1]
        outs = call(
            functools.partial(left_terms_kernel, group), (wide if group == [0] else tile,) * len(group),
            grad_panel, right, flops=work,
        )
        terms.update(zip(group, outs))
    total, last = terms[0], []
    for step in steps:
        term = swap(terms[step], "col", step)
        if step == steps[-1]:
            last.append(term)
        else:
            (total,) = call(add_kernel, (wide,), total, term, flops=wait)
    (share,) = call(
        functools.partial(right_back_kernel, gather_steps), (flat,),
        left_panel, *grads[1:], right_grad, factors, in_weights, partial,
        scratch=[pltpu.VMEM(wide.shape, f32)],
    )
    (pair_grad,) = call(
        back_kernel, (tile,), total, *last[::-1], normed, scale, factors, share, in_weights,
        flops=2 * pairs * channels * 2 * channels,
    )
    return (update, pair_grad)


def solution(mesh):
    return jax.shard_map(
        local,
        mesh=mesh,
        in_specs=(
            P(("group", "row"), "col", None),
            P(("group", "row"), "col"),
            P("group"),
            P(("group", "row"), "col", None),
            P(),
            P(),
        ),
        out_specs=(P(("group", "row"), "col", None), P(("group", "row"), "col", None)),
        check_vma=False,
    )
```

```python
import functools

import jax
import jax.numpy as jnp
from jax import lax
from jax.experimental import pallas as pl
from jax.experimental.pallas import tpu as pltpu
from jax.sharding import PartitionSpec as P

epsilon = 1e-05
f32 = jnp.float32
bf16 = jnp.bfloat16


def mean_lanes(values):
    return jnp.sum(values, axis=-1, keepdims=True) * (1.0 / values.shape[-1])


def normalize(values):
    center = values - mean_lanes(values)
    variance = mean_lanes(center * center)
    scale = lax.rsqrt(variance + epsilon)
    return (center * scale, scale)


def normalize_back(normed, scale, upstream):
    average = mean_lanes(upstream)
    project = mean_lanes(upstream * normed)
    return scale * (upstream - average - normed * project)


def sigmoid(values):
    return 1.0 / (1.0 + jnp.exp(-values))


def dot(a, b):
    return jnp.dot(a, b, preferred_element_type=f32)


def dot_t(a, b):
    return lax.dot_general(a, b, (((1,), (1,)), ((), ())), preferred_element_type=f32)


def live_pairs(crop_ref, row, col, shape):
    rows = row * shape[0] + lax.broadcasted_iota(jnp.int32, shape, 0)
    cols = col * shape[1] + lax.broadcasted_iota(jnp.int32, shape, 1)
    return jnp.where(jnp.maximum(rows, cols) < crop_ref[0], 1.0, 0.0)


def spread(mask, channels):
    size = mask.shape[0]
    pair = lax.broadcasted_iota(jnp.int32, (size * size, size), 0)
    lane = lax.broadcasted_iota(jnp.int32, (size * size, size), 1)
    pick_row = jnp.where(pair // size == lane, 1.0, 0.0).astype(bf16)
    pick_col = jnp.where(pair % size == lane, 1.0, 0.0)
    picked = (dot(pick_row, mask.astype(bf16)) * pick_col).astype(bf16)
    return dot(picked, jnp.ones((size, channels), bf16))


def start_copies(sems, *pairs):
    copies = [pltpu.make_async_copy(src, dst, sems.at[n]) for n, (src, dst) in enumerate(pairs)]
    for copy in copies:
        copy.start()
    return copies


def gated(projected, block, keep):
    channels = keep.shape[1]
    value = projected[:, block * channels : (block + 1) * channels]
    opened = sigmoid(projected[:, (block + 1) * channels : (block + 2) * channels])
    return (opened * value * keep).astype(bf16), opened, value


def left_kernel(acts_in, mask_in, weights_in, left_ref, acts_ref, mask_ref, weights_ref, sems):
    size, _, channels = acts_ref.shape
    copies = start_copies(
        sems, (acts_in, acts_ref), (weights_in.at[:, pl.ds(0, 2 * channels)], weights_ref), (mask_in, mask_ref),
    )
    copies[0].wait()
    normed, _ = normalize(acts_ref[...].astype(f32).reshape(size * size, channels))
    normed = normed.astype(bf16)
    for copy in copies[1:]:
        copy.wait()
    left, _, _ = gated(dot(normed, weights_ref[...]), 0, spread(mask_ref[...].astype(f32), channels))
    left_ref[...] = left.reshape(size, size, channels)


def factors_kernel(
    acts_in, mask_in, crop_ref, cotangent_in, weights_in, out_weight_in,
    right_ref, normed_ref, scale_ref, factor_ref, open_ref, gate_factor_ref, upstream_ref,
    acts_ref, mask_ref, cotangent_ref, weights_ref, out_weight_ref, sems,
):
    copies = start_copies(
        sems, (acts_in, acts_ref), (weights_in, weights_ref), (mask_in, mask_ref),
        (cotangent_in, cotangent_ref), (out_weight_in, out_weight_ref),
    )
    size, _, channels = acts_ref.shape
    pairs = size * size
    copies[0].wait()
    normed, scale = normalize(acts_ref[...].astype(f32).reshape(pairs, channels))
    normed_ref[...] = normed
    scale_ref[...] = jnp.broadcast_to(scale, (pairs, channels))
    for copy in copies[1:]:
        copy.wait()
    projected = dot(normed.astype(bf16), weights_ref[...])
    live = live_pairs(crop_ref, lax.axis_index("row"), lax.axis_index("col"), (size, size))
    keep = spread(mask_ref[...].astype(f32) * live, channels)
    for block in (0, 2):
        tile, opened, value = gated(projected, block, keep)
        factor_ref[block] = keep * opened
        factor_ref[block + 1] = keep * value * opened * (1.0 - opened)
    right_ref[...] = tile.astype(f32).reshape(size, size, channels)
    out_open = sigmoid(projected[:, 4 * channels :])
    cotangent = cotangent_ref[...].astype(f32).reshape(pairs, channels)
    lin_grad = (cotangent * out_open).astype(bf16)
    open_ref[...] = out_open
    gate_factor_ref[...] = cotangent * out_open * (1.0 - out_open)
    upstream_ref[...] = dot_t(lin_grad, out_weight_ref[...])


def weighted_sums(weights, start, terms, out, base=None):
    def step(k, _):
        total = weights[start + k, pl.ds(0, 1), :] * terms[0]
        for n in range(1, len(terms)):
            total = total + weights[start + k, pl.ds(n, 1), :] * terms[n]
        if base is not None:
            total = total + base[k]
        out[k] = total.astype(out.dtype)
        return 0

    lax.fori_loop(0, out.shape[0], step, 0, unroll=4)


def left_panel_kernel(steps, crop_ref, *refs):
    row, col, panel = lax.axis_index("row"), lax.axis_index("col"), refs[-1]
    size, _, channels = refs[0].shape
    rows = row * size + lax.broadcasted_iota(jnp.int32, (size, 1, channels), 0)
    row_live = jnp.where(rows < crop_ref[0], 1.0, 0.0)
    for step, ref in zip(steps, refs):
        place = col ^ step
        cols = place * size + lax.broadcasted_iota(jnp.int32, (1, size, channels), 1)
        col_live = jnp.where(cols < crop_ref[0], 1.0, 0.0)
        panel[pl.ds(place * size, size)] = ref[...].astype(f32) * (row_live * col_live)


def partial_kernel(steps, crop_ref, *refs):
    count = len(steps)
    lefts, right_ref, outs, left = refs[:count], refs[count], refs[count + 1 : -1], refs[-1]
    size, _, channels = right_ref.shape
    rows = lax.axis_index("row") * size + lax.broadcasted_iota(jnp.int32, (size, 1, channels), 0)
    row_live = jnp.where(rows < crop_ref[0], 1.0, 0.0)
    for step, left_ref, out in zip(steps, lefts, outs):
        cols = (lax.axis_index("col") ^ step) * size + lax.broadcasted_iota(jnp.int32, (1, size, channels), 1)
        left[...] = left_ref[...].astype(f32) * (row_live * jnp.where(cols < crop_ref[0], 1.0, 0.0))

        def add(k, sums):
            other = right_ref[k]
            return tuple(sums[i] + left[k, pl.ds(i, 1), :] * other for i in range(size))

        zero = jnp.zeros((size, channels), f32)
        sums = lax.fori_loop(0, size, add, (zero,) * size, unroll=4)
        for i in range(size):
            out[i] = sums[i]


def pick_kernel(steps, *refs):
    here = lax.axis_index("row") ^ lax.axis_index("col")
    tiles, outs = refs[: len(steps)], refs[len(steps) :]
    for step, out in zip(steps, outs):
        for other, tile in enumerate(tiles):

            @pl.when((here ^ step) == other)
            def _():
                out[...] = tile[...].astype(out.dtype)


def triangle_kernel(base, tile_ref, upstream_ref, tri_normed_ref, grad_ref):
    size = grad_ref.shape[0]
    for i in range(size):
        here = pl.ds(i * size, size)
        tri_normed, scale = normalize(base[i] + tile_ref[i].astype(f32))
        tri_normed_ref[here, :] = tri_normed
        grad_ref[i] = normalize_back(tri_normed, scale, upstream_ref[here, :]).astype(bf16)


def left_terms_kernel(grad_ref, right, *refs):
    out, grad = refs[-2:]
    size, _, channels = out.shape
    grad[...] = grad_ref[...].astype(f32).reshape(size * size, channels)
    weighted_sums(right, 0, [grad[pl.ds(j, size, stride=size), :] for j in range(size)], out)


def right_grad_kernel(steps, panel, *refs):
    out, base = refs[-1], refs[len(steps)] if len(refs) > len(steps) + 1 else None
    size = out.shape[0]
    for step, grad in zip(steps, refs):
        start = (lax.axis_index("row") ^ step) * size
        weighted_sums(panel, start, [grad[i].astype(f32) for i in range(size)], out, base)
        base = out


def right_back_kernel(steps, panel, *refs):
    factor_ref, weights_ref, share_ref, out, right_ref = refs[-5:]
    right_grad_kernel(steps, panel, *refs[: len(steps) + 1], right_ref)
    pairs, channels = out.shape
    right = right_ref[...].reshape(pairs, channels)
    grads = jnp.concatenate([(right * factor_ref[block]).astype(bf16) for block in (2, 3)], axis=1)
    out[...] = share_ref[...] + dot_t(grads, weights_ref[:, 2 * channels : 4 * channels])


def add_kernel(base, tile_ref, out):
    out[...] = base[...] + tile_ref[...].astype(f32)


def update_kernel(
    tri_normed_ref, open_ref, gate_factor_ref, weights_ref, out_weight_ref, update_ref, normed_grad_ref
):
    size, _, channels = update_ref.shape
    linear = dot(tri_normed_ref[...].astype(bf16), out_weight_ref[...])
    update = (open_ref[...] * linear).astype(bf16)
    update_ref[...] = update.reshape(size, size, channels)
    out_gate_grad = (gate_factor_ref[...] * linear).astype(bf16)
    normed_grad_ref[...] = dot_t(out_gate_grad, weights_ref[:, 4 * channels :])


def back_kernel(base, *refs):
    *tiles, normed_ref, scale_ref, factor_ref, share_ref, weights_ref, out = refs
    size, _, channels = out.shape
    pairs = size * size
    left = base[...]
    for ref in tiles:
        left = left + ref[...].astype(f32)
    left = left.reshape(pairs, channels)
    grads = jnp.concatenate([(left * factor_ref[block]).astype(bf16) for block in (0, 1)], axis=1)
    normed_grad = share_ref[...] + dot_t(grads, weights_ref[:, : 2 * channels])
    back = normalize_back(normed_ref[...], scale_ref[...], normed_grad)
    out[...] = back.astype(bf16).reshape(size, size, channels)


def call(kernel, outs, *args, scratch=(), flops=0, smem=(), hbm=()):
    spec = pl.BlockSpec(memory_space=pltpu.VMEM)
    total = sum(a.size * a.dtype.itemsize for a in (*args, *outs))
    specs = [spec] * len(args)
    for n in smem:
        specs[n] = pl.BlockSpec(memory_space=pltpu.SMEM)
    args = list(args)
    for n in hbm:
        specs[n] = pl.BlockSpec(memory_space=pltpu.HBM)
        args[n] = pltpu.with_memory_space_constraint(args[n], pltpu.HBM)
    return pl.pallas_call(
        kernel,
        out_shape=tuple(outs),
        in_specs=specs,
        out_specs=(spec,) * len(outs),
        scratch_shapes=scratch,
        compiler_params=pltpu.CompilerParams(vmem_limit_bytes=24 * 2**20),
        cost_estimate=pl.CostEstimate(flops=flops, bytes_accessed=total if flops else 0, transcendentals=0),
    )(*args)


def local(pair_acts, pair_mask, crop_length, cotangent, in_weights, out_weight):
    size, _, channels = pair_acts.shape
    pairs = size * size
    n = lax.axis_size("row")
    tile = jax.ShapeDtypeStruct((size, size, channels), bf16)
    flat = jax.ShapeDtypeStruct((pairs, channels), f32)

    wide = jax.ShapeDtypeStruct((size, size, channels), f32)
    panel = jax.ShapeDtypeStruct((n * size, size, channels), f32)
    work = 2 * size * pairs * channels
    wait = 2**31
    steps = [step for bit in range(n.bit_length() - 2, -1, -1) for step in range(2**bit, 2 ** (bit + 1))]
    row_steps = list(range(n - 1, 0, -1))
    gather_steps = [n - 1] + list(range(1, n - 1))


    def swap(values, axis, step):
        return lax.ppermute(values, axis, [(a, a ^ step) for a in range(n)])

    def gather(values, axis, steps):
        return [values] + [swap(values, axis, step) for step in steps]

    (left,) = call(
        left_kernel, (tile,), pair_acts, pair_mask, in_weights,
        hbm=(0, 1, 2), flops=2 * pairs * channels * 2 * channels,
        scratch=[
            pltpu.VMEM(pair_acts.shape, bf16),
            pltpu.VMEM(pair_mask.shape, jnp.int32),
            pltpu.VMEM((channels, 2 * channels), bf16),
            pltpu.SemaphoreType.DMA((3,)),
        ],
    )
    lefts = gather(left, "col", steps)
    right, normed, scale, factors, out_open, gate_factor, upstream = call(
        factors_kernel,
        (wide, flat, flat, jax.ShapeDtypeStruct((4, pairs, channels), f32), flat, flat, flat),
        pair_acts, pair_mask, crop_length, cotangent, in_weights, out_weight,
        smem=(2,), hbm=(0, 1, 3, 4, 5), flops=2 * pairs * channels * 6 * channels,
        scratch=[
            pltpu.VMEM(pair_acts.shape, bf16),
            pltpu.VMEM(pair_mask.shape, jnp.int32),
            pltpu.VMEM(cotangent.shape, bf16),
            pltpu.VMEM(in_weights.shape, bf16),
            pltpu.VMEM(out_weight.shape, bf16),
            pltpu.SemaphoreType.DMA((5,)),
        ],
    )
    parts = []
    order = [0] + steps
    for group in [[at] for at in range(n - 2)] + [[n - 2, n - 1]]:
        parts += call(
            functools.partial(partial_kernel, [order[at] for at in group]), (wide,) * len(group),
            crop_length, *(lefts[at] for at in group), right, smem=(0,), flops=work,
            scratch=[pltpu.VMEM(wide.shape, f32)],
        )
    parts = [part for _, part in sorted(zip(order, parts), key=lambda each: each[0])]
    total, *parts = call(
        functools.partial(pick_kernel, [0] + row_steps), (wide,) + (tile,) * (n - 1), *parts,
        flops=pairs * channels,
    )
    (left_panel,) = call(
        functools.partial(left_panel_kernel, [0] + steps), (panel,), crop_length, *lefts, smem=(0,)
    )
    for step, part in zip(row_steps, parts):
        part = swap(part, "row", step)
        if step != row_steps[-1]:
            (total,) = call(add_kernel, (wide,), total, part, flops=wait)
    tri_normed, tri_grad = call(
        triangle_kernel, (flat, tile), total, part, upstream, flops=20 * pairs * channels,
    )
    grads = gather(tri_grad, "row", gather_steps)
    update, partial = call(
        update_kernel, (tile, flat), tri_normed, out_open, gate_factor, in_weights, out_weight,
        flops=4 * pairs * channels * channels,
    )
    (right_grad,) = call(functools.partial(right_grad_kernel, [0]), (wide,), left_panel, tri_grad)
    terms, before = [None] * n, (partial, right_grad)
    for step, grad in zip([0] + gather_steps, grads):
        before = call(
            left_terms_kernel, (wide,), grad, right, *before,
            scratch=[pltpu.VMEM((pairs, channels), f32)], flops=work,
        )
        terms[step] = before[0]
    total, *terms = call(
        functools.partial(pick_kernel, [0] + steps), (wide,) + (tile,) * (n - 1), *terms, flops=pairs * channels,
    )
    for step, term in zip(steps, terms):
        term = swap(term, "col", step)
        if step != steps[-1]:
            (total,) = call(add_kernel, (wide,), total, term, flops=wait)
    (share,) = call(
        functools.partial(right_back_kernel, gather_steps), (flat,),
        left_panel, *grads[1:], right_grad, factors, in_weights, partial,
        scratch=[pltpu.VMEM(wide.shape, f32)],
    )
    (pair_grad,) = call(
        back_kernel, (tile,), total, term, normed, scale, factors, share, in_weights,
        flops=2 * pairs * channels * 2 * channels,
    )
    return (update, pair_grad)


def solution(mesh):
    return jax.shard_map(
        local,
        mesh=mesh,
        in_specs=(
            P(("group", "row"), "col", None),
            P(("group", "row"), "col"),
            P("group"),
            P(("group", "row"), "col", None),
            P(),
            P(),
        ),
        out_specs=(P(("group", "row"), "col", None), P(("group", "row"), "col", None)),
        check_vma=False,
    )
```

```python
import functools

import jax
import jax.numpy as jnp
from jax import lax
from jax.experimental import pallas as pl
from jax.experimental.pallas import tpu as pltpu
from jax.sharding import PartitionSpec as P

epsilon = 1e-05
f32 = jnp.float32
bf16 = jnp.bfloat16


def mean_lanes(values):
    return jnp.sum(values, axis=-1, keepdims=True) * (1.0 / values.shape[-1])


def normalize(values):
    center = values - mean_lanes(values)
    variance = mean_lanes(center * center)
    scale = lax.rsqrt(variance + epsilon)
    return (center * scale, scale)


def normalize_back(normed, scale, upstream):
    average = mean_lanes(upstream)
    project = mean_lanes(upstream * normed)
    return scale * (upstream - average - normed * project)


def sigmoid(values):
    return 1.0 / (1.0 + jnp.exp(-values))


def dot(a, b):
    return jnp.dot(a, b, preferred_element_type=f32)


def dot_t(a, b):
    return lax.dot_general(a, b, (((1,), (1,)), ((), ())), preferred_element_type=f32)


def live_pairs(crop_ref, row, col, shape):
    rows = row * shape[0] + lax.broadcasted_iota(jnp.int32, shape, 0)
    cols = col * shape[1] + lax.broadcasted_iota(jnp.int32, shape, 1)
    return jnp.where(jnp.maximum(rows, cols) < crop_ref[0], 1.0, 0.0)


def spread(mask, channels):
    size = mask.shape[0]
    pair = lax.broadcasted_iota(jnp.int32, (size * size, size), 0)
    lane = lax.broadcasted_iota(jnp.int32, (size * size, size), 1)
    pick_row = jnp.where(pair // size == lane, 1.0, 0.0).astype(bf16)
    pick_col = jnp.where(pair % size == lane, 1.0, 0.0)
    picked = (dot(pick_row, mask.astype(bf16)) * pick_col).astype(bf16)
    return dot(picked, jnp.ones((size, channels), bf16))


def start_copies(sems, *pairs):
    copies = [pltpu.make_async_copy(src, dst, sems.at[n]) for n, (src, dst) in enumerate(pairs)]
    for copy in copies:
        copy.start()
    return copies


def gated(projected, block, keep):
    channels = keep.shape[1]
    value = projected[:, block * channels : (block + 1) * channels]
    opened = sigmoid(projected[:, (block + 1) * channels : (block + 2) * channels])
    return (opened * value * keep).astype(bf16), opened, value


def left_kernel(acts_in, mask_in, weights_in, left_ref, acts_ref, mask_ref, weights_ref, sems):
    size, _, channels = acts_ref.shape
    copies = start_copies(
        sems, (acts_in, acts_ref), (weights_in.at[:, pl.ds(0, 2 * channels)], weights_ref), (mask_in, mask_ref),
    )
    copies[0].wait()
    normed, _ = normalize(acts_ref[...].astype(f32).reshape(size * size, channels))
    normed = normed.astype(bf16)
    for copy in copies[1:]:
        copy.wait()
    left, _, _ = gated(dot(normed, weights_ref[...]), 0, spread(mask_ref[...].astype(f32), channels))
    left_ref[...] = left.reshape(size, size, channels)


def factors_kernel(
    acts_in, mask_in, crop_ref, cotangent_in, weights_in, out_weight_in,
    right_ref, normed_ref, scale_ref, factor_ref, open_ref, gate_factor_ref, upstream_ref,
    acts_ref, mask_ref, cotangent_ref, weights_ref, out_weight_ref, sems,
):
    copies = start_copies(
        sems, (acts_in, acts_ref), (weights_in, weights_ref), (mask_in, mask_ref),
        (cotangent_in, cotangent_ref), (out_weight_in, out_weight_ref),
    )
    size, _, channels = acts_ref.shape
    pairs = size * size
    copies[0].wait()
    normed, scale = normalize(acts_ref[...].astype(f32).reshape(pairs, channels))
    normed_ref[...] = normed
    scale_ref[...] = jnp.broadcast_to(scale, (pairs, channels))
    for copy in copies[1:]:
        copy.wait()
    projected = dot(normed.astype(bf16), weights_ref[...])
    live = live_pairs(crop_ref, lax.axis_index("row"), lax.axis_index("col"), (size, size))
    keep = spread(mask_ref[...].astype(f32) * live, channels)
    for block in (0, 2):
        tile, opened, value = gated(projected, block, keep)
        factor_ref[block] = keep * opened
        factor_ref[block + 1] = keep * value * opened * (1.0 - opened)
    right_ref[...] = tile.astype(f32).reshape(size, size, channels)
    out_open = sigmoid(projected[:, 4 * channels :])
    cotangent = cotangent_ref[...].astype(f32).reshape(pairs, channels)
    lin_grad = (cotangent * out_open).astype(bf16)
    open_ref[...] = out_open
    gate_factor_ref[...] = cotangent * out_open * (1.0 - out_open)
    upstream_ref[...] = dot_t(lin_grad, out_weight_ref[...])


def weighted_sums(weights, start, terms, out, base=None):
    def step(k, _):
        total = weights[start + k, pl.ds(0, 1), :] * terms[0]
        for n in range(1, len(terms)):
            total = total + weights[start + k, pl.ds(n, 1), :] * terms[n]
        if base is not None:
            total = total + base[k]
        out[k] = total.astype(out.dtype)
        return 0

    lax.fori_loop(0, out.shape[0], step, 0, unroll=4)


def left_panel_kernel(steps, crop_ref, *refs):
    row, col, panel = lax.axis_index("row"), lax.axis_index("col"), refs[-1]
    size, _, channels = refs[0].shape
    rows = row * size + lax.broadcasted_iota(jnp.int32, (size, 1, channels), 0)
    row_live = jnp.where(rows < crop_ref[0], 1.0, 0.0)
    for step, ref in zip(steps, refs):
        place = col ^ step
        cols = place * size + lax.broadcasted_iota(jnp.int32, (1, size, channels), 1)
        col_live = jnp.where(cols < crop_ref[0], 1.0, 0.0)
        panel[pl.ds(place * size, size)] = ref[...].astype(f32) * (row_live * col_live)


def partial_kernel(steps, crop_ref, *refs):
    count = len(steps)
    lefts, right_ref, outs, left = refs[:count], refs[count], refs[count + 1 : -1], refs[-1]
    size, _, channels = right_ref.shape
    rows = lax.axis_index("row") * size + lax.broadcasted_iota(jnp.int32, (size, 1, channels), 0)
    row_live = jnp.where(rows < crop_ref[0], 1.0, 0.0)
    for step, left_ref, out in zip(steps, lefts, outs):
        cols = (lax.axis_index("col") ^ step) * size + lax.broadcasted_iota(jnp.int32, (1, size, channels), 1)
        left[...] = left_ref[...].astype(f32) * (row_live * jnp.where(cols < crop_ref[0], 1.0, 0.0))

        def add(k, sums):
            other = right_ref[k]
            return tuple(sums[i] + left[k, pl.ds(i, 1), :] * other for i in range(size))

        zero = jnp.zeros((size, channels), f32)
        sums = lax.fori_loop(0, size, add, (zero,) * size, unroll=4)
        for i in range(size):
            out[i] = sums[i]


def pick_kernel(steps, *refs):
    here = lax.axis_index("row") ^ lax.axis_index("col")
    tiles, outs = refs[: len(steps)], refs[len(steps) :]
    for step, out in zip(steps, outs):
        for other, tile in enumerate(tiles):

            @pl.when((here ^ step) == other)
            def _():
                out[...] = tile[...].astype(out.dtype)


def triangle_kernel(base, tile_ref, upstream_ref, tri_normed_ref, grad_ref):
    size = grad_ref.shape[0]
    for i in range(size):
        here = pl.ds(i * size, size)
        tri_normed, scale = normalize(base[i] + tile_ref[i].astype(f32))
        tri_normed_ref[here, :] = tri_normed
        grad_ref[i] = normalize_back(tri_normed, scale, upstream_ref[here, :]).astype(bf16)


def left_terms_kernel(grad_ref, right, *refs):
    out, grad = refs[-2:]
    size, _, channels = out.shape
    grad[...] = grad_ref[...].astype(f32).reshape(size * size, channels)
    weighted_sums(right, 0, [grad[pl.ds(j, size, stride=size), :] for j in range(size)], out)


def right_grad_kernel(steps, panel, *refs):
    out, base = refs[-1], refs[len(steps)] if len(refs) > len(steps) + 1 else None
    size = out.shape[0]
    for step, grad in zip(steps, refs):
        start = (lax.axis_index("row") ^ step) * size
        weighted_sums(panel, start, [grad[i].astype(f32) for i in range(size)], out, base)
        base = out


def right_back_kernel(steps, panel, *refs):
    factor_ref, weights_ref, share_ref, out, right_ref = refs[-5:]
    right_grad_kernel(steps, panel, *refs[: len(steps) + 1], right_ref)
    pairs, channels = out.shape
    right = right_ref[...].reshape(pairs, channels)
    grads = jnp.concatenate([(right * factor_ref[block]).astype(bf16) for block in (2, 3)], axis=1)
    out[...] = share_ref[...] + dot_t(grads, weights_ref[:, 2 * channels : 4 * channels])


def add_kernel(base, tile_ref, out):
    out[...] = base[...] + tile_ref[...].astype(f32)


def update_kernel(
    tri_normed_ref, open_ref, gate_factor_ref, weights_ref, out_weight_ref, update_ref, normed_grad_ref
):
    size, _, channels = update_ref.shape
    linear = dot(tri_normed_ref[...].astype(bf16), out_weight_ref[...])
    update = (open_ref[...] * linear).astype(bf16)
    update_ref[...] = update.reshape(size, size, channels)
    out_gate_grad = (gate_factor_ref[...] * linear).astype(bf16)
    normed_grad_ref[...] = dot_t(out_gate_grad, weights_ref[:, 4 * channels :])


def back_kernel(base, *refs):
    *tiles, normed_ref, scale_ref, factor_ref, share_ref, weights_ref, out = refs
    size, _, channels = out.shape
    pairs = size * size
    left = base[...]
    for ref in tiles:
        left = left + ref[...].astype(f32)
    left = left.reshape(pairs, channels)
    grads = jnp.concatenate([(left * factor_ref[block]).astype(bf16) for block in (0, 1)], axis=1)
    normed_grad = share_ref[...] + dot_t(grads, weights_ref[:, : 2 * channels])
    back = normalize_back(normed_ref[...], scale_ref[...], normed_grad)
    out[...] = back.astype(bf16).reshape(size, size, channels)


def call(kernel, outs, *args, scratch=(), flops=0, smem=(), hbm=()):
    spec = pl.BlockSpec(memory_space=pltpu.VMEM)
    total = sum(a.size * a.dtype.itemsize for a in (*args, *outs))
    specs = [spec] * len(args)
    for n in smem:
        specs[n] = pl.BlockSpec(memory_space=pltpu.SMEM)
    args = list(args)
    for n in hbm:
        specs[n] = pl.BlockSpec(memory_space=pltpu.HBM)
        args[n] = pltpu.with_memory_space_constraint(args[n], pltpu.HBM)
    return pl.pallas_call(
        kernel,
        out_shape=tuple(outs),
        in_specs=specs,
        out_specs=(spec,) * len(outs),
        scratch_shapes=scratch,
        compiler_params=pltpu.CompilerParams(vmem_limit_bytes=24 * 2**20),
        cost_estimate=pl.CostEstimate(flops=flops, bytes_accessed=total if flops else 0, transcendentals=0),
    )(*args)


def local(pair_acts, pair_mask, crop_length, cotangent, in_weights, out_weight):
    size, _, channels = pair_acts.shape
    pairs = size * size
    n = lax.axis_size("row")
    tile = jax.ShapeDtypeStruct((size, size, channels), bf16)
    flat = jax.ShapeDtypeStruct((pairs, channels), f32)

    wide = jax.ShapeDtypeStruct((size, size, channels), f32)
    panel = jax.ShapeDtypeStruct((n * size, size, channels), f32)
    work = 2 * size * pairs * channels
    wait = 2**31
    steps = [step for bit in range(n.bit_length() - 2, -1, -1) for step in range(2**bit, 2 ** (bit + 1))]
    row_steps = list(range(n - 1, 0, -1))
    gather_steps = steps


    def swap(values, axis, step):
        return lax.ppermute(values, axis, [(a, a ^ step) for a in range(n)])

    def gather(values, axis, steps):
        return [values] + [swap(values, axis, step) for step in steps]

    (left,) = call(
        left_kernel, (tile,), pair_acts, pair_mask, in_weights,
        hbm=(0, 1, 2), flops=2 * pairs * channels * 2 * channels,
        scratch=[
            pltpu.VMEM(pair_acts.shape, bf16),
            pltpu.VMEM(pair_mask.shape, jnp.int32),
            pltpu.VMEM((channels, 2 * channels), bf16),
            pltpu.SemaphoreType.DMA((3,)),
        ],
    )
    lefts = gather(left, "col", steps)
    right, normed, scale, factors, out_open, gate_factor, upstream = call(
        factors_kernel,
        (wide, flat, flat, jax.ShapeDtypeStruct((4, pairs, channels), f32), flat, flat, flat),
        pair_acts, pair_mask, crop_length, cotangent, in_weights, out_weight,
        smem=(2,), hbm=(0, 1, 3, 4, 5), flops=2 * pairs * channels * 6 * channels,
        scratch=[
            pltpu.VMEM(pair_acts.shape, bf16),
            pltpu.VMEM(pair_mask.shape, jnp.int32),
            pltpu.VMEM(cotangent.shape, bf16),
            pltpu.VMEM(in_weights.shape, bf16),
            pltpu.VMEM(out_weight.shape, bf16),
            pltpu.SemaphoreType.DMA((5,)),
        ],
    )
    parts = []
    order = [0] + steps
    for group in [[at] for at in range(n - 2)] + [[n - 2, n - 1]]:
        parts += call(
            functools.partial(partial_kernel, [order[at] for at in group]), (wide,) * len(group),
            crop_length, *(lefts[at] for at in group), right, smem=(0,), flops=work,
            scratch=[pltpu.VMEM(wide.shape, f32)],
        )
    parts = [part for _, part in sorted(zip(order, parts), key=lambda each: each[0])]
    total, *parts = call(
        functools.partial(pick_kernel, [0] + row_steps), (wide,) + (tile,) * (n - 1), *parts,
        flops=pairs * channels,
    )
    (left_panel,) = call(
        functools.partial(left_panel_kernel, [0] + steps), (panel,), crop_length, *lefts, smem=(0,)
    )
    for step, part in zip(row_steps, parts):
        part = swap(part, "row", step)
        if step != row_steps[-1]:
            (total,) = call(add_kernel, (wide,), total, part, flops=wait)
    tri_normed, tri_grad = call(
        triangle_kernel, (flat, tile), total, part, upstream, flops=20 * pairs * channels,
    )
    grads = gather(tri_grad, "row", gather_steps)
    update, partial = call(
        update_kernel, (tile, flat), tri_normed, out_open, gate_factor, in_weights, out_weight,
        flops=4 * pairs * channels * channels,
    )
    (right_grad,) = call(functools.partial(right_grad_kernel, [0]), (wide,), left_panel, tri_grad)
    terms, before = [None] * n, (partial, right_grad)
    for step, grad in zip([0] + gather_steps, grads):
        before = call(
            left_terms_kernel, (wide,), grad, right, *before,
            scratch=[pltpu.VMEM((pairs, channels), f32)], flops=work,
        )
        terms[step] = before[0]
    total, *terms = call(
        functools.partial(pick_kernel, [0] + steps), (wide,) + (tile,) * (n - 1), *terms, flops=pairs * channels,
    )
    for step, term in zip(steps, terms):
        term = swap(term, "col", step)
        if step != steps[-1]:
            (total,) = call(add_kernel, (wide,), total, term, flops=wait)
    (share,) = call(
        functools.partial(right_back_kernel, gather_steps), (flat,),
        left_panel, *grads[1:], right_grad, factors, in_weights, partial,
        scratch=[pltpu.VMEM(wide.shape, f32)],
    )
    (pair_grad,) = call(
        back_kernel, (tile,), total, term, normed, scale, factors, share, in_weights,
        flops=2 * pairs * channels * 2 * channels,
    )
    return (update, pair_grad)


def solution(mesh):
    return jax.shard_map(
        local,
        mesh=mesh,
        in_specs=(
            P(("group", "row"), "col", None),
            P(("group", "row"), "col"),
            P("group"),
            P(("group", "row"), "col", None),
            P(),
            P(),
        ),
        out_specs=(P(("group", "row"), "col", None), P(("group", "row"), "col", None)),
        check_vma=False,
    )
```

```python
import functools

import jax
import jax.numpy as jnp
from jax import lax
from jax.experimental import pallas as pl
from jax.experimental.pallas import tpu as pltpu
from jax.sharding import PartitionSpec as P

epsilon = 1e-05
f32 = jnp.float32
bf16 = jnp.bfloat16


def mean_lanes(values):
    return jnp.sum(values, axis=-1, keepdims=True) * (1.0 / values.shape[-1])


def normalize(values):
    center = values - mean_lanes(values)
    variance = mean_lanes(center * center)
    scale = lax.rsqrt(variance + epsilon)
    return (center * scale, scale)


def normalize_back(normed, scale, upstream):
    average = mean_lanes(upstream)
    project = mean_lanes(upstream * normed)
    return scale * (upstream - average - normed * project)


def sigmoid(values):
    return 1.0 / (1.0 + jnp.exp(-values))


def dot(a, b):
    return jnp.dot(a, b, preferred_element_type=f32)


def dot_t(a, b):
    return lax.dot_general(a, b, (((1,), (1,)), ((), ())), preferred_element_type=f32)


def live_pairs(crop_ref, row, col, shape):
    rows = row * shape[0] + lax.broadcasted_iota(jnp.int32, shape, 0)
    cols = col * shape[1] + lax.broadcasted_iota(jnp.int32, shape, 1)
    return jnp.where(jnp.maximum(rows, cols) < crop_ref[0], 1.0, 0.0)


def spread(mask, channels):
    size = mask.shape[0]
    pair = lax.broadcasted_iota(jnp.int32, (size * size, size), 0)
    lane = lax.broadcasted_iota(jnp.int32, (size * size, size), 1)
    pick_row = jnp.where(pair // size == lane, 1.0, 0.0).astype(bf16)
    pick_col = jnp.where(pair % size == lane, 1.0, 0.0)
    picked = (dot(pick_row, mask.astype(bf16)) * pick_col).astype(bf16)
    return dot(picked, jnp.ones((size, channels), bf16))


def start_copies(sems, *pairs):
    copies = [pltpu.make_async_copy(src, dst, sems.at[n]) for n, (src, dst) in enumerate(pairs)]
    for copy in copies:
        copy.start()
    return copies


def gated(projected, block, keep):
    channels = keep.shape[1]
    value = projected[:, block * channels : (block + 1) * channels]
    opened = sigmoid(projected[:, (block + 1) * channels : (block + 2) * channels])
    return (opened * value * keep).astype(bf16), opened, value


def left_kernel(acts_in, mask_in, weights_in, left_ref, acts_ref, mask_ref, weights_ref, sems):
    size, _, channels = acts_ref.shape
    copies = start_copies(
        sems, (acts_in, acts_ref), (weights_in.at[:, pl.ds(0, 2 * channels)], weights_ref), (mask_in, mask_ref),
    )
    copies[0].wait()
    normed, _ = normalize(acts_ref[...].astype(f32).reshape(size * size, channels))
    normed = normed.astype(bf16)
    for copy in copies[1:]:
        copy.wait()
    left, _, _ = gated(dot(normed, weights_ref[...]), 0, spread(mask_ref[...].astype(f32), channels))
    left_ref[...] = left.reshape(size, size, channels)


def factors_kernel(
    acts_in, mask_in, crop_ref, cotangent_in, weights_in, out_weight_in,
    right_ref, normed_ref, scale_ref, factor_ref, open_ref, gate_factor_ref, upstream_ref,
    acts_ref, mask_ref, cotangent_ref, weights_ref, out_weight_ref, sems,
):
    copies = start_copies(
        sems, (acts_in, acts_ref), (weights_in, weights_ref), (mask_in, mask_ref),
        (cotangent_in, cotangent_ref), (out_weight_in, out_weight_ref),
    )
    size, _, channels = acts_ref.shape
    pairs = size * size
    copies[0].wait()
    normed, scale = normalize(acts_ref[...].astype(f32).reshape(pairs, channels))
    normed_ref[...] = normed
    scale_ref[...] = jnp.broadcast_to(scale, (pairs, channels))
    for copy in copies[1:]:
        copy.wait()
    projected = dot(normed.astype(bf16), weights_ref[...])
    live = live_pairs(crop_ref, lax.axis_index("row"), lax.axis_index("col"), (size, size))
    keep = spread(mask_ref[...].astype(f32) * live, channels)
    for block in (0, 2):
        tile, opened, value = gated(projected, block, keep)
        factor_ref[block] = keep * opened
        factor_ref[block + 1] = keep * value * opened * (1.0 - opened)
    right_ref[...] = tile.astype(f32).reshape(size, size, channels)
    out_open = sigmoid(projected[:, 4 * channels :])
    cotangent = cotangent_ref[...].astype(f32).reshape(pairs, channels)
    lin_grad = (cotangent * out_open).astype(bf16)
    open_ref[...] = out_open
    gate_factor_ref[...] = cotangent * out_open * (1.0 - out_open)
    upstream_ref[...] = dot_t(lin_grad, out_weight_ref[...])


def weighted_sums(weights, start, terms, out, base=None):
    def step(k, _):
        total = weights[start + k, pl.ds(0, 1), :] * terms[0]
        for n in range(1, len(terms)):
            total = total + weights[start + k, pl.ds(n, 1), :] * terms[n]
        if base is not None:
            total = total + base[k]
        out[k] = total.astype(out.dtype)
        return 0

    lax.fori_loop(0, out.shape[0], step, 0, unroll=4)


def left_panel_kernel(steps, crop_ref, *refs):
    row, col, panel = lax.axis_index("row"), lax.axis_index("col"), refs[-1]
    size, _, channels = refs[0].shape
    rows = row * size + lax.broadcasted_iota(jnp.int32, (size, 1, channels), 0)
    row_live = jnp.where(rows < crop_ref[0], 1.0, 0.0)
    for step, ref in zip(steps, refs):
        place = col ^ step
        cols = place * size + lax.broadcasted_iota(jnp.int32, (1, size, channels), 1)
        col_live = jnp.where(cols < crop_ref[0], 1.0, 0.0)
        panel[pl.ds(place * size, size)] = ref[...].astype(f32) * (row_live * col_live)


def partial_kernel(steps, crop_ref, *refs):
    count = len(steps)
    lefts, right_ref, outs, left = refs[:count], refs[count], refs[count + 1 : -1], refs[-1]
    size, _, channels = right_ref.shape
    rows = lax.axis_index("row") * size + lax.broadcasted_iota(jnp.int32, (size, 1, channels), 0)
    row_live = jnp.where(rows < crop_ref[0], 1.0, 0.0)
    for step, left_ref, out in zip(steps, lefts, outs):
        cols = (lax.axis_index("col") ^ step) * size + lax.broadcasted_iota(jnp.int32, (1, size, channels), 1)
        left[...] = left_ref[...].astype(f32) * (row_live * jnp.where(cols < crop_ref[0], 1.0, 0.0))

        def add(k, sums):
            other = right_ref[k]
            return tuple(sums[i] + left[k, pl.ds(i, 1), :] * other for i in range(size))

        zero = jnp.zeros((size, channels), f32)
        sums = lax.fori_loop(0, size, add, (zero,) * size, unroll=4)
        for i in range(size):
            out[i] = sums[i]


def pick_kernel(steps, *refs):
    here = lax.axis_index("row") ^ lax.axis_index("col")
    tiles, outs = refs[: len(steps)], refs[len(steps) :]
    for step, out in zip(steps, outs):
        for other, tile in enumerate(tiles):

            @pl.when((here ^ step) == other)
            def _():
                out[...] = tile[...].astype(out.dtype)


def triangle_kernel(base, tile_ref, upstream_ref, tri_normed_ref, grad_ref):
    size = grad_ref.shape[0]
    for i in range(size):
        here = pl.ds(i * size, size)
        tri_normed, scale = normalize(base[i] + tile_ref[i].astype(f32))
        tri_normed_ref[here, :] = tri_normed
        grad_ref[i] = normalize_back(tri_normed, scale, upstream_ref[here, :]).astype(bf16)


def left_terms_kernel(grad_ref, right, *refs):
    out, grad = refs[-2:]
    size, _, channels = out.shape
    grad[...] = grad_ref[...].astype(f32).reshape(size * size, channels)
    weighted_sums(right, 0, [grad[pl.ds(j, size, stride=size), :] for j in range(size)], out)


def right_grad_kernel(steps, panel, *refs):
    out, base = refs[-1], refs[len(steps)] if len(refs) > len(steps) + 1 else None
    size = out.shape[0]
    for step, grad in zip(steps, refs):
        start = (lax.axis_index("row") ^ step) * size
        weighted_sums(panel, start, [grad[i].astype(f32) for i in range(size)], out, base)
        base = out


def right_back_kernel(steps, panel, *refs):
    factor_ref, weights_ref, share_ref, out, right_ref = refs[-5:]
    right_grad_kernel(steps, panel, *refs[: len(steps) + 1], right_ref)
    pairs, channels = out.shape
    right = right_ref[...].reshape(pairs, channels)
    grads = jnp.concatenate([(right * factor_ref[block]).astype(bf16) for block in (2, 3)], axis=1)
    out[...] = share_ref[...] + dot_t(grads, weights_ref[:, 2 * channels : 4 * channels])


def add_kernel(base, tile_ref, out):
    out[...] = base[...] + tile_ref[...].astype(f32)


def update_kernel(
    tri_normed_ref, open_ref, gate_factor_ref, weights_ref, out_weight_ref, update_ref, normed_grad_ref
):
    size, _, channels = update_ref.shape
    linear = dot(tri_normed_ref[...].astype(bf16), out_weight_ref[...])
    update = (open_ref[...] * linear).astype(bf16)
    update_ref[...] = update.reshape(size, size, channels)
    out_gate_grad = (gate_factor_ref[...] * linear).astype(bf16)
    normed_grad_ref[...] = dot_t(out_gate_grad, weights_ref[:, 4 * channels :])


def back_kernel(base, *refs):
    *tiles, normed_ref, scale_ref, factor_ref, share_ref, weights_ref, out = refs
    size, _, channels = out.shape
    pairs = size * size
    left = base[...]
    for ref in tiles:
        left = left + ref[...].astype(f32)
    left = left.reshape(pairs, channels)
    grads = jnp.concatenate([(left * factor_ref[block]).astype(bf16) for block in (0, 1)], axis=1)
    normed_grad = share_ref[...] + dot_t(grads, weights_ref[:, : 2 * channels])
    back = normalize_back(normed_ref[...], scale_ref[...], normed_grad)
    out[...] = back.astype(bf16).reshape(size, size, channels)


def call(kernel, outs, *args, scratch=(), flops=0, smem=(), hbm=()):
    spec = pl.BlockSpec(memory_space=pltpu.VMEM)
    total = sum(a.size * a.dtype.itemsize for a in (*args, *outs))
    specs = [spec] * len(args)
    for n in smem:
        specs[n] = pl.BlockSpec(memory_space=pltpu.SMEM)
    args = list(args)
    for n in hbm:
        specs[n] = pl.BlockSpec(memory_space=pltpu.HBM)
        args[n] = pltpu.with_memory_space_constraint(args[n], pltpu.HBM)
    return pl.pallas_call(
        kernel,
        out_shape=tuple(outs),
        in_specs=specs,
        out_specs=(spec,) * len(outs),
        scratch_shapes=scratch,
        compiler_params=pltpu.CompilerParams(vmem_limit_bytes=24 * 2**20),
        cost_estimate=pl.CostEstimate(flops=flops, bytes_accessed=total if flops else 0, transcendentals=0),
    )(*args)


def local(pair_acts, pair_mask, crop_length, cotangent, in_weights, out_weight):
    size, _, channels = pair_acts.shape
    pairs = size * size
    n = lax.axis_size("row")
    tile = jax.ShapeDtypeStruct((size, size, channels), bf16)
    flat = jax.ShapeDtypeStruct((pairs, channels), f32)

    wide = jax.ShapeDtypeStruct((size, size, channels), f32)
    panel = jax.ShapeDtypeStruct((n * size, size, channels), f32)
    work = 2 * size * pairs * channels
    wait = 2**31
    steps = [step for bit in range(n.bit_length() - 2, -1, -1) for step in range(2**bit, 2 ** (bit + 1))]
    row_steps = steps
    gather_steps = [n - 1] + list(range(1, n - 1))


    def swap(values, axis, step):
        return lax.ppermute(values, axis, [(a, a ^ step) for a in range(n)])

    def gather(values, axis, steps):
        return [values] + [swap(values, axis, step) for step in steps]

    (left,) = call(
        left_kernel, (tile,), pair_acts, pair_mask, in_weights,
        hbm=(0, 1, 2), flops=2 * pairs * channels * 2 * channels,
        scratch=[
            pltpu.VMEM(pair_acts.shape, bf16),
            pltpu.VMEM(pair_mask.shape, jnp.int32),
            pltpu.VMEM((channels, 2 * channels), bf16),
            pltpu.SemaphoreType.DMA((3,)),
        ],
    )
    lefts = gather(left, "col", steps)
    right, normed, scale, factors, out_open, gate_factor, upstream = call(
        factors_kernel,
        (wide, flat, flat, jax.ShapeDtypeStruct((4, pairs, channels), f32), flat, flat, flat),
        pair_acts, pair_mask, crop_length, cotangent, in_weights, out_weight,
        smem=(2,), hbm=(0, 1, 3, 4, 5), flops=2 * pairs * channels * 6 * channels,
        scratch=[
            pltpu.VMEM(pair_acts.shape, bf16),
            pltpu.VMEM(pair_mask.shape, jnp.int32),
            pltpu.VMEM(cotangent.shape, bf16),
            pltpu.VMEM(in_weights.shape, bf16),
            pltpu.VMEM(out_weight.shape, bf16),
            pltpu.SemaphoreType.DMA((5,)),
        ],
    )
    parts = []
    order = [0] + steps
    for group in [[at] for at in range(n - 2)] + [[n - 2, n - 1]]:
        parts += call(
            functools.partial(partial_kernel, [order[at] for at in group]), (wide,) * len(group),
            crop_length, *(lefts[at] for at in group), right, smem=(0,), flops=work,
            scratch=[pltpu.VMEM(wide.shape, f32)],
        )
    parts = [part for _, part in sorted(zip(order, parts), key=lambda each: each[0])]
    total, *parts = call(
        functools.partial(pick_kernel, [0] + row_steps), (wide,) + (tile,) * (n - 1), *parts,
        flops=pairs * channels,
    )
    (left_panel,) = call(
        functools.partial(left_panel_kernel, [0] + steps), (panel,), crop_length, *lefts, smem=(0,)
    )
    for step, part in zip(row_steps, parts):
        part = swap(part, "row", step)
        if step != row_steps[-1]:
            (total,) = call(add_kernel, (wide,), total, part, flops=wait)
    tri_normed, tri_grad = call(
        triangle_kernel, (flat, tile), total, part, upstream, flops=20 * pairs * channels,
    )
    grads = gather(tri_grad, "row", gather_steps)
    update, partial = call(
        update_kernel, (tile, flat), tri_normed, out_open, gate_factor, in_weights, out_weight,
        flops=4 * pairs * channels * channels,
    )
    (right_grad,) = call(functools.partial(right_grad_kernel, [0]), (wide,), left_panel, tri_grad)
    terms, before = [None] * n, (partial, right_grad)
    for step, grad in zip([0] + gather_steps, grads):
        before = call(
            left_terms_kernel, (wide,), grad, right, *before,
            scratch=[pltpu.VMEM((pairs, channels), f32)], flops=work,
        )
        terms[step] = before[0]
    total, *terms = call(
        functools.partial(pick_kernel, [0] + steps), (wide,) + (tile,) * (n - 1), *terms, flops=pairs * channels,
    )
    for step, term in zip(steps, terms):
        term = swap(term, "col", step)
        if step != steps[-1]:
            (total,) = call(add_kernel, (wide,), total, term, flops=wait)
    (share,) = call(
        functools.partial(right_back_kernel, gather_steps), (flat,),
        left_panel, *grads[1:], right_grad, factors, in_weights, partial,
        scratch=[pltpu.VMEM(wide.shape, f32)],
    )
    (pair_grad,) = call(
        back_kernel, (tile,), total, term, normed, scale, factors, share, in_weights,
        flops=2 * pairs * channels * 2 * channels,
    )
    return (update, pair_grad)


def solution(mesh):
    return jax.shard_map(
        local,
        mesh=mesh,
        in_specs=(
            P(("group", "row"), "col", None),
            P(("group", "row"), "col"),
            P("group"),
            P(("group", "row"), "col", None),
            P(),
            P(),
        ),
        out_specs=(P(("group", "row"), "col", None), P(("group", "row"), "col", None)),
        check_vma=False,
    )
```

```python
import functools

import jax
import jax.numpy as jnp
from jax import lax
from jax.experimental import pallas as pl
from jax.experimental.pallas import tpu as pltpu
from jax.sharding import PartitionSpec as P

epsilon = 1e-05
f32 = jnp.float32
bf16 = jnp.bfloat16


def mean_lanes(values):
    return jnp.sum(values, axis=-1, keepdims=True) * (1.0 / values.shape[-1])


def normalize(values):
    center = values - mean_lanes(values)
    variance = mean_lanes(center * center)
    scale = lax.rsqrt(variance + epsilon)
    return (center * scale, scale)


def normalize_back(normed, scale, upstream):
    average = mean_lanes(upstream)
    project = mean_lanes(upstream * normed)
    return scale * (upstream - average - normed * project)


def sigmoid(values):
    return 1.0 / (1.0 + jnp.exp(-values))


def dot(a, b):
    return jnp.dot(a, b, preferred_element_type=f32)


def dot_t(a, b):
    return lax.dot_general(a, b, (((1,), (1,)), ((), ())), preferred_element_type=f32)


def live_pairs(crop_ref, row, col, shape):
    rows = row * shape[0] + lax.broadcasted_iota(jnp.int32, shape, 0)
    cols = col * shape[1] + lax.broadcasted_iota(jnp.int32, shape, 1)
    return jnp.where(jnp.maximum(rows, cols) < crop_ref[0], 1.0, 0.0)


def spread(mask, channels):
    size = mask.shape[0]
    shape = (size, size, size)
    diagonal = lax.broadcasted_iota(jnp.int32, shape, 1) == lax.broadcasted_iota(jnp.int32, shape, 2)
    picked = jnp.where(diagonal, jnp.broadcast_to(mask[:, None, :], shape), 0.0)
    rows = jnp.sum(picked, axis=-1, keepdims=True)
    return jnp.broadcast_to(rows, (size, size, channels)).reshape(size * size, channels)


def start_copies(sems, *pairs):
    copies = [pltpu.make_async_copy(src, dst, sems.at[n]) for n, (src, dst) in enumerate(pairs)]
    for copy in copies:
        copy.start()
    return copies


def gated(projected, block, keep):
    channels = keep.shape[1]
    value = projected[:, block * channels : (block + 1) * channels]
    opened = sigmoid(projected[:, (block + 1) * channels : (block + 2) * channels])
    return (opened * value * keep).astype(bf16), opened, value


def left_kernel(acts_in, mask_in, weights_in, left_ref, acts_ref, mask_ref, weights_ref, sems):
    size, _, channels = acts_ref.shape
    copies = start_copies(
        sems, (acts_in, acts_ref), (weights_in.at[:, pl.ds(0, 2 * channels)], weights_ref), (mask_in, mask_ref),
    )
    copies[0].wait()
    normed, _ = normalize(acts_ref[...].astype(f32).reshape(size * size, channels))
    normed = normed.astype(bf16)
    for copy in copies[1:]:
        copy.wait()
    left, _, _ = gated(dot(normed, weights_ref[...]), 0, spread(mask_ref[...].astype(f32), channels))
    left_ref[...] = left.reshape(size, size, channels)


def factors_kernel(
    acts_in, mask_in, crop_ref, cotangent_in, weights_in, out_weight_in,
    right_ref, normed_ref, scale_ref, factor_ref, open_ref, gate_factor_ref, upstream_ref,
    acts_ref, mask_ref, cotangent_ref, weights_ref, out_weight_ref, sems,
):
    copies = start_copies(
        sems, (acts_in, acts_ref), (weights_in, weights_ref), (mask_in, mask_ref),
        (cotangent_in, cotangent_ref), (out_weight_in, out_weight_ref),
    )
    size, _, channels = acts_ref.shape
    pairs = size * size
    copies[0].wait()
    normed, scale = normalize(acts_ref[...].astype(f32).reshape(pairs, channels))
    normed_ref[...] = normed
    scale_ref[...] = jnp.broadcast_to(scale, (pairs, channels))
    for copy in copies[1:]:
        copy.wait()
    projected = dot(normed.astype(bf16), weights_ref[...])
    live = live_pairs(crop_ref, lax.axis_index("row"), lax.axis_index("col"), (size, size))
    keep = spread(mask_ref[...].astype(f32) * live, channels)
    for block in (0, 2):
        tile, opened, value = gated(projected, block, keep)
        factor_ref[block] = keep * opened
        factor_ref[block + 1] = keep * value * opened * (1.0 - opened)
    right_ref[...] = tile.astype(f32).reshape(size, size, channels)
    out_open = sigmoid(projected[:, 4 * channels :])
    cotangent = cotangent_ref[...].astype(f32).reshape(pairs, channels)
    lin_grad = (cotangent * out_open).astype(bf16)
    open_ref[...] = out_open
    gate_factor_ref[...] = cotangent * out_open * (1.0 - out_open)
    upstream_ref[...] = dot_t(lin_grad, out_weight_ref[...])


def weighted_sums(weights, start, terms, out, base=None):
    def step(k, _):
        total = weights[start + k, pl.ds(0, 1), :] * terms[0]
        for n in range(1, len(terms)):
            total = total + weights[start + k, pl.ds(n, 1), :] * terms[n]
        if base is not None:
            total = total + base[k]
        out[k] = total.astype(out.dtype)
        return 0

    lax.fori_loop(0, out.shape[0], step, 0, unroll=4)


def left_panel_kernel(steps, crop_ref, *refs):
    row, col, panel = lax.axis_index("row"), lax.axis_index("col"), refs[-1]
    size, _, channels = refs[0].shape
    rows = row * size + lax.broadcasted_iota(jnp.int32, (size, 1, channels), 0)
    row_live = jnp.where(rows < crop_ref[0], 1.0, 0.0)
    for step, ref in zip(steps, refs):
        place = col ^ step
        cols = place * size + lax.broadcasted_iota(jnp.int32, (1, size, channels), 1)
        col_live = jnp.where(cols < crop_ref[0], 1.0, 0.0)
        panel[pl.ds(place * size, size)] = ref[...].astype(f32) * (row_live * col_live)


def partial_kernel(steps, crop_ref, *refs):
    count = len(steps)
    lefts, right_ref, outs, left = refs[:count], refs[count], refs[count + 1 : -1], refs[-1]
    size, _, channels = right_ref.shape
    rows = lax.axis_index("row") * size + lax.broadcasted_iota(jnp.int32, (size, 1, channels), 0)
    row_live = jnp.where(rows < crop_ref[0], 1.0, 0.0)
    for step, left_ref, out in zip(steps, lefts, outs):
        cols = (lax.axis_index("col") ^ step) * size + lax.broadcasted_iota(jnp.int32, (1, size, channels), 1)
        left[...] = left_ref[...].astype(f32) * (row_live * jnp.where(cols < crop_ref[0], 1.0, 0.0))

        def add(k, sums):
            other = right_ref[k]
            return tuple(sums[i] + left[k, pl.ds(i, 1), :] * other for i in range(size))

        zero = jnp.zeros((size, channels), f32)
        sums = lax.fori_loop(0, size, add, (zero,) * size, unroll=4)
        for i in range(size):
            out[i] = sums[i]


def pick_kernel(steps, *refs):
    here = lax.axis_index("row") ^ lax.axis_index("col")
    tiles, outs = refs[: len(steps)], refs[len(steps) :]
    for step, out in zip(steps, outs):
        for other, tile in enumerate(tiles):

            @pl.when((here ^ step) == other)
            def _():
                out[...] = tile[...].astype(out.dtype)


def last_partial_kernel(steps, early, row_steps, crop_ref, *refs):
    count, known = len(steps), len(early)
    left, parts = refs[-2:]
    partial_kernel(steps, crop_ref, *refs[: count + 1], *(parts.at[at] for at in range(count)), left)
    tiles = dict(zip(early, refs[count + 1 : count + 1 + known]))
    tiles.update((step, parts.at[at]) for at, step in enumerate(steps))
    pick_kernel(row_steps, *(tiles[step] for step in range(count + known)), *refs[count + 1 + known : -2])


def triangle_kernel(base, tile_ref, upstream_ref, tri_normed_ref, grad_ref):
    size = grad_ref.shape[0]
    for i in range(size):
        here = pl.ds(i * size, size)
        tri_normed, scale = normalize(base[i] + tile_ref[i].astype(f32))
        tri_normed_ref[here, :] = tri_normed
        grad_ref[i] = normalize_back(tri_normed, scale, upstream_ref[here, :]).astype(bf16)


def left_terms_kernel(grad_ref, right, *refs):
    out, grad = refs[-2:]
    size, _, channels = out.shape
    grad[...] = grad_ref[...].astype(f32).reshape(size * size, channels)
    weighted_sums(right, 0, [grad[pl.ds(j, size, stride=size), :] for j in range(size)], out)


def last_terms_kernel(early, last, steps, grad_ref, right, *refs):
    known = len(early)
    term, grad = refs[-2:]
    left_terms_kernel(grad_ref, right, term, grad)
    tiles = dict(zip(early, refs[:known]))
    tiles[last] = term
    pick_kernel(steps, *(tiles[step] for step in range(known + 1)), *refs[known:-2])


def right_grad_kernel(steps, panel, *refs):
    out, base = refs[-1], refs[len(steps)] if len(refs) > len(steps) + 1 else None
    size = out.shape[0]
    for step, grad in zip(steps, refs):
        start = (lax.axis_index("row") ^ step) * size
        weighted_sums(panel, start, [grad[i].astype(f32) for i in range(size)], out, base)
        base = out


def right_back_kernel(steps, panel, *refs):
    factor_ref, weights_ref, share_ref, out, right_ref = refs[-5:]
    right_grad_kernel(steps, panel, *refs[: len(steps) + 1], right_ref)
    pairs, channels = out.shape
    right = right_ref[...].reshape(pairs, channels)
    grads = jnp.concatenate([(right * factor_ref[block]).astype(bf16) for block in (2, 3)], axis=1)
    out[...] = share_ref[...] + dot_t(grads, weights_ref[:, 2 * channels : 4 * channels])


def add_kernel(base, tile_ref, out):
    out[...] = base[...] + tile_ref[...].astype(f32)


def update_kernel(
    tri_normed_ref, open_ref, gate_factor_ref, weights_ref, out_weight_ref, update_ref, normed_grad_ref
):
    size, _, channels = update_ref.shape
    linear = dot(tri_normed_ref[...].astype(bf16), out_weight_ref[...])
    update = (open_ref[...] * linear).astype(bf16)
    update_ref[...] = update.reshape(size, size, channels)
    out_gate_grad = (gate_factor_ref[...] * linear).astype(bf16)
    normed_grad_ref[...] = dot_t(out_gate_grad, weights_ref[:, 4 * channels :])


def back_kernel(base, *refs):
    *tiles, normed_ref, scale_ref, factor_ref, share_ref, weights_ref, out = refs
    size, _, channels = out.shape
    pairs = size * size
    left = base[...]
    for ref in tiles:
        left = left + ref[...].astype(f32)
    left = left.reshape(pairs, channels)
    grads = jnp.concatenate([(left * factor_ref[block]).astype(bf16) for block in (0, 1)], axis=1)
    normed_grad = share_ref[...] + dot_t(grads, weights_ref[:, : 2 * channels])
    back = normalize_back(normed_ref[...], scale_ref[...], normed_grad)
    out[...] = back.astype(bf16).reshape(size, size, channels)


def call(kernel, outs, *args, scratch=(), flops=0, smem=(), hbm=()):
    spec = pl.BlockSpec(memory_space=pltpu.VMEM)
    total = sum(a.size * a.dtype.itemsize for a in (*args, *outs))
    specs = [spec] * len(args)
    for n in smem:
        specs[n] = pl.BlockSpec(memory_space=pltpu.SMEM)
    args = list(args)
    for n in hbm:
        specs[n] = pl.BlockSpec(memory_space=pltpu.HBM)
        args[n] = pltpu.with_memory_space_constraint(args[n], pltpu.HBM)
    return pl.pallas_call(
        kernel,
        out_shape=tuple(outs),
        in_specs=specs,
        out_specs=(spec,) * len(outs),
        scratch_shapes=scratch,
        compiler_params=pltpu.CompilerParams(vmem_limit_bytes=24 * 2**20),
        cost_estimate=pl.CostEstimate(flops=flops, bytes_accessed=total if flops else 0, transcendentals=0),
    )(*args)


def local(pair_acts, pair_mask, crop_length, cotangent, in_weights, out_weight):
    size, _, channels = pair_acts.shape
    pairs = size * size
    n = lax.axis_size("row")
    tile = jax.ShapeDtypeStruct((size, size, channels), bf16)
    flat = jax.ShapeDtypeStruct((pairs, channels), f32)

    wide = jax.ShapeDtypeStruct((size, size, channels), f32)
    panel = jax.ShapeDtypeStruct((n * size, size, channels), f32)
    work = 2 * size * pairs * channels
    wait = 2**31
    steps = [step for bit in range(n.bit_length() - 2, -1, -1) for step in range(2**bit, 2 ** (bit + 1))]
    row_steps = steps
    gather_steps = [n - 1] + list(range(1, n - 1))


    def swap(values, axis, step):
        return lax.ppermute(values, axis, [(a, a ^ step) for a in range(n)])

    def gather(values, axis, steps):
        return [values] + [swap(values, axis, step) for step in steps]

    (left,) = call(
        left_kernel, (tile,), pair_acts, pair_mask, in_weights,
        hbm=(0, 1, 2), flops=2 * pairs * channels * 2 * channels,
        scratch=[
            pltpu.VMEM(pair_acts.shape, bf16),
            pltpu.VMEM(pair_mask.shape, jnp.int32),
            pltpu.VMEM((channels, 2 * channels), bf16),
            pltpu.SemaphoreType.DMA((3,)),
        ],
    )
    lefts = gather(left, "col", steps)
    right, normed, scale, factors, out_open, gate_factor, upstream = call(
        factors_kernel,
        (wide, flat, flat, jax.ShapeDtypeStruct((4, pairs, channels), f32), flat, flat, flat),
        pair_acts, pair_mask, crop_length, cotangent, in_weights, out_weight,
        smem=(2,), hbm=(0, 1, 3, 4, 5), flops=2 * pairs * channels * 6 * channels,
        scratch=[
            pltpu.VMEM(pair_acts.shape, bf16),
            pltpu.VMEM(pair_mask.shape, jnp.int32),
            pltpu.VMEM(cotangent.shape, bf16),
            pltpu.VMEM(in_weights.shape, bf16),
            pltpu.VMEM(out_weight.shape, bf16),
            pltpu.SemaphoreType.DMA((5,)),
        ],
    )
    order = [0] + steps
    parts = [
        call(
            functools.partial(partial_kernel, [order[at]]), (wide,), crop_length, lefts[at], right, smem=(0,),
            flops=work, scratch=[pltpu.VMEM(wide.shape, f32)],
        )[0]
        for at in range(n - 2)
    ]
    total, *parts = call(
        functools.partial(last_partial_kernel, order[-2:], order[:-2], [0] + row_steps),
        (wide,) + (tile,) * (n - 1), crop_length, *lefts[-2:], right, *parts, smem=(0,), flops=work,
        scratch=[pltpu.VMEM(wide.shape, f32), pltpu.VMEM((2,) + wide.shape, f32)],
    )
    (left_panel,) = call(
        functools.partial(left_panel_kernel, [0] + steps), (panel,), crop_length, *lefts, smem=(0,)
    )
    for step, part in zip(row_steps, parts):
        part = swap(part, "row", step)
        if step != row_steps[-1]:
            (total,) = call(add_kernel, (wide,), total, part, flops=wait)
    tri_normed, tri_grad = call(
        triangle_kernel, (flat, tile), total, part, upstream, flops=20 * pairs * channels,
    )
    grads = gather(tri_grad, "row", gather_steps)
    update, partial = call(
        update_kernel, (tile, flat), tri_normed, out_open, gate_factor, in_weights, out_weight,
        flops=4 * pairs * channels * channels,
    )
    (right_grad,) = call(functools.partial(right_grad_kernel, [0]), (wide,), left_panel, tri_grad)
    terms, before = [], (partial, right_grad)
    for grad in grads[:-1]:
        before = call(
            left_terms_kernel, (wide,), grad, right, *before,
            scratch=[pltpu.VMEM((pairs, channels), f32)], flops=work,
        )
        terms += before
    total, *terms = call(
        functools.partial(last_terms_kernel, [0] + gather_steps[:-1], gather_steps[-1], [0] + steps),
        (wide,) + (tile,) * (n - 1), grads[-1], right, *terms, flops=work,
        scratch=[pltpu.VMEM(wide.shape, f32), pltpu.VMEM((pairs, channels), f32)],
    )
    for step, term in zip(steps, terms):
        term = swap(term, "col", step)
        if step != steps[-1]:
            (total,) = call(add_kernel, (wide,), total, term, flops=wait)
    (share,) = call(
        functools.partial(right_back_kernel, gather_steps), (flat,),
        left_panel, *grads[1:], right_grad, factors, in_weights, partial,
        scratch=[pltpu.VMEM(wide.shape, f32)],
    )
    (pair_grad,) = call(
        back_kernel, (tile,), total, term, normed, scale, factors, share, in_weights,
        flops=2 * pairs * channels * 2 * channels,
    )
    return (update, pair_grad)


def solution(mesh):
    return jax.shard_map(
        local,
        mesh=mesh,
        in_specs=(
            P(("group", "row"), "col", None),
            P(("group", "row"), "col"),
            P("group"),
            P(("group", "row"), "col", None),
            P(),
            P(),
        ),
        out_specs=(P(("group", "row"), "col", None), P(("group", "row"), "col", None)),
        check_vma=False,
    )
```

```python
import functools

import jax
import jax.numpy as jnp
from jax import lax
from jax.experimental import pallas as pl
from jax.experimental.pallas import tpu as pltpu
from jax.sharding import PartitionSpec as P

epsilon = 1e-05
f32 = jnp.float32
bf16 = jnp.bfloat16


def mean_lanes(values):
    return jnp.sum(values, axis=-1, keepdims=True) * (1.0 / values.shape[-1])


def normalize(values):
    center = values - mean_lanes(values)
    variance = mean_lanes(center * center)
    scale = lax.rsqrt(variance + epsilon)
    return (center * scale, scale)


def normalize_back(normed, scale, upstream):
    average = mean_lanes(upstream)
    project = mean_lanes(upstream * normed)
    return scale * (upstream - average - normed * project)


def sigmoid(values):
    return 1.0 / (1.0 + jnp.exp(-values))


def dot(a, b):
    return jnp.dot(a, b, preferred_element_type=f32)


def dot_t(a, b):
    return lax.dot_general(a, b, (((1,), (1,)), ((), ())), preferred_element_type=f32)


def live_pairs(crop_ref, row, col, shape):
    rows = row * shape[0] + lax.broadcasted_iota(jnp.int32, shape, 0)
    cols = col * shape[1] + lax.broadcasted_iota(jnp.int32, shape, 1)
    return jnp.where(jnp.maximum(rows, cols) < crop_ref[0], 1.0, 0.0)


def spread(mask, channels):
    size = mask.shape[0]
    shape = (size, size, size)
    diagonal = lax.broadcasted_iota(jnp.int32, shape, 1) == lax.broadcasted_iota(jnp.int32, shape, 2)
    picked = jnp.where(diagonal, jnp.broadcast_to(mask[:, None, :], shape), 0.0)
    rows = jnp.sum(picked, axis=-1, keepdims=True)
    return jnp.broadcast_to(rows, (size, size, channels)).reshape(size * size, channels)


def start_copies(sems, *pairs):
    copies = [pltpu.make_async_copy(src, dst, sems.at[n]) for n, (src, dst) in enumerate(pairs)]
    for copy in copies:
        copy.start()
    return copies


def gated(projected, block, keep):
    channels = keep.shape[1]
    value = projected[:, block * channels : (block + 1) * channels]
    opened = sigmoid(projected[:, (block + 1) * channels : (block + 2) * channels])
    return (opened * value * keep).astype(bf16), opened, value


def left_kernel(acts_in, mask_in, weights_in, left_ref, acts_ref, mask_ref, weights_ref, sems):
    size, _, channels = acts_ref.shape
    copies = start_copies(
        sems, (acts_in, acts_ref), (weights_in.at[:, pl.ds(0, 2 * channels)], weights_ref), (mask_in, mask_ref),
    )
    copies[0].wait()
    normed, _ = normalize(acts_ref[...].astype(f32).reshape(size * size, channels))
    normed = normed.astype(bf16)
    for copy in copies[1:]:
        copy.wait()
    left, _, _ = gated(dot(normed, weights_ref[...]), 0, spread(mask_ref[...].astype(f32), channels))
    left_ref[...] = left.reshape(size, size, channels)


def factors_kernel(
    acts_in, mask_in, crop_ref, cotangent_in, weights_in, out_weight_in,
    right_ref, normed_ref, scale_ref, factor_ref, open_ref, gate_factor_ref, upstream_ref,
    acts_ref, mask_ref, cotangent_ref, weights_ref, out_weight_ref, sems,
):
    copies = start_copies(
        sems, (acts_in, acts_ref), (weights_in, weights_ref), (mask_in, mask_ref),
        (cotangent_in, cotangent_ref), (out_weight_in, out_weight_ref),
    )
    size, _, channels = acts_ref.shape
    pairs = size * size
    copies[0].wait()
    normed, scale = normalize(acts_ref[...].astype(f32).reshape(pairs, channels))
    normed_ref[...] = normed
    scale_ref[...] = jnp.broadcast_to(scale, (pairs, channels))
    for copy in copies[1:]:
        copy.wait()
    projected = dot(normed.astype(bf16), weights_ref[...])
    live = live_pairs(crop_ref, lax.axis_index("row"), lax.axis_index("col"), (size, size))
    keep = spread(mask_ref[...].astype(f32) * live, channels)
    for block in (0, 2):
        tile, opened, value = gated(projected, block, keep)
        factor_ref[block] = keep * opened
        factor_ref[block + 1] = keep * value * opened * (1.0 - opened)
    right_ref[...] = tile.astype(f32).reshape(size, size, channels)
    out_open = sigmoid(projected[:, 4 * channels :])
    cotangent = cotangent_ref[...].astype(f32).reshape(pairs, channels)
    lin_grad = (cotangent * out_open).astype(bf16)
    open_ref[...] = out_open
    gate_factor_ref[...] = cotangent * out_open * (1.0 - out_open)
    upstream = dot_t(lin_grad, out_weight_ref[...])
    upstream_ref[...] = upstream - mean_lanes(upstream)


def weighted_sums(weights, start, terms, out, base=None):
    def step(k, _):
        total = weights[start + k, pl.ds(0, 1), :] * terms[0]
        for n in range(1, len(terms)):
            total = total + weights[start + k, pl.ds(n, 1), :] * terms[n]
        if base is not None:
            total = total + base[k]
        out[k] = total.astype(out.dtype)
        return 0

    lax.fori_loop(0, out.shape[0], step, 0, unroll=4)


def left_panel_kernel(steps, crop_ref, *refs):
    row, col, panel = lax.axis_index("row"), lax.axis_index("col"), refs[-1]
    size, _, channels = refs[0].shape
    rows = row * size + lax.broadcasted_iota(jnp.int32, (size, 1, channels), 0)
    row_live = jnp.where(rows < crop_ref[0], 1.0, 0.0)
    for step, ref in zip(steps, refs):
        place = col ^ step
        cols = place * size + lax.broadcasted_iota(jnp.int32, (1, size, channels), 1)
        col_live = jnp.where(cols < crop_ref[0], 1.0, 0.0)
        panel[pl.ds(place * size, size)] = ref[...].astype(f32) * (row_live * col_live)


def partial_kernel(steps, crop_ref, *refs):
    count = len(steps)
    lefts, right_ref, outs, left = refs[:count], refs[count], refs[count + 1 : -1], refs[-1]
    size, _, channels = right_ref.shape
    rows = lax.axis_index("row") * size + lax.broadcasted_iota(jnp.int32, (size, 1, channels), 0)
    row_live = jnp.where(rows < crop_ref[0], 1.0, 0.0)
    for step, left_ref, out in zip(steps, lefts, outs):
        cols = (lax.axis_index("col") ^ step) * size + lax.broadcasted_iota(jnp.int32, (1, size, channels), 1)
        left[...] = left_ref[...].astype(f32) * (row_live * jnp.where(cols < crop_ref[0], 1.0, 0.0))

        def add(k, sums):
            other = right_ref[k]
            return tuple(sums[i] + left[k, pl.ds(i, 1), :] * other for i in range(size))

        zero = jnp.zeros((size, channels), f32)
        sums = lax.fori_loop(0, size, add, (zero,) * size, unroll=4)
        for i in range(size):
            out[i] = sums[i]


def pick_kernel(steps, *refs):
    here = lax.axis_index("row") ^ lax.axis_index("col")
    tiles, outs = refs[: len(steps)], refs[len(steps) :]
    for step, out in zip(steps, outs):
        for other, tile in enumerate(tiles):

            @pl.when((here ^ step) == other)
            def _():
                out[...] = tile[...].astype(out.dtype)


def last_partial_kernel(steps, early, row_steps, crop_ref, *refs):
    count, known = len(steps), len(early)
    left, parts = refs[-2:]
    partial_kernel(steps, crop_ref, *refs[: count + 1], *(parts.at[at] for at in range(count)), left)
    tiles = dict(zip(early, refs[count + 1 : count + 1 + known]))
    tiles.update((step, parts.at[at]) for at, step in enumerate(steps))
    pick_kernel(row_steps, *(tiles[step] for step in range(count + known)), *refs[count + 1 + known : -2])


def triangle_kernel(base, *refs):
    *tiles, upstream_ref, tri_normed_ref, grad_ref = refs
    size = grad_ref.shape[0]
    for i in range(size):
        total = base[i]
        for ref in tiles:
            total = total + ref[i].astype(f32)
        here = pl.ds(i * size, size)
        upstream = upstream_ref[here, :]
        center = total - mean_lanes(total)
        scale = lax.rsqrt(mean_lanes(center * center) + epsilon)
        tri_normed = center * scale
        tri_normed_ref[here, :] = tri_normed
        project = mean_lanes(center * upstream) * scale
        grad_ref[i] = (scale * (upstream - tri_normed * project)).astype(bf16)


def left_terms_kernel(grad_ref, right, *refs):
    out, grad = refs[-2:]
    size, _, channels = out.shape
    grad[...] = grad_ref[...].astype(f32).reshape(size * size, channels)
    weighted_sums(right, 0, [grad[pl.ds(j, size, stride=size), :] for j in range(size)], out)


def last_terms_kernel(early, last, steps, grad_ref, right, *refs):
    known = len(early)
    term, grad = refs[-2:]
    left_terms_kernel(grad_ref, right, term, grad)
    tiles = dict(zip(early, refs[:known]))
    tiles[last] = term
    pick_kernel(steps, *(tiles[step] for step in range(known + 1)), *refs[known:-2])


def right_grad_kernel(steps, panel, *refs):
    out, base = refs[-1], refs[len(steps)] if len(refs) > len(steps) + 1 else None
    size = out.shape[0]
    for step, grad in zip(steps, refs):
        start = (lax.axis_index("row") ^ step) * size
        weighted_sums(panel, start, [grad[i].astype(f32) for i in range(size)], out, base)
        base = out


def right_back_kernel(steps, panel, *refs):
    factor_ref, weights_ref, share_ref, normed_ref, scale_ref, out, right_ref = refs[-7:]
    right_grad_kernel(steps, panel, *refs[: len(steps) + 1], right_ref)
    pairs, channels = out.shape
    right = right_ref[...].reshape(pairs, channels)
    grads = jnp.concatenate([(right * factor_ref[block]).astype(bf16) for block in (2, 3)], axis=1)
    share = share_ref[...] + dot_t(grads, weights_ref[:, 2 * channels : 4 * channels])
    out[...] = normalize_back(normed_ref[...], scale_ref[...], share)


def slopes_kernel(normed_ref, weights_ref, mean_ref, slope_ref):
    channels = normed_ref.shape[1]
    weights = weights_ref[:, : 2 * channels].astype(f32)
    mean = jnp.sum(weights, axis=0, keepdims=True) * (1.0 / channels)
    mean_ref[...] = jnp.broadcast_to(mean, mean_ref.shape)
    slope = jnp.dot(normed_ref[...], weights, precision=lax.Precision.HIGHEST, preferred_element_type=f32)
    slope_ref[...] = slope * (1.0 / channels)


def add_kernel(base, tile_ref, out):
    out[...] = base[...] + tile_ref[...].astype(f32)


def update_kernel(
    tri_normed_ref, open_ref, gate_factor_ref, weights_ref, out_weight_ref, update_ref, normed_grad_ref
):
    size, _, channels = update_ref.shape
    linear = dot(tri_normed_ref[...].astype(bf16), out_weight_ref[...])
    update = (open_ref[...] * linear).astype(bf16)
    update_ref[...] = update.reshape(size, size, channels)
    out_gate_grad = (gate_factor_ref[...] * linear).astype(bf16)
    normed_grad_ref[...] = dot_t(out_gate_grad, weights_ref[:, 4 * channels :])


def back_kernel(base, *refs):
    *tiles, normed_ref, scale_ref, factor_ref, done_ref, mean_ref, slope_ref, weights_ref, out = refs
    size, _, channels = out.shape
    pairs = size * size
    left = base[...]
    for ref in tiles:
        left = left + ref[...].astype(f32)
    left = left.reshape(pairs, channels)
    grads = jnp.concatenate([(left * factor_ref[block]).astype(bf16) for block in (0, 1)], axis=1)
    normed_grad = dot_t(grads, weights_ref[:, : 2 * channels])
    wide_grads = grads.astype(f32)
    average = jnp.sum(wide_grads * mean_ref[0:1, :], axis=-1, keepdims=True)
    project = jnp.sum(wide_grads * slope_ref[...], axis=-1, keepdims=True)
    back = done_ref[...] + scale_ref[...] * (normed_grad - average - normed_ref[...] * project)
    out[...] = back.astype(bf16).reshape(size, size, channels)


def call(kernel, outs, *args, scratch=(), flops=0, smem=(), hbm=()):
    spec = pl.BlockSpec(memory_space=pltpu.VMEM)
    total = sum(a.size * a.dtype.itemsize for a in (*args, *outs))
    specs = [spec] * len(args)
    for n in smem:
        specs[n] = pl.BlockSpec(memory_space=pltpu.SMEM)
    args = list(args)
    for n in hbm:
        specs[n] = pl.BlockSpec(memory_space=pltpu.HBM)
        args[n] = pltpu.with_memory_space_constraint(args[n], pltpu.HBM)
    return pl.pallas_call(
        kernel,
        out_shape=tuple(outs),
        in_specs=specs,
        out_specs=(spec,) * len(outs),
        scratch_shapes=scratch,
        compiler_params=pltpu.CompilerParams(vmem_limit_bytes=24 * 2**20),
        cost_estimate=pl.CostEstimate(flops=flops, bytes_accessed=total if flops else 0, transcendentals=0),
    )(*args)


def local(pair_acts, pair_mask, crop_length, cotangent, in_weights, out_weight):
    size, _, channels = pair_acts.shape
    pairs = size * size
    n = lax.axis_size("row")
    tile = jax.ShapeDtypeStruct((size, size, channels), bf16)
    flat = jax.ShapeDtypeStruct((pairs, channels), f32)

    wide = jax.ShapeDtypeStruct((size, size, channels), f32)
    panel = jax.ShapeDtypeStruct((n * size, size, channels), f32)
    work = 2 * size * pairs * channels
    wait = 2**31
    steps = [step for bit in range(n.bit_length() - 2, -1, -1) for step in range(2**bit, 2 ** (bit + 1))]
    row_steps = steps
    gather_steps = [n - 1] + list(range(1, n - 1))


    def swap(values, axis, step):
        return lax.ppermute(values, axis, [(a, a ^ step) for a in range(n)])

    def gather(values, axis, steps):
        return [values] + [swap(values, axis, step) for step in steps]

    (left,) = call(
        left_kernel, (tile,), pair_acts, pair_mask, in_weights,
        hbm=(0, 1, 2), flops=2 * pairs * channels * 2 * channels,
        scratch=[
            pltpu.VMEM(pair_acts.shape, bf16),
            pltpu.VMEM(pair_mask.shape, jnp.int32),
            pltpu.VMEM((channels, 2 * channels), bf16),
            pltpu.SemaphoreType.DMA((3,)),
        ],
    )
    lefts = gather(left, "col", steps)
    right, normed, scale, factors, out_open, gate_factor, upstream = call(
        factors_kernel,
        (wide, flat, flat, jax.ShapeDtypeStruct((4, pairs, channels), f32), flat, flat, flat),
        pair_acts, pair_mask, crop_length, cotangent, in_weights, out_weight,
        smem=(2,), hbm=(0, 1, 3, 4, 5), flops=2 * pairs * channels * 6 * channels,
        scratch=[
            pltpu.VMEM(pair_acts.shape, bf16),
            pltpu.VMEM(pair_mask.shape, jnp.int32),
            pltpu.VMEM(cotangent.shape, bf16),
            pltpu.VMEM(in_weights.shape, bf16),
            pltpu.VMEM(out_weight.shape, bf16),
            pltpu.SemaphoreType.DMA((5,)),
        ],
    )
    order = [0] + steps
    parts = [
        call(
            functools.partial(partial_kernel, [order[at]]), (wide,), crop_length, lefts[at], right, smem=(0,),
            flops=work, scratch=[pltpu.VMEM(wide.shape, f32)],
        )[0]
        for at in range(n - 2)
    ]
    total, *parts = call(
        functools.partial(last_partial_kernel, order[-2:], order[:-2], [0] + row_steps),
        (wide,) + (tile,) * (n - 1), crop_length, *lefts[-2:], right, *parts, smem=(0,), flops=work,
        scratch=[pltpu.VMEM(wide.shape, f32), pltpu.VMEM((2,) + wide.shape, f32)],
    )
    (left_panel,) = call(
        functools.partial(left_panel_kernel, [0] + steps), (panel,), crop_length, *lefts, smem=(0,)
    )
    last = []
    for step, part in zip(row_steps, parts):
        part = swap(part, "row", step)
        if step in row_steps[-2:]:
            last.append(part)
        else:
            (total,) = call(add_kernel, (wide,), total, part, flops=wait)
    tri_normed, tri_grad = call(
        triangle_kernel, (flat, tile), total, *last, upstream, flops=20 * pairs * channels,
    )
    grads = gather(tri_grad, "row", gather_steps)
    update, partial = call(
        update_kernel, (tile, flat), tri_normed, out_open, gate_factor, in_weights, out_weight,
        flops=4 * pairs * channels * channels,
    )
    means, slopes = call(
        slopes_kernel, (jax.ShapeDtypeStruct((8, 2 * channels), f32), jax.ShapeDtypeStruct((pairs, 2 * channels), f32)),
        normed, in_weights,
    )
    (right_grad,) = call(functools.partial(right_grad_kernel, [0]), (wide,), left_panel, tri_grad)
    terms, before = [], (partial, right_grad, slopes)
    for grad in grads[:-1]:
        before = call(
            left_terms_kernel, (wide,), grad, right, *before,
            scratch=[pltpu.VMEM((pairs, channels), f32)], flops=work,
        )
        terms += before
    total, *terms = call(
        functools.partial(last_terms_kernel, [0] + gather_steps[:-1], gather_steps[-1], [0] + steps),
        (wide,) + (tile,) * (n - 1), grads[-1], right, *terms, flops=work,
        scratch=[pltpu.VMEM(wide.shape, f32), pltpu.VMEM((pairs, channels), f32)],
    )
    last = []
    for step, term in zip(steps, terms):
        term = swap(term, "col", step)
        if step in steps[-2:]:
            last.append(term)
        else:
            (total,) = call(add_kernel, (wide,), total, term, flops=wait)
    (done,) = call(
        functools.partial(right_back_kernel, gather_steps), (flat,),
        left_panel, *grads[1:], right_grad, factors, in_weights, partial, normed, scale,
        scratch=[pltpu.VMEM(wide.shape, f32)],
    )
    (pair_grad,) = call(
        back_kernel, (tile,), total, *last, normed, scale, factors, done, means, slopes, in_weights,
        flops=2 * pairs * channels * 2 * channels,
    )
    return (update, pair_grad)


def solution(mesh):
    return jax.shard_map(
        local,
        mesh=mesh,
        in_specs=(
            P(("group", "row"), "col", None),
            P(("group", "row"), "col"),
            P("group"),
            P(("group", "row"), "col", None),
            P(),
            P(),
        ),
        out_specs=(P(("group", "row"), "col", None), P(("group", "row"), "col", None)),
        check_vma=False,
    )
```

```python
import functools

import jax
import jax.numpy as jnp
from jax import lax
from jax.experimental import pallas as pl
from jax.experimental.pallas import tpu as pltpu
from jax.sharding import PartitionSpec as P

epsilon = 1e-05
f32 = jnp.float32
bf16 = jnp.bfloat16


def mean_lanes(values):
    return jnp.sum(values, axis=-1, keepdims=True) * (1.0 / values.shape[-1])


def normalize(values):
    center = values - mean_lanes(values)
    variance = mean_lanes(center * center)
    scale = lax.rsqrt(variance + epsilon)
    return (center * scale, scale)


def normalize_back(normed, scale, upstream):
    average = mean_lanes(upstream)
    project = mean_lanes(upstream * normed)
    return scale * (upstream - average - normed * project)


def sigmoid(values):
    return 1.0 / (1.0 + jnp.exp(-values))


def dot(a, b):
    return jnp.dot(a, b, preferred_element_type=f32)


def dot_t(a, b):
    return lax.dot_general(a, b, (((1,), (1,)), ((), ())), preferred_element_type=f32)


def live_pairs(crop_ref, row, col, shape):
    rows = row * shape[0] + lax.broadcasted_iota(jnp.int32, shape, 0)
    cols = col * shape[1] + lax.broadcasted_iota(jnp.int32, shape, 1)
    return jnp.where(jnp.maximum(rows, cols) < crop_ref[0], 1.0, 0.0)


def spread(mask, channels):
    size = mask.shape[0]
    shape = (size, size, size)
    diagonal = lax.broadcasted_iota(jnp.int32, shape, 1) == lax.broadcasted_iota(jnp.int32, shape, 2)
    picked = jnp.where(diagonal, jnp.broadcast_to(mask[:, None, :], shape), 0.0)
    rows = jnp.sum(picked, axis=-1, keepdims=True)
    return jnp.broadcast_to(rows, (size, size, channels)).reshape(size * size, channels)


def start_copies(sems, *pairs):
    copies = [pltpu.make_async_copy(src, dst, sems.at[n]) for n, (src, dst) in enumerate(pairs)]
    for copy in copies:
        copy.start()
    return copies


def gated(projected, block, keep):
    channels = keep.shape[1]
    value = projected[:, block * channels : (block + 1) * channels]
    opened = sigmoid(projected[:, (block + 1) * channels : (block + 2) * channels])
    return (opened * value * keep).astype(bf16), opened, value


def left_kernel(acts_in, mask_in, weights_in, left_ref, acts_ref, mask_ref, weights_ref, sems):
    size, _, channels = acts_ref.shape
    copies = start_copies(
        sems, (acts_in, acts_ref), (weights_in.at[:, pl.ds(0, 2 * channels)], weights_ref), (mask_in, mask_ref),
    )
    copies[0].wait()
    normed, _ = normalize(acts_ref[...].astype(f32).reshape(size * size, channels))
    normed = normed.astype(bf16)
    for copy in copies[1:]:
        copy.wait()
    left, _, _ = gated(dot(normed, weights_ref[...]), 0, spread(mask_ref[...].astype(f32), channels))
    left_ref[...] = left.reshape(size, size, channels)


def factors_kernel(
    acts_in, mask_in, crop_ref, cotangent_in, weights_in, out_weight_in,
    right_ref, normed_ref, scale_ref, factor_ref, open_ref, gate_factor_ref, upstream_ref,
    acts_ref, mask_ref, cotangent_ref, weights_ref, out_weight_ref, sems,
):
    copies = start_copies(
        sems, (acts_in, acts_ref), (weights_in, weights_ref), (mask_in, mask_ref),
        (cotangent_in, cotangent_ref), (out_weight_in, out_weight_ref),
    )
    size, _, channels = acts_ref.shape
    pairs = size * size
    copies[0].wait()
    normed, scale = normalize(acts_ref[...].astype(f32).reshape(pairs, channels))
    normed_ref[...] = normed
    scale_ref[...] = jnp.broadcast_to(scale, (pairs, channels))
    for copy in copies[1:]:
        copy.wait()
    projected = dot(normed.astype(bf16), weights_ref[...])
    live = live_pairs(crop_ref, lax.axis_index("row"), lax.axis_index("col"), (size, size))
    keep = spread(mask_ref[...].astype(f32) * live, channels)
    for block in (0, 2):
        tile, opened, value = gated(projected, block, keep)
        factor_ref[block] = keep * opened
        factor_ref[block + 1] = keep * value * opened * (1.0 - opened)
    right_ref[...] = tile.astype(f32).reshape(size, size, channels)
    out_open = sigmoid(projected[:, 4 * channels :])
    cotangent = cotangent_ref[...].astype(f32).reshape(pairs, channels)
    lin_grad = (cotangent * out_open).astype(bf16)
    open_ref[...] = out_open
    gate_factor_ref[...] = cotangent * out_open * (1.0 - out_open)
    upstream = dot_t(lin_grad, out_weight_ref[...])
    upstream_ref[...] = upstream - mean_lanes(upstream)


def weighted_sums(weights, start, terms, out, base=None):
    def step(k, _):
        total = weights[start + k, pl.ds(0, 1), :] * terms[0]
        for n in range(1, len(terms)):
            total = total + weights[start + k, pl.ds(n, 1), :] * terms[n]
        if base is not None:
            total = total + base[k]
        out[k] = total.astype(out.dtype)
        return 0

    lax.fori_loop(0, out.shape[0], step, 0, unroll=4)


def left_panel_kernel(steps, crop_ref, *refs):
    row, col, panel = lax.axis_index("row"), lax.axis_index("col"), refs[-1]
    size, _, channels = refs[0].shape
    rows = row * size + lax.broadcasted_iota(jnp.int32, (size, 1, channels), 0)
    row_live = jnp.where(rows < crop_ref[0], 1.0, 0.0)
    for step, ref in zip(steps, refs):
        place = col ^ step
        cols = place * size + lax.broadcasted_iota(jnp.int32, (1, size, channels), 1)
        col_live = jnp.where(cols < crop_ref[0], 1.0, 0.0)
        panel[pl.ds(place * size, size)] = ref[...].astype(f32) * (row_live * col_live)


def partial_kernel(steps, crop_ref, *refs):
    count = len(steps)
    lefts, right_ref, outs, left = refs[:count], refs[count], refs[count + 1 : -1], refs[-1]
    size, _, channels = right_ref.shape
    rows = lax.axis_index("row") * size + lax.broadcasted_iota(jnp.int32, (size, 1, channels), 0)
    row_live = jnp.where(rows < crop_ref[0], 1.0, 0.0)
    for step, left_ref, out in zip(steps, lefts, outs):
        cols = (lax.axis_index("col") ^ step) * size + lax.broadcasted_iota(jnp.int32, (1, size, channels), 1)
        left[...] = left_ref[...].astype(f32) * (row_live * jnp.where(cols < crop_ref[0], 1.0, 0.0))

        def add(k, sums):
            other = right_ref[k]
            return tuple(sums[i] + left[k, pl.ds(i, 1), :] * other for i in range(size))

        zero = jnp.zeros((size, channels), f32)
        sums = lax.fori_loop(0, size, add, (zero,) * size, unroll=4)
        for i in range(size):
            out[i] = sums[i]


def pick_kernel(steps, *refs):
    here = lax.axis_index("row") ^ lax.axis_index("col")
    tiles, outs = refs[: len(steps)], refs[len(steps) :]
    for step, out in zip(steps, outs):
        for other, tile in enumerate(tiles):

            @pl.when((here ^ step) == other)
            def _():
                out[...] = tile[...].astype(out.dtype)


def last_partial_kernel(steps, early, row_steps, crop_ref, *refs):
    count, known = len(steps), len(early)
    left, parts = refs[-2:]
    partial_kernel(steps, crop_ref, *refs[: count + 1], *(parts.at[at] for at in range(count)), left)
    tiles = dict(zip(early, refs[count + 1 : count + 1 + known]))
    tiles.update((step, parts.at[at]) for at, step in enumerate(steps))
    pick_kernel(row_steps, *(tiles[step] for step in range(count + known)), *refs[count + 1 + known : -2])


def triangle_kernel(base, *refs):
    *tiles, upstream_ref, tri_normed_ref, grad_ref = refs
    size = grad_ref.shape[0]
    for i in range(size):
        total = base[i]
        for ref in tiles:
            total = total + ref[i].astype(f32)
        here = pl.ds(i * size, size)
        upstream = upstream_ref[here, :]
        center = total - mean_lanes(total)
        scale = lax.rsqrt(mean_lanes(center * center) + epsilon)
        tri_normed = center * scale
        tri_normed_ref[here, :] = tri_normed
        project = mean_lanes(center * upstream) * scale
        grad_ref[i] = (scale * (upstream - tri_normed * project)).astype(bf16)


def left_terms_kernel(grad_ref, right, *refs):
    out, grad = refs[-2:]
    size, _, channels = out.shape
    grad[...] = grad_ref[...].astype(f32).reshape(size * size, channels)
    weighted_sums(right, 0, [grad[pl.ds(j, size, stride=size), :] for j in range(size)], out)


def last_terms_kernel(early, last, steps, grad_ref, right, *refs):
    known = len(early)
    term, grad = refs[-2:]
    left_terms_kernel(grad_ref, right, term, grad)
    tiles = dict(zip(early, refs[:known]))
    tiles[last] = term
    pick_kernel(steps, *(tiles[step] for step in range(known + 1)), *refs[known:-2])


def right_grad_kernel(steps, panel, *refs):
    out, base = refs[-1], refs[len(steps)] if len(refs) > len(steps) + 1 else None
    size = out.shape[0]
    for step, grad in zip(steps, refs):
        start = (lax.axis_index("row") ^ step) * size
        weighted_sums(panel, start, [grad[i].astype(f32) for i in range(size)], out, base)
        base = out


def right_back_kernel(steps, panel, *refs):
    factor_ref, weights_ref, share_ref, normed_ref, scale_ref, out, right_ref = refs[-7:]
    right_grad_kernel(steps, panel, *refs[: len(steps) + 1], right_ref)
    pairs, channels = out.shape
    right = right_ref[...].reshape(pairs, channels)
    grads = jnp.concatenate([(right * factor_ref[block]).astype(bf16) for block in (2, 3)], axis=1)
    share = share_ref[...] + dot_t(grads, weights_ref[:, 2 * channels : 4 * channels])
    out[...] = normalize_back(normed_ref[...], scale_ref[...], share)


def slopes_kernel(normed_ref, weights_ref, mean_ref, slope_ref):
    channels = normed_ref.shape[1]
    weights = weights_ref[:, : 2 * channels].astype(f32)
    mean = jnp.sum(weights, axis=0, keepdims=True) * (1.0 / channels)
    mean_ref[...] = jnp.broadcast_to(mean, mean_ref.shape)
    slope = jnp.dot(normed_ref[...], weights, precision=lax.Precision.HIGHEST, preferred_element_type=f32)
    slope_ref[...] = slope * (1.0 / channels)


def add_kernel(base, tile_ref, out):
    out[...] = base[...] + tile_ref[...].astype(f32)


def update_kernel(
    tri_normed_ref, open_ref, gate_factor_ref, weights_ref, out_weight_ref, update_ref, normed_grad_ref
):
    size, _, channels = update_ref.shape
    linear = dot(tri_normed_ref[...].astype(bf16), out_weight_ref[...])
    update = (open_ref[...] * linear).astype(bf16)
    update_ref[...] = update.reshape(size, size, channels)
    out_gate_grad = (gate_factor_ref[...] * linear).astype(bf16)
    normed_grad_ref[...] = dot_t(out_gate_grad, weights_ref[:, 4 * channels :])


def back_kernel(base, *refs):
    *tiles, normed_ref, scale_ref, factor_ref, done_ref, mean_ref, slope_ref, weights_ref, out = refs
    size, _, channels = out.shape
    pairs = size * size
    left = base[...]
    for ref in tiles:
        left = left + ref[...].astype(f32)
    left = left.reshape(pairs, channels)
    grads = jnp.concatenate([(left * factor_ref[block]).astype(bf16) for block in (0, 1)], axis=1)
    normed_grad = dot_t(grads, weights_ref[:, : 2 * channels])
    wide_grads = grads.astype(f32)
    average = jnp.sum(wide_grads * mean_ref[0:1, :], axis=-1, keepdims=True)
    project = jnp.sum(wide_grads * slope_ref[...], axis=-1, keepdims=True)
    back = done_ref[...] + scale_ref[...] * (normed_grad - average - normed_ref[...] * project)
    out[...] = back.astype(bf16).reshape(size, size, channels)


def call(kernel, outs, *args, scratch=(), flops=0, smem=(), hbm=()):
    spec = pl.BlockSpec(memory_space=pltpu.VMEM)
    total = sum(a.size * a.dtype.itemsize for a in (*args, *outs))
    specs = [spec] * len(args)
    for n in smem:
        specs[n] = pl.BlockSpec(memory_space=pltpu.SMEM)
    args = list(args)
    for n in hbm:
        specs[n] = pl.BlockSpec(memory_space=pltpu.HBM)
        args[n] = pltpu.with_memory_space_constraint(args[n], pltpu.HBM)
    return pl.pallas_call(
        kernel,
        out_shape=tuple(outs),
        in_specs=specs,
        out_specs=(spec,) * len(outs),
        scratch_shapes=scratch,
        compiler_params=pltpu.CompilerParams(vmem_limit_bytes=24 * 2**20),
        cost_estimate=pl.CostEstimate(flops=flops, bytes_accessed=total if flops else 0, transcendentals=0),
    )(*args)


def local(pair_acts, pair_mask, crop_length, cotangent, in_weights, out_weight):
    size, _, channels = pair_acts.shape
    pairs = size * size
    n = lax.axis_size("row")
    tile = jax.ShapeDtypeStruct((size, size, channels), bf16)
    flat = jax.ShapeDtypeStruct((pairs, channels), f32)

    wide = jax.ShapeDtypeStruct((size, size, channels), f32)
    panel = jax.ShapeDtypeStruct((n * size, size, channels), f32)
    work = 2 * size * pairs * channels
    wait = 2**31
    steps = [step for bit in range(n.bit_length() - 2, -1, -1) for step in range(2**bit, 2 ** (bit + 1))]
    row_steps = steps
    gather_steps = steps


    def swap(values, axis, step):
        return lax.ppermute(values, axis, [(a, a ^ step) for a in range(n)])

    def gather(values, axis, steps):
        return [values] + [swap(values, axis, step) for step in steps]

    (left,) = call(
        left_kernel, (tile,), pair_acts, pair_mask, in_weights,
        hbm=(0, 1, 2), flops=2 * pairs * channels * 2 * channels,
        scratch=[
            pltpu.VMEM(pair_acts.shape, bf16),
            pltpu.VMEM(pair_mask.shape, jnp.int32),
            pltpu.VMEM((channels, 2 * channels), bf16),
            pltpu.SemaphoreType.DMA((3,)),
        ],
    )
    lefts = gather(left, "col", steps)
    right, normed, scale, factors, out_open, gate_factor, upstream = call(
        factors_kernel,
        (wide, flat, flat, jax.ShapeDtypeStruct((4, pairs, channels), f32), flat, flat, flat),
        pair_acts, pair_mask, crop_length, cotangent, in_weights, out_weight,
        smem=(2,), hbm=(0, 1, 3, 4, 5), flops=2 * pairs * channels * 6 * channels,
        scratch=[
            pltpu.VMEM(pair_acts.shape, bf16),
            pltpu.VMEM(pair_mask.shape, jnp.int32),
            pltpu.VMEM(cotangent.shape, bf16),
            pltpu.VMEM(in_weights.shape, bf16),
            pltpu.VMEM(out_weight.shape, bf16),
            pltpu.SemaphoreType.DMA((5,)),
        ],
    )
    order = [0] + steps
    parts = [
        call(
            functools.partial(partial_kernel, [order[at]]), (wide,), crop_length, lefts[at], right, smem=(0,),
            flops=work, scratch=[pltpu.VMEM(wide.shape, f32)],
        )[0]
        for at in range(n - 2)
    ]
    total, *parts = call(
        functools.partial(last_partial_kernel, order[-2:], order[:-2], [0] + row_steps),
        (wide,) + (tile,) * (n - 1), crop_length, *lefts[-2:], right, *parts, smem=(0,), flops=work,
        scratch=[pltpu.VMEM(wide.shape, f32), pltpu.VMEM((2,) + wide.shape, f32)],
    )
    (left_panel,) = call(
        functools.partial(left_panel_kernel, [0] + steps), (panel,), crop_length, *lefts, smem=(0,)
    )
    last = []
    for step, part in zip(row_steps, parts):
        part = swap(part, "row", step)
        if step in row_steps[-2:]:
            last.append(part)
        else:
            (total,) = call(add_kernel, (wide,), total, part, flops=wait)
    tri_normed, tri_grad = call(
        triangle_kernel, (flat, tile), total, *last, upstream, flops=20 * pairs * channels,
    )
    grads = gather(tri_grad, "row", gather_steps)
    update, partial = call(
        update_kernel, (tile, flat), tri_normed, out_open, gate_factor, in_weights, out_weight,
        flops=4 * pairs * channels * channels,
    )
    means, slopes = call(
        slopes_kernel, (jax.ShapeDtypeStruct((8, 2 * channels), f32), jax.ShapeDtypeStruct((pairs, 2 * channels), f32)),
        normed, in_weights,
    )
    (right_grad,) = call(functools.partial(right_grad_kernel, [0]), (wide,), left_panel, tri_grad)
    terms, before = [], (partial, right_grad, slopes)
    for grad in grads[:-1]:
        before = call(
            left_terms_kernel, (wide,), grad, right, *before,
            scratch=[pltpu.VMEM((pairs, channels), f32)], flops=work,
        )
        terms += before
    total, *terms = call(
        functools.partial(last_terms_kernel, [0] + gather_steps[:-1], gather_steps[-1], [0] + steps),
        (wide,) + (tile,) * (n - 1), grads[-1], right, *terms, flops=work,
        scratch=[pltpu.VMEM(wide.shape, f32), pltpu.VMEM((pairs, channels), f32)],
    )
    last = []
    for step, term in zip(steps, terms):
        term = swap(term, "col", step)
        if step in steps[-2:]:
            last.append(term)
        else:
            (total,) = call(add_kernel, (wide,), total, term, flops=wait)
    (done,) = call(
        functools.partial(right_back_kernel, gather_steps), (flat,),
        left_panel, *grads[1:], right_grad, factors, in_weights, partial, normed, scale,
        scratch=[pltpu.VMEM(wide.shape, f32)],
    )
    (pair_grad,) = call(
        back_kernel, (tile,), total, *last, normed, scale, factors, done, means, slopes, in_weights,
        flops=2 * pairs * channels * 2 * channels,
    )
    return (update, pair_grad)


def solution(mesh):
    return jax.shard_map(
        local,
        mesh=mesh,
        in_specs=(
            P(("group", "row"), "col", None),
            P(("group", "row"), "col"),
            P("group"),
            P(("group", "row"), "col", None),
            P(),
            P(),
        ),
        out_specs=(P(("group", "row"), "col", None), P(("group", "row"), "col", None)),
        check_vma=False,
    )
```

```python
import functools

import jax
import jax.numpy as jnp
from jax import lax
from jax.experimental import pallas as pl
from jax.experimental.pallas import tpu as pltpu
from jax.sharding import PartitionSpec as P

epsilon = 1e-05
f32 = jnp.float32
bf16 = jnp.bfloat16


def mean_lanes(values):
    return jnp.sum(values, axis=-1, keepdims=True) * (1.0 / values.shape[-1])


def normalize(values):
    center = values - mean_lanes(values)
    variance = mean_lanes(center * center)
    scale = lax.rsqrt(variance + epsilon)
    return (center * scale, scale)


def normalize_back(normed, scale, upstream):
    average = mean_lanes(upstream)
    project = mean_lanes(upstream * normed)
    return scale * (upstream - average - normed * project)


def sigmoid(values):
    return 1.0 / (1.0 + jnp.exp(-values))


def dot(a, b):
    return jnp.dot(a, b, preferred_element_type=f32)


def dot_t(a, b):
    return lax.dot_general(a, b, (((1,), (1,)), ((), ())), preferred_element_type=f32)


def live_pairs(crop_ref, row, col, shape):
    rows = row * shape[0] + lax.broadcasted_iota(jnp.int32, shape, 0)
    cols = col * shape[1] + lax.broadcasted_iota(jnp.int32, shape, 1)
    return jnp.where(jnp.maximum(rows, cols) < crop_ref[0], 1.0, 0.0)


def spread(mask, channels):
    size = mask.shape[0]
    shape = (size, size, size)
    diagonal = lax.broadcasted_iota(jnp.int32, shape, 1) == lax.broadcasted_iota(jnp.int32, shape, 2)
    picked = jnp.where(diagonal, jnp.broadcast_to(mask[:, None, :], shape), 0.0)
    rows = jnp.sum(picked, axis=-1, keepdims=True)
    return jnp.broadcast_to(rows, (size, size, channels)).reshape(size * size, channels)


def start_copies(sems, *pairs):
    copies = [pltpu.make_async_copy(src, dst, sems.at[n]) for n, (src, dst) in enumerate(pairs)]
    for copy in copies:
        copy.start()
    return copies


def gated(projected, block, keep):
    channels = keep.shape[1]
    value = projected[:, block * channels : (block + 1) * channels]
    opened = sigmoid(projected[:, (block + 1) * channels : (block + 2) * channels])
    return (opened * value * keep).astype(bf16), opened, value


def left_kernel(acts_in, mask_in, weights_in, left_ref, acts_ref, mask_ref, weights_ref, sems):
    size, _, channels = acts_ref.shape
    copies = start_copies(
        sems, (acts_in, acts_ref), (weights_in.at[:, pl.ds(0, 2 * channels)], weights_ref), (mask_in, mask_ref),
    )
    copies[0].wait()
    normed, _ = normalize(acts_ref[...].astype(f32).reshape(size * size, channels))
    normed = normed.astype(bf16)
    for copy in copies[1:]:
        copy.wait()
    left, _, _ = gated(dot(normed, weights_ref[...]), 0, spread(mask_ref[...].astype(f32), channels))
    left_ref[...] = left.reshape(size, size, channels)


def factors_kernel(
    acts_in, mask_in, crop_ref, cotangent_in, weights_in, out_weight_in,
    right_ref, normed_ref, scale_ref, factor_ref, open_ref, gate_factor_ref, upstream_ref,
    acts_ref, mask_ref, cotangent_ref, weights_ref, out_weight_ref, sems,
):
    copies = start_copies(
        sems, (acts_in, acts_ref), (weights_in, weights_ref), (mask_in, mask_ref),
        (cotangent_in, cotangent_ref), (out_weight_in, out_weight_ref),
    )
    size, _, channels = acts_ref.shape
    pairs = size * size
    copies[0].wait()
    normed, scale = normalize(acts_ref[...].astype(f32).reshape(pairs, channels))
    normed_ref[...] = normed
    scale_ref[...] = jnp.broadcast_to(scale, (pairs, channels))
    for copy in copies[1:]:
        copy.wait()
    projected = dot(normed.astype(bf16), weights_ref[...])
    live = live_pairs(crop_ref, lax.axis_index("row"), lax.axis_index("col"), (size, size))
    keep = spread(mask_ref[...].astype(f32) * live, channels)
    for block in (0, 2):
        tile, opened, value = gated(projected, block, keep)
        factor_ref[block] = keep * opened
        factor_ref[block + 1] = keep * value * opened * (1.0 - opened)
    right_ref[...] = tile.astype(f32).reshape(size, size, channels)
    out_open = sigmoid(projected[:, 4 * channels :])
    cotangent = cotangent_ref[...].astype(f32).reshape(pairs, channels)
    lin_grad = (cotangent * out_open).astype(bf16)
    open_ref[...] = out_open
    gate_factor_ref[...] = cotangent * out_open * (1.0 - out_open)
    upstream = dot_t(lin_grad, out_weight_ref[...])
    upstream_ref[...] = upstream - mean_lanes(upstream)


def weighted_sums(weights, start, terms, out, base=None):
    def step(k, _):
        total = weights[start + k, pl.ds(0, 1), :] * terms[0]
        for n in range(1, len(terms)):
            total = total + weights[start + k, pl.ds(n, 1), :] * terms[n]
        if base is not None:
            total = total + base[k]
        out[k] = total.astype(out.dtype)
        return 0

    lax.fori_loop(0, out.shape[0], step, 0, unroll=8)


def left_panel_kernel(steps, crop_ref, *refs):
    row, col, panel = lax.axis_index("row"), lax.axis_index("col"), refs[-1]
    size, _, channels = refs[0].shape
    rows = row * size + lax.broadcasted_iota(jnp.int32, (size, 1, channels), 0)
    row_live = jnp.where(rows < crop_ref[0], 1.0, 0.0)
    for step, ref in zip(steps, refs):
        place = col ^ step
        cols = place * size + lax.broadcasted_iota(jnp.int32, (1, size, channels), 1)
        col_live = jnp.where(cols < crop_ref[0], 1.0, 0.0)
        panel[pl.ds(place * size, size)] = ref[...].astype(f32) * (row_live * col_live)


def partial_kernel(steps, crop_ref, *refs):
    count = len(steps)
    lefts, right_ref, outs, left = refs[:count], refs[count], refs[count + 1 : -1], refs[-1]
    size, _, channels = right_ref.shape
    rows = lax.axis_index("row") * size + lax.broadcasted_iota(jnp.int32, (size, 1, channels), 0)
    row_live = jnp.where(rows < crop_ref[0], 1.0, 0.0)
    for step, left_ref, out in zip(steps, lefts, outs):
        cols = (lax.axis_index("col") ^ step) * size + lax.broadcasted_iota(jnp.int32, (1, size, channels), 1)
        left[...] = left_ref[...].astype(f32) * (row_live * jnp.where(cols < crop_ref[0], 1.0, 0.0))

        def add(k, sums):
            other = right_ref[k]
            return tuple(sums[i] + left[k, pl.ds(i, 1), :] * other for i in range(size))

        zero = jnp.zeros((size, channels), f32)
        sums = lax.fori_loop(0, size, add, (zero,) * size, unroll=8)
        for i in range(size):
            out[i] = sums[i].astype(out.dtype)


def pick_kernel(steps, *refs):
    here = lax.axis_index("row") ^ lax.axis_index("col")
    tiles, outs = refs[: len(steps)], refs[len(steps) :]
    for step, out in zip(steps, outs):
        for other, tile in enumerate(tiles):

            @pl.when((here ^ step) == other)
            def _():
                out[...] = tile[...].astype(out.dtype)


def last_partial_kernel(steps, early, row_steps, crop_ref, *refs):
    count, known = len(steps), len(early)
    left, parts = refs[-2:]
    partial_kernel(steps, crop_ref, *refs[: count + 1], *(parts.at[at] for at in range(count)), left)
    tiles = dict(zip(early, refs[count + 1 : count + 1 + known]))
    tiles.update((step, parts.at[at]) for at, step in enumerate(steps))
    pick_kernel(row_steps, *(tiles[step] for step in range(count + known)), *refs[count + 1 + known : -2])


def triangle_kernel(base, *refs):
    *tiles, upstream_ref, tri_normed_ref, grad_ref = refs
    size = grad_ref.shape[0]
    for i in range(size):
        total = base[i]
        for ref in tiles:
            total = total + ref[i].astype(f32)
        here = pl.ds(i * size, size)
        upstream = upstream_ref[here, :]
        center = total - mean_lanes(total)
        scale = lax.rsqrt(mean_lanes(center * center) + epsilon)
        tri_normed = center * scale
        tri_normed_ref[here, :] = tri_normed
        project = mean_lanes(center * upstream) * scale
        grad_ref[i] = (scale * (upstream - tri_normed * project)).astype(bf16)


def left_terms_kernel(grad_ref, right, *refs):
    out, grad = refs[-2:]
    size, _, channels = out.shape
    grad[...] = grad_ref[...].astype(f32).reshape(size * size, channels)
    weighted_sums(right, 0, [grad[pl.ds(j, size, stride=size), :] for j in range(size)], out)


def last_terms_kernel(early, last, steps, grad_ref, right, *refs):
    known = len(early)
    term, grad = refs[-2:]
    left_terms_kernel(grad_ref, right, term, grad)
    tiles = dict(zip(early, refs[:known]))
    tiles[last] = term
    pick_kernel(steps, *(tiles[step] for step in range(known + 1)), *refs[known:-2])


def right_grad_kernel(steps, panel, *refs):
    out, base = refs[-1], refs[len(steps)] if len(refs) > len(steps) + 1 else None
    size = out.shape[0]
    for step, grad in zip(steps, refs):
        start = (lax.axis_index("row") ^ step) * size
        weighted_sums(panel, start, [grad[i].astype(f32) for i in range(size)], out, base)
        base = out


def right_back_kernel(steps, panel, *refs):
    factor_ref, weights_ref, share_ref, normed_ref, scale_ref, out, right_ref = refs[-7:]
    right_grad_kernel(steps, panel, *refs[: len(steps) + 1], right_ref)
    pairs, channels = out.shape
    right = right_ref[...].reshape(pairs, channels)
    grads = jnp.concatenate([(right * factor_ref[block]).astype(bf16) for block in (2, 3)], axis=1)
    share = share_ref[...] + dot_t(grads, weights_ref[:, 2 * channels : 4 * channels])
    out[...] = normalize_back(normed_ref[...], scale_ref[...], share)


def slopes_kernel(normed_ref, weights_ref, mean_ref, slope_ref):
    channels = normed_ref.shape[1]
    weights = weights_ref[:, : 2 * channels].astype(f32)
    mean = jnp.sum(weights, axis=0, keepdims=True) * (1.0 / channels)
    mean_ref[...] = jnp.broadcast_to(mean, mean_ref.shape)
    slope = jnp.dot(normed_ref[...], weights, precision=lax.Precision.HIGHEST, preferred_element_type=f32)
    slope_ref[...] = slope * (1.0 / channels)


def add_kernel(base, tile_ref, out):
    out[...] = base[...] + tile_ref[...].astype(f32)


def update_kernel(
    tri_normed_ref, open_ref, gate_factor_ref, weights_ref, out_weight_ref, update_ref, normed_grad_ref
):
    size, _, channels = update_ref.shape
    linear = dot(tri_normed_ref[...].astype(bf16), out_weight_ref[...])
    update = (open_ref[...] * linear).astype(bf16)
    update_ref[...] = update.reshape(size, size, channels)
    out_gate_grad = (gate_factor_ref[...] * linear).astype(bf16)
    normed_grad_ref[...] = dot_t(out_gate_grad, weights_ref[:, 4 * channels :])


def back_kernel(base, *refs):
    *tiles, normed_ref, scale_ref, factor_ref, done_ref, mean_ref, slope_ref, weights_ref, out = refs
    size, _, channels = out.shape
    pairs = size * size
    left = base[...]
    for ref in tiles:
        left = left + ref[...].astype(f32)
    left = left.reshape(pairs, channels)
    grads = jnp.concatenate([(left * factor_ref[block]).astype(bf16) for block in (0, 1)], axis=1)
    normed_grad = dot_t(grads, weights_ref[:, : 2 * channels])
    wide_grads = grads.astype(f32)
    average = jnp.sum(wide_grads * mean_ref[0:1, :], axis=-1, keepdims=True)
    project = jnp.sum(wide_grads * slope_ref[...], axis=-1, keepdims=True)
    back = done_ref[...] + scale_ref[...] * (normed_grad - average - normed_ref[...] * project)
    out[...] = back.astype(bf16).reshape(size, size, channels)


def call(kernel, outs, *args, scratch=(), flops=0, smem=(), hbm=()):
    spec = pl.BlockSpec(memory_space=pltpu.VMEM)
    total = sum(a.size * a.dtype.itemsize for a in (*args, *outs))
    specs = [spec] * len(args)
    for n in smem:
        specs[n] = pl.BlockSpec(memory_space=pltpu.SMEM)
    args = list(args)
    for n in hbm:
        specs[n] = pl.BlockSpec(memory_space=pltpu.HBM)
        args[n] = pltpu.with_memory_space_constraint(args[n], pltpu.HBM)
    return pl.pallas_call(
        kernel,
        out_shape=tuple(outs),
        in_specs=specs,
        out_specs=(spec,) * len(outs),
        scratch_shapes=scratch,
        compiler_params=pltpu.CompilerParams(vmem_limit_bytes=24 * 2**20),
        cost_estimate=pl.CostEstimate(flops=flops, bytes_accessed=total if flops else 0, transcendentals=0),
    )(*args)


def local(pair_acts, pair_mask, crop_length, cotangent, in_weights, out_weight):
    size, _, channels = pair_acts.shape
    pairs = size * size
    n = lax.axis_size("row")
    tile = jax.ShapeDtypeStruct((size, size, channels), bf16)
    flat = jax.ShapeDtypeStruct((pairs, channels), f32)

    wide = jax.ShapeDtypeStruct((size, size, channels), f32)
    panel = jax.ShapeDtypeStruct((n * size, size, channels), f32)
    work = 2 * size * pairs * channels
    wait = 2**31
    steps = [step for bit in range(n.bit_length() - 2, -1, -1) for step in range(2**bit, 2 ** (bit + 1))]
    row_steps = steps
    gather_steps = [n - 1] + list(range(1, n - 1))


    def swap(values, axis, step):
        return lax.ppermute(values, axis, [(a, a ^ step) for a in range(n)])

    def gather(values, axis, steps):
        return [values] + [swap(values, axis, step) for step in steps]

    (left,) = call(
        left_kernel, (tile,), pair_acts, pair_mask, in_weights,
        hbm=(0, 1, 2), flops=2 * pairs * channels * 2 * channels,
        scratch=[
            pltpu.VMEM(pair_acts.shape, bf16),
            pltpu.VMEM(pair_mask.shape, jnp.int32),
            pltpu.VMEM((channels, 2 * channels), bf16),
            pltpu.SemaphoreType.DMA((3,)),
        ],
    )
    lefts = gather(left, "col", steps)
    right, normed, scale, factors, out_open, gate_factor, upstream = call(
        factors_kernel,
        (wide, flat, flat, jax.ShapeDtypeStruct((4, pairs, channels), f32), flat, flat, flat),
        pair_acts, pair_mask, crop_length, cotangent, in_weights, out_weight,
        smem=(2,), hbm=(0, 1, 3, 4, 5), flops=2 * pairs * channels * 6 * channels,
        scratch=[
            pltpu.VMEM(pair_acts.shape, bf16),
            pltpu.VMEM(pair_mask.shape, jnp.int32),
            pltpu.VMEM(cotangent.shape, bf16),
            pltpu.VMEM(in_weights.shape, bf16),
            pltpu.VMEM(out_weight.shape, bf16),
            pltpu.SemaphoreType.DMA((5,)),
        ],
    )
    order = [0] + steps
    parts = [
        call(
            functools.partial(partial_kernel, [order[at]]), (tile,), crop_length, lefts[at], right, smem=(0,),
            flops=work, scratch=[pltpu.VMEM(wide.shape, f32)],
        )[0]
        for at in range(n - 2)
    ]
    total, *parts = call(
        functools.partial(last_partial_kernel, order[-2:], order[:-2], [0] + row_steps),
        (wide,) + (tile,) * (n - 1), crop_length, *lefts[-2:], right, *parts, smem=(0,), flops=work,
        scratch=[pltpu.VMEM(wide.shape, f32), pltpu.VMEM((2,) + wide.shape, bf16)],
    )
    (left_panel,) = call(
        functools.partial(left_panel_kernel, [0] + steps), (panel,), crop_length, *lefts, smem=(0,)
    )
    last = []
    for step, part in zip(row_steps, parts):
        part = swap(part, "row", step)
        if step in row_steps[-2:]:
            last.append(part)
        else:
            (total,) = call(add_kernel, (wide,), total, part, flops=wait)
    tri_normed, tri_grad = call(
        triangle_kernel, (flat, tile), total, *last, upstream, flops=20 * pairs * channels,
    )
    grads = gather(tri_grad, "row", gather_steps)
    update, partial = call(
        update_kernel, (tile, flat), tri_normed, out_open, gate_factor, in_weights, out_weight,
        flops=4 * pairs * channels * channels,
    )
    means, slopes = call(
        slopes_kernel, (jax.ShapeDtypeStruct((8, 2 * channels), f32), jax.ShapeDtypeStruct((pairs, 2 * channels), f32)),
        normed, in_weights,
    )
    (right_grad,) = call(functools.partial(right_grad_kernel, [0]), (wide,), left_panel, tri_grad)
    terms, before = [], (partial, right_grad, slopes)
    for grad in grads[:-1]:
        before = call(
            left_terms_kernel, (tile,), grad, right, *before,
            scratch=[pltpu.VMEM((pairs, channels), f32)], flops=work,
        )
        terms += before
    total, *terms = call(
        functools.partial(last_terms_kernel, [0] + gather_steps[:-1], gather_steps[-1], [0] + steps),
        (wide,) + (tile,) * (n - 1), grads[-1], right, *terms, flops=work,
        scratch=[pltpu.VMEM(tile.shape, bf16), pltpu.VMEM((pairs, channels), f32)],
    )
    last = []
    for step, term in zip(steps, terms):
        term = swap(term, "col", step)
        if step in steps[-2:]:
            last.append(term)
        else:
            (total,) = call(add_kernel, (wide,), total, term, flops=wait)
    (done,) = call(
        functools.partial(right_back_kernel, gather_steps), (flat,),
        left_panel, *grads[1:], right_grad, factors, in_weights, partial, normed, scale,
        scratch=[pltpu.VMEM(wide.shape, f32)],
    )
    (pair_grad,) = call(
        back_kernel, (tile,), total, *last, normed, scale, factors, done, means, slopes, in_weights,
        flops=2 * pairs * channels * 2 * channels,
    )
    return (update, pair_grad)


def solution(mesh):
    return jax.shard_map(
        local,
        mesh=mesh,
        in_specs=(
            P(("group", "row"), "col", None),
            P(("group", "row"), "col"),
            P("group"),
            P(("group", "row"), "col", None),
            P(),
            P(),
        ),
        out_specs=(P(("group", "row"), "col", None), P(("group", "row"), "col", None)),
        check_vma=False,
    )
```

```python
import functools

import jax
import jax.numpy as jnp
from jax import lax
from jax.experimental import pallas as pl
from jax.experimental.pallas import tpu as pltpu
from jax.sharding import PartitionSpec as P

epsilon = 1e-05
f32 = jnp.float32
bf16 = jnp.bfloat16


def mean_lanes(values):
    return jnp.sum(values, axis=-1, keepdims=True) * (1.0 / values.shape[-1])


def normalize(values):
    center = values - mean_lanes(values)
    variance = mean_lanes(center * center)
    scale = lax.rsqrt(variance + epsilon)
    return (center * scale, scale)


def normalize_back(normed, scale, upstream):
    average = mean_lanes(upstream)
    project = mean_lanes(upstream * normed)
    return scale * (upstream - average - normed * project)


def sigmoid(values):
    return 1.0 / (1.0 + jnp.exp(-values))


def dot(a, b):
    return jnp.dot(a, b, preferred_element_type=f32)


def dot_t(a, b):
    return lax.dot_general(a, b, (((1,), (1,)), ((), ())), preferred_element_type=f32)


def live_pairs(crop_ref, row, col, shape):
    rows = row * shape[0] + lax.broadcasted_iota(jnp.int32, shape, 0)
    cols = col * shape[1] + lax.broadcasted_iota(jnp.int32, shape, 1)
    return jnp.where(jnp.maximum(rows, cols) < crop_ref[0], 1.0, 0.0)


def spread(mask, channels):
    size = mask.shape[0]
    shape = (size, size, size)
    diagonal = lax.broadcasted_iota(jnp.int32, shape, 1) == lax.broadcasted_iota(jnp.int32, shape, 2)
    picked = jnp.where(diagonal, jnp.broadcast_to(mask[:, None, :], shape), 0.0)
    rows = jnp.sum(picked, axis=-1, keepdims=True)
    return jnp.broadcast_to(rows, (size, size, channels)).reshape(size * size, channels)


def start_copies(sems, *pairs):
    copies = [pltpu.make_async_copy(src, dst, sems.at[n]) for n, (src, dst) in enumerate(pairs)]
    for copy in copies:
        copy.start()
    return copies


def gated(projected, block, keep):
    channels = keep.shape[1]
    value = projected[:, block * channels : (block + 1) * channels]
    opened = sigmoid(projected[:, (block + 1) * channels : (block + 2) * channels])
    return (opened * value * keep).astype(bf16), opened, value


def left_kernel(acts_in, mask_in, weights_in, left_ref, acts_ref, mask_ref, weights_ref, sems):
    size, _, channels = acts_ref.shape
    copies = start_copies(
        sems, (acts_in, acts_ref), (weights_in.at[:, pl.ds(0, 2 * channels)], weights_ref), (mask_in, mask_ref),
    )
    copies[0].wait()
    normed, _ = normalize(acts_ref[...].astype(f32).reshape(size * size, channels))
    normed = normed.astype(bf16)
    for copy in copies[1:]:
        copy.wait()
    left, _, _ = gated(dot(normed, weights_ref[...]), 0, spread(mask_ref[...].astype(f32), channels))
    left_ref[...] = left.reshape(size, size, channels)


def factors_kernel(
    acts_in, mask_in, crop_ref, cotangent_in, weights_in, out_weight_in,
    right_ref, normed_ref, scale_ref, factor_ref, open_ref, gate_factor_ref, upstream_ref,
    acts_ref, mask_ref, cotangent_ref, weights_ref, out_weight_ref, sems,
):
    copies = start_copies(
        sems, (acts_in, acts_ref), (weights_in, weights_ref), (mask_in, mask_ref),
        (cotangent_in, cotangent_ref), (out_weight_in, out_weight_ref),
    )
    size, _, channels = acts_ref.shape
    pairs = size * size
    copies[0].wait()
    normed, scale = normalize(acts_ref[...].astype(f32).reshape(pairs, channels))
    normed_ref[...] = normed
    scale_ref[...] = jnp.broadcast_to(scale, (pairs, channels))
    for copy in copies[1:]:
        copy.wait()
    projected = dot(normed.astype(bf16), weights_ref[...])
    live = live_pairs(crop_ref, lax.axis_index("row"), lax.axis_index("col"), (size, size))
    keep = spread(mask_ref[...].astype(f32) * live, channels)
    for block in (0, 2):
        tile, opened, value = gated(projected, block, keep)
        factor_ref[block] = keep * opened
        factor_ref[block + 1] = keep * value * opened * (1.0 - opened)
    right_ref[...] = tile.astype(f32).reshape(size, size, channels)
    out_open = sigmoid(projected[:, 4 * channels :])
    cotangent = cotangent_ref[...].astype(f32).reshape(pairs, channels)
    lin_grad = (cotangent * out_open).astype(bf16)
    open_ref[...] = out_open
    gate_factor_ref[...] = cotangent * out_open * (1.0 - out_open)
    upstream = dot_t(lin_grad, out_weight_ref[...])
    upstream_ref[...] = upstream - mean_lanes(upstream)


def weighted_sums(weights, start, terms, out, base=None):
    def step(k, _):
        total = weights[start + k, pl.ds(0, 1), :] * terms[0]
        for n in range(1, len(terms)):
            total = total + weights[start + k, pl.ds(n, 1), :] * terms[n]
        if base is not None:
            total = total + base[k]
        out[k] = total.astype(out.dtype)
        return 0

    lax.fori_loop(0, out.shape[0], step, 0, unroll=16)


def left_panel_kernel(steps, crop_ref, *refs):
    row, col, panel = lax.axis_index("row"), lax.axis_index("col"), refs[-1]
    size, _, channels = refs[0].shape
    rows = row * size + lax.broadcasted_iota(jnp.int32, (size, 1, channels), 0)
    row_live = jnp.where(rows < crop_ref[0], 1.0, 0.0)
    for step, ref in zip(steps, refs):
        place = col ^ step
        cols = place * size + lax.broadcasted_iota(jnp.int32, (1, size, channels), 1)
        col_live = jnp.where(cols < crop_ref[0], 1.0, 0.0)
        panel[pl.ds(place * size, size)] = ref[...].astype(f32) * (row_live * col_live)


def partial_kernel(steps, crop_ref, *refs):
    count = len(steps)
    lefts, right_ref, outs, left = refs[:count], refs[count], refs[count + 1 : -1], refs[-1]
    size, _, channels = right_ref.shape
    rows = lax.axis_index("row") * size + lax.broadcasted_iota(jnp.int32, (size, 1, channels), 0)
    row_live = jnp.where(rows < crop_ref[0], 1.0, 0.0)
    for step, left_ref, out in zip(steps, lefts, outs):
        cols = (lax.axis_index("col") ^ step) * size + lax.broadcasted_iota(jnp.int32, (1, size, channels), 1)
        left[...] = left_ref[...].astype(f32) * (row_live * jnp.where(cols < crop_ref[0], 1.0, 0.0))

        def add(k, sums):
            other = right_ref[k]
            return tuple(sums[i] + left[k, pl.ds(i, 1), :] * other for i in range(size))

        zero = jnp.zeros((size, channels), f32)
        sums = lax.fori_loop(0, size, add, (zero,) * size, unroll=16)
        for i in range(size):
            out[i] = sums[i].astype(out.dtype)


def pick_kernel(steps, *refs):
    here = lax.axis_index("row") ^ lax.axis_index("col")
    tiles, outs = refs[: len(steps)], refs[len(steps) :]
    for step, out in zip(steps, outs):
        for other, tile in enumerate(tiles):

            @pl.when((here ^ step) == other)
            def _():
                out[...] = tile[...].astype(out.dtype)


def last_partial_kernel(steps, early, row_steps, crop_ref, *refs):
    count, known = len(steps), len(early)
    left, parts = refs[-2:]
    partial_kernel(steps, crop_ref, *refs[: count + 1], *(parts.at[at] for at in range(count)), left)
    tiles = dict(zip(early, refs[count + 1 : count + 1 + known]))
    tiles.update((step, parts.at[at]) for at, step in enumerate(steps))
    pick_kernel(row_steps, *(tiles[step] for step in range(count + known)), *refs[count + 1 + known : -2])


def triangle_kernel(base, *refs):
    *tiles, upstream_ref, tri_normed_ref, grad_ref = refs
    size = grad_ref.shape[0]
    for i in range(size):
        total = base[i]
        for ref in tiles:
            total = total + ref[i].astype(f32)
        here = pl.ds(i * size, size)
        upstream = upstream_ref[here, :]
        center = total - mean_lanes(total)
        scale = lax.rsqrt(mean_lanes(center * center) + epsilon)
        tri_normed = center * scale
        tri_normed_ref[here, :] = tri_normed
        project = mean_lanes(center * upstream) * scale
        grad_ref[i] = (scale * (upstream - tri_normed * project)).astype(bf16)


def left_terms_kernel(grad_ref, right, *refs):
    out, grad = refs[-2:]
    size, _, channels = out.shape
    grad[...] = grad_ref[...].astype(f32).reshape(size * size, channels)
    weighted_sums(right, 0, [grad[pl.ds(j, size, stride=size), :] for j in range(size)], out)


def last_terms_kernel(early, last, steps, grad_ref, right, *refs):
    known = len(early)
    term, grad = refs[-2:]
    left_terms_kernel(grad_ref, right, term, grad)
    tiles = dict(zip(early, refs[:known]))
    tiles[last] = term
    pick_kernel(steps, *(tiles[step] for step in range(known + 1)), *refs[known:-2])


def right_grad_kernel(steps, panel, *refs):
    out, base = refs[-1], refs[len(steps)] if len(refs) > len(steps) + 1 else None
    size = out.shape[0]
    for step, grad in zip(steps, refs):
        start = (lax.axis_index("row") ^ step) * size
        weighted_sums(panel, start, [grad[i].astype(f32) for i in range(size)], out, base)
        base = out


def right_back_kernel(steps, panel, *refs):
    factor_ref, weights_ref, share_ref, normed_ref, scale_ref, out, right_ref = refs[-7:]
    right_grad_kernel(steps, panel, *refs[: len(steps) + 1], right_ref)
    pairs, channels = out.shape
    right = right_ref[...].reshape(pairs, channels)
    grads = jnp.concatenate([(right * factor_ref[block]).astype(bf16) for block in (2, 3)], axis=1)
    share = share_ref[...] + dot_t(grads, weights_ref[:, 2 * channels : 4 * channels])
    out[...] = normalize_back(normed_ref[...], scale_ref[...], share)


def slopes_kernel(normed_ref, weights_ref, mean_ref, slope_ref):
    channels = normed_ref.shape[1]
    weights = weights_ref[:, : 2 * channels].astype(f32)
    mean = jnp.sum(weights, axis=0, keepdims=True) * (1.0 / channels)
    mean_ref[...] = jnp.broadcast_to(mean, mean_ref.shape)
    slope = jnp.dot(normed_ref[...], weights, precision=lax.Precision.HIGHEST, preferred_element_type=f32)
    slope_ref[...] = slope * (1.0 / channels)


def add_kernel(base, tile_ref, out):
    out[...] = base[...] + tile_ref[...].astype(f32)


def update_kernel(
    tri_normed_ref, open_ref, gate_factor_ref, weights_ref, out_weight_ref, update_ref, normed_grad_ref
):
    size, _, channels = update_ref.shape
    linear = dot(tri_normed_ref[...].astype(bf16), out_weight_ref[...])
    update = (open_ref[...] * linear).astype(bf16)
    update_ref[...] = update.reshape(size, size, channels)
    out_gate_grad = (gate_factor_ref[...] * linear).astype(bf16)
    normed_grad_ref[...] = dot_t(out_gate_grad, weights_ref[:, 4 * channels :])


def back_kernel(base, *refs):
    *tiles, normed_ref, scale_ref, factor_ref, done_ref, mean_ref, slope_ref, weights_ref, out = refs
    size, _, channels = out.shape
    pairs = size * size
    left = base[...]
    for ref in tiles:
        left = left + ref[...].astype(f32)
    left = left.reshape(pairs, channels)
    grads = jnp.concatenate([(left * factor_ref[block]).astype(bf16) for block in (0, 1)], axis=1)
    normed_grad = dot_t(grads, weights_ref[:, : 2 * channels])
    wide_grads = grads.astype(f32)
    average = jnp.sum(wide_grads * mean_ref[0:1, :], axis=-1, keepdims=True)
    project = jnp.sum(wide_grads * slope_ref[...], axis=-1, keepdims=True)
    back = done_ref[...] + scale_ref[...] * (normed_grad - average - normed_ref[...] * project)
    out[...] = back.astype(bf16).reshape(size, size, channels)


def call(kernel, outs, *args, scratch=(), flops=0, smem=(), hbm=()):
    spec = pl.BlockSpec(memory_space=pltpu.VMEM)
    total = sum(a.size * a.dtype.itemsize for a in (*args, *outs))
    specs = [spec] * len(args)
    for n in smem:
        specs[n] = pl.BlockSpec(memory_space=pltpu.SMEM)
    args = list(args)
    for n in hbm:
        specs[n] = pl.BlockSpec(memory_space=pltpu.HBM)
        args[n] = pltpu.with_memory_space_constraint(args[n], pltpu.HBM)
    return pl.pallas_call(
        kernel,
        out_shape=tuple(outs),
        in_specs=specs,
        out_specs=(spec,) * len(outs),
        scratch_shapes=scratch,
        compiler_params=pltpu.CompilerParams(vmem_limit_bytes=24 * 2**20),
        cost_estimate=pl.CostEstimate(flops=flops, bytes_accessed=total if flops else 0, transcendentals=0),
    )(*args)


def local(pair_acts, pair_mask, crop_length, cotangent, in_weights, out_weight):
    size, _, channels = pair_acts.shape
    pairs = size * size
    n = lax.axis_size("row")
    tile = jax.ShapeDtypeStruct((size, size, channels), bf16)
    flat = jax.ShapeDtypeStruct((pairs, channels), f32)

    wide = jax.ShapeDtypeStruct((size, size, channels), f32)
    panel = jax.ShapeDtypeStruct((n * size, size, channels), f32)
    work = 2 * size * pairs * channels
    wait = 2**31
    steps = [step for bit in range(n.bit_length() - 2, -1, -1) for step in range(2**bit, 2 ** (bit + 1))]
    row_steps = steps
    gather_steps = [n - 1] + list(range(1, n - 1))


    def swap(values, axis, step):
        return lax.ppermute(values, axis, [(a, a ^ step) for a in range(n)])

    def gather(values, axis, steps):
        return [values] + [swap(values, axis, step) for step in steps]

    (left,) = call(
        left_kernel, (tile,), pair_acts, pair_mask, in_weights,
        hbm=(0, 1, 2), flops=2 * pairs * channels * 2 * channels,
        scratch=[
            pltpu.VMEM(pair_acts.shape, bf16),
            pltpu.VMEM(pair_mask.shape, jnp.int32),
            pltpu.VMEM((channels, 2 * channels), bf16),
            pltpu.SemaphoreType.DMA((3,)),
        ],
    )
    lefts = gather(left, "col", steps)
    right, normed, scale, factors, out_open, gate_factor, upstream = call(
        factors_kernel,
        (wide, flat, flat, jax.ShapeDtypeStruct((4, pairs, channels), f32), flat, flat, flat),
        pair_acts, pair_mask, crop_length, cotangent, in_weights, out_weight,
        smem=(2,), hbm=(0, 1, 3, 4, 5), flops=2 * pairs * channels * 6 * channels,
        scratch=[
            pltpu.VMEM(pair_acts.shape, bf16),
            pltpu.VMEM(pair_mask.shape, jnp.int32),
            pltpu.VMEM(cotangent.shape, bf16),
            pltpu.VMEM(in_weights.shape, bf16),
            pltpu.VMEM(out_weight.shape, bf16),
            pltpu.SemaphoreType.DMA((5,)),
        ],
    )
    order = [0] + steps
    parts = [
        call(
            functools.partial(partial_kernel, [order[at]]), (tile,), crop_length, lefts[at], right, smem=(0,),
            flops=work, scratch=[pltpu.VMEM(wide.shape, f32)],
        )[0]
        for at in range(n - 2)
    ]
    total, *parts = call(
        functools.partial(last_partial_kernel, order[-2:], order[:-2], [0] + row_steps),
        (wide,) + (tile,) * (n - 1), crop_length, *lefts[-2:], right, *parts, smem=(0,), flops=work,
        scratch=[pltpu.VMEM(wide.shape, f32), pltpu.VMEM((2,) + wide.shape, bf16)],
    )
    (left_panel,) = call(
        functools.partial(left_panel_kernel, [0] + steps), (panel,), crop_length, *lefts, smem=(0,)
    )
    last = []
    for step, part in zip(row_steps, parts):
        part = swap(part, "row", step)
        if step in row_steps[-2:]:
            last.append(part)
        else:
            (total,) = call(add_kernel, (wide,), total, part, flops=wait)
    tri_normed, tri_grad = call(
        triangle_kernel, (flat, tile), total, *last, upstream, flops=20 * pairs * channels,
    )
    grads = gather(tri_grad, "row", gather_steps)
    update, partial = call(
        update_kernel, (tile, flat), tri_normed, out_open, gate_factor, in_weights, out_weight,
        flops=4 * pairs * channels * channels,
    )
    means, slopes = call(
        slopes_kernel, (jax.ShapeDtypeStruct((8, 2 * channels), f32), jax.ShapeDtypeStruct((pairs, 2 * channels), f32)),
        normed, in_weights,
    )
    (right_grad,) = call(functools.partial(right_grad_kernel, [0]), (wide,), left_panel, tri_grad)
    terms, before = [], (partial, right_grad, slopes)
    for grad in grads[:-1]:
        before = call(
            left_terms_kernel, (tile,), grad, right, *before,
            scratch=[pltpu.VMEM((pairs, channels), f32)], flops=work,
        )
        terms += before
    total, *terms = call(
        functools.partial(last_terms_kernel, [0] + gather_steps[:-1], gather_steps[-1], [0] + steps),
        (wide,) + (tile,) * (n - 1), grads[-1], right, *terms, flops=work,
        scratch=[pltpu.VMEM(tile.shape, bf16), pltpu.VMEM((pairs, channels), f32)],
    )
    last = []
    for step, term in zip(steps, terms):
        term = swap(term, "col", step)
        if step in steps[-2:]:
            last.append(term)
        else:
            (total,) = call(add_kernel, (wide,), total, term, flops=wait)
    (done,) = call(
        functools.partial(right_back_kernel, gather_steps), (flat,),
        left_panel, *grads[1:], right_grad, factors, in_weights, partial, normed, scale,
        scratch=[pltpu.VMEM(wide.shape, f32)],
    )
    (pair_grad,) = call(
        back_kernel, (tile,), total, *last, normed, scale, factors, done, means, slopes, in_weights,
        flops=2 * pairs * channels * 2 * channels,
    )
    return (update, pair_grad)


def solution(mesh):
    return jax.shard_map(
        local,
        mesh=mesh,
        in_specs=(
            P(("group", "row"), "col", None),
            P(("group", "row"), "col"),
            P("group"),
            P(("group", "row"), "col", None),
            P(),
            P(),
        ),
        out_specs=(P(("group", "row"), "col", None), P(("group", "row"), "col", None)),
        check_vma=False,
    )
```

```python
import functools

import jax
import jax.numpy as jnp
from jax import lax
from jax.experimental import pallas as pl
from jax.experimental.pallas import tpu as pltpu
from jax.sharding import PartitionSpec as P

epsilon = 1e-05
f32 = jnp.float32
bf16 = jnp.bfloat16


def mean_lanes(values):
    return jnp.sum(values, axis=-1, keepdims=True) * (1.0 / values.shape[-1])


def normalize(values):
    center = values - mean_lanes(values)
    variance = mean_lanes(center * center)
    scale = lax.rsqrt(variance + epsilon)
    return (center * scale, scale)


def normalize_back(normed, scale, upstream):
    average = mean_lanes(upstream)
    project = mean_lanes(upstream * normed)
    return scale * (upstream - average - normed * project)


def sigmoid(values):
    return 1.0 / (1.0 + jnp.exp(-values))


def dot(a, b):
    return jnp.dot(a, b, preferred_element_type=f32)


def dot_t(a, b):
    return lax.dot_general(a, b, (((1,), (1,)), ((), ())), preferred_element_type=f32)


def live_pairs(crop_ref, row, col, shape):
    rows = row * shape[0] + lax.broadcasted_iota(jnp.int32, shape, 0)
    cols = col * shape[1] + lax.broadcasted_iota(jnp.int32, shape, 1)
    return jnp.where(jnp.maximum(rows, cols) < crop_ref[0], 1.0, 0.0)


def spread(mask, channels):
    size = mask.shape[0]
    shape = (size, size, size)
    diagonal = lax.broadcasted_iota(jnp.int32, shape, 1) == lax.broadcasted_iota(jnp.int32, shape, 2)
    picked = jnp.where(diagonal, jnp.broadcast_to(mask[:, None, :], shape), 0.0)
    rows = jnp.sum(picked, axis=-1, keepdims=True)
    return jnp.broadcast_to(rows, (size, size, channels)).reshape(size * size, channels)


def start_copies(sems, *pairs):
    copies = [pltpu.make_async_copy(src, dst, sems.at[n]) for n, (src, dst) in enumerate(pairs)]
    for copy in copies:
        copy.start()
    return copies


def gated(projected, block, keep):
    channels = keep.shape[1]
    value = projected[:, block * channels : (block + 1) * channels]
    opened = sigmoid(projected[:, (block + 1) * channels : (block + 2) * channels])
    return (opened * value * keep).astype(bf16), opened, value


def left_kernel(acts_in, mask_in, weights_in, left_ref, acts_ref, mask_ref, weights_ref, sems):
    size, _, channels = acts_ref.shape
    copies = start_copies(
        sems, (acts_in, acts_ref), (weights_in.at[:, pl.ds(0, 2 * channels)], weights_ref), (mask_in, mask_ref),
    )
    copies[0].wait()
    normed, _ = normalize(acts_ref[...].astype(f32).reshape(size * size, channels))
    normed = normed.astype(bf16)
    for copy in copies[1:]:
        copy.wait()
    left, _, _ = gated(dot(normed, weights_ref[...]), 0, spread(mask_ref[...].astype(f32), channels))
    left_ref[...] = left.reshape(size, size, channels)


def factors_kernel(
    acts_in, mask_in, crop_ref, cotangent_in, weights_in, out_weight_in,
    right_ref, normed_ref, scale_ref, factor_ref, open_ref, gate_factor_ref, upstream_ref,
    acts_ref, mask_ref, cotangent_ref, weights_ref, out_weight_ref, sems,
):
    copies = start_copies(
        sems, (acts_in, acts_ref), (weights_in, weights_ref), (mask_in, mask_ref),
        (cotangent_in, cotangent_ref), (out_weight_in, out_weight_ref),
    )
    size, _, channels = acts_ref.shape
    pairs = size * size
    copies[0].wait()
    normed, scale = normalize(acts_ref[...].astype(f32).reshape(pairs, channels))
    normed_ref[...] = normed
    scale_ref[...] = jnp.broadcast_to(scale, (pairs, channels))
    for copy in copies[1:]:
        copy.wait()
    projected = dot(normed.astype(bf16), weights_ref[...])
    live = live_pairs(crop_ref, lax.axis_index("row"), lax.axis_index("col"), (size, size))
    keep = spread(mask_ref[...].astype(f32) * live, channels)
    for block in (0, 2):
        tile, opened, value = gated(projected, block, keep)
        factor_ref[block] = keep * opened
        factor_ref[block + 1] = keep * value * opened * (1.0 - opened)
    right_ref[...] = tile.astype(f32).reshape(size, size, channels)
    out_open = sigmoid(projected[:, 4 * channels :])
    cotangent = cotangent_ref[...].astype(f32).reshape(pairs, channels)
    lin_grad = (cotangent * out_open).astype(bf16)
    open_ref[...] = out_open
    gate_factor_ref[...] = cotangent * out_open * (1.0 - out_open)
    upstream = dot_t(lin_grad, out_weight_ref[...])
    upstream_ref[...] = upstream - mean_lanes(upstream)


def weighted_sums(weights, start, terms, out, base=None):
    def step(k, _):
        total = weights[start + k, pl.ds(0, 1), :] * terms[0]
        for n in range(1, len(terms)):
            total = total + weights[start + k, pl.ds(n, 1), :] * terms[n]
        if base is not None:
            total = total + base[k]
        out[k] = total.astype(out.dtype)
        return 0

    lax.fori_loop(0, out.shape[0], step, 0, unroll=16)


def left_panel_kernel(steps, crop_ref, *refs):
    row, col, panel = lax.axis_index("row"), lax.axis_index("col"), refs[-1]
    size, _, channels = refs[0].shape
    rows = row * size + lax.broadcasted_iota(jnp.int32, (size, 1, channels), 0)
    row_live = jnp.where(rows < crop_ref[0], 1.0, 0.0)
    for step, ref in zip(steps, refs):
        place = col ^ step
        cols = place * size + lax.broadcasted_iota(jnp.int32, (1, size, channels), 1)
        col_live = jnp.where(cols < crop_ref[0], 1.0, 0.0)
        panel[pl.ds(place * size, size)] = ref[...].astype(f32) * (row_live * col_live)


def partial_kernel(steps, crop_ref, *refs):
    count = len(steps)
    lefts, right_ref, outs, left = refs[:count], refs[count], refs[count + 1 : -1], refs[-1]
    size, _, channels = right_ref.shape
    rows = lax.axis_index("row") * size + lax.broadcasted_iota(jnp.int32, (size, 1, channels), 0)
    row_live = jnp.where(rows < crop_ref[0], 1.0, 0.0)
    for step, left_ref, out in zip(steps, lefts, outs):
        cols = (lax.axis_index("col") ^ step) * size + lax.broadcasted_iota(jnp.int32, (1, size, channels), 1)
        left[...] = left_ref[...].astype(f32) * (row_live * jnp.where(cols < crop_ref[0], 1.0, 0.0))

        def add(k, sums):
            other = right_ref[k]
            return tuple(sums[i] + left[k, pl.ds(i, 1), :] * other for i in range(size))

        zero = jnp.zeros((size, channels), f32)
        sums = lax.fori_loop(0, size, add, (zero,) * size, unroll=16)
        for i in range(size):
            out[i] = sums[i].astype(out.dtype)


def pick_kernel(steps, *refs):
    here = lax.axis_index("row") ^ lax.axis_index("col")
    tiles, outs = refs[: len(steps)], refs[len(steps) :]
    for step, out in zip(steps, outs):
        for other, tile in enumerate(tiles):

            @pl.when((here ^ step) == other)
            def _():
                out[...] = tile[...].astype(out.dtype)


def last_partial_kernel(steps, early, row_steps, crop_ref, *refs):
    count, known = len(steps), len(early)
    left, parts = refs[-2:]
    partial_kernel(steps, crop_ref, *refs[: count + 1], *(parts.at[at] for at in range(count)), left)
    tiles = dict(zip(early, refs[count + 1 : count + 1 + known]))
    tiles.update((step, parts.at[at]) for at, step in enumerate(steps))
    pick_kernel(row_steps, *(tiles[step] for step in range(count + known)), *refs[count + 1 + known : -2])


def triangle_kernel(base, *refs):
    *tiles, upstream_ref, tri_normed_ref, grad_ref = refs
    size = grad_ref.shape[0]
    for i in range(size):
        total = base[i]
        for ref in tiles:
            total = total + ref[i].astype(f32)
        here = pl.ds(i * size, size)
        upstream = upstream_ref[here, :]
        center = total - mean_lanes(total)
        scale = lax.rsqrt(mean_lanes(center * center) + epsilon)
        tri_normed = center * scale
        tri_normed_ref[here, :] = tri_normed
        project = mean_lanes(center * upstream) * scale
        grad_ref[i] = (scale * (upstream - tri_normed * project)).astype(bf16)


def left_terms_kernel(grad_ref, right, *refs):
    out, grad = refs[-2:]
    size, _, channels = out.shape
    grad[...] = grad_ref[...].astype(f32).reshape(size * size, channels)
    weighted_sums(right, 0, [grad[pl.ds(j, size, stride=size), :] for j in range(size)], out)


def last_terms_kernel(early, last, steps, grad_ref, right, *refs):
    known = len(early)
    term, grad = refs[-2:]
    left_terms_kernel(grad_ref, right, term, grad)
    tiles = dict(zip(early, refs[:known]))
    tiles[last] = term
    pick_kernel(steps, *(tiles[step] for step in range(known + 1)), *refs[known:-2])


def right_grad_kernel(steps, panel, *refs):
    out, base = refs[-1], refs[len(steps)] if len(refs) > len(steps) + 1 else None
    size = out.shape[0]
    for step, grad in zip(steps, refs):
        start = (lax.axis_index("row") ^ step) * size
        weighted_sums(panel, start, [grad[i].astype(f32) for i in range(size)], out, base)
        base = out


def right_back_kernel(steps, panel, *refs):
    factor_ref, weights_ref, share_ref, normed_ref, scale_ref, out, right_ref = refs[-7:]
    right_grad_kernel(steps, panel, *refs[: len(steps) + 1], right_ref)
    pairs, channels = out.shape
    right = right_ref[...].reshape(pairs, channels)
    grads = jnp.concatenate([(right * factor_ref[block]).astype(bf16) for block in (2, 3)], axis=1)
    share = share_ref[...] + dot_t(grads, weights_ref[:, 2 * channels : 4 * channels])
    out[...] = normalize_back(normed_ref[...], scale_ref[...], share)


def slopes_kernel(normed_ref, weights_ref, mean_ref, slope_ref, turned_ref):
    channels = normed_ref.shape[1]
    weights = weights_ref[:, : 2 * channels].astype(f32)
    mean = jnp.sum(weights, axis=0, keepdims=True) * (1.0 / channels)
    mean_ref[...] = jnp.broadcast_to(mean, mean_ref.shape)
    slope = jnp.dot(normed_ref[...], weights, precision=lax.Precision.HIGHEST, preferred_element_type=f32)
    slope_ref[...] = slope * (1.0 / channels)
    turned_ref[...] = weights.T.astype(bf16)


def add_kernel(base, tile_ref, out):
    out[...] = base[...] + tile_ref[...].astype(f32)


def update_kernel(
    tri_normed_ref, open_ref, gate_factor_ref, weights_ref, out_weight_ref, update_ref, normed_grad_ref
):
    size, _, channels = update_ref.shape
    linear = dot(tri_normed_ref[...].astype(bf16), out_weight_ref[...])
    update = (open_ref[...] * linear).astype(bf16)
    update_ref[...] = update.reshape(size, size, channels)
    out_gate_grad = (gate_factor_ref[...] * linear).astype(bf16)
    normed_grad_ref[...] = dot_t(out_gate_grad, weights_ref[:, 4 * channels :])


def back_kernel(base, *refs):
    *tiles, normed_ref, scale_ref, factor_ref, done_ref, mean_ref, slope_ref, turned_ref, out = refs
    size, _, channels = out.shape
    pairs = size * size
    left = base[...]
    for ref in tiles:
        left = left + ref[...].astype(f32)
    left = left.reshape(pairs, channels)
    grads = jnp.concatenate([(left * factor_ref[block]).astype(bf16) for block in (0, 1)], axis=1)
    normed_grad = dot(grads, turned_ref[...])
    wide_grads = grads.astype(f32)
    average = jnp.sum(wide_grads * mean_ref[0:1, :], axis=-1, keepdims=True)
    project = jnp.sum(wide_grads * slope_ref[...], axis=-1, keepdims=True)
    back = done_ref[...] + scale_ref[...] * (normed_grad - average - normed_ref[...] * project)
    out[...] = back.astype(bf16).reshape(size, size, channels)


def call(kernel, outs, *args, scratch=(), flops=0, smem=(), hbm=()):
    spec = pl.BlockSpec(memory_space=pltpu.VMEM)
    total = sum(a.size * a.dtype.itemsize for a in (*args, *outs))
    specs = [spec] * len(args)
    for n in smem:
        specs[n] = pl.BlockSpec(memory_space=pltpu.SMEM)
    args = list(args)
    for n in hbm:
        specs[n] = pl.BlockSpec(memory_space=pltpu.HBM)
        args[n] = pltpu.with_memory_space_constraint(args[n], pltpu.HBM)
    return pl.pallas_call(
        kernel,
        out_shape=tuple(outs),
        in_specs=specs,
        out_specs=(spec,) * len(outs),
        scratch_shapes=scratch,
        compiler_params=pltpu.CompilerParams(vmem_limit_bytes=24 * 2**20),
        cost_estimate=pl.CostEstimate(flops=flops, bytes_accessed=total if flops else 0, transcendentals=0),
    )(*args)


def local(pair_acts, pair_mask, crop_length, cotangent, in_weights, out_weight):
    size, _, channels = pair_acts.shape
    pairs = size * size
    n = lax.axis_size("row")
    tile = jax.ShapeDtypeStruct((size, size, channels), bf16)
    flat = jax.ShapeDtypeStruct((pairs, channels), f32)

    wide = jax.ShapeDtypeStruct((size, size, channels), f32)
    panel = jax.ShapeDtypeStruct((n * size, size, channels), f32)
    work = 2 * size * pairs * channels
    wait = 2**31
    steps = [step for bit in range(n.bit_length() - 2, -1, -1) for step in range(2**bit, 2 ** (bit + 1))]
    row_steps = steps
    gather_steps = [n - 1] + list(range(1, n - 1))


    def swap(values, axis, step):
        return lax.ppermute(values, axis, [(a, a ^ step) for a in range(n)])

    def gather(values, axis, steps):
        return [values] + [swap(values, axis, step) for step in steps]

    (left,) = call(
        left_kernel, (tile,), pair_acts, pair_mask, in_weights,
        hbm=(0, 1, 2), flops=2 * pairs * channels * 2 * channels,
        scratch=[
            pltpu.VMEM(pair_acts.shape, bf16),
            pltpu.VMEM(pair_mask.shape, jnp.int32),
            pltpu.VMEM((channels, 2 * channels), bf16),
            pltpu.SemaphoreType.DMA((3,)),
        ],
    )
    lefts = gather(left, "col", steps)
    right, normed, scale, factors, out_open, gate_factor, upstream = call(
        factors_kernel,
        (wide, flat, flat, jax.ShapeDtypeStruct((4, pairs, channels), f32), flat, flat, flat),
        pair_acts, pair_mask, crop_length, cotangent, in_weights, out_weight,
        smem=(2,), hbm=(0, 1, 3, 4, 5), flops=2 * pairs * channels * 6 * channels,
        scratch=[
            pltpu.VMEM(pair_acts.shape, bf16),
            pltpu.VMEM(pair_mask.shape, jnp.int32),
            pltpu.VMEM(cotangent.shape, bf16),
            pltpu.VMEM(in_weights.shape, bf16),
            pltpu.VMEM(out_weight.shape, bf16),
            pltpu.SemaphoreType.DMA((5,)),
        ],
    )
    order = [0] + steps
    parts = [
        call(
            functools.partial(partial_kernel, [order[at]]), (tile,), crop_length, lefts[at], right, smem=(0,),
            flops=work, scratch=[pltpu.VMEM(wide.shape, f32)],
        )[0]
        for at in range(n - 2)
    ]
    total, *parts = call(
        functools.partial(last_partial_kernel, order[-2:], order[:-2], [0] + row_steps),
        (wide,) + (tile,) * (n - 1), crop_length, *lefts[-2:], right, *parts, smem=(0,), flops=work,
        scratch=[pltpu.VMEM(wide.shape, f32), pltpu.VMEM((2,) + wide.shape, bf16)],
    )
    (left_panel,) = call(
        functools.partial(left_panel_kernel, [0] + steps), (panel,), crop_length, *lefts, smem=(0,)
    )
    last = []
    for step, part in zip(row_steps, parts):
        part = swap(part, "row", step)
        if step in row_steps[-2:]:
            last.append(part)
        else:
            (total,) = call(add_kernel, (wide,), total, part, flops=wait)
    tri_normed, tri_grad = call(
        triangle_kernel, (flat, tile), total, *last, upstream, flops=20 * pairs * channels,
    )
    grads = gather(tri_grad, "row", gather_steps)
    update, partial = call(
        update_kernel, (tile, flat), tri_normed, out_open, gate_factor, in_weights, out_weight,
        flops=4 * pairs * channels * channels,
    )
    means, slopes, turned = call(
        slopes_kernel,
        (
            jax.ShapeDtypeStruct((8, 2 * channels), f32),
            jax.ShapeDtypeStruct((pairs, 2 * channels), f32),
            jax.ShapeDtypeStruct((2 * channels, channels), bf16),
        ),
        normed, in_weights,
    )
    (right_grad,) = call(functools.partial(right_grad_kernel, [0]), (wide,), left_panel, tri_grad)
    terms, before = [], (partial, right_grad, slopes)
    for grad in grads[:-1]:
        before = call(
            left_terms_kernel, (tile,), grad, right, *before,
            scratch=[pltpu.VMEM((pairs, channels), f32)], flops=work,
        )
        terms += before
    total, *terms = call(
        functools.partial(last_terms_kernel, [0] + gather_steps[:-1], gather_steps[-1], [0] + steps),
        (wide,) + (tile,) * (n - 1), grads[-1], right, *terms, flops=work,
        scratch=[pltpu.VMEM(tile.shape, bf16), pltpu.VMEM((pairs, channels), f32)],
    )
    last = []
    for step, term in zip(steps, terms):
        term = swap(term, "col", step)
        if step in steps[-2:]:
            last.append(term)
        else:
            (total,) = call(add_kernel, (wide,), total, term, flops=wait)
    (done,) = call(
        functools.partial(right_back_kernel, gather_steps), (flat,),
        left_panel, *grads[1:], right_grad, factors, in_weights, partial, normed, scale,
        scratch=[pltpu.VMEM(wide.shape, f32)],
    )
    (pair_grad,) = call(
        back_kernel, (tile,), total, *last, normed, scale, factors, done, means, slopes, turned,
        flops=2 * pairs * channels * 2 * channels,
    )
    return (update, pair_grad)


def solution(mesh):
    return jax.shard_map(
        local,
        mesh=mesh,
        in_specs=(
            P(("group", "row"), "col", None),
            P(("group", "row"), "col"),
            P("group"),
            P(("group", "row"), "col", None),
            P(),
            P(),
        ),
        out_specs=(P(("group", "row"), "col", None), P(("group", "row"), "col", None)),
        check_vma=False,
    )
```

```python
import functools

import jax
import jax.numpy as jnp
from jax import lax
from jax.experimental import pallas as pl
from jax.experimental.pallas import tpu as pltpu
from jax.sharding import PartitionSpec as P

epsilon = 1e-05
f32 = jnp.float32
bf16 = jnp.bfloat16


def mean_lanes(values):
    return jnp.sum(values, axis=-1, keepdims=True) * (1.0 / values.shape[-1])


def normalize(values):
    center = values - mean_lanes(values)
    variance = mean_lanes(center * center)
    scale = lax.rsqrt(variance + epsilon)
    return (center * scale, scale)


def normalize_back(normed, scale, upstream):
    average = mean_lanes(upstream)
    project = mean_lanes(upstream * normed)
    return scale * (upstream - average - normed * project)


def sigmoid(values):
    return 1.0 / (1.0 + jnp.exp(-values))


def dot(a, b):
    return jnp.dot(a, b, preferred_element_type=f32)


def dot_t(a, b):
    return lax.dot_general(a, b, (((1,), (1,)), ((), ())), preferred_element_type=f32)


def live_pairs(crop_ref, row, col, shape):
    rows = row * shape[0] + lax.broadcasted_iota(jnp.int32, shape, 0)
    cols = col * shape[1] + lax.broadcasted_iota(jnp.int32, shape, 1)
    return jnp.where(jnp.maximum(rows, cols) < crop_ref[0], 1.0, 0.0)


def spread(mask, channels):
    size = mask.shape[0]
    shape = (size, size, size)
    diagonal = lax.broadcasted_iota(jnp.int32, shape, 1) == lax.broadcasted_iota(jnp.int32, shape, 2)
    picked = jnp.where(diagonal, jnp.broadcast_to(mask[:, None, :], shape), 0.0)
    rows = jnp.sum(picked, axis=-1, keepdims=True)
    return jnp.broadcast_to(rows, (size, size, channels)).reshape(size * size, channels)


def start_copies(sems, *pairs):
    copies = [pltpu.make_async_copy(src, dst, sems.at[n]) for n, (src, dst) in enumerate(pairs)]
    for copy in copies:
        copy.start()
    return copies


def gated(projected, block, keep):
    channels = keep.shape[1]
    value = projected[:, block * channels : (block + 1) * channels]
    opened = sigmoid(projected[:, (block + 1) * channels : (block + 2) * channels])
    return (opened * value * keep).astype(bf16), opened, value


def left_kernel(acts_in, mask_in, weights_in, left_ref, acts_ref, mask_ref, weights_ref, sems):
    size, _, channels = acts_ref.shape
    copies = start_copies(
        sems, (acts_in, acts_ref), (weights_in.at[:, pl.ds(0, 2 * channels)], weights_ref), (mask_in, mask_ref),
    )
    copies[0].wait()
    normed, _ = normalize(acts_ref[...].astype(f32).reshape(size * size, channels))
    normed = normed.astype(bf16)
    for copy in copies[1:]:
        copy.wait()
    left, _, _ = gated(dot(normed, weights_ref[...]), 0, spread(mask_ref[...].astype(f32), channels))
    left_ref[...] = left.reshape(size, size, channels)


def factors_kernel(
    acts_in, mask_in, crop_ref, cotangent_in, weights_in, out_weight_in,
    right_ref, normed_ref, scale_ref, factor_ref, open_ref, gate_factor_ref, upstream_ref,
    acts_ref, mask_ref, cotangent_ref, weights_ref, out_weight_ref, sems,
):
    copies = start_copies(
        sems, (acts_in, acts_ref), (weights_in, weights_ref), (mask_in, mask_ref),
        (cotangent_in, cotangent_ref), (out_weight_in, out_weight_ref),
    )
    size, _, channels = acts_ref.shape
    pairs = size * size
    copies[0].wait()
    normed, scale = normalize(acts_ref[...].astype(f32).reshape(pairs, channels))
    normed_ref[...] = normed
    scale_ref[...] = jnp.broadcast_to(scale, (pairs, channels))
    for copy in copies[1:]:
        copy.wait()
    projected = dot(normed.astype(bf16), weights_ref[...])
    live = live_pairs(crop_ref, lax.axis_index("row"), lax.axis_index("col"), (size, size))
    keep = spread(mask_ref[...].astype(f32) * live, channels)
    for block in (0, 2):
        tile, opened, value = gated(projected, block, keep)
        factor_ref[block] = keep * opened
        factor_ref[block + 1] = keep * value * opened * (1.0 - opened)
    right_ref[...] = tile.astype(f32).reshape(size, size, channels)
    out_open = sigmoid(projected[:, 4 * channels :])
    cotangent = cotangent_ref[...].astype(f32).reshape(pairs, channels)
    lin_grad = (cotangent * out_open).astype(bf16)
    open_ref[...] = out_open
    gate_factor_ref[...] = cotangent * out_open * (1.0 - out_open)
    upstream = dot_t(lin_grad, out_weight_ref[...])
    upstream_ref[...] = upstream - mean_lanes(upstream)


def weighted_sums(weights, start, terms, out, base=None):
    def step(k, _):
        total = weights[start + k, pl.ds(0, 1), :] * terms[0]
        for n in range(1, len(terms)):
            total = total + weights[start + k, pl.ds(n, 1), :] * terms[n]
        if base is not None:
            total = total + base[k]
        out[k] = total.astype(out.dtype)
        return 0

    lax.fori_loop(0, out.shape[0], step, 0, unroll=16)


def left_panel_kernel(steps, crop_ref, *refs):
    row, col, panel = lax.axis_index("row"), lax.axis_index("col"), refs[-1]
    size, _, channels = refs[0].shape
    rows = row * size + lax.broadcasted_iota(jnp.int32, (size, 1, channels), 0)
    row_live = jnp.where(rows < crop_ref[0], 1.0, 0.0)
    for step, ref in zip(steps, refs):
        place = col ^ step
        cols = place * size + lax.broadcasted_iota(jnp.int32, (1, size, channels), 1)
        col_live = jnp.where(cols < crop_ref[0], 1.0, 0.0)
        panel[pl.ds(place * size, size)] = ref[...].astype(f32) * (row_live * col_live)


def partial_kernel(steps, crop_ref, *refs):
    count = len(steps)
    lefts, right_ref, outs, left = refs[:count], refs[count], refs[count + 1 : -1], refs[-1]
    size, _, channels = right_ref.shape
    rows = lax.axis_index("row") * size + lax.broadcasted_iota(jnp.int32, (size, 1, channels), 0)
    row_live = jnp.where(rows < crop_ref[0], 1.0, 0.0)
    for step, left_ref, out in zip(steps, lefts, outs):
        cols = (lax.axis_index("col") ^ step) * size + lax.broadcasted_iota(jnp.int32, (1, size, channels), 1)
        left[...] = left_ref[...].astype(f32) * (row_live * jnp.where(cols < crop_ref[0], 1.0, 0.0))

        def add(k, sums):
            other = right_ref[k]
            return tuple(sums[i] + left[k, pl.ds(i, 1), :] * other for i in range(size))

        zero = jnp.zeros((size, channels), f32)
        sums = lax.fori_loop(0, size, add, (zero,) * size, unroll=16)
        for i in range(size):
            out[i] = sums[i].astype(out.dtype)


def pick_kernel(steps, *refs):
    here = lax.axis_index("row") ^ lax.axis_index("col")
    tiles, outs = refs[: len(steps)], refs[len(steps) :]
    for step, out in zip(steps, outs):
        for other, tile in enumerate(tiles):

            @pl.when((here ^ step) == other)
            def _():
                out[...] = tile[...].astype(out.dtype)


def last_partial_kernel(steps, early, row_steps, crop_ref, *refs):
    count, known = len(steps), len(early)
    left, parts = refs[-2:]
    partial_kernel(steps, crop_ref, *refs[: count + 1], *(parts.at[at] for at in range(count)), left)
    tiles = dict(zip(early, refs[count + 1 : count + 1 + known]))
    tiles.update((step, parts.at[at]) for at, step in enumerate(steps))
    pick_kernel(row_steps, *(tiles[step] for step in range(count + known)), *refs[count + 1 + known : -2])


def triangle_kernel(base, *refs):
    *tiles, upstream_ref, tri_normed_ref, grad_ref = refs
    size = grad_ref.shape[0]
    for i in range(size):
        total = base[i]
        for ref in tiles:
            total = total + ref[i].astype(f32)
        here = pl.ds(i * size, size)
        upstream = upstream_ref[here, :]
        center = total - mean_lanes(total)
        scale = lax.rsqrt(mean_lanes(center * center) + epsilon)
        tri_normed = center * scale
        tri_normed_ref[here, :] = tri_normed
        project = mean_lanes(center * upstream) * scale
        grad_ref[i] = (scale * (upstream - tri_normed * project)).astype(bf16)


def left_terms_kernel(grad_ref, right, *refs):
    out, grad = refs[-2:]
    size, _, channels = out.shape
    grad[...] = grad_ref[...].astype(f32).reshape(size * size, channels)
    weighted_sums(right, 0, [grad[pl.ds(j, size, stride=size), :] for j in range(size)], out)


def last_terms_kernel(early, last, steps, grad_ref, right, *refs):
    known = len(early)
    term, grad = refs[-2:]
    left_terms_kernel(grad_ref, right, term, grad)
    tiles = dict(zip(early, refs[:known]))
    tiles[last] = term
    pick_kernel(steps, *(tiles[step] for step in range(known + 1)), *refs[known:-2])


def right_grad_kernel(steps, panel, *refs):
    out, base = refs[-1], refs[len(steps)] if len(refs) > len(steps) + 1 else None
    size = out.shape[0]
    for step, grad in zip(steps, refs):
        start = (lax.axis_index("row") ^ step) * size
        weighted_sums(panel, start, [grad[i].astype(f32) for i in range(size)], out, base)
        base = out


def right_back_kernel(steps, panel, *refs):
    factor_ref, weights_ref, share_ref, normed_ref, scale_ref, out, right_ref = refs[-7:]
    right_grad_kernel(steps, panel, *refs[: len(steps) + 1], right_ref)
    pairs, channels = out.shape
    right = right_ref[...].reshape(pairs, channels)
    grads = jnp.concatenate([(right * factor_ref[block]).astype(bf16) for block in (2, 3)], axis=1)
    share = share_ref[...] + dot_t(grads, weights_ref[:, 2 * channels : 4 * channels])
    out[...] = normalize_back(normed_ref[...], scale_ref[...], share)


def slopes_kernel(normed_ref, weights_ref, mean_ref, slope_ref):
    channels = normed_ref.shape[1]
    weights = weights_ref[:, : 2 * channels].astype(f32)
    mean = jnp.sum(weights, axis=0, keepdims=True) * (1.0 / channels)
    mean_ref[...] = jnp.broadcast_to(mean, mean_ref.shape)
    slope = jnp.dot(normed_ref[...], weights, precision=lax.Precision.HIGHEST, preferred_element_type=f32)
    slope_ref[...] = slope * (1.0 / channels)


def add_kernel(base, tile_ref, out):
    out[...] = base[...] + tile_ref[...].astype(f32)


def update_kernel(
    tri_normed_ref, open_ref, gate_factor_ref, weights_ref, out_weight_ref, update_ref, normed_grad_ref
):
    size, _, channels = update_ref.shape
    linear = dot(tri_normed_ref[...].astype(bf16), out_weight_ref[...])
    update = (open_ref[...] * linear).astype(bf16)
    update_ref[...] = update.reshape(size, size, channels)
    out_gate_grad = (gate_factor_ref[...] * linear).astype(bf16)
    normed_grad_ref[...] = dot_t(out_gate_grad, weights_ref[:, 4 * channels :])


def back_kernel(base, *refs):
    *tiles, normed_ref, scale_ref, factor_ref, done_ref, mean_ref, slope_ref, weights_ref, out = refs
    size, _, channels = out.shape
    pairs = size * size
    left = base[...]
    for ref in tiles:
        left = left + ref[...].astype(f32)
    left = left.reshape(pairs, channels)
    grads = jnp.concatenate([(left * factor_ref[block]).astype(bf16) for block in (0, 1)], axis=1)
    normed_grad = dot_t(grads, weights_ref[:, : 2 * channels])
    wide_grads = grads.astype(f32)
    average = jnp.sum(wide_grads * mean_ref[0:1, :], axis=-1, keepdims=True)
    project = jnp.sum(wide_grads * slope_ref[...], axis=-1, keepdims=True)
    back = done_ref[...] + scale_ref[...] * (normed_grad - average - normed_ref[...] * project)
    out[...] = back.astype(bf16).reshape(size, size, channels)


def call(kernel, outs, *args, scratch=(), flops=0, smem=(), hbm=()):
    spec = pl.BlockSpec(memory_space=pltpu.VMEM)
    total = sum(a.size * a.dtype.itemsize for a in (*args, *outs))
    specs = [spec] * len(args)
    for n in smem:
        specs[n] = pl.BlockSpec(memory_space=pltpu.SMEM)
    args = list(args)
    for n in hbm:
        specs[n] = pl.BlockSpec(memory_space=pltpu.HBM)
        args[n] = pltpu.with_memory_space_constraint(args[n], pltpu.HBM)
    return pl.pallas_call(
        kernel,
        out_shape=tuple(outs),
        in_specs=specs,
        out_specs=(spec,) * len(outs),
        scratch_shapes=scratch,
        compiler_params=pltpu.CompilerParams(vmem_limit_bytes=24 * 2**20),
        cost_estimate=pl.CostEstimate(flops=flops, bytes_accessed=total if flops else 0, transcendentals=0),
    )(*args)


def local(pair_acts, pair_mask, crop_length, cotangent, in_weights, out_weight):
    size, _, channels = pair_acts.shape
    pairs = size * size
    n = lax.axis_size("row")
    tile = jax.ShapeDtypeStruct((size, size, channels), bf16)
    flat = jax.ShapeDtypeStruct((pairs, channels), f32)

    wide = jax.ShapeDtypeStruct((size, size, channels), f32)
    panel = jax.ShapeDtypeStruct((n * size, size, channels), f32)
    work = 2 * size * pairs * channels
    wait = 2**31
    steps = [step for bit in range(n.bit_length() - 2, -1, -1) for step in range(2**bit, 2 ** (bit + 1))]
    row_steps = steps
    gather_steps = [n - 1] + list(range(1, n - 1))


    def swap(values, axis, step):
        return lax.ppermute(values, axis, [(a, a ^ step) for a in range(n)])

    def gather(values, axis, steps):
        return [values] + [swap(values, axis, step) for step in steps]

    (left,) = call(
        left_kernel, (tile,), pair_acts, pair_mask, in_weights,
        hbm=(0, 1, 2), flops=2 * pairs * channels * 2 * channels,
        scratch=[
            pltpu.VMEM(pair_acts.shape, bf16),
            pltpu.VMEM(pair_mask.shape, jnp.int32),
            pltpu.VMEM((channels, 2 * channels), bf16),
            pltpu.SemaphoreType.DMA((3,)),
        ],
    )
    lefts = gather(left, "col", steps)
    right, normed, scale, factors, out_open, gate_factor, upstream = call(
        factors_kernel,
        (wide, flat, flat, jax.ShapeDtypeStruct((4, pairs, channels), f32), flat, flat, flat),
        pair_acts, pair_mask, crop_length, cotangent, in_weights, out_weight,
        smem=(2,), hbm=(0, 1, 3, 4, 5), flops=2 * pairs * channels * 6 * channels,
        scratch=[
            pltpu.VMEM(pair_acts.shape, bf16),
            pltpu.VMEM(pair_mask.shape, jnp.int32),
            pltpu.VMEM(cotangent.shape, bf16),
            pltpu.VMEM(in_weights.shape, bf16),
            pltpu.VMEM(out_weight.shape, bf16),
            pltpu.SemaphoreType.DMA((5,)),
        ],
    )
    order = [0] + steps
    parts = [
        call(
            functools.partial(partial_kernel, [order[at]]), (tile,), crop_length, lefts[at], right, smem=(0,),
            flops=work, scratch=[pltpu.VMEM(wide.shape, f32)],
        )[0]
        for at in range(n - 2)
    ]
    total, *parts = call(
        functools.partial(last_partial_kernel, order[-2:], order[:-2], [0] + row_steps),
        (wide,) + (tile,) * (n - 1), crop_length, *lefts[-2:], right, *parts, smem=(0,), flops=work,
        scratch=[pltpu.VMEM(wide.shape, f32), pltpu.VMEM((2,) + wide.shape, bf16)],
    )
    (left_panel,) = call(
        functools.partial(left_panel_kernel, [0] + steps), (panel,), crop_length, *lefts, smem=(0,)
    )
    last = []
    for step, part in zip(row_steps, parts):
        part = swap(part, "row", step)
        if step in row_steps[-2:]:
            last.append(part)
        else:
            (total,) = call(add_kernel, (wide,), total, part, flops=wait)
    tri_normed, tri_grad = call(
        triangle_kernel, (flat, tile), total, *last, upstream, flops=20 * pairs * channels,
    )
    grads = gather(tri_grad, "row", gather_steps)
    update, partial = call(
        update_kernel, (tile, flat), tri_normed, out_open, gate_factor, in_weights, out_weight,
        flops=4 * pairs * channels * channels,
    )
    means, slopes = call(
        slopes_kernel, (jax.ShapeDtypeStruct((8, 2 * channels), f32), jax.ShapeDtypeStruct((pairs, 2 * channels), f32)),
        normed, in_weights,
    )
    (right_grad,) = call(functools.partial(right_grad_kernel, [0]), (wide,), left_panel, tri_grad)
    terms, before = [], (partial, right_grad, slopes)
    for grad in grads[:-1]:
        before = call(
            left_terms_kernel, (tile,), grad, right, *before,
            scratch=[pltpu.VMEM((pairs, channels), f32)], flops=work,
        )
        terms += before
    last_steps = list(range(n - 1, 0, -1))
    total, *terms = call(
        functools.partial(last_terms_kernel, [0] + gather_steps[:-1], gather_steps[-1], [0] + last_steps),
        (wide,) + (tile,) * (n - 1), grads[-1], right, *terms, flops=work,
        scratch=[pltpu.VMEM(tile.shape, bf16), pltpu.VMEM((pairs, channels), f32)],
    )
    last = []
    for step, term in zip(last_steps, terms):
        term = swap(term, "col", step)
        if step in last_steps[-2:]:
            last.append(term)
        else:
            (total,) = call(add_kernel, (wide,), total, term, flops=wait)
    (done,) = call(
        functools.partial(right_back_kernel, gather_steps), (flat,),
        left_panel, *grads[1:], right_grad, factors, in_weights, partial, normed, scale,
        scratch=[pltpu.VMEM(wide.shape, f32)],
    )
    (pair_grad,) = call(
        back_kernel, (tile,), total, *last, normed, scale, factors, done, means, slopes, in_weights,
        flops=2 * pairs * channels * 2 * channels,
    )
    return (update, pair_grad)


def solution(mesh):
    return jax.shard_map(
        local,
        mesh=mesh,
        in_specs=(
            P(("group", "row"), "col", None),
            P(("group", "row"), "col"),
            P("group"),
            P(("group", "row"), "col", None),
            P(),
            P(),
        ),
        out_specs=(P(("group", "row"), "col", None), P(("group", "row"), "col", None)),
        check_vma=False,
    )
```

```python
import functools

import jax
import jax.numpy as jnp
from jax import lax
from jax.experimental import pallas as pl
from jax.experimental.pallas import tpu as pltpu
from jax.sharding import PartitionSpec as P

epsilon = 1e-05
f32 = jnp.float32
bf16 = jnp.bfloat16


def mean_lanes(values):
    return jnp.sum(values, axis=-1, keepdims=True) * (1.0 / values.shape[-1])


def normalize(values):
    center = values - mean_lanes(values)
    variance = mean_lanes(center * center)
    scale = lax.rsqrt(variance + epsilon)
    return (center * scale, scale)


def normalize_back(normed, scale, upstream):
    average = mean_lanes(upstream)
    project = mean_lanes(upstream * normed)
    return scale * (upstream - average - normed * project)


def sigmoid(values):
    return 1.0 / (1.0 + jnp.exp(-values))


def dot(a, b):
    return jnp.dot(a, b, preferred_element_type=f32)


def dot_t(a, b):
    return lax.dot_general(a, b, (((1,), (1,)), ((), ())), preferred_element_type=f32)


def live_pairs(crop_ref, row, col, shape):
    rows = row * shape[0] + lax.broadcasted_iota(jnp.int32, shape, 0)
    cols = col * shape[1] + lax.broadcasted_iota(jnp.int32, shape, 1)
    return jnp.where(jnp.maximum(rows, cols) < crop_ref[0], 1.0, 0.0)


def spread(mask, channels):
    size = mask.shape[0]
    shape = (size, size, size)
    diagonal = lax.broadcasted_iota(jnp.int32, shape, 1) == lax.broadcasted_iota(jnp.int32, shape, 2)
    picked = jnp.where(diagonal, jnp.broadcast_to(mask[:, None, :], shape), 0.0)
    rows = jnp.sum(picked, axis=-1, keepdims=True)
    return jnp.broadcast_to(rows, (size, size, channels)).reshape(size * size, channels)


def start_copies(sems, *pairs):
    copies = [pltpu.make_async_copy(src, dst, sems.at[n]) for n, (src, dst) in enumerate(pairs)]
    for copy in copies:
        copy.start()
    return copies


def gated(projected, block, keep):
    channels = keep.shape[1]
    value = projected[:, block * channels : (block + 1) * channels]
    opened = sigmoid(projected[:, (block + 1) * channels : (block + 2) * channels])
    return (opened * value * keep).astype(bf16), opened, value


def left_kernel(acts_in, mask_in, weights_in, left_ref, acts_ref, mask_ref, weights_ref, sems):
    size, _, channels = acts_ref.shape
    copies = start_copies(
        sems, (acts_in, acts_ref), (weights_in.at[:, pl.ds(0, 2 * channels)], weights_ref), (mask_in, mask_ref),
    )
    copies[0].wait()
    normed, _ = normalize(acts_ref[...].astype(f32).reshape(size * size, channels))
    normed = normed.astype(bf16)
    for copy in copies[1:]:
        copy.wait()
    left, _, _ = gated(dot(normed, weights_ref[...]), 0, spread(mask_ref[...].astype(f32), channels))
    left_ref[...] = left.reshape(size, size, channels)


def factors_kernel(
    acts_in, mask_in, crop_ref, cotangent_in, weights_in, out_weight_in,
    right_ref, normed_ref, scale_ref, factor_ref, open_ref, gate_factor_ref, upstream_ref,
    acts_ref, mask_ref, cotangent_ref, weights_ref, out_weight_ref, sems,
):
    copies = start_copies(
        sems, (acts_in, acts_ref), (weights_in, weights_ref), (mask_in, mask_ref),
        (cotangent_in, cotangent_ref), (out_weight_in, out_weight_ref),
    )
    size, _, channels = acts_ref.shape
    pairs = size * size
    copies[0].wait()
    normed, scale = normalize(acts_ref[...].astype(f32).reshape(pairs, channels))
    normed_ref[...] = normed
    scale_ref[...] = jnp.broadcast_to(scale, (pairs, channels))
    for copy in copies[1:]:
        copy.wait()
    projected = dot(normed.astype(bf16), weights_ref[...])
    live = live_pairs(crop_ref, lax.axis_index("row"), lax.axis_index("col"), (size, size))
    keep = spread(mask_ref[...].astype(f32) * live, channels)
    for block in (0, 2):
        tile, opened, value = gated(projected, block, keep)
        factor_ref[block] = keep * opened
        factor_ref[block + 1] = keep * value * opened * (1.0 - opened)
    right_ref[...] = tile.astype(f32).reshape(size, size, channels)
    out_open = sigmoid(projected[:, 4 * channels :])
    cotangent = cotangent_ref[...].astype(f32).reshape(pairs, channels)
    lin_grad = (cotangent * out_open).astype(bf16)
    open_ref[...] = out_open
    gate_factor_ref[...] = cotangent * out_open * (1.0 - out_open)
    upstream = dot_t(lin_grad, out_weight_ref[...])
    upstream_ref[...] = upstream - mean_lanes(upstream)


def weighted_sums(weights, start, terms, out, base=None):
    def step(k, _):
        total = weights[start + k, pl.ds(0, 1), :] * terms[0]
        for n in range(1, len(terms)):
            total = total + weights[start + k, pl.ds(n, 1), :] * terms[n]
        if base is not None:
            total = total + base[k]
        out[k] = total.astype(out.dtype)
        return 0

    lax.fori_loop(0, out.shape[0], step, 0, unroll=16)


def left_panel_kernel(steps, crop_ref, *refs):
    row, col, panel = lax.axis_index("row"), lax.axis_index("col"), refs[-1]
    size, _, channels = refs[0].shape
    rows = row * size + lax.broadcasted_iota(jnp.int32, (size, 1, channels), 0)
    row_live = jnp.where(rows < crop_ref[0], 1.0, 0.0)
    for step, ref in zip(steps, refs):
        place = col ^ step
        cols = place * size + lax.broadcasted_iota(jnp.int32, (1, size, channels), 1)
        col_live = jnp.where(cols < crop_ref[0], 1.0, 0.0)
        panel[pl.ds(place * size, size)] = ref[...].astype(f32) * (row_live * col_live)


def partial_kernel(steps, crop_ref, *refs):
    count = len(steps)
    lefts, right_ref, outs, left = refs[:count], refs[count], refs[count + 1 : -1], refs[-1]
    size, _, channels = right_ref.shape
    rows = lax.axis_index("row") * size + lax.broadcasted_iota(jnp.int32, (size, 1, channels), 0)
    row_live = jnp.where(rows < crop_ref[0], 1.0, 0.0)
    for step, left_ref, out in zip(steps, lefts, outs):
        cols = (lax.axis_index("col") ^ step) * size + lax.broadcasted_iota(jnp.int32, (1, size, channels), 1)
        left[...] = left_ref[...].astype(f32) * (row_live * jnp.where(cols < crop_ref[0], 1.0, 0.0))

        def add(k, sums):
            other = right_ref[k]
            return tuple(sums[i] + left[k, pl.ds(i, 1), :] * other for i in range(size))

        zero = jnp.zeros((size, channels), f32)
        sums = lax.fori_loop(0, size, add, (zero,) * size, unroll=16)
        for i in range(size):
            out[i] = sums[i].astype(out.dtype)


def pick_kernel(steps, *refs):
    here = lax.axis_index("row") ^ lax.axis_index("col")
    tiles, outs = refs[: len(steps)], refs[len(steps) :]
    for step, out in zip(steps, outs):
        for other, tile in enumerate(tiles):

            @pl.when((here ^ step) == other)
            def _():
                out[...] = tile[...].astype(out.dtype)


def last_partial_kernel(steps, early, row_steps, crop_ref, *refs):
    count, known = len(steps), len(early)
    left, parts = refs[-2:]
    partial_kernel(steps, crop_ref, *refs[: count + 1], *(parts.at[at] for at in range(count)), left)
    tiles = dict(zip(early, refs[count + 1 : count + 1 + known]))
    tiles.update((step, parts.at[at]) for at, step in enumerate(steps))
    pick_kernel(row_steps, *(tiles[step] for step in range(count + known)), *refs[count + 1 + known : -2])


def triangle_kernel(base, *refs):
    *tiles, upstream_ref, tri_normed_ref, grad_ref = refs
    size = grad_ref.shape[0]
    for i in range(size):
        total = base[i]
        for ref in tiles:
            total = total + ref[i].astype(f32)
        here = pl.ds(i * size, size)
        upstream = upstream_ref[here, :]
        center = total - mean_lanes(total)
        scale = lax.rsqrt(mean_lanes(center * center) + epsilon)
        tri_normed = center * scale
        tri_normed_ref[here, :] = tri_normed
        project = mean_lanes(center * upstream) * scale
        grad_ref[i] = (scale * (upstream - tri_normed * project)).astype(bf16)


def left_terms_kernel(grad_ref, right, *refs):
    out, grad = refs[-2:]
    size, _, channels = out.shape
    grad[...] = grad_ref[...].astype(f32).reshape(size * size, channels)
    weighted_sums(right, 0, [grad[pl.ds(j, size, stride=size), :] for j in range(size)], out)


def last_terms_kernel(early, last, steps, grad_ref, right, *refs):
    known = len(early)
    term, grad = refs[-2:]
    left_terms_kernel(grad_ref, right, term, grad)
    tiles = dict(zip(early, refs[:known]))
    tiles[last] = term
    pick_kernel(steps, *(tiles[step] for step in range(known + 1)), *refs[known:-2])


def right_grad_kernel(steps, panel, *refs):
    out, base = refs[-1], refs[len(steps)] if len(refs) > len(steps) + 1 else None
    size = out.shape[0]
    for step, grad in zip(steps, refs):
        start = (lax.axis_index("row") ^ step) * size
        weighted_sums(panel, start, [grad[i].astype(f32) for i in range(size)], out, base)
        base = out


def right_back_kernel(steps, panel, *refs):
    factor_ref, weights_ref, share_ref, normed_ref, scale_ref, out, right_ref = refs[-7:]
    right_grad_kernel(steps, panel, *refs[: len(steps) + 1], right_ref)
    pairs, channels = out.shape
    right = right_ref[...].reshape(pairs, channels)
    grads = jnp.concatenate([(right * factor_ref[block]).astype(bf16) for block in (2, 3)], axis=1)
    share = share_ref[...] + dot_t(grads, weights_ref[:, 2 * channels : 4 * channels])
    out[...] = normalize_back(normed_ref[...], scale_ref[...], share)


def slopes_kernel(normed_ref, weights_ref, mean_ref, slope_ref):
    channels = normed_ref.shape[1]
    weights = weights_ref[:, : 2 * channels].astype(f32)
    mean = jnp.sum(weights, axis=0, keepdims=True) * (1.0 / channels)
    mean_ref[...] = jnp.broadcast_to(mean, mean_ref.shape)
    slope = jnp.dot(normed_ref[...], weights, precision=lax.Precision.HIGHEST, preferred_element_type=f32)
    slope_ref[...] = slope * (1.0 / channels)


def add_kernel(base, tile_ref, out):
    out[...] = base[...] + tile_ref[...].astype(f32)


def update_kernel(
    tri_normed_ref, open_ref, gate_factor_ref, weights_ref, out_weight_ref, update_ref, normed_grad_ref
):
    size, _, channels = update_ref.shape
    linear = dot(tri_normed_ref[...].astype(bf16), out_weight_ref[...])
    update = (open_ref[...] * linear).astype(bf16)
    update_ref[...] = update.reshape(size, size, channels)
    out_gate_grad = (gate_factor_ref[...] * linear).astype(bf16)
    normed_grad_ref[...] = dot_t(out_gate_grad, weights_ref[:, 4 * channels :])


def back_kernel(base, *refs):
    *tiles, normed_ref, scale_ref, factor_ref, done_ref, mean_ref, slope_ref, weights_ref, out = refs
    size, _, channels = out.shape
    pairs = size * size
    left = base[...]
    for ref in tiles:
        left = left + ref[...].astype(f32)
    left = left.reshape(pairs, channels)
    grads = jnp.concatenate([(left * factor_ref[block]).astype(bf16) for block in (0, 1)], axis=1)
    normed_grad = dot_t(grads, weights_ref[:, : 2 * channels])
    wide_grads = grads.astype(f32)
    average = jnp.sum(wide_grads * mean_ref[0:1, :], axis=-1, keepdims=True)
    project = jnp.sum(wide_grads * slope_ref[...], axis=-1, keepdims=True)
    back = done_ref[...] + scale_ref[...] * (normed_grad - average - normed_ref[...] * project)
    out[...] = back.astype(bf16).reshape(size, size, channels)


def call(kernel, outs, *args, scratch=(), flops=0, smem=(), hbm=()):
    spec = pl.BlockSpec(memory_space=pltpu.VMEM)
    total = sum(a.size * a.dtype.itemsize for a in (*args, *outs))
    specs = [spec] * len(args)
    for n in smem:
        specs[n] = pl.BlockSpec(memory_space=pltpu.SMEM)
    args = list(args)
    for n in hbm:
        specs[n] = pl.BlockSpec(memory_space=pltpu.HBM)
        args[n] = pltpu.with_memory_space_constraint(args[n], pltpu.HBM)
    return pl.pallas_call(
        kernel,
        out_shape=tuple(outs),
        in_specs=specs,
        out_specs=(spec,) * len(outs),
        scratch_shapes=scratch,
        compiler_params=pltpu.CompilerParams(vmem_limit_bytes=24 * 2**20),
        cost_estimate=pl.CostEstimate(flops=flops, bytes_accessed=total if flops else 0, transcendentals=0),
    )(*args)


def local(pair_acts, pair_mask, crop_length, cotangent, in_weights, out_weight):
    size, _, channels = pair_acts.shape
    pairs = size * size
    n = lax.axis_size("row")
    tile = jax.ShapeDtypeStruct((size, size, channels), bf16)
    flat = jax.ShapeDtypeStruct((pairs, channels), f32)

    wide = jax.ShapeDtypeStruct((size, size, channels), f32)
    panel = jax.ShapeDtypeStruct((n * size, size, channels), f32)
    work = 2 * size * pairs * channels
    wait = 2**31
    steps = [step for bit in range(n.bit_length() - 2, -1, -1) for step in range(2**bit, 2 ** (bit + 1))]
    row_steps = steps
    gather_steps = [n - 1] + list(range(1, n - 1))


    def swap(values, axis, step):
        return lax.ppermute(values, axis, [(a, a ^ step) for a in range(n)])

    def gather(values, axis, steps):
        return [values] + [swap(values, axis, step) for step in steps]

    (left,) = call(
        left_kernel, (tile,), pair_acts, pair_mask, in_weights,
        hbm=(0, 1, 2), flops=2 * pairs * channels * 2 * channels,
        scratch=[
            pltpu.VMEM(pair_acts.shape, bf16),
            pltpu.VMEM(pair_mask.shape, jnp.int32),
            pltpu.VMEM((channels, 2 * channels), bf16),
            pltpu.SemaphoreType.DMA((3,)),
        ],
    )
    lefts = gather(left, "col", steps)
    right, normed, scale, factors, out_open, gate_factor, upstream = call(
        factors_kernel,
        (wide, flat, flat, jax.ShapeDtypeStruct((4, pairs, channels), f32), flat, flat, flat),
        pair_acts, pair_mask, crop_length, cotangent, in_weights, out_weight,
        smem=(2,), hbm=(0, 1, 3, 4, 5), flops=2 * pairs * channels * 6 * channels,
        scratch=[
            pltpu.VMEM(pair_acts.shape, bf16),
            pltpu.VMEM(pair_mask.shape, jnp.int32),
            pltpu.VMEM(cotangent.shape, bf16),
            pltpu.VMEM(in_weights.shape, bf16),
            pltpu.VMEM(out_weight.shape, bf16),
            pltpu.SemaphoreType.DMA((5,)),
        ],
    )
    order = [0] + steps
    early = order[:-2] + order[-1:]
    tile_at = dict(zip(order, lefts))
    parts = [
        call(
            functools.partial(partial_kernel, [step]), (tile,), crop_length, tile_at[step], right, smem=(0,),
            flops=work, scratch=[pltpu.VMEM(wide.shape, f32)],
        )[0]
        for step in early
    ]
    total, *parts = call(
        functools.partial(last_partial_kernel, order[-2:-1], early, [0] + row_steps),
        (wide,) + (tile,) * (n - 1), crop_length, tile_at[order[-2]], right, *parts, smem=(0,), flops=work,
        scratch=[pltpu.VMEM(wide.shape, f32), pltpu.VMEM((1,) + wide.shape, bf16)],
    )
    (left_panel,) = call(
        functools.partial(left_panel_kernel, [0] + steps), (panel,), crop_length, *lefts, smem=(0,)
    )
    last = []
    for step, part in zip(row_steps, parts):
        part = swap(part, "row", step)
        if step in row_steps[-2:]:
            last.append(part)
        else:
            (total,) = call(add_kernel, (wide,), total, part, flops=wait)
    tri_normed, tri_grad = call(
        triangle_kernel, (flat, tile), total, *last, upstream, flops=20 * pairs * channels,
    )
    grads = gather(tri_grad, "row", gather_steps)
    update, partial = call(
        update_kernel, (tile, flat), tri_normed, out_open, gate_factor, in_weights, out_weight,
        flops=4 * pairs * channels * channels,
    )
    means, slopes = call(
        slopes_kernel, (jax.ShapeDtypeStruct((8, 2 * channels), f32), jax.ShapeDtypeStruct((pairs, 2 * channels), f32)),
        normed, in_weights,
    )
    (right_grad,) = call(functools.partial(right_grad_kernel, [0]), (wide,), left_panel, tri_grad)
    terms, before = [], (partial, right_grad, slopes)
    for grad in grads[:-1]:
        before = call(
            left_terms_kernel, (tile,), grad, right, *before,
            scratch=[pltpu.VMEM((pairs, channels), f32)], flops=work,
        )
        terms += before
    total, *terms = call(
        functools.partial(last_terms_kernel, [0] + gather_steps[:-1], gather_steps[-1], [0] + steps),
        (wide,) + (tile,) * (n - 1), grads[-1], right, *terms, flops=work,
        scratch=[pltpu.VMEM(tile.shape, bf16), pltpu.VMEM((pairs, channels), f32)],
    )
    last = []
    for step, term in zip(steps, terms):
        term = swap(term, "col", step)
        if step in steps[-2:]:
            last.append(term)
        else:
            (total,) = call(add_kernel, (wide,), total, term, flops=wait)
    (done,) = call(
        functools.partial(right_back_kernel, gather_steps), (flat,),
        left_panel, *grads[1:], right_grad, factors, in_weights, partial, normed, scale,
        scratch=[pltpu.VMEM(wide.shape, f32)],
    )
    (pair_grad,) = call(
        back_kernel, (tile,), total, *last, normed, scale, factors, done, means, slopes, in_weights,
        flops=2 * pairs * channels * 2 * channels,
    )
    return (update, pair_grad)


def solution(mesh):
    return jax.shard_map(
        local,
        mesh=mesh,
        in_specs=(
            P(("group", "row"), "col", None),
            P(("group", "row"), "col"),
            P("group"),
            P(("group", "row"), "col", None),
            P(),
            P(),
        ),
        out_specs=(P(("group", "row"), "col", None), P(("group", "row"), "col", None)),
        check_vma=False,
    )
```

```python
import functools

import jax
import jax.numpy as jnp
from jax import lax
from jax.experimental import pallas as pl
from jax.experimental.pallas import tpu as pltpu
from jax.sharding import PartitionSpec as P

epsilon = 1e-05
f32 = jnp.float32
bf16 = jnp.bfloat16


def mean_lanes(values):
    return jnp.sum(values, axis=-1, keepdims=True) * (1.0 / values.shape[-1])


def normalize(values):
    center = values - mean_lanes(values)
    variance = mean_lanes(center * center)
    scale = lax.rsqrt(variance + epsilon)
    return (center * scale, scale)


def normalize_back(normed, scale, upstream):
    average = mean_lanes(upstream)
    project = mean_lanes(upstream * normed)
    return scale * (upstream - average - normed * project)


def sigmoid(values):
    return 1.0 / (1.0 + jnp.exp(-values))


def dot(a, b):
    return jnp.dot(a, b, preferred_element_type=f32)


def dot_t(a, b):
    return lax.dot_general(a, b, (((1,), (1,)), ((), ())), preferred_element_type=f32)


def live_pairs(crop_ref, row, col, shape):
    rows = row * shape[0] + lax.broadcasted_iota(jnp.int32, shape, 0)
    cols = col * shape[1] + lax.broadcasted_iota(jnp.int32, shape, 1)
    return jnp.where(jnp.maximum(rows, cols) < crop_ref[0], 1.0, 0.0)


def spread(mask, channels):
    size = mask.shape[0]
    shape = (size, size, size)
    diagonal = lax.broadcasted_iota(jnp.int32, shape, 1) == lax.broadcasted_iota(jnp.int32, shape, 2)
    picked = jnp.where(diagonal, jnp.broadcast_to(mask[:, None, :], shape), 0.0)
    rows = jnp.sum(picked, axis=-1, keepdims=True)
    return jnp.broadcast_to(rows, (size, size, channels)).reshape(size * size, channels)


def start_copies(sems, *pairs):
    copies = [pltpu.make_async_copy(src, dst, sems.at[n]) for n, (src, dst) in enumerate(pairs)]
    for copy in copies:
        copy.start()
    return copies


def gated(projected, block, keep):
    channels = keep.shape[1]
    value = projected[:, block * channels : (block + 1) * channels]
    opened = sigmoid(projected[:, (block + 1) * channels : (block + 2) * channels])
    return (opened * value * keep).astype(bf16), opened, value


def left_kernel(acts_in, mask_in, weights_in, left_ref, acts_ref, mask_ref, weights_ref, sems):
    size, _, channels = acts_ref.shape
    copies = start_copies(
        sems, (acts_in, acts_ref), (weights_in.at[:, pl.ds(0, 2 * channels)], weights_ref), (mask_in, mask_ref),
    )
    copies[0].wait()
    normed, _ = normalize(acts_ref[...].astype(f32).reshape(size * size, channels))
    normed = normed.astype(bf16)
    for copy in copies[1:]:
        copy.wait()
    left, _, _ = gated(dot(normed, weights_ref[...]), 0, spread(mask_ref[...].astype(f32), channels))
    left_ref[...] = left.reshape(size, size, channels)


def factors_kernel(
    acts_in, mask_in, crop_ref, cotangent_in, weights_in, out_weight_in,
    right_ref, normed_ref, scale_ref, factor_ref, open_ref, gate_factor_ref, upstream_ref,
    acts_ref, mask_ref, cotangent_ref, weights_ref, out_weight_ref, sems,
):
    copies = start_copies(
        sems, (acts_in, acts_ref), (weights_in, weights_ref), (mask_in, mask_ref),
        (cotangent_in, cotangent_ref), (out_weight_in, out_weight_ref),
    )
    size, _, channels = acts_ref.shape
    pairs = size * size
    copies[0].wait()
    normed, scale = normalize(acts_ref[...].astype(f32).reshape(pairs, channels))
    normed_ref[...] = normed
    scale_ref[...] = jnp.broadcast_to(scale, (pairs, channels))
    for copy in copies[1:]:
        copy.wait()
    projected = dot(normed.astype(bf16), weights_ref[...])
    live = live_pairs(crop_ref, lax.axis_index("row"), lax.axis_index("col"), (size, size))
    keep = spread(mask_ref[...].astype(f32) * live, channels)
    for block in (0, 2):
        tile, opened, value = gated(projected, block, keep)
        factor_ref[block] = keep * opened
        factor_ref[block + 1] = keep * value * opened * (1.0 - opened)
    right_ref[...] = tile.astype(f32).reshape(size, size, channels)
    out_open = sigmoid(projected[:, 4 * channels :])
    cotangent = cotangent_ref[...].astype(f32).reshape(pairs, channels)
    lin_grad = (cotangent * out_open).astype(bf16)
    open_ref[...] = out_open
    gate_factor_ref[...] = cotangent * out_open * (1.0 - out_open)
    upstream = dot_t(lin_grad, out_weight_ref[...])
    upstream_ref[...] = upstream - mean_lanes(upstream)


def weighted_sums(weights, start, terms, out, base=None):
    def step(k, _):
        total = weights[start + k, pl.ds(0, 1), :] * terms[0]
        for n in range(1, len(terms)):
            total = total + weights[start + k, pl.ds(n, 1), :] * terms[n]
        if base is not None:
            total = total + base[k]
        out[k] = total.astype(out.dtype)
        return 0

    lax.fori_loop(0, out.shape[0], step, 0, unroll=16)


def left_panel_kernel(steps, crop_ref, *refs):
    row, col, panel = lax.axis_index("row"), lax.axis_index("col"), refs[-1]
    size, _, channels = refs[0].shape
    rows = row * size + lax.broadcasted_iota(jnp.int32, (size, 1, channels), 0)
    row_live = jnp.where(rows < crop_ref[0], 1.0, 0.0)
    for step, ref in zip(steps, refs):
        place = col ^ step
        cols = place * size + lax.broadcasted_iota(jnp.int32, (1, size, channels), 1)
        col_live = jnp.where(cols < crop_ref[0], 1.0, 0.0)
        panel[pl.ds(place * size, size)] = ref[...].astype(f32) * (row_live * col_live)


def partial_kernel(steps, crop_ref, *refs):
    count = len(steps)
    lefts, right_ref, outs, left = refs[:count], refs[count], refs[count + 1 : -1], refs[-1]
    size, _, channels = right_ref.shape
    rows = lax.axis_index("row") * size + lax.broadcasted_iota(jnp.int32, (size, 1, channels), 0)
    row_live = jnp.where(rows < crop_ref[0], 1.0, 0.0)
    for step, left_ref, out in zip(steps, lefts, outs):
        cols = (lax.axis_index("col") ^ step) * size + lax.broadcasted_iota(jnp.int32, (1, size, channels), 1)
        left[...] = left_ref[...].astype(f32) * (row_live * jnp.where(cols < crop_ref[0], 1.0, 0.0))

        def add(k, sums):
            other = right_ref[k]
            return tuple(sums[i] + left[k, pl.ds(i, 1), :] * other for i in range(size))

        zero = jnp.zeros((size, channels), f32)
        sums = lax.fori_loop(0, size, add, (zero,) * size, unroll=16)
        for i in range(size):
            out[i] = sums[i].astype(out.dtype)


def pick_kernel(steps, *refs):
    here = lax.axis_index("row") ^ lax.axis_index("col")
    tiles, outs = refs[: len(steps)], refs[len(steps) :]
    for step, out in zip(steps, outs):
        for other, tile in enumerate(tiles):

            @pl.when((here ^ step) == other)
            def _():
                out[...] = tile[...].astype(out.dtype)


def last_partial_kernel(steps, early, row_steps, crop_ref, *refs):
    count, known = len(steps), len(early)
    left, parts = refs[-2:]
    partial_kernel(steps, crop_ref, *refs[: count + 1], *(parts.at[at] for at in range(count)), left)
    tiles = dict(zip(early, refs[count + 1 : count + 1 + known]))
    tiles.update((step, parts.at[at]) for at, step in enumerate(steps))
    pick_kernel(row_steps, *(tiles[step] for step in range(count + known)), *refs[count + 1 + known : -2])


def triangle_kernel(base, *refs):
    *tiles, upstream_ref, tri_normed_ref, grad_ref = refs
    size = grad_ref.shape[0]
    for i in range(size):
        total = base[i]
        for ref in tiles:
            total = total + ref[i].astype(f32)
        here = pl.ds(i * size, size)
        upstream = upstream_ref[here, :]
        center = total - mean_lanes(total)
        scale = lax.rsqrt(mean_lanes(center * center) + epsilon)
        tri_normed = center * scale
        tri_normed_ref[here, :] = tri_normed
        project = mean_lanes(center * upstream) * scale
        grad_ref[i] = (scale * (upstream - tri_normed * project)).astype(bf16)


def left_terms_kernel(grad_ref, right, *refs):
    out, grad = refs[-2:]
    size, _, channels = out.shape
    grad[...] = grad_ref[...].astype(f32).reshape(size * size, channels)
    weighted_sums(right, 0, [grad[pl.ds(j, size, stride=size), :] for j in range(size)], out)


def last_terms_kernel(early, last, steps, grad_ref, right, *refs):
    known = len(early)
    term, grad = refs[-2:]
    left_terms_kernel(grad_ref, right, term, grad)
    tiles = dict(zip(early, refs[:known]))
    tiles[last] = term
    pick_kernel(steps, *(tiles[step] for step in range(known + 1)), *refs[known:-2])


def right_grad_kernel(steps, panel, *refs):
    out, base = refs[-1], refs[len(steps)] if len(refs) > len(steps) + 1 else None
    size = out.shape[0]
    for step, grad in zip(steps, refs):
        start = (lax.axis_index("row") ^ step) * size
        weighted_sums(panel, start, [grad[i].astype(f32) for i in range(size)], out, base)
        base = out


def right_back_kernel(steps, panel, *refs):
    factor_ref, weights_ref, share_ref, normed_ref, scale_ref, out, right_ref = refs[-7:]
    right_grad_kernel(steps, panel, *refs[: len(steps) + 1], right_ref)
    pairs, channels = out.shape
    right = right_ref[...].reshape(pairs, channels)
    grads = jnp.concatenate([(right * factor_ref[block]).astype(bf16) for block in (2, 3)], axis=1)
    share = share_ref[...] + dot_t(grads, weights_ref[:, 2 * channels : 4 * channels])
    out[...] = normalize_back(normed_ref[...], scale_ref[...], share)


def slopes_kernel(normed_ref, weights_ref, mean_ref, slope_ref):
    channels = normed_ref.shape[1]
    weights = weights_ref[:, : 2 * channels].astype(f32)
    mean = jnp.sum(weights, axis=0, keepdims=True) * (1.0 / channels)
    mean_ref[...] = jnp.broadcast_to(mean, mean_ref.shape)
    slope = jnp.dot(normed_ref[...], weights, precision=lax.Precision.HIGHEST, preferred_element_type=f32)
    slope_ref[...] = slope * (1.0 / channels)


def add_kernel(base, tile_ref, out):
    out[...] = base[...] + tile_ref[...].astype(f32)


def update_kernel(
    tri_normed_ref, open_ref, gate_factor_ref, weights_ref, out_weight_ref, update_ref, normed_grad_ref
):
    size, _, channels = update_ref.shape
    linear = dot(tri_normed_ref[...].astype(bf16), out_weight_ref[...])
    update = (open_ref[...] * linear).astype(bf16)
    update_ref[...] = update.reshape(size, size, channels)
    out_gate_grad = (gate_factor_ref[...] * linear).astype(bf16)
    normed_grad_ref[...] = dot_t(out_gate_grad, weights_ref[:, 4 * channels :])


def back_kernel(base, *refs):
    *tiles, normed_ref, scale_ref, factor_ref, done_ref, mean_ref, slope_ref, weights_ref, out = refs
    size, _, channels = out.shape
    pairs = size * size
    left = base[...]
    for ref in tiles:
        left = left + ref[...].astype(f32)
    left = left.reshape(pairs, channels)
    grads = jnp.concatenate([(left * factor_ref[block]).astype(bf16) for block in (0, 1)], axis=1)
    normed_grad = dot_t(grads, weights_ref[:, : 2 * channels])
    wide_grads = grads.astype(f32)
    average = jnp.sum(wide_grads * mean_ref[0:1, :], axis=-1, keepdims=True)
    project = jnp.sum(wide_grads * slope_ref[...], axis=-1, keepdims=True)
    back = done_ref[...] + scale_ref[...] * (normed_grad - average - normed_ref[...] * project)
    out[...] = back.astype(bf16).reshape(size, size, channels)


def call(kernel, outs, *args, scratch=(), flops=0, smem=(), hbm=()):
    spec = pl.BlockSpec(memory_space=pltpu.VMEM)
    total = sum(a.size * a.dtype.itemsize for a in (*args, *outs))
    specs = [spec] * len(args)
    for n in smem:
        specs[n] = pl.BlockSpec(memory_space=pltpu.SMEM)
    args = list(args)
    for n in hbm:
        specs[n] = pl.BlockSpec(memory_space=pltpu.HBM)
        args[n] = pltpu.with_memory_space_constraint(args[n], pltpu.HBM)
    return pl.pallas_call(
        kernel,
        out_shape=tuple(outs),
        in_specs=specs,
        out_specs=(spec,) * len(outs),
        scratch_shapes=scratch,
        compiler_params=pltpu.CompilerParams(vmem_limit_bytes=24 * 2**20),
        cost_estimate=pl.CostEstimate(flops=flops, bytes_accessed=total if flops else 0, transcendentals=0),
    )(*args)


def local(pair_acts, pair_mask, crop_length, cotangent, in_weights, out_weight):
    size, _, channels = pair_acts.shape
    pairs = size * size
    n = lax.axis_size("row")
    tile = jax.ShapeDtypeStruct((size, size, channels), bf16)
    flat = jax.ShapeDtypeStruct((pairs, channels), f32)

    wide = jax.ShapeDtypeStruct((size, size, channels), f32)
    panel = jax.ShapeDtypeStruct((n * size, size, channels), f32)
    work = 2 * size * pairs * channels
    wait = 2**31
    steps = [step for bit in range(n.bit_length() - 2, -1, -1) for step in range(2**bit, 2 ** (bit + 1))]
    row_steps = steps
    gather_steps = [n - 1] + list(range(1, n - 1))


    def swap(values, axis, step):
        return lax.ppermute(values, axis, [(a, a ^ step) for a in range(n)])

    def gather(values, axis, steps):
        return [values] + [swap(values, axis, step) for step in steps]

    (left,) = call(
        left_kernel, (tile,), pair_acts, pair_mask, in_weights,
        hbm=(0, 1, 2), flops=2 * pairs * channels * 2 * channels,
        scratch=[
            pltpu.VMEM(pair_acts.shape, bf16),
            pltpu.VMEM(pair_mask.shape, jnp.int32),
            pltpu.VMEM((channels, 2 * channels), bf16),
            pltpu.SemaphoreType.DMA((3,)),
        ],
    )
    first_steps = list(range(n - 1, 0, -1))
    lefts = gather(left, "col", first_steps)
    right, normed, scale, factors, out_open, gate_factor, upstream = call(
        factors_kernel,
        (wide, flat, flat, jax.ShapeDtypeStruct((4, pairs, channels), f32), flat, flat, flat),
        pair_acts, pair_mask, crop_length, cotangent, in_weights, out_weight,
        smem=(2,), hbm=(0, 1, 3, 4, 5), flops=2 * pairs * channels * 6 * channels,
        scratch=[
            pltpu.VMEM(pair_acts.shape, bf16),
            pltpu.VMEM(pair_mask.shape, jnp.int32),
            pltpu.VMEM(cotangent.shape, bf16),
            pltpu.VMEM(in_weights.shape, bf16),
            pltpu.VMEM(out_weight.shape, bf16),
            pltpu.SemaphoreType.DMA((5,)),
        ],
    )
    order = [0] + first_steps
    parts = [
        call(
            functools.partial(partial_kernel, [order[at]]), (tile,), crop_length, lefts[at], right, smem=(0,),
            flops=work, scratch=[pltpu.VMEM(wide.shape, f32)],
        )[0]
        for at in range(n - 2)
    ]
    total, *parts = call(
        functools.partial(last_partial_kernel, order[-2:], order[:-2], [0] + row_steps),
        (wide,) + (tile,) * (n - 1), crop_length, *lefts[-2:], right, *parts, smem=(0,), flops=work,
        scratch=[pltpu.VMEM(wide.shape, f32), pltpu.VMEM((2,) + wide.shape, bf16)],
    )
    (left_panel,) = call(
        functools.partial(left_panel_kernel, [0] + first_steps), (panel,), crop_length, *lefts, smem=(0,)
    )
    last = []
    for step, part in zip(row_steps, parts):
        part = swap(part, "row", step)
        if step in row_steps[-2:]:
            last.append(part)
        else:
            (total,) = call(add_kernel, (wide,), total, part, flops=wait)
    tri_normed, tri_grad = call(
        triangle_kernel, (flat, tile), total, *last, upstream, flops=20 * pairs * channels,
    )
    grads = gather(tri_grad, "row", gather_steps)
    update, partial = call(
        update_kernel, (tile, flat), tri_normed, out_open, gate_factor, in_weights, out_weight,
        flops=4 * pairs * channels * channels,
    )
    means, slopes = call(
        slopes_kernel, (jax.ShapeDtypeStruct((8, 2 * channels), f32), jax.ShapeDtypeStruct((pairs, 2 * channels), f32)),
        normed, in_weights,
    )
    (right_grad,) = call(functools.partial(right_grad_kernel, [0]), (wide,), left_panel, tri_grad)
    terms, before = [], (partial, right_grad, slopes)
    for grad in grads[:-1]:
        before = call(
            left_terms_kernel, (tile,), grad, right, *before,
            scratch=[pltpu.VMEM((pairs, channels), f32)], flops=work,
        )
        terms += before
    total, *terms = call(
        functools.partial(last_terms_kernel, [0] + gather_steps[:-1], gather_steps[-1], [0] + steps),
        (wide,) + (tile,) * (n - 1), grads[-1], right, *terms, flops=work,
        scratch=[pltpu.VMEM(tile.shape, bf16), pltpu.VMEM((pairs, channels), f32)],
    )
    last = []
    for step, term in zip(steps, terms):
        term = swap(term, "col", step)
        if step in steps[-2:]:
            last.append(term)
        else:
            (total,) = call(add_kernel, (wide,), total, term, flops=wait)
    (done,) = call(
        functools.partial(right_back_kernel, gather_steps), (flat,),
        left_panel, *grads[1:], right_grad, factors, in_weights, partial, normed, scale,
        scratch=[pltpu.VMEM(wide.shape, f32)],
    )
    (pair_grad,) = call(
        back_kernel, (tile,), total, *last, normed, scale, factors, done, means, slopes, in_weights,
        flops=2 * pairs * channels * 2 * channels,
    )
    return (update, pair_grad)


def solution(mesh):
    return jax.shard_map(
        local,
        mesh=mesh,
        in_specs=(
            P(("group", "row"), "col", None),
            P(("group", "row"), "col"),
            P("group"),
            P(("group", "row"), "col", None),
            P(),
            P(),
        ),
        out_specs=(P(("group", "row"), "col", None), P(("group", "row"), "col", None)),
        check_vma=False,
    )
```

```python
import functools

import jax
import jax.numpy as jnp
from jax import lax
from jax.experimental import pallas as pl
from jax.experimental.pallas import tpu as pltpu
from jax.sharding import PartitionSpec as P

epsilon = 1e-05
f32 = jnp.float32
bf16 = jnp.bfloat16


def mean_lanes(values):
    return jnp.sum(values, axis=-1, keepdims=True) * (1.0 / values.shape[-1])


def normalize(values):
    center = values - mean_lanes(values)
    variance = mean_lanes(center * center)
    scale = lax.rsqrt(variance + epsilon)
    return (center * scale, scale)


def normalize_back(normed, scale, upstream):
    average = mean_lanes(upstream)
    project = mean_lanes(upstream * normed)
    return scale * (upstream - average - normed * project)


def sigmoid(values):
    return 1.0 / (1.0 + jnp.exp(-values))


def dot(a, b):
    return jnp.dot(a, b, preferred_element_type=f32)


def dot_t(a, b):
    return lax.dot_general(a, b, (((1,), (1,)), ((), ())), preferred_element_type=f32)


def live_pairs(crop_ref, row, col, shape):
    rows = row * shape[0] + lax.broadcasted_iota(jnp.int32, shape, 0)
    cols = col * shape[1] + lax.broadcasted_iota(jnp.int32, shape, 1)
    return jnp.where(jnp.maximum(rows, cols) < crop_ref[0], 1.0, 0.0)


def spread(mask, channels):
    size = mask.shape[0]
    shape = (size, size, size)
    diagonal = lax.broadcasted_iota(jnp.int32, shape, 1) == lax.broadcasted_iota(jnp.int32, shape, 2)
    picked = jnp.where(diagonal, jnp.broadcast_to(mask[:, None, :], shape), 0.0)
    rows = jnp.sum(picked, axis=-1, keepdims=True)
    return jnp.broadcast_to(rows, (size, size, channels)).reshape(size * size, channels)


def start_copies(sems, *pairs):
    copies = [pltpu.make_async_copy(src, dst, sems.at[n]) for n, (src, dst) in enumerate(pairs)]
    for copy in copies:
        copy.start()
    return copies


def gated(projected, block, keep):
    channels = keep.shape[1]
    value = projected[:, block * channels : (block + 1) * channels]
    opened = sigmoid(projected[:, (block + 1) * channels : (block + 2) * channels])
    return (opened * value * keep).astype(bf16), opened, value


def left_kernel(acts_in, mask_in, weights_in, left_ref, acts_ref, mask_ref, weights_ref, sems):
    size, _, channels = acts_ref.shape
    copies = start_copies(
        sems, (acts_in, acts_ref), (weights_in.at[:, pl.ds(0, 2 * channels)], weights_ref), (mask_in, mask_ref),
    )
    copies[0].wait()
    normed, _ = normalize(acts_ref[...].astype(f32).reshape(size * size, channels))
    normed = normed.astype(bf16)
    for copy in copies[1:]:
        copy.wait()
    left, _, _ = gated(dot(normed, weights_ref[...]), 0, spread(mask_ref[...].astype(f32), channels))
    left_ref[...] = left.reshape(size, size, channels)


def factors_kernel(
    acts_in, mask_in, crop_ref, cotangent_in, weights_in, out_weight_in,
    right_ref, normed_ref, scale_ref, factor_ref, open_ref, gate_factor_ref, upstream_ref,
    acts_ref, mask_ref, cotangent_ref, weights_ref, out_weight_ref, sems,
):
    copies = start_copies(
        sems, (acts_in, acts_ref), (weights_in, weights_ref), (mask_in, mask_ref),
        (cotangent_in, cotangent_ref), (out_weight_in, out_weight_ref),
    )
    size, _, channels = acts_ref.shape
    pairs = size * size
    copies[0].wait()
    normed, scale = normalize(acts_ref[...].astype(f32).reshape(pairs, channels))
    normed_ref[...] = normed
    scale_ref[...] = jnp.broadcast_to(scale, (pairs, channels))
    for copy in copies[1:]:
        copy.wait()
    projected = dot(normed.astype(bf16), weights_ref[...])
    live = live_pairs(crop_ref, lax.axis_index("row"), lax.axis_index("col"), (size, size))
    keep = spread(mask_ref[...].astype(f32) * live, channels)
    for block in (0, 2):
        tile, opened, value = gated(projected, block, keep)
        factor_ref[block] = keep * opened
        factor_ref[block + 1] = keep * value * opened * (1.0 - opened)
    right_ref[...] = tile.astype(f32).reshape(size, size, channels)
    out_open = sigmoid(projected[:, 4 * channels :])
    cotangent = cotangent_ref[...].astype(f32).reshape(pairs, channels)
    lin_grad = (cotangent * out_open).astype(bf16)
    open_ref[...] = out_open
    gate_factor_ref[...] = cotangent * out_open * (1.0 - out_open)
    upstream = dot_t(lin_grad, out_weight_ref[...])
    upstream_ref[...] = upstream - mean_lanes(upstream)


def weighted_sums(weights, start, terms, out, base=None):
    def step(k, _):
        total = weights[start + k, pl.ds(0, 1), :] * terms[0]
        for n in range(1, len(terms)):
            total = total + weights[start + k, pl.ds(n, 1), :] * terms[n]
        if base is not None:
            total = total + base[k]
        out[k] = total.astype(out.dtype)
        return 0

    lax.fori_loop(0, out.shape[0], step, 0, unroll=16)


def left_panel_kernel(steps, crop_ref, *refs):
    row, col, panel = lax.axis_index("row"), lax.axis_index("col"), refs[-1]
    size, _, channels = refs[0].shape
    rows = row * size + lax.broadcasted_iota(jnp.int32, (size, 1, channels), 0)
    row_live = jnp.where(rows < crop_ref[0], 1.0, 0.0)
    for step, ref in zip(steps, refs):
        place = col ^ step
        cols = place * size + lax.broadcasted_iota(jnp.int32, (1, size, channels), 1)
        col_live = jnp.where(cols < crop_ref[0], 1.0, 0.0)
        panel[pl.ds(place * size, size)] = ref[...].astype(f32) * (row_live * col_live)


def partial_kernel(steps, crop_ref, *refs):
    count = len(steps)
    lefts, right_ref, outs, left = refs[:count], refs[count], refs[count + 1 : -1], refs[-1]
    size, _, channels = right_ref.shape
    rows = lax.axis_index("row") * size + lax.broadcasted_iota(jnp.int32, (size, 1, channels), 0)
    row_live = jnp.where(rows < crop_ref[0], 1.0, 0.0)
    for step, left_ref, out in zip(steps, lefts, outs):
        cols = (lax.axis_index("col") ^ step) * size + lax.broadcasted_iota(jnp.int32, (1, size, channels), 1)
        left[...] = left_ref[...].astype(f32) * (row_live * jnp.where(cols < crop_ref[0], 1.0, 0.0))

        def add(k, sums):
            other = right_ref[k]
            return tuple(sums[i] + left[k, pl.ds(i, 1), :] * other for i in range(size))

        zero = jnp.zeros((size, channels), f32)
        sums = lax.fori_loop(0, size, add, (zero,) * size, unroll=16)
        for i in range(size):
            out[i] = sums[i].astype(out.dtype)


def pick_kernel(steps, *refs):
    here = lax.axis_index("row") ^ lax.axis_index("col")
    tiles, outs = refs[: len(steps)], refs[len(steps) :]
    for step, out in zip(steps, outs):
        for other, tile in enumerate(tiles):

            @pl.when((here ^ step) == other)
            def _():
                out[...] = tile[...].astype(out.dtype)


def last_partial_kernel(steps, early, row_steps, crop_ref, *refs):
    count, known = len(steps), len(early)
    left, parts = refs[-2:]
    partial_kernel(steps, crop_ref, *refs[: count + 1], *(parts.at[at] for at in range(count)), left)
    tiles = dict(zip(early, refs[count + 1 : count + 1 + known]))
    tiles.update((step, parts.at[at]) for at, step in enumerate(steps))
    pick_kernel(row_steps, *(tiles[step] for step in range(count + known)), *refs[count + 1 + known : -2])


def triangle_kernel(base, *refs):
    *tiles, upstream_ref, tri_normed_ref, grad_ref = refs
    size = grad_ref.shape[0]
    for i in range(size):
        total = base[i]
        for ref in tiles:
            total = total + ref[i].astype(f32)
        here = pl.ds(i * size, size)
        upstream = upstream_ref[here, :]
        center = total - mean_lanes(total)
        scale = lax.rsqrt(mean_lanes(center * center) + epsilon)
        tri_normed = center * scale
        tri_normed_ref[i] = tri_normed.astype(bf16)
        project = mean_lanes(center * upstream) * scale
        grad_ref[i] = (scale * (upstream - tri_normed * project)).astype(bf16)


def left_terms_kernel(grad_ref, right, *refs):
    out, grad = refs[-2:]
    size, _, channels = out.shape
    grad[...] = grad_ref[...].astype(f32).reshape(size * size, channels)
    weighted_sums(right, 0, [grad[pl.ds(j, size, stride=size), :] for j in range(size)], out)


def last_terms_kernel(early, last, steps, grad_ref, right, *refs):
    known = len(early)
    term, grad = refs[-2:]
    left_terms_kernel(grad_ref, right, term, grad)
    tiles = dict(zip(early, refs[:known]))
    tiles[last] = term
    pick_kernel(steps, *(tiles[step] for step in range(known + 1)), *refs[known:-2])


def right_grad_kernel(steps, panel, *refs):
    out, base = refs[-1], refs[len(steps)] if len(refs) > len(steps) + 1 else None
    size = out.shape[0]
    for step, grad in zip(steps, refs):
        start = (lax.axis_index("row") ^ step) * size
        weighted_sums(panel, start, [grad[i].astype(f32) for i in range(size)], out, base)
        base = out


def right_back_kernel(steps, panel, *refs):
    factor_ref, weights_ref, share_ref, normed_ref, scale_ref, out, right_ref = refs[-7:]
    right_grad_kernel(steps, panel, *refs[: len(steps) + 1], right_ref)
    pairs, channels = out.shape
    right = right_ref[...].reshape(pairs, channels)
    grads = jnp.concatenate([(right * factor_ref[block]).astype(bf16) for block in (2, 3)], axis=1)
    share = share_ref[...] + dot_t(grads, weights_ref[:, 2 * channels : 4 * channels])
    out[...] = normalize_back(normed_ref[...], scale_ref[...], share)


def slopes_kernel(normed_ref, weights_ref, mean_ref, slope_ref):
    channels = normed_ref.shape[1]
    weights = weights_ref[:, : 2 * channels].astype(f32)
    mean = jnp.sum(weights, axis=0, keepdims=True) * (1.0 / channels)
    mean_ref[...] = jnp.broadcast_to(mean, mean_ref.shape)
    slope = jnp.dot(normed_ref[...], weights, precision=lax.Precision.HIGHEST, preferred_element_type=f32)
    slope_ref[...] = slope * (1.0 / channels)


def add_kernel(base, tile_ref, out):
    out[...] = base[...] + tile_ref[...].astype(f32)


def update_kernel(
    tri_normed_ref, open_ref, gate_factor_ref, weights_ref, out_weight_ref, update_ref, normed_grad_ref
):
    size, _, channels = update_ref.shape
    linear = dot(tri_normed_ref[...].reshape(size * size, channels), out_weight_ref[...])
    update = (open_ref[...] * linear).astype(bf16)
    update_ref[...] = update.reshape(size, size, channels)
    out_gate_grad = (gate_factor_ref[...] * linear).astype(bf16)
    normed_grad_ref[...] = dot_t(out_gate_grad, weights_ref[:, 4 * channels :])


def back_kernel(base, *refs):
    *tiles, normed_ref, scale_ref, factor_ref, done_ref, mean_ref, slope_ref, weights_ref, out = refs
    size, _, channels = out.shape
    pairs = size * size
    left = base[...]
    for ref in tiles:
        left = left + ref[...].astype(f32)
    left = left.reshape(pairs, channels)
    grads = jnp.concatenate([(left * factor_ref[block]).astype(bf16) for block in (0, 1)], axis=1)
    normed_grad = dot_t(grads, weights_ref[:, : 2 * channels])
    wide_grads = grads.astype(f32)
    average = jnp.sum(wide_grads * mean_ref[0:1, :], axis=-1, keepdims=True)
    project = jnp.sum(wide_grads * slope_ref[...], axis=-1, keepdims=True)
    back = done_ref[...] + scale_ref[...] * (normed_grad - average - normed_ref[...] * project)
    out[...] = back.astype(bf16).reshape(size, size, channels)


def call(kernel, outs, *args, scratch=(), flops=0, smem=(), hbm=()):
    spec = pl.BlockSpec(memory_space=pltpu.VMEM)
    total = sum(a.size * a.dtype.itemsize for a in (*args, *outs))
    specs = [spec] * len(args)
    for n in smem:
        specs[n] = pl.BlockSpec(memory_space=pltpu.SMEM)
    args = list(args)
    for n in hbm:
        specs[n] = pl.BlockSpec(memory_space=pltpu.HBM)
        args[n] = pltpu.with_memory_space_constraint(args[n], pltpu.HBM)
    return pl.pallas_call(
        kernel,
        out_shape=tuple(outs),
        in_specs=specs,
        out_specs=(spec,) * len(outs),
        scratch_shapes=scratch,
        compiler_params=pltpu.CompilerParams(vmem_limit_bytes=24 * 2**20),
        cost_estimate=pl.CostEstimate(flops=flops, bytes_accessed=total if flops else 0, transcendentals=0),
    )(*args)


def local(pair_acts, pair_mask, crop_length, cotangent, in_weights, out_weight):
    size, _, channels = pair_acts.shape
    pairs = size * size
    n = lax.axis_size("row")
    tile = jax.ShapeDtypeStruct((size, size, channels), bf16)
    flat = jax.ShapeDtypeStruct((pairs, channels), f32)

    wide = jax.ShapeDtypeStruct((size, size, channels), f32)
    panel = jax.ShapeDtypeStruct((n * size, size, channels), f32)
    work = 2 * size * pairs * channels
    wait = 2**31
    steps = [step for bit in range(n.bit_length() - 2, -1, -1) for step in range(2**bit, 2 ** (bit + 1))]
    row_steps = steps
    gather_steps = [n - 1] + list(range(1, n - 1))


    def swap(values, axis, step):
        return lax.ppermute(values, axis, [(a, a ^ step) for a in range(n)])

    def gather(values, axis, steps):
        return [values] + [swap(values, axis, step) for step in steps]

    (left,) = call(
        left_kernel, (tile,), pair_acts, pair_mask, in_weights,
        hbm=(0, 1, 2), flops=2 * pairs * channels * 2 * channels,
        scratch=[
            pltpu.VMEM(pair_acts.shape, bf16),
            pltpu.VMEM(pair_mask.shape, jnp.int32),
            pltpu.VMEM((channels, 2 * channels), bf16),
            pltpu.SemaphoreType.DMA((3,)),
        ],
    )
    lefts = gather(left, "col", steps)
    right, normed, scale, factors, out_open, gate_factor, upstream = call(
        factors_kernel,
        (wide, flat, flat, jax.ShapeDtypeStruct((4, pairs, channels), f32), flat, flat, flat),
        pair_acts, pair_mask, crop_length, cotangent, in_weights, out_weight,
        smem=(2,), hbm=(0, 1, 3, 4, 5), flops=2 * pairs * channels * 6 * channels,
        scratch=[
            pltpu.VMEM(pair_acts.shape, bf16),
            pltpu.VMEM(pair_mask.shape, jnp.int32),
            pltpu.VMEM(cotangent.shape, bf16),
            pltpu.VMEM(in_weights.shape, bf16),
            pltpu.VMEM(out_weight.shape, bf16),
            pltpu.SemaphoreType.DMA((5,)),
        ],
    )
    order = [0] + steps
    parts = [
        call(
            functools.partial(partial_kernel, [order[at]]), (tile,), crop_length, lefts[at], right, smem=(0,),
            flops=work, scratch=[pltpu.VMEM(wide.shape, f32)],
        )[0]
        for at in range(n - 2)
    ]
    total, *parts = call(
        functools.partial(last_partial_kernel, order[-2:], order[:-2], [0] + row_steps),
        (wide,) + (tile,) * (n - 1), crop_length, *lefts[-2:], right, *parts, smem=(0,), flops=work,
        scratch=[pltpu.VMEM(wide.shape, f32), pltpu.VMEM((2,) + wide.shape, bf16)],
    )
    (left_panel,) = call(
        functools.partial(left_panel_kernel, [0] + steps), (panel,), crop_length, *lefts, smem=(0,)
    )
    last = []
    for step, part in zip(row_steps, parts):
        part = swap(part, "row", step)
        if step in row_steps[-2:]:
            last.append(part)
        else:
            (total,) = call(add_kernel, (wide,), total, part, flops=wait)
    tri_normed, tri_grad = call(
        triangle_kernel, (tile, tile), total, *last, upstream, flops=20 * pairs * channels,
    )
    grads = gather(tri_grad, "row", gather_steps)
    update, partial = call(
        update_kernel, (tile, flat), tri_normed, out_open, gate_factor, in_weights, out_weight,
        flops=4 * pairs * channels * channels,
    )
    means, slopes = call(
        slopes_kernel, (jax.ShapeDtypeStruct((8, 2 * channels), f32), jax.ShapeDtypeStruct((pairs, 2 * channels), f32)),
        normed, in_weights,
    )
    (right_grad,) = call(functools.partial(right_grad_kernel, [0]), (wide,), left_panel, tri_grad)
    terms, before = [], (partial, right_grad, slopes)
    for grad in grads[:-1]:
        before = call(
            left_terms_kernel, (tile,), grad, right, *before,
            scratch=[pltpu.VMEM((pairs, channels), f32)], flops=work,
        )
        terms += before
    last_steps = list(range(n - 1, 0, -1))
    total, *terms = call(
        functools.partial(last_terms_kernel, [0] + gather_steps[:-1], gather_steps[-1], [0] + last_steps),
        (wide,) + (tile,) * (n - 1), grads[-1], right, *terms, flops=work,
        scratch=[pltpu.VMEM(tile.shape, bf16), pltpu.VMEM((pairs, channels), f32)],
    )
    last = []
    for step, term in zip(last_steps, terms):
        term = swap(term, "col", step)
        if step in last_steps[-2:]:
            last.append(term)
        else:
            (total,) = call(add_kernel, (wide,), total, term, flops=wait)
    (done,) = call(
        functools.partial(right_back_kernel, gather_steps), (flat,),
        left_panel, *grads[1:], right_grad, factors, in_weights, partial, normed, scale,
        scratch=[pltpu.VMEM(wide.shape, f32)],
    )
    (pair_grad,) = call(
        back_kernel, (tile,), total, *last, normed, scale, factors, done, means, slopes, in_weights,
        flops=2 * pairs * channels * 2 * channels,
    )
    return (update, pair_grad)


def solution(mesh):
    return jax.shard_map(
        local,
        mesh=mesh,
        in_specs=(
            P(("group", "row"), "col", None),
            P(("group", "row"), "col"),
            P("group"),
            P(("group", "row"), "col", None),
            P(),
            P(),
        ),
        out_specs=(P(("group", "row"), "col", None), P(("group", "row"), "col", None)),
        check_vma=False,
    )
```
